32 devices in a mesh: seq: 8 (over z, x), head: 4 (over y, core).
Axes of the slice: x: 2, y: 2, z: 4, core: 2. Of those that a mesh axis runs over, the one named last changes fastest.
Arguments:
- inputs: bfloat16 [6, 2, 1024, 768], P(None, None, 'seq', 'head'), may hold values from -15 to 15
- doc_lengths: int32 [6, 8], replicated, may hold values from 0 to 1024, as said below
- attn_gain: float32 [768], P('head'), may hold values from 0.5 to 1.5
- attn_bias: float32 [768], P('head'), may hold values from -2 to 2
- w_qkv: bfloat16 [768, 3, 768], P(None, None, 'head'), may hold values from -0.21875 to 0.21875
- w_out: bfloat16 [768, 768], P('head'), may hold values from -1.75 to 1.75
- ffn_gain: float32 [768], P('head'), may hold values from 0.5 to 1.5
- ffn_bias: float32 [768], P('head'), may hold values from -2 to 2
- w_up: bfloat16 [768, 3072], P(None, 'head'), may hold values from -0.21875 to 0.21875
- w_down: bfloat16 [3072, 768], P('head'), may hold values from -0.109375 to 0.109375
- cotangent: bfloat16 [6, 2, 1024, 768], P(None, None, 'seq', 'head'), may hold values from -6 to 6
Outputs:
- outputs: bfloat16 [6, 2, 1024, 768], P(None, None, 'seq', 'head')
- input_grad: float32 [6, 2, 1024, 768], P(None, None, 'seq', 'head')
- qkv_grad: float32 [768, 3, 768], P(None, None, 'head')
- out_grad: float32 [768, 768], P('head')
- up_grad: float32 [768, 3072], P(None, 'head')
- down_grad: float32 [3072, 768], P('head')
- attn_gain_grad: float32 [768], P('head')
- attn_bias_grad: float32 [768], P('head')
- ffn_gain_grad: float32 [768], P('head')
- ffn_bias_grad: float32 [768], P('head')
The draws below stay inside these ranges and needn't reach their ends.
Inputs may be any that keep to these rules, and one draw needn't show every extreme that they name: `doc_lengths`: each row sums to at most 1024. In one row, which one varies, the first entry is 1024 and the others are 0; in the other rows every entry is at least 64 and at most 128.
All inputs are finite; a program needn't handle non-finite values.
Results may differ from the reference program's by a relative error of at most 0.013.
Values may be sent and summed in bfloat16 or wider, within the bound.
A program may use at most 512 MiB of HBM per device.

```python
import jax
import jax.numpy as jnp
from jax import lax

D = 768
HEADS = 12
HEAD_DIM = 64
FF = 3072
BLOCK = 16
SEQS = 6
DOCS = 8
LEN = 1024


def draw_inputs(key, part):
    key = jax.random.fold_in(key, 11)
    shape = (SEQS, 2, LEN, D)
    feature_scale = 0.6 * 3.0 ** (jnp.arange(D, dtype=jnp.float32) / (D - 1))
    values = jax.random.normal(key, shape, jnp.float32) * feature_scale
    return values.astype(jnp.bfloat16)


def draw_doc_lengths(key, part):
    key = jax.random.fold_in(key, 5)
    pick_key, size_key = jax.random.split(key)
    chosen = jax.random.randint(pick_key, (), 0, SEQS)
    ragged = jax.random.randint(size_key, (SEQS, DOCS), LEN // (2 * DOCS), LEN // DOCS + 1)
    whole_row = jnp.where(jnp.arange(DOCS, dtype=jnp.int32) == 0, LEN, 0)
    picked = jnp.arange(SEQS, dtype=jnp.int32)[:, None] == chosen
    return jnp.where(picked, whole_row[None, :], ragged).astype(jnp.int32)


def level_of(stream_key, dims, cuts, low, largest):
    def one(axis_at, parts):
        steps = jax.random.uniform(jax.random.fold_in(jax.random.fold_in(stream_key, 6), axis_at), (parts,), jnp.float32, low / len(cuts), largest / len(cuts))
        return jnp.repeat(jnp.exp(steps), dims[axis_at] // parts).reshape((-1,) + (1,) * (len(dims) - axis_at - 1))

    level = one(*cuts[0])
    for cut in cuts[1:]:
        level = level * one(*cut)
    return level


def scatter_about(stream_key, extent, scale, bound, shards=(), kind=jnp.bfloat16):
    factor_of = level_of(stream_key, extent, shards, -0.22, 0.18) if shards else 1.0
    values = jax.random.normal(stream_key, extent, jnp.float32) * scale * factor_of
    return jnp.minimum(jnp.maximum(values, -bound), bound).astype(kind)


def setup_inputs(seed: int = 0) -> dict:
    keys = jax.random.split(jax.random.key(seed), 12)
    inputs = draw_inputs(jax.random.fold_in(keys[11], 71), 0)
    doc_lengths = draw_doc_lengths(jax.random.fold_in(keys[11], 71), 0)
    attn_gain = jnp.clip(1.0 + 0.1 * jax.random.normal(keys[2], (D,), jnp.float32), 0.5, 1.5)
    attn_bias = scatter_about(keys[3], (D,), 0.5, 2.0, ((0, 4),), jnp.float32)
    w_qkv = scatter_about(keys[4], (D, 3, HEADS * HEAD_DIM), D ** -0.5, 0.21875, ((2, 4),))
    w_out = scatter_about(keys[5], (HEADS * HEAD_DIM, D), (D // 64) ** -0.5, 1.75, ((0, 4),))
    ffn_gain = jnp.clip(1.0 + 0.1 * jax.random.normal(keys[6], (D,), jnp.float32), 0.5, 1.5)
    ffn_bias = scatter_about(keys[7], (D,), 0.5, 2.0, ((0, 4),), jnp.float32)
    w_up = scatter_about(keys[8], (D, FF), D ** -0.5, 0.21875, ((1, 4),))
    w_down = scatter_about(keys[9], (FF, D), FF ** -0.5, 0.109375, ((0, 4),))
    cotangent = scatter_about(keys[10], (SEQS, 2, LEN, D), 1.0, 6.0, ((2, 8), (3, 4)))
    return dict(inputs=inputs, doc_lengths=doc_lengths, attn_gain=attn_gain, attn_bias=attn_bias, w_qkv=w_qkv, w_out=w_out, ffn_gain=ffn_gain, ffn_bias=ffn_bias, w_up=w_up, w_down=w_down, cotangent=cotangent)


norm_eps = 1e-05
masked_score = -1e+30
rotary_base = 10000.0

@jax.custom_vjp
def low(v):
    return lax.optimization_barrier(v.astype(jnp.bfloat16)).astype(jnp.float32)

@jax.custom_vjp
def low_back(v):
    return v

def low_keep(v):
    return (low(v), None)

def low_pass(kept, grad):
    return (grad,)

def back_keep(v):
    return (v, None)

def back_low(kept, grad):
    return (low(grad),)
low.defvjp(low_keep, low_pass)
low_back.defvjp(back_keep, back_low)

def segment_ids(doc_lengths, positions):
    doc_ends = jnp.cumsum(doc_lengths, axis=1)
    return lax.optimization_barrier(jnp.sum((doc_ends[:, :, None] <= positions[None, None, :]).astype(jnp.int32), axis=1))

def rotate(values, positions, sign):
    half_dim = values.shape[-1] // 2
    freqs = rotary_base ** (-jnp.arange(half_dim, dtype=jnp.float32) / half_dim)
    angles = positions.astype(jnp.float32)[:, None, None] * freqs
    cosine = jnp.cos(angles)
    sine = sign * jnp.sin(angles)
    first_half = values[..., :half_dim]
    second_half = values[..., half_dim:]
    return jnp.concatenate([first_half * cosine - second_half * sine, second_half * cosine + first_half * sine], axis=-1)

def layer_norm(values, gain, bias):
    mean_value = lax.optimization_barrier(jnp.mean(values, axis=-1, keepdims=True))
    variance = lax.optimization_barrier(jnp.mean(values * values, axis=-1, keepdims=True)) - mean_value * mean_value
    return (values - mean_value) * lax.rsqrt(variance + norm_eps) * gain + bias

def attend(queries, key_rows, value_rows, segments):
    seq_count = queries.shape[0]
    length = queries.shape[2]
    total_rows = 2 * length
    block_rows = min(512, total_rows)
    block_count = total_rows // block_rows
    flat_queries = queries.reshape(seq_count * block_count, block_rows, HEADS, HEAD_DIM)
    flat_keys = key_rows.reshape(seq_count, total_rows, HEADS, HEAD_DIM)
    flat_values = value_rows.reshape(seq_count, total_rows, HEADS, HEAD_DIM)
    key_pos = jnp.tile(jnp.arange(length, dtype=jnp.int32), 2)
    key_copy = jnp.repeat(jnp.arange(2, dtype=jnp.int32), length)
    block_ids = jnp.arange(seq_count * block_count, dtype=jnp.int32)

    @jax.checkpoint
    def one_block(block_item):
        block_query, block_id = block_item
        seq_id = block_id // block_count
        row_ids = block_id % block_count * block_rows + jnp.arange(block_rows, dtype=jnp.int32)
        query_copy = row_ids // length
        query_pos = row_ids % length
        seg_row = segments[seq_id]
        query_seg = seg_row[query_pos]
        key_seg = seg_row[key_pos]
        query_block = (query_pos // BLOCK)[:, None]
        key_block = (key_pos // BLOCK)[None, :]
        noisy_rule = jnp.where(key_copy[None, :] == 0, key_block == query_block, key_block < query_block)
        clean_rule = jnp.logical_and(key_copy[None, :] == 1, key_block <= query_block)
        allowed = jnp.where(query_copy[:, None] == 0, noisy_rule, clean_rule)
        allowed = jnp.logical_and(allowed, query_seg[:, None] == key_seg[None, :])
        key_block_rows = flat_keys[seq_id]
        value_block_rows = flat_values[seq_id]
        scores = low_back(jnp.einsum('qhd,khd->hqk', block_query, key_block_rows, precision=lax.Precision.HIGHEST))
        masked = jnp.where(allowed[None], scores, masked_score)
        row_max = lax.optimization_barrier(jnp.max(masked, axis=-1, keepdims=True))
        expon = jnp.exp(masked - row_max)
        probs = expon / lax.optimization_barrier(jnp.sum(expon, axis=-1, keepdims=True))
        return jnp.einsum('hqk,khd->qhd', probs, value_block_rows, precision=lax.Precision.HIGHEST)
    result = lax.map(one_block, (flat_queries, block_ids))
    return result.reshape(seq_count, 2, length, HEADS, HEAD_DIM)

def reference(inputs, doc_lengths, attn_gain, attn_bias, w_qkv, w_out, ffn_gain, ffn_bias, w_up, w_down, cotangent):
    positions = jnp.arange(LEN, dtype=jnp.int32)
    segments = segment_ids(doc_lengths, positions)
    highest = lax.Precision.HIGHEST

    def forward(values, gain_one, bias_one, qkv_weight, out_weight, gain_two, bias_two, up_weight, down_weight):
        normed_one = low(layer_norm(values, gain_one, bias_one))
        projected = low_back(jnp.einsum('scld,dtk->scltk', normed_one, qkv_weight, precision=highest))
        split_rows = projected.reshape(SEQS, 2, LEN, 3, HEADS, HEAD_DIM)
        queries = low(rotate(split_rows[:, :, :, 0], positions, 1.0) * HEAD_DIM ** (-0.5))
        key_rows = low(rotate(split_rows[:, :, :, 1], positions, 1.0))
        value_rows = low(split_rows[:, :, :, 2])
        attended = attend(queries, key_rows, value_rows, segments)
        attended_low = low_back(low(attended))
        out_heads = out_weight.reshape(HEADS, HEAD_DIM, D)
        attn_branch = low_back(jnp.einsum('sclhd,hdm->sclm', attended_low, out_heads, precision=highest))
        hidden_res = values + attn_branch
        normed_two = low(layer_norm(hidden_res, gain_two, bias_two))
        up_value = low_back(jnp.einsum('scld,df->sclf', normed_two, up_weight, precision=highest))
        activated = low(jax.nn.gelu(up_value, approximate=True))
        ffn_branch = low_back(jnp.einsum('sclf,fm->sclm', activated, down_weight, precision=highest))
        return hidden_res + ffn_branch
    outputs, pullback = jax.vjp(forward, inputs.astype(jnp.float32), attn_gain, attn_bias, w_qkv.astype(jnp.float32), w_out.astype(jnp.float32), ffn_gain, ffn_bias, w_up.astype(jnp.float32), w_down.astype(jnp.float32))
    grads = pullback(cotangent.astype(jnp.float32))
    return (outputs.astype(jnp.bfloat16), grads[0], grads[3], grads[4], grads[7], grads[8], grads[1], grads[2], grads[5], grads[6])
```

```python
import functools

import jax
import jax.numpy as jnp
from jax import lax
from jax.experimental import pallas as pl
from jax.experimental.pallas import tpu as pltpu
from jax.sharding import PartitionSpec as P

D = 768
HEAD_DIM = 64
BLOCK = 16


norm_eps = 1e-05
masked_score = -1e30
rotary_base = 10000.0

MESH = pl.DeviceIdType.MESH
VMEM = pltpu.VMEM
F32 = jnp.float32
BF16 = jnp.bfloat16
ROWS_LIMIT = 16 << 20
VMEM_LIMIT = 60 << 20


def passed_along(block, axis, distance):
    devices = range(lax.axis_size(axis))
    route = [(i - distance, i) for i in devices if i - distance in devices]
    return lax.ppermute(block, axis, route)


def from_behind(x, axis, by):
    devices = lax.axis_size(axis)
    return lax.ppermute(x, axis, [(i, (i + by) % devices) for i in range(devices)])


def segment_ids(doc_lengths, positions):
    doc_ends = jnp.cumsum(doc_lengths, axis=1)
    return jnp.sum((doc_ends[:, :, None] <= positions[None, None, :]).astype(jnp.int32), axis=1)


def rotate(values, positions, sign):
    half_dim = values.shape[-1] // 2
    freqs = rotary_base ** (-jnp.arange(half_dim, dtype=jnp.float32) / half_dim)
    angles = positions.astype(jnp.float32)[:, None, None] * freqs
    cosine = jnp.cos(angles)
    sine = sign * jnp.sin(angles)
    first_half = values[..., :half_dim]
    second_half = values[..., half_dim:]
    return jnp.concatenate(
        [first_half * cosine - second_half * sine, second_half * cosine + first_half * sine],
        axis=-1,
    )


def row_pair(first_sum, second_sum):
    return lax.psum((first_sum, second_sum), "head")


def normalize(share, gain, bias):
    row_total, row_square = row_pair(jnp.sum(share, axis=-1), jnp.sum(share * share, axis=-1))
    mean_value = row_total / D
    inv_std = lax.rsqrt(row_square / D - mean_value * mean_value + norm_eps)
    centered = (share - mean_value[..., None]) * inv_std[..., None]
    scaled = (centered * gain + bias).astype(jnp.bfloat16)
    gathered = lax.all_gather(scaled, "head", axis=3, tiled=True)
    return (gathered, centered, inv_std)


def norm_backward(partial_value, gain, centered, inv_std):
    share = lax.psum_scatter(partial_value, "head", scatter_dimension=3, tiled=True)
    scaled = share * gain
    first_mean, second_mean = row_pair(
        jnp.sum(scaled, axis=-1), jnp.sum(scaled * centered, axis=-1)
    )
    grad_in = inv_std[..., None] * (
        scaled - first_mean[..., None] / D - centered * (second_mean[..., None] / D)
    )
    gain_grad = jnp.sum(share * centered, axis=(0, 1, 2))
    bias_grad = jnp.sum(share, axis=(0, 1, 2))
    return (grad_in, gain_grad, bias_grad)


def branch_total(partial_value):
    return lax.psum_scatter(partial_value, "head", scatter_dimension=3, tiled=True)


def gradient_rows(share):
    return lax.all_gather(share, "head", axis=3, tiled=True)


def mask_rule(query_pos, query_seg, key_pos, key_seg):
    query_block = (query_pos // BLOCK)[:, None]
    key_block = (key_pos // BLOCK)[None, :]
    order = jnp.stack([key_block < query_block, key_block <= query_block])
    same_doc = query_seg[:, :, None] == key_seg[:, None, :]
    return jnp.logical_and(order[None, :, None], same_doc[:, None, None])


def absorb(state_now, scores, allowed, value_piece):
    run_max, run_sum, run_acc = state_now
    masked = jnp.where(allowed, scores, masked_score)
    new_max = jnp.maximum(run_max, jnp.max(masked, axis=-1))
    weights_now = jnp.where(allowed, jnp.exp(masked - new_max[..., None]), 0.0)
    factor = jnp.exp(run_max - new_max)
    new_sum = run_sum * factor + jnp.sum(weights_now, axis=-1)
    added = jnp.einsum(
        "schlk,skhd->schld",
        weights_now,
        value_piece.astype(jnp.float32),
        precision=lax.Precision.HIGHEST,
    )
    return (new_max, new_sum, run_acc * factor[..., None] + added)


def gathered_body(
    inputs,
    doc_lengths,
    attn_gain,
    attn_bias,
    w_qkv,
    w_out,
    ffn_gain,
    ffn_bias,
    w_up,
    w_down,
    cotangent,
):
    seqs_here, _, local_len, _ = inputs.shape
    head_local = w_qkv.shape[2] // HEAD_DIM
    first_pos = lax.axis_index("seq") * local_len
    positions = first_pos + jnp.arange(local_len, dtype=jnp.int32)
    segments = segment_ids(doc_lengths, positions)
    inputs_wide = inputs.astype(jnp.float32)
    normed_one, centered_one, inv_one = normalize(inputs_wide, attn_gain, attn_bias)
    projected = jnp.einsum("scld,dtk->scltk", normed_one, w_qkv, preferred_element_type=jnp.float32)
    split_rows = projected.reshape(seqs_here, 2, local_len, 3, head_local, HEAD_DIM)
    queries = (rotate(split_rows[:, :, :, 0], positions, 1.0) * HEAD_DIM ** (-0.5)).astype(
        jnp.bfloat16
    )
    key_rows = rotate(split_rows[:, :, :, 1], positions, 1.0).astype(jnp.bfloat16)
    value_rows = split_rows[:, :, :, 2].astype(jnp.bfloat16)
    clean_keys = key_rows[:, 1].reshape(seqs_here, local_len, head_local * HEAD_DIM)
    clean_values = value_rows[:, 1].reshape(seqs_here, local_len, head_local * HEAD_DIM)
    block_ids = positions // BLOCK
    own_allowed = jnp.logical_and(
        (block_ids[:, None] == block_ids[None, :])[None],
        segments[:, :, None] == segments[:, None, :],
    )[:, None, None]
    noisy_scores = jnp.einsum(
        "sclhd,skhd->schlk", queries[:, :1], key_rows[:, 0], preferred_element_type=jnp.float32
    )
    half_shape = (seqs_here, 1, head_local, local_len)
    empty_state = (
        jnp.full(half_shape, masked_score, jnp.float32),
        jnp.zeros(half_shape, jnp.float32),
        jnp.zeros(half_shape + (HEAD_DIM,), jnp.float32),
    )
    noisy_state = absorb(empty_state, noisy_scores, own_allowed, value_rows[:, 0])
    start_state = jax.tree.map(
        lambda first, second: jnp.concatenate([first, second], axis=1), noisy_state, empty_state
    )
    piece_keys = lax.all_gather(clean_keys, "seq", axis=1, tiled=True)
    piece_values = lax.all_gather(clean_values, "seq", axis=1, tiled=True)
    piece_len = piece_keys.shape[1]
    key_pos = jnp.arange(piece_len, dtype=jnp.int32)
    key_seg = segment_ids(doc_lengths, key_pos)
    key_heads = piece_keys.reshape(seqs_here, piece_len, head_local, HEAD_DIM)
    value_heads = piece_values.reshape(seqs_here, piece_len, head_local, HEAD_DIM)
    scores = jnp.einsum("sclhd,skhd->schlk", queries, key_heads, preferred_element_type=jnp.float32)
    final_max, final_sum, final_acc = absorb(
        start_state, scores, mask_rule(positions, segments, key_pos, key_seg), value_heads
    )
    attended = final_acc / final_sum[..., None]
    log_total = final_max + jnp.log(final_sum)
    attended_low = attended.astype(jnp.bfloat16)
    out_heads = w_out.reshape(head_local, HEAD_DIM, w_out.shape[1])
    attn_share = branch_total(
        jnp.einsum("schld,hdm->sclm", attended_low, out_heads, preferred_element_type=jnp.float32)
    )
    hidden_res = inputs_wide + attn_share
    normed_two, centered_two, inv_two = normalize(hidden_res, ffn_gain, ffn_bias)
    up_value = jnp.einsum("scld,df->sclf", normed_two, w_up, preferred_element_type=jnp.float32)
    activated, gelu_back = jax.vjp(lambda inner: jax.nn.gelu(inner, approximate=True), up_value)
    act_low = activated.astype(jnp.bfloat16)
    ffn_share = branch_total(
        jnp.einsum("sclf,fm->sclm", act_low, w_down, preferred_element_type=jnp.float32)
    )
    outputs = (hidden_res + ffn_share).astype(jnp.bfloat16)
    grad_out = cotangent.astype(jnp.float32)
    grad_full = gradient_rows(cotangent)
    down_grad = jnp.einsum("sclf,sclm->fm", act_low, grad_full, preferred_element_type=jnp.float32)
    act_grad = jnp.einsum("sclm,fm->sclf", grad_full, w_down, preferred_element_type=jnp.float32)
    up_pre_grad = gelu_back(act_grad)[0].astype(jnp.bfloat16)
    up_grad = jnp.einsum(
        "scld,sclf->df", normed_two, up_pre_grad, preferred_element_type=jnp.float32
    )
    normed_two_grad = jnp.einsum(
        "sclf,df->scld", up_pre_grad, w_up, preferred_element_type=jnp.float32
    )
    back_two, ffn_gain_grad, ffn_bias_grad = norm_backward(
        normed_two_grad, ffn_gain, centered_two, inv_two
    )
    resid_grad = grad_out + back_two
    resid_full = gradient_rows(resid_grad.astype(jnp.bfloat16))
    out_grad = jnp.einsum(
        "schld,sclm->hdm", attended_low, resid_full, preferred_element_type=jnp.float32
    ).reshape(w_out.shape)
    attended_grad = jnp.einsum(
        "sclm,hdm->schld", resid_full, out_heads, preferred_element_type=jnp.float32
    ).astype(jnp.bfloat16)
    grad_wide = attended_grad.astype(jnp.float32)
    row_delta = jnp.sum(grad_wide * attended, axis=-1)
    noisy_probs = jnp.where(own_allowed, jnp.exp(noisy_scores - log_total[:, :1, :, :, None]), 0.0)
    noisy_prob_grad = jnp.einsum(
        "schld,skhd->schlk",
        attended_grad[:, :1],
        value_rows[:, 0],
        preferred_element_type=jnp.float32,
    )
    noisy_score_grad = (noisy_probs * (noisy_prob_grad - row_delta[:, :1, :, :, None])).astype(
        jnp.bfloat16
    )
    noisy_query_grad = jnp.einsum(
        "schlk,skhd->schld", noisy_score_grad, key_rows[:, 0], preferred_element_type=jnp.float32
    )
    noisy_key_grad = jnp.einsum(
        "schlk,sclhd->skhd", noisy_score_grad, queries[:, :1], preferred_element_type=jnp.float32
    )
    noisy_value_grad = jnp.einsum(
        "schlk,schld->skhd", noisy_probs, grad_wide[:, :1], precision=lax.Precision.HIGHEST
    )
    query_start = jnp.concatenate([noisy_query_grad, jnp.zeros_like(noisy_query_grad)], axis=1)
    flat_zero = jnp.zeros((seqs_here, local_len, head_local * HEAD_DIM), jnp.float32)

    def piece_grads(piece_keys, piece_values, first_row, query_total):
        key_pos = first_row + jnp.arange(local_len, dtype=jnp.int32)
        key_seg = segment_ids(doc_lengths, key_pos)
        key_heads = piece_keys.reshape(seqs_here, local_len, head_local, HEAD_DIM)
        value_heads = piece_values.reshape(seqs_here, local_len, head_local, HEAD_DIM)
        scores = jnp.einsum(
            "sclhd,skhd->schlk", queries, key_heads, preferred_element_type=jnp.float32
        )
        allowed = mask_rule(positions, segments, key_pos, key_seg)
        weights_now = jnp.where(allowed, jnp.exp(scores - log_total[..., None]), 0.0)
        prob_grad = jnp.einsum(
            "schld,skhd->schlk", attended_grad, value_heads, preferred_element_type=jnp.float32
        )
        score_grad = (weights_now * (prob_grad - row_delta[..., None])).astype(jnp.bfloat16)
        query_out = query_total + jnp.einsum(
            "schlk,skhd->schld", score_grad, key_heads, preferred_element_type=jnp.float32
        )
        key_part = jnp.einsum(
            "schlk,sclhd->skhd", score_grad, queries, preferred_element_type=jnp.float32
        )
        value_part = jnp.einsum(
            "schlk,schld->skhd", weights_now, grad_wide, precision=lax.Precision.HIGHEST
        )
        return (key_part.reshape(flat_zero.shape), value_part.reshape(flat_zero.shape), query_out)

    def cycle_body(cycle_step, carried):
        piece_keys, piece_values, key_acc, value_acc, query_acc = carried
        source = (lax.axis_index("seq") - cycle_step) % lax.axis_size("seq")
        first_row = source * local_len
        key_part, value_part, query_acc = piece_grads(
            piece_keys, piece_values, first_row, query_acc
        )
        key_acc = key_acc + key_part
        value_acc = value_acc + value_part
        piece_keys, piece_values = passed_along((piece_keys, piece_values), "seq", 1)
        key_acc, value_acc = (
            from_behind(key_acc.astype(jnp.bfloat16), "seq", 1).astype(key_acc.dtype),
            from_behind(value_acc.astype(jnp.bfloat16), "seq", 1).astype(value_acc.dtype),
        )
        return (piece_keys, piece_values, key_acc, value_acc, query_acc)

    cycle_start = (clean_keys, clean_values, flat_zero, flat_zero, query_start)
    _, _, clean_key_grad, clean_value_grad, query_acc = lax.fori_loop(
        0, lax.axis_size("seq"), cycle_body, cycle_start
    )
    head_shape = (seqs_here, local_len, head_local, HEAD_DIM)
    query_total = rotate(jnp.transpose(query_acc, (0, 1, 3, 2, 4)), positions, -1.0) * HEAD_DIM ** (
        -0.5
    )
    key_total = rotate(
        jnp.stack([noisy_key_grad, clean_key_grad.reshape(head_shape)], axis=1), positions, -1.0
    )
    value_total = jnp.stack([noisy_value_grad, clean_value_grad.reshape(head_shape)], axis=1)
    qkv_pre_grad = (
        jnp.stack([query_total, key_total, value_total], axis=3)
        .reshape(seqs_here, 2, local_len, 3, head_local * HEAD_DIM)
        .astype(jnp.bfloat16)
    )
    qkv_grad = jnp.einsum(
        "scld,scltk->dtk", normed_one, qkv_pre_grad, preferred_element_type=jnp.float32
    )
    normed_one_grad = jnp.einsum(
        "scltk,dtk->scld", qkv_pre_grad, w_qkv, preferred_element_type=jnp.float32
    )
    back_one, attn_gain_grad, attn_bias_grad = norm_backward(
        normed_one_grad, attn_gain, centered_one, inv_one
    )
    input_grad = resid_grad + back_one
    (
        qkv_grad,
        out_grad,
        up_grad,
        down_grad,
        attn_gain_grad,
        attn_bias_grad,
        ffn_gain_grad,
        ffn_bias_grad,
    ) = lax.psum(
        (
            qkv_grad,
            out_grad,
            up_grad,
            down_grad,
            attn_gain_grad,
            attn_bias_grad,
            ffn_gain_grad,
            ffn_bias_grad,
        ),
        "seq",
    )
    return (
        outputs,
        input_grad,
        qkv_grad,
        out_grad,
        up_grad,
        down_grad,
        attn_gain_grad,
        attn_bias_grad,
        ffn_gain_grad,
        ffn_bias_grad,
    )


def dot(a, b, ca, cb):
    return lax.dot_general(a, b, (((ca,), (cb,)), ((), ())), preferred_element_type=F32)


def remote(src, dst, send, recv, device):
    return pltpu.make_async_remote_copy(
        src_ref=src, dst_ref=dst, send_sem=send, recv_sem=recv, device_id=device, device_id_type=MESH
    )


class Place:
    def __init__(self, n):
        self.n = n
        self.me = lax.axis_index("seq")
        self.head = lax.axis_index("head")
        self.core = lax.rem(self.head, 2)
        self.y = lax.div(self.head, 2)
        self.sib = (self.me, self.y * 2 + 1 - self.core)
        self.yp = (self.me, (1 - self.y) * 2 + self.core)
        self.diag = (self.me, (1 - self.y) * 2 + 1 - self.core)
        self.half = n // 2
        self.band = max(1, n // 8)

    def lowest(self, slot, i):
        near = i - self.band
        short = jnp.where(i >= self.half, jnp.minimum(near, self.half), near)
        return jnp.where(slot == 0, 0, jnp.maximum(short, 0))

    def greet(self, near, everyone):
        bar = pltpu.get_barrier_semaphore()
        for d in near:
            pl.semaphore_signal(bar, inc=1, device_id=d, device_id_type=MESH)
        count = len(near)
        if everyone:
            for d in range(1, self.n):
                there = lax.rem(self.me + d, self.n)
                pl.semaphore_signal(bar, inc=1, device_id=(there, self.head), device_id_type=MESH)
            count += self.n - 1
        pl.semaphore_wait(bar, count)


def each(count, step):
    def run(i, carry):
        step(i)
        return carry

    lax.fori_loop(0, count, run, 0)


def row_stats(x):
    mean = jnp.sum(x, axis=1, keepdims=True) / D
    var = jnp.sum(x * x, axis=1, keepdims=True) / D - mean * mean
    return mean, lax.rsqrt(var + norm_eps)


def whole_rows(ref, s):
    return jnp.concatenate([ref[s, 0], ref[s, 1]], axis=1)


def turn(v, cosine, sine):
    parts = []
    for h in range(v.shape[0] // HEAD_DIM):
        a = v[h * 64 : h * 64 + 32]
        b = v[h * 64 + 32 : h * 64 + 64]
        parts += [a * cosine - b * sine, b * cosine + a * sine]
    return jnp.concatenate(parts, axis=0)


def masks(me, length, start, end):
    shape = (length, 2 * length)
    key = lax.broadcasted_iota(jnp.int32, shape, 0)
    row = lax.broadcasted_iota(jnp.int32, shape, 1)
    noisy = row < length
    at = jnp.where(noisy, row, row - length)
    key_block = key >> 4
    row_block = at >> 4
    pos = key + me * length
    same = jnp.logical_and(pos >= start, pos < end)
    clean = jnp.logical_and(same, key_block < row_block + jnp.where(noisy, 0, 1))
    own = jnp.logical_and(same, key_block == row_block)[:, :length]
    return clean, own


def front(n, perm, x_in, c_in, gb_in, w_t, wo_in, cos, sin, bounds,
          xg, cg, ag, wog, gbf, n1, qt, kvn, kvo, kvb, att, lse,
          own, land, gland, acc, mrow, lrow,
          ss, sr, ys, yr, fs, fr, gs, gr, ws, wr, ks, kr):
    at = Place(n)
    slots, _, length, feat = x_in.shape
    rows = 2 * length
    hl = feat // HEAD_DIM
    core, y, me = at.core, at.y, at.me
    fulls = (xg, cg, ag)

    def sib_copy(k, s):
        return remote(own.at[k, s], land.at[k, s], ss.at[k, s], sr.at[k, s], at.sib)

    def build(k, s):
        a, b = own[k, s], land[k, s]

        @pl.when(core == 0)
        def _():
            fulls[k][s, y] = jnp.concatenate([a, b], axis=1)

        @pl.when(core == 1)
        def _():
            fulls[k][s, y] = jnp.concatenate([b, a], axis=1)

    def y_copy(k, s):
        part = fulls[k].at[s, y, pl.ds(length * core, length)]
        return remote(part, part, ys.at[k, s], yr.at[k, s], at.yp)

    def f_copy(k, s):
        part = fulls[k].at[s, 1 - y, pl.ds(length * core, length)]
        return remote(part, part, fs.at[k, s], fr.at[k, s], at.sib)

    def kv_copy(s, i):
        return remote(kvo.at[s], kvb.at[s, me], ks.at[s, i], kr.at[s, me], (i, at.head))

    at.greet([at.sib, at.yp, at.diag], True)

    def stage(s):
        own[0, s] = x_in[perm[s]].reshape(rows, feat)
        sib_copy(0, s).start()

    each(slots, stage)
    gland[at.head] = gb_in[...]
    g_copies = [
        remote(gb_in, gland.at[at.head], gs.at[k], gr.at[k], d)
        for k, d in enumerate((at.sib, at.yp, at.diag))
    ]
    for copy in g_copies:
        copy.start()

    def stage_cot(s):
        own[1, s] = c_in[perm[s]].reshape(rows, feat)
        sib_copy(1, s).start()

    def first_y(s):
        sib_copy(0, s).wait_recv()
        build(0, s)
        y_copy(0, s).start()

    each(slots, first_y)
    each(slots, stage_cot)
    for copy in g_copies:
        copy.wait()
    gbf[...] = jnp.concatenate([gland[i] for i in range(4)], axis=1)

    def project(s):
        x = whole_rows(xg, s).astype(F32)
        mean, inv = row_stats(x)
        normed = ((x - mean) * inv * gbf[0:1] + gbf[1:2]).astype(BF16)
        n1[s] = normed
        pt = dot(w_t[...], normed, 1, 1)
        qk = turn(pt[: 2 * feat], cos[...], sin[...])
        qt[s] = (qk[:feat] * HEAD_DIM**-0.5).astype(BF16)
        kv = jnp.concatenate([qk[feat:], pt[2 * feat :]], axis=0).astype(BF16)
        kvn[s] = kv[:, :length]
        kvo[s] = kv[:, length:]
        for d in range(1, n):
            i = me + d

            @pl.when(jnp.logical_and(i < n, at.lowest(s, i) <= me))
            def _():
                kv_copy(s, i).start()

    def arrive(t):
        @pl.when(t < slots)
        def _():
            y_copy(0, t).wait_recv()
            f_copy(0, t).start()

        @pl.when(t >= 1)
        def _():
            f_copy(0, t - 1).wait_recv()
            project(t - 1)

    each(slots + 1, arrive)

    def first_y_cot(s):
        sib_copy(1, s).wait_recv()
        build(1, s)
        y_copy(1, s).start()

    each(slots, first_y_cot)

    def wo_block(who):
        return wog.at[pl.ds(pl.multiple_of(feat * who, 16), feat)]

    wog[pl.ds(pl.multiple_of(feat * at.head, 16), feat)] = wo_in[...]
    wo_sib = remote(wo_in, wo_block(at.head), ws.at[0], wr.at[0], at.sib)
    wo_y = remote(wo_in, wo_block(at.head), ws.at[1], wr.at[1], at.yp)
    wo_f = remote(wo_block(at.yp[1]), wo_block(at.yp[1]), ws.at[2], wr.at[2], at.sib)
    wo_sib.start()
    wo_y.start()

    def absorb(s, h, keys, values, lanes, allowed, first):
        hd = slice(h * HEAD_DIM, (h + 1) * HEAD_DIM)
        sc = dot(keys[hd], qt[s, hd, lanes], 0, 0)
        sc = jnp.where(allowed, sc, masked_score)
        top = jnp.max(sc, axis=0, keepdims=True)
        if first:
            new = top
        else:
            old = mrow[h : h + 1, lanes]
            new = jnp.maximum(old, top)
            scale = jnp.exp(old - new)
        p = jnp.exp(sc - new)
        total = jnp.sum(p, axis=0, keepdims=True)
        add = dot(values[hd], p.astype(BF16), 1, 0)
        mrow[h : h + 1, lanes] = new
        if first:
            lrow[h : h + 1, lanes] = total
            acc[hd, lanes] = add
        else:
            lrow[h : h + 1, lanes] = lrow[h : h + 1, lanes] * scale + total
            acc[hd, lanes] = acc[hd, lanes] * scale + add

    every = slice(0, rows)

    def attend(s):
        start, end = bounds[s, 0:1], bounds[s, 1:2]
        clean, noisy = masks(me, length, start, end)
        kc, kn = kvo[s], kvn[s]
        for h in range(hl):
            absorb(s, h, kc[:feat], kc[feat:], every, clean, True)
            absorb(s, h, kn[:feat], kn[feat:], slice(0, length), noisy, False)

        def one(j, carry):
            remote(kvo.at[s], kvb.at[s, j], ks.at[s, j], kr.at[s, j], at.sib).wait_recv()
            kv = kvb[s, j]
            pos = lax.broadcasted_iota(jnp.int32, (length, rows), 0) + j * length
            allowed = pos >= start
            for h in range(hl):
                absorb(s, h, kv[:feat], kv[feat:], every, allowed, False)
            return carry

        lax.fori_loop(at.lowest(s, me), me, one, 0)
        for h in range(hl):
            hd = slice(h * HEAD_DIM, (h + 1) * HEAD_DIM)
            att[s, hd] = acc[hd] / lrow[h : h + 1]
        lse[s] = mrow[...] + jnp.log(lrow[...])
        own[2, s] = att[s].T.astype(BF16)
        sib_copy(2, s).start()

    mrow[...] = jnp.zeros_like(mrow)
    lrow[...] = jnp.ones_like(lrow)

    def second(t):
        @pl.when(t < slots)
        def _():
            attend(t)
            y_copy(1, t).wait_recv()
            f_copy(1, t).start()

        @pl.when(t >= 1)
        def _():
            sib_copy(2, t - 1).wait_recv()
            build(2, t - 1)
            y_copy(2, t - 1).start()

    each(slots + 1, second)
    wo_y.wait_recv()
    wo_f.start()

    def last(s):
        y_copy(2, s).wait_recv()
        f_copy(2, s).start()

    each(slots, last)

    def finish(s):
        for k in range(3):
            sib_copy(k, s).wait_send()
            y_copy(k, s).wait_send()
            f_copy(k, s).wait_send()
        f_copy(1, s).wait_recv()
        f_copy(2, s).wait_recv()
        for d in range(1, n):
            i = me + d

            @pl.when(jnp.logical_and(i < n, at.lowest(s, i) <= me))
            def _():
                kv_copy(s, i).wait_send()

    each(slots, finish)
    wo_sib.wait()
    wo_y.wait_send()
    wo_f.wait()


def middle(n, perm, xg, ag, cg, wog, gbf, wu, wd,
           out, rl, rf, up_g, dn_g, gsum,
           hid, n2, act, upre, ep, er, es, ey, ef, fp, fc, fh, fy, ob, osd,
           e1s, e1r, e2s, e2r, e3s, e3r, f1s, f1r, f2s, f2r, f3s, f3r):
    at = Place(n)
    slots, _, rows, half = xg.shape
    length = rows // 2
    feat = half // 2
    core, y = at.core, at.y
    mine = pl.ds(length * core, length)
    other = pl.ds(length * (1 - core), length)
    at.greet([at.sib, at.yp], False)

    def e_core(s):
        return remote(ep.at[s, other], er.at[s], e1s.at[s], e1r.at[s], at.sib)

    def e_y(s):
        return remote(es.at[s], ey.at[s], e2s.at[s], e2r.at[s], at.yp)

    def e_back(s):
        return remote(ef.at[s, mine], ef.at[s, mine], e3s.at[s], e3r.at[s], at.sib)

    def f_core(s):
        return remote(fp.at[s, other], fc.at[s], f1s.at[s], f1r.at[s], at.sib)

    def f_y(s):
        return remote(fh.at[s, 1 - y], fy.at[s], f2s.at[s], f2r.at[s], at.yp)

    def f_back(s):
        return remote(osd.at[s], ob.at[s, core], f3s.at[s], f3r.at[s], at.sib)

    def forward(s):
        x = whole_rows(xg, s).astype(F32)
        branch = dot(ag[s, 0], wog[:half], 1, 0) + dot(ag[s, 1], wog[half:], 1, 0)
        h = x + branch
        hid[s, 0] = h[:, :half]
        hid[s, 1] = h[:, half:]
        mean, inv = row_stats(h)
        normed = ((h - mean) * inv * gbf[2:3] + gbf[3:4]).astype(BF16)
        n2[s] = normed
        up = dot(normed, wu[...], 1, 0)
        cube = 0.7978845608028654 * (up + 0.044715 * up * up * up)
        t = jnp.tanh(cube)
        act[s] = (0.5 * up * (1.0 + t)).astype(BF16)
        slope = 0.5 * (1.0 + t) + 0.5 * up * (1.0 - t * t) * (
            0.7978845608028654 * (1.0 + 3 * 0.044715 * up * up)
        )
        da = dot(whole_rows(cg, s), wd[...], 1, 1)
        pre = (da * slope).astype(BF16)
        upre[s] = pre
        ep[s] = dot(pre, wu[...], 1, 1).astype(BF16)
        e_core(s).start()

    def loop_one(t):
        @pl.when(t < slots)
        def _():
            forward(t)

        @pl.when(t >= 1)
        def _():
            s = t - 1
            e_core(s).wait_recv()
            es[s] = (ep[s, mine].astype(F32) + er[s].astype(F32)).astype(BF16)
            e_y(s).start()

    each(slots + 1, loop_one)
    dn_g[...] = jnp.zeros_like(dn_g)
    up_g[...] = jnp.zeros_like(up_g)
    gsum[...] = jnp.zeros_like(gsum)

    def loop_two(t):
        @pl.when(t < slots)
        def _():
            fp[t] = dot(act[t], wd[...], 1, 0).astype(BF16)
            f_core(t).start()
            dn_g[...] += dot(act[t], whole_rows(cg, t), 0, 0)
            up_g[...] += dot(n2[t], upre[t], 0, 0)
            e_y(t).wait_recv()
            ef[t, mine] = (es[t].astype(F32) + ey[t].astype(F32)).astype(BF16)
            e_back(t).start()

        @pl.when(t >= 1)
        def _():
            s = t - 1
            f_core(s).wait_recv()
            both = fp[s, mine].astype(F32) + fc[s].astype(F32)
            fh[s, 0] = both[:, :half].astype(BF16)
            fh[s, 1] = both[:, half:].astype(BF16)
            f_y(s).start()

    each(slots + 1, loop_two)

    def loop_three(s):
        e_back(s).wait_recv()
        e = ef[s].astype(F32)
        h = whole_rows(hid, s)
        mean, inv = row_stats(h)
        xh = (h - mean) * inv
        gsum[0:1] += jnp.sum(e * xh, axis=0, keepdims=True)
        gsum[1:2] += jnp.sum(e, axis=0, keepdims=True)
        g = e * gbf[2:3]
        first = jnp.sum(g, axis=1, keepdims=True) / D
        second = jnp.sum(g * xh, axis=1, keepdims=True) / D
        resid = whole_rows(cg, s).astype(F32) + inv * (g - first - xh * second)
        rl[s] = resid.astype(BF16)

        for yy in range(2):
            for cc in range(2):

                @pl.when(jnp.logical_and(y == yy, core == cc))
                def _():
                    rf[s] = resid[cc * length : (cc + 1) * length, yy * half : (yy + 1) * half]

    each(slots, loop_three)

    def loop_four(s):
        f_y(s).wait_recv()
        total = hid[s, y, mine] + (fh[s, y].astype(F32) + fy[s].astype(F32))
        lo = total[:, :feat].astype(BF16)
        hi = total[:, feat:].astype(BF16)

        @pl.when(core == 0)
        def _():
            ob[s, 0] = lo
            osd[s] = hi

        @pl.when(core == 1)
        def _():
            ob[s, 1] = hi
            osd[s] = lo

        f_back(s).start()

    each(slots, loop_four)

    def finish(s):
        e_core(s).wait_send()
        e_y(s).wait_send()
        e_back(s).wait_send()
        f_core(s).wait_send()
        f_y(s).wait_send()
        f_back(s).wait()

    each(slots, finish)

    def place(s):
        out[s] = ob[perm[s]]

    each(slots, place)


def back(n, perm, xg, n1, gbf, w_t, wo, rl, rf, att, lse, qt, kvn, kvo, kvb, cos, sin, bounds,
         ig, qg, og, gsum,
         do, dq, drow, dkv, dst, dla, qp, ep, er, st, sr_, es, ss_, ey, sy, ib, isd,
         ks, kr, a1s, a1r, b1s, b1r, a2s, a2r, b2s, b2r, a3s, a3r):
    at = Place(n)
    slots, _, rows, half = xg.shape
    length = rows // 2
    feat = half // 2
    hl = feat // HEAD_DIM
    core, y, me = at.core, at.y, at.me
    mine = pl.ds(length * core, length)
    other = pl.ds(length * (1 - core), length)
    at.greet([at.sib, at.yp], True)
    every = slice(0, rows)

    def kv_copy(s, j):
        return remote(dst.at[s, j], dla.at[s, me], ks.at[s, j], kr.at[s, me], (j, at.head))

    def e_core(s):
        return remote(ep.at[s, other], er.at[s], a1s.at[s], a1r.at[s], at.sib)

    def s_core(s):
        return remote(st.at[s, 1 - core], sr_.at[s], b1s.at[s], b1r.at[s], at.sib)

    def e_y(s):
        return remote(es.at[s, 1 - y], ey.at[s], a2s.at[s], a2r.at[s], at.yp)

    def s_y(s):
        return remote(ss_.at[s], sy.at[s], b2s.at[s], b2r.at[s], at.yp)

    def i_back(s):
        return remote(isd.at[s], ib.at[s, core], a3s.at[s], a3r.at[s], at.sib)

    og[...] = jnp.zeros_like(og)
    qg[...] = jnp.zeros_like(qg)
    gsum[...] = jnp.zeros_like(gsum)
    drow[...] = jnp.zeros_like(drow)

    def head_grads(s, h, keys, values, lanes, allowed):
        hd = slice(h * HEAD_DIM, (h + 1) * HEAD_DIM)
        q = qt[s, hd, lanes]
        d_out = do[hd, lanes]
        sc = dot(keys[hd], q, 0, 0)
        p = jnp.exp(jnp.where(allowed, sc, masked_score) - lse[s, h : h + 1, lanes])
        dp = dot(values[hd], d_out, 0, 0)
        ds = (p * (dp - drow[h : h + 1, lanes])).astype(BF16)
        dq_add = dot(keys[hd], ds, 1, 0)
        dk = dot(q, ds, 1, 1)
        dv = dot(d_out, p.astype(BF16), 1, 1)
        return dq_add, dk, dv

    def attend_back(s):
        low_rows = rl[s]
        d_out = dot(wo[...], low_rows, 1, 1).astype(BF16)
        do[...] = d_out
        a = att[s]
        og[...] += dot(a.astype(BF16), low_rows, 1, 0)
        prod = d_out.astype(F32) * a
        for h in range(hl):
            drow[h : h + 1] = jnp.sum(prod[h * HEAD_DIM : (h + 1) * HEAD_DIM], axis=0, keepdims=True)
        start, end = bounds[s, 0:1], bounds[s, 1:2]
        clean, noisy = masks(me, length, start, end)
        kc, kn = kvo[s], kvn[s]
        first = slice(0, length)
        noisy_k = []
        for h in range(hl):
            hd = slice(h * HEAD_DIM, (h + 1) * HEAD_DIM)
            vd = slice(feat + h * HEAD_DIM, feat + (h + 1) * HEAD_DIM)
            dqa, dk, dv = head_grads(s, h, kc[:feat], kc[feat:], every, clean)
            dq[hd] = dqa
            dkv[s, hd] = dk
            dkv[s, vd] = dv
            dqa, dk, dv = head_grads(s, h, kn[:feat], kn[feat:], first, noisy)
            dq[hd, first] += dqa
            noisy_k.append(dk)
            qp[s, 2 * feat + h * HEAD_DIM : 2 * feat + (h + 1) * HEAD_DIM, first] = dv.astype(BF16)
        qp[s, feat : 2 * feat, first] = turn(
            jnp.concatenate(noisy_k, axis=0), cos[:, :length], -sin[:, :length]
        ).astype(BF16)

        def one(j, carry):
            kv = kvb[s, j]
            pos = lax.broadcasted_iota(jnp.int32, (length, rows), 0) + j * length
            allowed = pos >= start
            for h in range(hl):
                hd = slice(h * HEAD_DIM, (h + 1) * HEAD_DIM)
                vd = slice(feat + h * HEAD_DIM, feat + (h + 1) * HEAD_DIM)
                dqa, dk, dv = head_grads(s, h, kv[:feat], kv[feat:], every, allowed)
                dq[hd] += dqa
                dst[s, j, hd] = dk.astype(BF16)
                dst[s, j, vd] = dv.astype(BF16)
            kv_copy(s, j).start()
            return carry

        lax.fori_loop(at.lowest(s, me), me, one, 0)
        qp[s, :feat] = (turn(dq[...], cos[...], -sin[...]) * HEAD_DIM**-0.5).astype(BF16)

    each(slots, attend_back)

    def project_back(s):
        for d in range(1, n):
            i = me + d

            @pl.when(jnp.logical_and(i < n, at.lowest(s, i) <= me))
            def _():
                remote(dst.at[s, i], dla.at[s, i], ks.at[s, i], kr.at[s, i], at.sib).wait_recv()
                dkv[s] += dla[s, i].astype(F32)

        late = slice(length, rows)
        total = dkv[s]
        qp[s, feat : 2 * feat, late] = turn(total[:feat], cos[:, late], -sin[:, late]).astype(BF16)
        qp[s, 2 * feat :, late] = total[feat:].astype(BF16)
        pre = qp[s]
        qg[...] += dot(pre, n1[s], 1, 0)
        e = dot(pre, w_t[...], 0, 0)
        x = whole_rows(xg, s).astype(F32)
        mean, inv = row_stats(x)
        xh = (x - mean) * inv
        gsum[0:1] += jnp.sum(e * xh, axis=0, keepdims=True)
        gsum[1:2] += jnp.sum(e, axis=0, keepdims=True)
        ep[s] = e.astype(BF16)
        g = e * gbf[0:1]
        one_sum = jnp.sum(g, axis=1, keepdims=True)
        two_sum = jnp.sum(g * xh, axis=1, keepdims=True)
        lane = lax.broadcasted_iota(jnp.int32, (rows, 128), 1)
        packed = jnp.where(lane == 0, one_sum, jnp.where(lane == 1, two_sum, 0.0)).T
        st[s, 0] = packed[:8, :length]
        st[s, 1] = packed[:8, length:]
        e_core(s).start()
        s_core(s).start()

    def send_on(s):
        e_core(s).wait_recv()
        s_core(s).wait_recv()
        both = ep[s, mine].astype(F32) + er[s].astype(F32)
        es[s, 0] = both[:, :half].astype(BF16)
        es[s, 1] = both[:, half:].astype(BF16)
        ss_[s] = st[s, core] + sr_[s]
        e_y(s).start()
        s_y(s).start()

    def loop_two(t):
        @pl.when(t < slots)
        def _():
            project_back(t)

        @pl.when(t >= 1)
        def _():
            send_on(t - 1)

    each(slots + 1, loop_two)

    def input_part(s):
        e_y(s).wait_recv()
        s_y(s).wait_recv()
        e = es[s, y].astype(F32) + ey[s].astype(F32)
        sums = ss_[s] + sy[s]
        cols = jnp.concatenate([sums, jnp.zeros((120, length), F32)], axis=0).T
        first, second = cols[:, 0:1] / D, cols[:, 1:2] / D
        x = jnp.concatenate([xg[s, 0, mine], xg[s, 1, mine]], axis=1).astype(F32)
        mean, inv = row_stats(x)
        xh = (xg[s, y, mine].astype(F32) - mean) * inv
        gain = jnp.where(y == 0, gbf[0:1, :half], gbf[0:1, half:])
        grad = rf[s] + inv * (e * gain - first - xh * second)
        lo, hi = grad[:, :feat], grad[:, feat:]

        @pl.when(core == 0)
        def _():
            ib[s, 0] = lo
            isd[s] = hi

        @pl.when(core == 1)
        def _():
            ib[s, 1] = hi
            isd[s] = lo

        i_back(s).start()

    each(slots, input_part)

    def finish(s):
        e_core(s).wait_send()
        s_core(s).wait_send()
        e_y(s).wait_send()
        s_y(s).wait_send()
        i_back(s).wait()

        def sent(j, carry):
            kv_copy(s, j).wait_send()
            return carry

        lax.fori_loop(at.lowest(s, me), me, sent, 0)

    each(slots, finish)

    def place(s):
        ig[s] = ib[perm[s]]

    each(slots, place)


def call(kernel, ident, n, operands, outs, scratch, flops):
    specs = [
        pl.BlockSpec(memory_space=pltpu.SMEM if o.ndim == 1 else VMEM) for o in operands
    ]
    return pl.pallas_call(
        functools.partial(kernel, n),
        out_shape=[jax.ShapeDtypeStruct(s, t) for s, t in outs],
        in_specs=specs,
        out_specs=[pl.BlockSpec(memory_space=VMEM)] * len(outs),
        scratch_shapes=scratch,
        compiler_params=pltpu.CompilerParams(
            collective_id=ident, has_side_effects=True, vmem_limit_bytes=VMEM_LIMIT
        ),
        cost_estimate=pl.CostEstimate(flops=flops, bytes_accessed=20 << 20, transcendentals=0),
        name=kernel.__name__,
    )(*operands)


def body(
    inputs,
    doc_lengths,
    attn_gain,
    attn_bias,
    w_qkv,
    w_out,
    ffn_gain,
    ffn_bias,
    w_up,
    w_down,
    cotangent,
):
    n = lax.axis_size("seq")
    slots, _, length, feat = inputs.shape
    rows, half, hl = 2 * length, 2 * feat, feat // HEAD_DIM
    held = slots * n * half * length * 2
    if held > ROWS_LIMIT:
        return gathered_body(
            inputs, doc_lengths, attn_gain, attn_bias, w_qkv, w_out, ffn_gain, ffn_bias, w_up, w_down, cotangent
        )
    sem = pltpu.SemaphoreType.DMA
    me = lax.axis_index("seq")
    long = jnp.argmax(doc_lengths[:, 0]).astype(jnp.int32)
    ids = jnp.arange(slots, dtype=jnp.int32)
    perm = jnp.where(ids == 0, long, jnp.where(ids == long, 0, ids))
    ends = jnp.cumsum(doc_lengths, axis=1)[perm]
    positions = me * length + jnp.arange(length, dtype=jnp.int32)
    past = ends[:, :, None] <= positions[None, None, :]
    first_key = jnp.max(jnp.where(past, ends[:, :, None], 0), axis=1)
    last_key = jnp.min(jnp.where(past, 2**30, ends[:, :, None]), axis=1)
    bounds = jnp.zeros((slots, 8, rows), jnp.int32)
    bounds = bounds.at[:, 0].set(jnp.tile(first_key, (1, 2))).at[:, 1].set(jnp.tile(last_key, (1, 2)))
    half_dim = HEAD_DIM // 2
    freqs = rotary_base ** (-jnp.arange(half_dim, dtype=F32) / half_dim)
    angles = freqs[:, None] * positions.astype(F32)[None, :]
    cos = jnp.tile(jnp.cos(angles), (1, 2))
    sin = jnp.tile(jnp.sin(angles), (1, 2))
    w_t = w_qkv.reshape(D, 3 * feat).T
    gains = jnp.concatenate(
        [jnp.stack([attn_gain, attn_bias, ffn_gain, ffn_bias]), jnp.zeros((4, feat), F32)], axis=0
    )
    fulls = [((slots, 2, rows, half), BF16)] * 3
    kinds = (3, slots)
    xg, cg, ag, wog, gbf, n1, qt, kvn, kvo, kvb, att, lse = call(
        front,
        0,
        n,
        (perm, inputs, cotangent, gains, w_t, w_out, cos, sin, bounds),
        fulls
        + [
            ((D, D), BF16),
            ((8, D), F32),
            ((slots, rows, D), BF16),
            ((slots, feat, rows), BF16),
            ((slots, half, length), BF16),
            ((slots, half, length), BF16),
            ((slots, n, half, length), BF16),
            ((slots, feat, rows), F32),
            ((slots, 8, rows), F32),
        ],
        [
            VMEM((3, slots, rows, feat), BF16),
            VMEM((3, slots, rows, feat), BF16),
            VMEM((4, 8, feat), F32),
            VMEM((feat, rows), F32),
            VMEM((8, rows), F32),
            VMEM((8, rows), F32),
            *[sem(kinds)] * 6,
            *[sem((3,))] * 4,
            *[sem((slots, n))] * 2,
        ],
        3 * 10**9,
    )
    wide = VMEM((slots, rows, D), BF16)
    part = VMEM((slots, length, D), BF16)
    outputs, rl, rf, up_grad, down_grad, gsum2 = call(
        middle,
        1,
        n,
        (perm, xg, ag, cg, wog, gbf, w_up, w_down),
        [
            ((slots, 2, length, feat), BF16),
            ((slots, rows, D), BF16),
            ((slots, length, half), F32),
            (w_up.shape, F32),
            (w_down.shape, F32),
            ((8, D), F32),
        ],
        [
            VMEM((slots, 2, rows, half), F32),
            *[wide] * 4,
            *[part] * 3,
            *[wide] * 2,
            part,
            VMEM((slots, 2, length, half), BF16),
            VMEM((slots, length, half), BF16),
            VMEM((slots, 2, length, feat), BF16),
            VMEM((slots, length, feat), BF16),
            *[sem((slots,))] * 12,
        ],
        15 * 10**9,
    )
    stat = VMEM((slots, 8, length), F32)
    input_grad, qkv_grad, out_grad, gsum1 = call(
        back,
        2,
        n,
        (perm, xg, n1, gbf, w_t, w_out, rl, rf, att, lse, qt, kvn, kvo, kvb, cos, sin, bounds),
        [
            ((slots, 2, length, feat), F32),
            ((3 * feat, D), F32),
            ((feat, D), F32),
            ((8, D), F32),
        ],
        [
            VMEM((feat, rows), BF16),
            VMEM((feat, rows), F32),
            VMEM((8, rows), F32),
            VMEM((slots, half, length), F32),
            VMEM((slots, n, half, length), BF16),
            VMEM((slots, n, half, length), BF16),
            VMEM((slots, 3 * feat, rows), BF16),
            wide,
            part,
            VMEM((slots, 2, 8, length), F32),
            stat,
            VMEM((slots, 2, length, half), BF16),
            stat,
            VMEM((slots, length, half), BF16),
            stat,
            VMEM((slots, 2, length, feat), F32),
            VMEM((slots, length, feat), F32),
            *[sem((slots, n))] * 2,
            *[sem((slots,))] * 10,
        ],
        10 * 10**9,
    )
    gains_sum = lax.psum(jnp.concatenate([gsum1[:2], gsum2[:2] * 0.25], axis=0), ("seq", "head"))
    gains_own = lax.dynamic_slice(gains_sum, (0, lax.axis_index("head") * feat), (4, feat))
    up_low, down_low = lax.psum((up_grad.astype(BF16), down_grad.astype(BF16)), "seq")
    qkv_low, out_low = lax.psum((qkv_grad.astype(BF16), out_grad.astype(BF16)), "seq")
    return (
        outputs,
        input_grad,
        qkv_low.astype(F32).T.reshape(w_qkv.shape),
        out_low.astype(F32),
        up_low.astype(F32),
        down_low.astype(F32),
        gains_own[0],
        gains_own[1],
        gains_own[2],
        gains_own[3],
    )


def solution(mesh):
    in_specs = (
        P(None, None, "seq", "head"),
        P(),
        P("head"),
        P("head"),
        P(None, None, "head"),
        P("head", None),
        P("head"),
        P("head"),
        P(None, "head"),
        P("head", None),
        P(None, None, "seq", "head"),
    )
    out_specs = (
        P(None, None, "seq", "head"),
        P(None, None, "seq", "head"),
        P(None, None, "head"),
        P("head", None),
        P(None, "head"),
        P("head", None),
        P("head"),
        P("head"),
        P("head"),
        P("head"),
    )
    return jax.shard_map(body, mesh=mesh, in_specs=in_specs, out_specs=out_specs, check_vma=False)
```

```python
import functools

import jax
import jax.numpy as jnp
from jax import lax
from jax.experimental import pallas as pl
from jax.experimental.pallas import tpu as pltpu
from jax.sharding import PartitionSpec as P

D = 768
HEAD_DIM = 64
BLOCK = 16


norm_eps = 1e-05
masked_score = -1e30
rotary_base = 10000.0

MESH = pl.DeviceIdType.MESH
VMEM = pltpu.VMEM
F32 = jnp.float32
BF16 = jnp.bfloat16
ROWS_LIMIT = 16 << 20
VMEM_LIMIT = 60 << 20


def passed_along(block, axis, distance):
    devices = range(lax.axis_size(axis))
    route = [(i - distance, i) for i in devices if i - distance in devices]
    return lax.ppermute(block, axis, route)


def from_behind(x, axis, by):
    devices = lax.axis_size(axis)
    return lax.ppermute(x, axis, [(i, (i + by) % devices) for i in range(devices)])


def segment_ids(doc_lengths, positions):
    doc_ends = jnp.cumsum(doc_lengths, axis=1)
    return jnp.sum((doc_ends[:, :, None] <= positions[None, None, :]).astype(jnp.int32), axis=1)


def rotate(values, positions, sign):
    half_dim = values.shape[-1] // 2
    freqs = rotary_base ** (-jnp.arange(half_dim, dtype=jnp.float32) / half_dim)
    angles = positions.astype(jnp.float32)[:, None, None] * freqs
    cosine = jnp.cos(angles)
    sine = sign * jnp.sin(angles)
    first_half = values[..., :half_dim]
    second_half = values[..., half_dim:]
    return jnp.concatenate(
        [first_half * cosine - second_half * sine, second_half * cosine + first_half * sine],
        axis=-1,
    )


def row_pair(first_sum, second_sum):
    return lax.psum((first_sum, second_sum), "head")


def normalize(share, gain, bias):
    row_total, row_square = row_pair(jnp.sum(share, axis=-1), jnp.sum(share * share, axis=-1))
    mean_value = row_total / D
    inv_std = lax.rsqrt(row_square / D - mean_value * mean_value + norm_eps)
    centered = (share - mean_value[..., None]) * inv_std[..., None]
    scaled = (centered * gain + bias).astype(jnp.bfloat16)
    gathered = lax.all_gather(scaled, "head", axis=3, tiled=True)
    return (gathered, centered, inv_std)


def norm_backward(partial_value, gain, centered, inv_std):
    share = lax.psum_scatter(partial_value, "head", scatter_dimension=3, tiled=True)
    scaled = share * gain
    first_mean, second_mean = row_pair(
        jnp.sum(scaled, axis=-1), jnp.sum(scaled * centered, axis=-1)
    )
    grad_in = inv_std[..., None] * (
        scaled - first_mean[..., None] / D - centered * (second_mean[..., None] / D)
    )
    gain_grad = jnp.sum(share * centered, axis=(0, 1, 2))
    bias_grad = jnp.sum(share, axis=(0, 1, 2))
    return (grad_in, gain_grad, bias_grad)


def branch_total(partial_value):
    return lax.psum_scatter(partial_value, "head", scatter_dimension=3, tiled=True)


def gradient_rows(share):
    return lax.all_gather(share, "head", axis=3, tiled=True)


def mask_rule(query_pos, query_seg, key_pos, key_seg):
    query_block = (query_pos // BLOCK)[:, None]
    key_block = (key_pos // BLOCK)[None, :]
    order = jnp.stack([key_block < query_block, key_block <= query_block])
    same_doc = query_seg[:, :, None] == key_seg[:, None, :]
    return jnp.logical_and(order[None, :, None], same_doc[:, None, None])


def absorb(state_now, scores, allowed, value_piece):
    run_max, run_sum, run_acc = state_now
    masked = jnp.where(allowed, scores, masked_score)
    new_max = jnp.maximum(run_max, jnp.max(masked, axis=-1))
    weights_now = jnp.where(allowed, jnp.exp(masked - new_max[..., None]), 0.0)
    factor = jnp.exp(run_max - new_max)
    new_sum = run_sum * factor + jnp.sum(weights_now, axis=-1)
    added = jnp.einsum(
        "schlk,skhd->schld",
        weights_now,
        value_piece.astype(jnp.float32),
        precision=lax.Precision.HIGHEST,
    )
    return (new_max, new_sum, run_acc * factor[..., None] + added)


def gathered_body(
    inputs,
    doc_lengths,
    attn_gain,
    attn_bias,
    w_qkv,
    w_out,
    ffn_gain,
    ffn_bias,
    w_up,
    w_down,
    cotangent,
):
    seqs_here, _, local_len, _ = inputs.shape
    head_local = w_qkv.shape[2] // HEAD_DIM
    first_pos = lax.axis_index("seq") * local_len
    positions = first_pos + jnp.arange(local_len, dtype=jnp.int32)
    segments = segment_ids(doc_lengths, positions)
    inputs_wide = inputs.astype(jnp.float32)
    normed_one, centered_one, inv_one = normalize(inputs_wide, attn_gain, attn_bias)
    projected = jnp.einsum("scld,dtk->scltk", normed_one, w_qkv, preferred_element_type=jnp.float32)
    split_rows = projected.reshape(seqs_here, 2, local_len, 3, head_local, HEAD_DIM)
    queries = (rotate(split_rows[:, :, :, 0], positions, 1.0) * HEAD_DIM ** (-0.5)).astype(
        jnp.bfloat16
    )
    key_rows = rotate(split_rows[:, :, :, 1], positions, 1.0).astype(jnp.bfloat16)
    value_rows = split_rows[:, :, :, 2].astype(jnp.bfloat16)
    clean_keys = key_rows[:, 1].reshape(seqs_here, local_len, head_local * HEAD_DIM)
    clean_values = value_rows[:, 1].reshape(seqs_here, local_len, head_local * HEAD_DIM)
    block_ids = positions // BLOCK
    own_allowed = jnp.logical_and(
        (block_ids[:, None] == block_ids[None, :])[None],
        segments[:, :, None] == segments[:, None, :],
    )[:, None, None]
    noisy_scores = jnp.einsum(
        "sclhd,skhd->schlk", queries[:, :1], key_rows[:, 0], preferred_element_type=jnp.float32
    )
    half_shape = (seqs_here, 1, head_local, local_len)
    empty_state = (
        jnp.full(half_shape, masked_score, jnp.float32),
        jnp.zeros(half_shape, jnp.float32),
        jnp.zeros(half_shape + (HEAD_DIM,), jnp.float32),
    )
    noisy_state = absorb(empty_state, noisy_scores, own_allowed, value_rows[:, 0])
    start_state = jax.tree.map(
        lambda first, second: jnp.concatenate([first, second], axis=1), noisy_state, empty_state
    )
    piece_keys = lax.all_gather(clean_keys, "seq", axis=1, tiled=True)
    piece_values = lax.all_gather(clean_values, "seq", axis=1, tiled=True)
    piece_len = piece_keys.shape[1]
    key_pos = jnp.arange(piece_len, dtype=jnp.int32)
    key_seg = segment_ids(doc_lengths, key_pos)
    key_heads = piece_keys.reshape(seqs_here, piece_len, head_local, HEAD_DIM)
    value_heads = piece_values.reshape(seqs_here, piece_len, head_local, HEAD_DIM)
    scores = jnp.einsum("sclhd,skhd->schlk", queries, key_heads, preferred_element_type=jnp.float32)
    final_max, final_sum, final_acc = absorb(
        start_state, scores, mask_rule(positions, segments, key_pos, key_seg), value_heads
    )
    attended = final_acc / final_sum[..., None]
    log_total = final_max + jnp.log(final_sum)
    attended_low = attended.astype(jnp.bfloat16)
    out_heads = w_out.reshape(head_local, HEAD_DIM, w_out.shape[1])
    attn_share = branch_total(
        jnp.einsum("schld,hdm->sclm", attended_low, out_heads, preferred_element_type=jnp.float32)
    )
    hidden_res = inputs_wide + attn_share
    normed_two, centered_two, inv_two = normalize(hidden_res, ffn_gain, ffn_bias)
    up_value = jnp.einsum("scld,df->sclf", normed_two, w_up, preferred_element_type=jnp.float32)
    activated, gelu_back = jax.vjp(lambda inner: jax.nn.gelu(inner, approximate=True), up_value)
    act_low = activated.astype(jnp.bfloat16)
    ffn_share = branch_total(
        jnp.einsum("sclf,fm->sclm", act_low, w_down, preferred_element_type=jnp.float32)
    )
    outputs = (hidden_res + ffn_share).astype(jnp.bfloat16)
    grad_out = cotangent.astype(jnp.float32)
    grad_full = gradient_rows(cotangent)
    down_grad = jnp.einsum("sclf,sclm->fm", act_low, grad_full, preferred_element_type=jnp.float32)
    act_grad = jnp.einsum("sclm,fm->sclf", grad_full, w_down, preferred_element_type=jnp.float32)
    up_pre_grad = gelu_back(act_grad)[0].astype(jnp.bfloat16)
    up_grad = jnp.einsum(
        "scld,sclf->df", normed_two, up_pre_grad, preferred_element_type=jnp.float32
    )
    normed_two_grad = jnp.einsum(
        "sclf,df->scld", up_pre_grad, w_up, preferred_element_type=jnp.float32
    )
    back_two, ffn_gain_grad, ffn_bias_grad = norm_backward(
        normed_two_grad, ffn_gain, centered_two, inv_two
    )
    resid_grad = grad_out + back_two
    resid_full = gradient_rows(resid_grad.astype(jnp.bfloat16))
    out_grad = jnp.einsum(
        "schld,sclm->hdm", attended_low, resid_full, preferred_element_type=jnp.float32
    ).reshape(w_out.shape)
    attended_grad = jnp.einsum(
        "sclm,hdm->schld", resid_full, out_heads, preferred_element_type=jnp.float32
    ).astype(jnp.bfloat16)
    grad_wide = attended_grad.astype(jnp.float32)
    row_delta = jnp.sum(grad_wide * attended, axis=-1)
    noisy_probs = jnp.where(own_allowed, jnp.exp(noisy_scores - log_total[:, :1, :, :, None]), 0.0)
    noisy_prob_grad = jnp.einsum(
        "schld,skhd->schlk",
        attended_grad[:, :1],
        value_rows[:, 0],
        preferred_element_type=jnp.float32,
    )
    noisy_score_grad = (noisy_probs * (noisy_prob_grad - row_delta[:, :1, :, :, None])).astype(
        jnp.bfloat16
    )
    noisy_query_grad = jnp.einsum(
        "schlk,skhd->schld", noisy_score_grad, key_rows[:, 0], preferred_element_type=jnp.float32
    )
    noisy_key_grad = jnp.einsum(
        "schlk,sclhd->skhd", noisy_score_grad, queries[:, :1], preferred_element_type=jnp.float32
    )
    noisy_value_grad = jnp.einsum(
        "schlk,schld->skhd", noisy_probs, grad_wide[:, :1], precision=lax.Precision.HIGHEST
    )
    query_start = jnp.concatenate([noisy_query_grad, jnp.zeros_like(noisy_query_grad)], axis=1)
    flat_zero = jnp.zeros((seqs_here, local_len, head_local * HEAD_DIM), jnp.float32)

    def piece_grads(piece_keys, piece_values, first_row, query_total):
        key_pos = first_row + jnp.arange(local_len, dtype=jnp.int32)
        key_seg = segment_ids(doc_lengths, key_pos)
        key_heads = piece_keys.reshape(seqs_here, local_len, head_local, HEAD_DIM)
        value_heads = piece_values.reshape(seqs_here, local_len, head_local, HEAD_DIM)
        scores = jnp.einsum(
            "sclhd,skhd->schlk", queries, key_heads, preferred_element_type=jnp.float32
        )
        allowed = mask_rule(positions, segments, key_pos, key_seg)
        weights_now = jnp.where(allowed, jnp.exp(scores - log_total[..., None]), 0.0)
        prob_grad = jnp.einsum(
            "schld,skhd->schlk", attended_grad, value_heads, preferred_element_type=jnp.float32
        )
        score_grad = (weights_now * (prob_grad - row_delta[..., None])).astype(jnp.bfloat16)
        query_out = query_total + jnp.einsum(
            "schlk,skhd->schld", score_grad, key_heads, preferred_element_type=jnp.float32
        )
        key_part = jnp.einsum(
            "schlk,sclhd->skhd", score_grad, queries, preferred_element_type=jnp.float32
        )
        value_part = jnp.einsum(
            "schlk,schld->skhd", weights_now, grad_wide, precision=lax.Precision.HIGHEST
        )
        return (key_part.reshape(flat_zero.shape), value_part.reshape(flat_zero.shape), query_out)

    def cycle_body(cycle_step, carried):
        piece_keys, piece_values, key_acc, value_acc, query_acc = carried
        source = (lax.axis_index("seq") - cycle_step) % lax.axis_size("seq")
        first_row = source * local_len
        key_part, value_part, query_acc = piece_grads(
            piece_keys, piece_values, first_row, query_acc
        )
        key_acc = key_acc + key_part
        value_acc = value_acc + value_part
        piece_keys, piece_values = passed_along((piece_keys, piece_values), "seq", 1)
        key_acc, value_acc = (
            from_behind(key_acc.astype(jnp.bfloat16), "seq", 1).astype(key_acc.dtype),
            from_behind(value_acc.astype(jnp.bfloat16), "seq", 1).astype(value_acc.dtype),
        )
        return (piece_keys, piece_values, key_acc, value_acc, query_acc)

    cycle_start = (clean_keys, clean_values, flat_zero, flat_zero, query_start)
    _, _, clean_key_grad, clean_value_grad, query_acc = lax.fori_loop(
        0, lax.axis_size("seq"), cycle_body, cycle_start
    )
    head_shape = (seqs_here, local_len, head_local, HEAD_DIM)
    query_total = rotate(jnp.transpose(query_acc, (0, 1, 3, 2, 4)), positions, -1.0) * HEAD_DIM ** (
        -0.5
    )
    key_total = rotate(
        jnp.stack([noisy_key_grad, clean_key_grad.reshape(head_shape)], axis=1), positions, -1.0
    )
    value_total = jnp.stack([noisy_value_grad, clean_value_grad.reshape(head_shape)], axis=1)
    qkv_pre_grad = (
        jnp.stack([query_total, key_total, value_total], axis=3)
        .reshape(seqs_here, 2, local_len, 3, head_local * HEAD_DIM)
        .astype(jnp.bfloat16)
    )
    qkv_grad = jnp.einsum(
        "scld,scltk->dtk", normed_one, qkv_pre_grad, preferred_element_type=jnp.float32
    )
    normed_one_grad = jnp.einsum(
        "scltk,dtk->scld", qkv_pre_grad, w_qkv, preferred_element_type=jnp.float32
    )
    back_one, attn_gain_grad, attn_bias_grad = norm_backward(
        normed_one_grad, attn_gain, centered_one, inv_one
    )
    input_grad = resid_grad + back_one
    (
        qkv_grad,
        out_grad,
        up_grad,
        down_grad,
        attn_gain_grad,
        attn_bias_grad,
        ffn_gain_grad,
        ffn_bias_grad,
    ) = lax.psum(
        (
            qkv_grad,
            out_grad,
            up_grad,
            down_grad,
            attn_gain_grad,
            attn_bias_grad,
            ffn_gain_grad,
            ffn_bias_grad,
        ),
        "seq",
    )
    return (
        outputs,
        input_grad,
        qkv_grad,
        out_grad,
        up_grad,
        down_grad,
        attn_gain_grad,
        attn_bias_grad,
        ffn_gain_grad,
        ffn_bias_grad,
    )


def dot(a, b, ca, cb):
    return lax.dot_general(a, b, (((ca,), (cb,)), ((), ())), preferred_element_type=F32)


def remote(src, dst, send, recv, device):
    return pltpu.make_async_remote_copy(
        src_ref=src, dst_ref=dst, send_sem=send, recv_sem=recv, device_id=device, device_id_type=MESH
    )


class Place:
    def __init__(self, n):
        self.n = n
        self.me = lax.axis_index("seq")
        self.head = lax.axis_index("head")
        self.core = lax.rem(self.head, 2)
        self.y = lax.div(self.head, 2)
        self.sib = (self.me, self.y * 2 + 1 - self.core)
        self.yp = (self.me, (1 - self.y) * 2 + self.core)
        self.diag = (self.me, (1 - self.y) * 2 + 1 - self.core)
        self.half = n // 2
        self.band = max(1, n // 8)

    def lowest(self, slot, i):
        near = i - self.band
        short = jnp.where(i >= self.half, jnp.minimum(near, self.half), near)
        return jnp.where(slot == 0, 0, jnp.maximum(short, 0))

    def greet(self, near, everyone):
        bar = pltpu.get_barrier_semaphore()
        for d in near:
            pl.semaphore_signal(bar, inc=1, device_id=d, device_id_type=MESH)
        count = len(near)
        if everyone:
            for d in range(1, self.n):
                there = lax.rem(self.me + d, self.n)
                pl.semaphore_signal(bar, inc=1, device_id=(there, self.head), device_id_type=MESH)
            count += self.n - 1
        pl.semaphore_wait(bar, count)


def each(count, step):
    def run(i, carry):
        step(i)
        return carry

    lax.fori_loop(0, count, run, 0)


def row_stats(x):
    mean = jnp.sum(x, axis=1, keepdims=True) / D
    var = jnp.sum(x * x, axis=1, keepdims=True) / D - mean * mean
    return mean, lax.rsqrt(var + norm_eps)


def whole_rows(ref, s):
    return jnp.concatenate([ref[s, 0], ref[s, 1]], axis=1)


def turn(v, cosine, sine):
    parts = []
    for h in range(v.shape[0] // HEAD_DIM):
        a = v[h * 64 : h * 64 + 32]
        b = v[h * 64 + 32 : h * 64 + 64]
        parts += [a * cosine - b * sine, b * cosine + a * sine]
    return jnp.concatenate(parts, axis=0)


def masks(me, length, start, end):
    shape = (length, 2 * length)
    key = lax.broadcasted_iota(jnp.int32, shape, 0)
    row = lax.broadcasted_iota(jnp.int32, shape, 1)
    noisy = row < length
    at = jnp.where(noisy, row, row - length)
    key_block = key >> 4
    row_block = at >> 4
    pos = key + me * length
    same = jnp.logical_and(pos >= start, pos < end)
    clean = jnp.logical_and(same, key_block < row_block + jnp.where(noisy, 0, 1))
    own = jnp.logical_and(same, key_block == row_block)[:, :length]
    return clean, own


class Sum:
    def __init__(self, at, src, res, gx, part, gz, xs, xr, zs, zr, cs, cr, fs, fr):
        self.m = at.n // 2
        self.lo = lax.rem(at.me, 2)
        self.hi = lax.div(at.me, 2)
        self.head = at.head
        self.pair = (at.me + 1 - 2 * self.lo, at.head)
        self.src, self.res, self.gx, self.part, self.gz = src, res, gx, part, gz
        self.xs, self.xr, self.zs, self.zr = xs, xr, zs, zr
        self.cs, self.cr, self.fs, self.fr = cs, cr, fs, fr

    def at_z(self, k):
        return (2 * k + self.lo, self.head)

    def x(self, k):
        return remote(self.src.at[1 - self.lo, k], self.gx.at[k], self.xs.at[k], self.xr.at[k], self.pair)

    def z(self, k):
        return remote(self.part.at[k], self.gz.at[self.hi], self.zs.at[k], self.zr.at[self.hi], self.at_z(k))

    def z_in(self, k):
        return remote(self.part.at[k], self.gz.at[k], self.zs.at[k], self.zr.at[k], self.at_z(k))

    def c(self, k):
        own = self.res.at[self.lo, self.hi]
        return remote(own, own, self.cs.at[k], self.cr.at[self.hi], self.at_z(k))

    def c_in(self, k):
        part = self.res.at[self.lo, k]
        return remote(part, part, self.cs.at[k], self.cr.at[k], self.at_z(k))

    def f(self, k):
        part = self.res.at[self.lo, k]
        return remote(part, part, self.fs.at[k], self.fr.at[k], self.pair)

    def others(self):
        return [lax.rem(self.hi + d, self.m) for d in range(1, self.m)]

    def begin(self):
        each(self.m, lambda k: self.x(k).start())

    def pass_on(self, k):
        self.x(k).wait_recv()
        self.part[k] = (self.src[self.lo, k].astype(F32) + self.gx[k].astype(F32)).astype(BF16)

        @pl.when(k != self.hi)
        def _():
            self.z(k).start()

    def reduce(self):
        total = self.part[self.hi].astype(F32)
        for k in self.others():
            self.z_in(k).wait_recv()
            total += self.gz[k].astype(F32)
        self.res[self.lo, self.hi] = total.astype(BF16)
        for k in self.others():
            self.c(k).start()
        self.f(self.hi).start()

    def forward(self, d):
        k = lax.rem(self.hi + d, self.m)
        self.c_in(k).wait_recv()
        self.f(k).start()

    def finish(self):
        each(self.m, lambda k: self.x(k).wait_send())
        for k in self.others():
            self.z(k).wait_send()
            self.c(k).wait_send()
        each(self.m, lambda k: self.f(k).wait())


def front(n, perm, x_in, c_in, gb_in, w_t, wo_in, cos, sin, bounds,
          xg, cg, ag, wog, gbf, n1, qt, kvn, kvo, kvb, att, lse,
          own, land, gland, acc, mrow, lrow,
          ss, sr, ys, yr, fs, fr, gs, gr, ws, wr, ks, kr):
    at = Place(n)
    slots, _, length, feat = x_in.shape
    rows = 2 * length
    hl = feat // HEAD_DIM
    core, y, me = at.core, at.y, at.me
    fulls = (xg, cg, ag)

    def sib_copy(k, s):
        return remote(own.at[k, s], land.at[k, s], ss.at[k, s], sr.at[k, s], at.sib)

    def build(k, s):
        a, b = own[k, s], land[k, s]

        @pl.when(core == 0)
        def _():
            fulls[k][s, y] = jnp.concatenate([a, b], axis=1)

        @pl.when(core == 1)
        def _():
            fulls[k][s, y] = jnp.concatenate([b, a], axis=1)

    def y_copy(k, s):
        part = fulls[k].at[s, y, pl.ds(length * core, length)]
        return remote(part, part, ys.at[k, s], yr.at[k, s], at.yp)

    def f_copy(k, s):
        part = fulls[k].at[s, 1 - y, pl.ds(length * core, length)]
        return remote(part, part, fs.at[k, s], fr.at[k, s], at.sib)

    def kv_copy(s, i):
        return remote(kvo.at[s], kvb.at[s, me], ks.at[s, i], kr.at[s, me], (i, at.head))

    at.greet([at.sib, at.yp, at.diag], True)

    def stage(s):
        own[0, s] = x_in[perm[s]].reshape(rows, feat)
        sib_copy(0, s).start()

    each(slots, stage)
    gland[at.head] = gb_in[...]
    g_copies = [
        remote(gb_in, gland.at[at.head], gs.at[k], gr.at[k], d)
        for k, d in enumerate((at.sib, at.yp, at.diag))
    ]
    for copy in g_copies:
        copy.start()

    def stage_cot(s):
        own[1, s] = c_in[perm[s]].reshape(rows, feat)
        sib_copy(1, s).start()

    def first_y(s):
        sib_copy(0, s).wait_recv()
        build(0, s)
        y_copy(0, s).start()

    each(slots, first_y)
    each(slots, stage_cot)
    for copy in g_copies:
        copy.wait()
    gbf[...] = jnp.concatenate([gland[i] for i in range(4)], axis=1)

    def project(s):
        x = whole_rows(xg, s).astype(F32)
        mean, inv = row_stats(x)
        normed = ((x - mean) * inv * gbf[0:1] + gbf[1:2]).astype(BF16)
        n1[s] = normed
        pt = dot(w_t[...], normed, 1, 1)
        qk = turn(pt[: 2 * feat], cos[...], sin[...])
        qt[s] = (qk[:feat] * HEAD_DIM**-0.5).astype(BF16)
        kv = jnp.concatenate([qk[feat:], pt[2 * feat :]], axis=0).astype(BF16)
        kvn[s] = kv[:, :length]
        kvo[s] = kv[:, length:]
        for d in range(1, n):
            i = me + d

            @pl.when(jnp.logical_and(i < n, at.lowest(s, i) <= me))
            def _():
                kv_copy(s, i).start()

    def arrive(t):
        @pl.when(t < slots)
        def _():
            y_copy(0, t).wait_recv()
            f_copy(0, t).start()

        @pl.when(t >= 1)
        def _():
            f_copy(0, t - 1).wait_recv()
            project(t - 1)

    each(slots + 1, arrive)

    def first_y_cot(s):
        sib_copy(1, s).wait_recv()
        build(1, s)
        y_copy(1, s).start()

    each(slots, first_y_cot)

    def wo_block(who):
        return wog.at[pl.ds(pl.multiple_of(feat * who, 16), feat)]

    wog[pl.ds(pl.multiple_of(feat * at.head, 16), feat)] = wo_in[...]
    wo_sib = remote(wo_in, wo_block(at.head), ws.at[0], wr.at[0], at.sib)
    wo_y = remote(wo_in, wo_block(at.head), ws.at[1], wr.at[1], at.yp)
    wo_f = remote(wo_block(at.yp[1]), wo_block(at.yp[1]), ws.at[2], wr.at[2], at.sib)
    wo_sib.start()
    wo_y.start()

    heads = [slice(h * HEAD_DIM, (h + 1) * HEAD_DIM) for h in range(hl)]
    first_half = slice(0, length)

    def attend(s):
        start, end = bounds[s, 0:1], bounds[s, 1:2]
        clean, noisy = masks(me, length, start, end)
        kc, kn = kvo[s], kvn[s]
        q = [qt[s, hd] for hd in heads]
        sc = [dot(kc[hd], q[h], 0, 0) for h, hd in enumerate(heads)]
        sn = [dot(kn[hd], q[h][:, :length], 0, 0) for h, hd in enumerate(heads)]
        sc = [jnp.where(clean, v, masked_score) for v in sc]
        sn = [jnp.where(noisy, v, masked_score) for v in sn]
        top = []
        for h in range(hl):
            tc = jnp.max(sc[h], axis=0, keepdims=True)
            tn = jnp.max(sn[h], axis=0, keepdims=True)
            top.append(
                jnp.concatenate([jnp.maximum(tc[:, :length], tn), tc[:, length:]], axis=1)
            )
        pc = [jnp.exp(sc[h] - top[h]) for h in range(hl)]
        pn = [jnp.exp(sn[h] - top[h][:, :length]) for h in range(hl)]
        oc = [dot(kc[feat:][hd], pc[h].astype(BF16), 1, 0) for h, hd in enumerate(heads)]
        on = [dot(kn[feat:][hd], pn[h].astype(BF16), 1, 0) for h, hd in enumerate(heads)]
        for h, hd in enumerate(heads):
            tc = jnp.sum(pc[h], axis=0, keepdims=True)
            tn = jnp.sum(pn[h], axis=0, keepdims=True)
            mrow[h : h + 1] = top[h]
            lrow[h : h + 1] = jnp.concatenate([tc[:, :length] + tn, tc[:, length:]], axis=1)
            acc[hd, first_half] = oc[h][:, :length] + on[h]
            acc[hd, slice(length, rows)] = oc[h][:, length:]

        def one(j, carry):
            remote(kvo.at[s], kvb.at[s, j], ks.at[s, j], kr.at[s, j], at.sib).wait_recv()
            kv = kvb[s, j]
            q = [qt[s, hd] for hd in heads]
            old = [mrow[h : h + 1] for h in range(hl)]
            total = [lrow[h : h + 1] for h in range(hl)]
            pos = lax.broadcasted_iota(jnp.int32, (length, rows), 0) + j * length
            allowed = pos >= start
            sc = [dot(kv[hd], q[h], 0, 0) for h, hd in enumerate(heads)]
            sc = [jnp.where(allowed, v, masked_score) for v in sc]
            new = [jnp.maximum(old[h], jnp.max(sc[h], axis=0, keepdims=True)) for h in range(hl)]
            p = [jnp.exp(sc[h] - new[h]) for h in range(hl)]
            add = [dot(kv[feat:][hd], p[h].astype(BF16), 1, 0) for h, hd in enumerate(heads)]
            scale = [jnp.exp(old[h] - new[h]) for h in range(hl)]
            for h, hd in enumerate(heads):
                mrow[h : h + 1] = new[h]
                lrow[h : h + 1] = total[h] * scale[h] + jnp.sum(p[h], axis=0, keepdims=True)
                acc[hd] = acc[hd] * scale[h] + add[h]
            return carry

        lax.fori_loop(at.lowest(s, me), me, one, 0)
        for h in range(hl):
            hd = slice(h * HEAD_DIM, (h + 1) * HEAD_DIM)
            att[s, hd] = acc[hd] / lrow[h : h + 1]
        lse[s] = mrow[...] + jnp.log(lrow[...])
        own[2, s] = att[s].T.astype(BF16)
        sib_copy(2, s).start()

    mrow[...] = jnp.zeros_like(mrow)
    lrow[...] = jnp.ones_like(lrow)

    def second(t):
        @pl.when(t < slots)
        def _():
            attend(t)
            y_copy(1, t).wait_recv()
            f_copy(1, t).start()

        @pl.when(t >= 1)
        def _():
            sib_copy(2, t - 1).wait_recv()
            build(2, t - 1)
            y_copy(2, t - 1).start()

    each(slots + 1, second)
    wo_y.wait_recv()
    wo_f.start()

    def last(s):
        y_copy(2, s).wait_recv()
        f_copy(2, s).start()

    each(slots, last)

    def finish(s):
        for k in range(3):
            sib_copy(k, s).wait_send()
            y_copy(k, s).wait_send()
            f_copy(k, s).wait_send()
        f_copy(1, s).wait_recv()
        f_copy(2, s).wait_recv()
        for d in range(1, n):
            i = me + d

            @pl.when(jnp.logical_and(i < n, at.lowest(s, i) <= me))
            def _():
                kv_copy(s, i).wait_send()

    each(slots, finish)
    wo_sib.wait()
    wo_y.wait_send()
    wo_f.wait()


def middle(n, perm, xg, ag, cg, wog, gbf, wu, wd,
           out, rl, rf, gl, gsum,
           up_g, dn_g, hid, n2, act, upre, ep, er, es, ey, ef, fp, fc, fh, fy, ob, osd,
           e1s, e1r, e2s, e2r, e3s, e3r, f1s, f1r, f2s, f2r, f3s, f3r):
    at = Place(n)
    slots, _, rows, half = xg.shape
    length = rows // 2
    feat = half // 2
    core, y = at.core, at.y
    mine = pl.ds(length * core, length)
    other = pl.ds(length * (1 - core), length)
    at.greet([at.sib, at.yp], False)

    def e_core(s):
        return remote(ep.at[s, other], er.at[s], e1s.at[s], e1r.at[s], at.sib)

    def e_y(s):
        return remote(es.at[s], ey.at[s], e2s.at[s], e2r.at[s], at.yp)

    def e_back(s):
        return remote(ef.at[s, mine], ef.at[s, mine], e3s.at[s], e3r.at[s], at.sib)

    def f_core(s):
        return remote(fp.at[s, other], fc.at[s], f1s.at[s], f1r.at[s], at.sib)

    def f_y(s):
        return remote(fh.at[s, 1 - y], fy.at[s], f2s.at[s], f2r.at[s], at.yp)

    def f_back(s):
        return remote(osd.at[s], ob.at[s, core], f3s.at[s], f3r.at[s], at.sib)

    def forward(s):
        x = whole_rows(xg, s).astype(F32)
        branch = dot(ag[s, 0], wog[:half], 1, 0) + dot(ag[s, 1], wog[half:], 1, 0)
        h = x + branch
        hid[s, 0] = h[:, :half]
        hid[s, 1] = h[:, half:]
        mean, inv = row_stats(h)
        normed = ((h - mean) * inv * gbf[2:3] + gbf[3:4]).astype(BF16)
        n2[s] = normed
        up = dot(normed, wu[...], 1, 0)
        cube = 0.7978845608028654 * (up + 0.044715 * up * up * up)
        t = jnp.tanh(cube)
        act[s] = (0.5 * up * (1.0 + t)).astype(BF16)
        slope = 0.5 * (1.0 + t) + 0.5 * up * (1.0 - t * t) * (
            0.7978845608028654 * (1.0 + 3 * 0.044715 * up * up)
        )
        da = dot(whole_rows(cg, s), wd[...], 1, 1)
        pre = (da * slope).astype(BF16)
        upre[s] = pre
        ep[s] = dot(pre, wu[...], 1, 1).astype(BF16)
        e_core(s).start()

    def loop_one(t):
        @pl.when(t < slots)
        def _():
            forward(t)

        @pl.when(t >= 1)
        def _():
            s = t - 1
            e_core(s).wait_recv()
            es[s] = (ep[s, mine].astype(F32) + er[s].astype(F32)).astype(BF16)
            e_y(s).start()

    each(slots + 1, loop_one)
    dn_g[...] = jnp.zeros_like(dn_g)
    up_g[...] = jnp.zeros_like(up_g)
    gsum[...] = jnp.zeros_like(gsum)

    def loop_two(t):
        @pl.when(t < slots)
        def _():
            fp[t] = dot(act[t], wd[...], 1, 0).astype(BF16)
            f_core(t).start()
            dn_g[...] += dot(act[t], whole_rows(cg, t), 0, 0)
            up_g[...] += dot(n2[t], upre[t], 0, 0)
            e_y(t).wait_recv()
            ef[t, mine] = (es[t].astype(F32) + ey[t].astype(F32)).astype(BF16)
            e_back(t).start()

        @pl.when(t >= 1)
        def _():
            s = t - 1
            f_core(s).wait_recv()
            both = fp[s, mine].astype(F32) + fc[s].astype(F32)
            fh[s, 0] = both[:, :half].astype(BF16)
            fh[s, 1] = both[:, half:].astype(BF16)
            f_y(s).start()

    each(slots + 1, loop_two)

    gl[0] = up_g[...].astype(BF16).reshape(gl.shape[1:])
    gl[1] = dn_g[...].astype(BF16).reshape(gl.shape[1:])

    def loop_three(s):
        e_back(s).wait_recv()
        e = ef[s].astype(F32)
        h = whole_rows(hid, s)
        mean, inv = row_stats(h)
        xh = (h - mean) * inv
        gsum[2:3] += jnp.sum(e * xh, axis=0, keepdims=True)
        gsum[3:4] += jnp.sum(e, axis=0, keepdims=True)
        g = e * gbf[2:3]
        first = jnp.sum(g, axis=1, keepdims=True) / D
        second = jnp.sum(g * xh, axis=1, keepdims=True) / D
        resid = whole_rows(cg, s).astype(F32) + inv * (g - first - xh * second)
        rl[s] = resid.astype(BF16)

        for yy in range(2):
            for cc in range(2):

                @pl.when(jnp.logical_and(y == yy, core == cc))
                def _():
                    rf[s] = resid[cc * length : (cc + 1) * length, yy * half : (yy + 1) * half]

    each(slots, loop_three)

    def loop_four(s):
        f_y(s).wait_recv()
        total = hid[s, y, mine] + (fh[s, y].astype(F32) + fy[s].astype(F32))
        lo = total[:, :feat].astype(BF16)
        hi = total[:, feat:].astype(BF16)

        @pl.when(core == 0)
        def _():
            ob[s, 0] = lo
            osd[s] = hi

        @pl.when(core == 1)
        def _():
            ob[s, 1] = hi
            osd[s] = lo

        f_back(s).start()

    each(slots, loop_four)

    def finish(s):
        e_core(s).wait_send()
        e_y(s).wait_send()
        e_back(s).wait_send()
        f_core(s).wait_send()
        f_y(s).wait_send()
        f_back(s).wait()

    each(slots, finish)

    def place(s):
        out[s] = ob[perm[s]]

    each(slots, place)


def back(n, perm, xg, n1, gbf, w_t, wo, rl, rf, att, lse, qt, kvn, kvo, kvb, cos, sin, bounds, gl, gs_two,
         ig, res1, res2, res3, gains,
         og, qq, qkv, gsum, do, dq, drow, dkv, dst, dla, qp, ep, er, st, sr_, es, ss_, ey, sy, ib, isd,
         src2, src3, gx1, pt1, gz1, gx2, pt2, gz2, gx3, pt3, gz3, gh, gq, gf,
         ks, kr, a1s, a1r, b1s, b1r, a2s, a2r, b2s, b2r, a3s, a3r, hs, hr, qs, qr, *sums):
    at = Place(n)
    slots, _, rows, half = xg.shape
    sum1 = Sum(at, gl, res1, gx1, pt1, gz1, *sums[0:8])
    sum2 = Sum(at, src2, res2, gx2, pt2, gz2, *sums[8:16])
    sum3 = Sum(at, src3, res3, gx3, pt3, gz3, *sums[16:24])
    m = n // 2
    length = rows // 2
    feat = half // 2
    hl = feat // HEAD_DIM
    core, y, me = at.core, at.y, at.me
    mine = pl.ds(length * core, length)
    other = pl.ds(length * (1 - core), length)
    at.greet([at.sib, at.yp, at.diag], True)
    sum1.begin()
    every = slice(0, rows)

    def kv_copy(s, j):
        return remote(dst.at[s, j], dla.at[s, me], ks.at[s, j], kr.at[s, me], (j, at.head))

    def e_core(s):
        return remote(ep.at[s, other], er.at[s], a1s.at[s], a1r.at[s], at.sib)

    def s_core(s):
        return remote(st.at[s, 1 - core], sr_.at[s], b1s.at[s], b1r.at[s], at.sib)

    def e_y(s):
        return remote(es.at[s, 1 - y], ey.at[s], a2s.at[s], a2r.at[s], at.yp)

    def s_y(s):
        return remote(ss_.at[s], sy.at[s], b2s.at[s], b2r.at[s], at.yp)

    def i_back(s):
        return remote(isd.at[s], ib.at[s, core], a3s.at[s], a3r.at[s], at.sib)

    og[...] = jnp.zeros_like(og)
    qq[...] = jnp.zeros_like(qq)
    qkv[...] = jnp.zeros_like(qkv)
    gsum[...] = jnp.zeros_like(gsum)
    drow[...] = jnp.zeros_like(drow)

    heads = [slice(h * HEAD_DIM, (h + 1) * HEAD_DIM) for h in range(hl)]

    def head_grads(s, kv, lanes, allowed):
        q = [qt[s, hd, lanes] for hd in heads]
        d_out = [do[hd, lanes] for hd in heads]
        sc = [dot(kv[hd], q[h], 0, 0) for h, hd in enumerate(heads)]
        dp = [dot(kv[feat:][hd], d_out[h], 0, 0) for h, hd in enumerate(heads)]
        p = [
            jnp.exp(jnp.where(allowed, sc[h], masked_score) - lse[s, h : h + 1, lanes])
            for h in range(hl)
        ]
        ds = [(p[h] * (dp[h] - drow[h : h + 1, lanes])).astype(BF16) for h in range(hl)]
        dv = [dot(d_out[h], p[h].astype(BF16), 1, 1) for h in range(hl)]
        dk = [dot(q[h], ds[h], 1, 1) for h in range(hl)]
        dq_add = [dot(kv[hd], ds[h], 1, 0) for h, hd in enumerate(heads)]
        together = [jnp.concatenate(v, axis=0) for v in (dq_add, dk, dv)]
        return together

    def attend_back(s):
        low_rows = rl[s]
        d_out = dot(wo[...], low_rows, 1, 1).astype(BF16)
        do[...] = d_out
        a = att[s]
        og[...] += dot(a.astype(BF16), low_rows, 1, 0)
        prod = d_out.astype(F32) * a
        for h in range(hl):
            drow[h : h + 1] = jnp.sum(prod[h * HEAD_DIM : (h + 1) * HEAD_DIM], axis=0, keepdims=True)
        start, end = bounds[s, 0:1], bounds[s, 1:2]
        clean, noisy = masks(me, length, start, end)
        kc, kn = kvo[s], kvn[s]
        first = slice(0, length)
        dqa, dk, dv = head_grads(s, kc, every, clean)
        dqn, dkn, dvn = head_grads(s, kn, first, noisy)
        dq[...] = dqa
        dq[:, first] += dqn
        dkv[s, :feat] = dk
        dkv[s, feat:] = dv
        qp[s, 2 * feat :, first] = dvn.astype(BF16)
        qp[s, feat : 2 * feat, first] = turn(dkn, cos[:, :length], -sin[:, :length]).astype(BF16)

        def one(j, carry):
            kv = kvb[s, j]
            pos = lax.broadcasted_iota(jnp.int32, (length, rows), 0) + j * length
            allowed = pos >= start
            dqa, dk, dv = head_grads(s, kv, every, allowed)
            dq[...] += dqa
            dst[s, j, :feat] = dk.astype(BF16)
            dst[s, j, feat:] = dv.astype(BF16)
            kv_copy(s, j).start()
            return carry

        lax.fori_loop(at.lowest(s, me), me, one, 0)
        qp[s, :feat] = (turn(dq[...], cos[...], -sin[...]) * HEAD_DIM**-0.5).astype(BF16)
        qq[...] += dot(qp[s, :feat], n1[s], 1, 0)

    def loop_one(t):
        attend_back(t)

        @pl.when(jnp.logical_and(t >= 1, t <= m))
        def _():
            sum1.pass_on(t - 1)

    each(slots, loop_one)
    src2[0] = og[...].astype(BF16).reshape(src2.shape[1:])
    src2[1] = qq[...].astype(BF16).reshape(src2.shape[1:])
    sum2.begin()
    sum1.reduce()

    def project_back(s):
        for d in range(1, n):
            i = me + d

            @pl.when(jnp.logical_and(i < n, at.lowest(s, i) <= me))
            def _():
                remote(dst.at[s, i], dla.at[s, i], ks.at[s, i], kr.at[s, i], at.sib).wait_recv()
                dkv[s] += dla[s, i].astype(F32)

        late = slice(length, rows)
        total = dkv[s]
        qp[s, feat : 2 * feat, late] = turn(total[:feat], cos[:, late], -sin[:, late]).astype(BF16)
        qp[s, 2 * feat :, late] = total[feat:].astype(BF16)
        pre = qp[s]
        qkv[...] += dot(pre[feat:], n1[s], 1, 0)
        e = dot(pre, w_t[...], 0, 0)
        x = whole_rows(xg, s).astype(F32)
        mean, inv = row_stats(x)
        xh = (x - mean) * inv
        gsum[0:1] += jnp.sum(e * xh, axis=0, keepdims=True)
        gsum[1:2] += jnp.sum(e, axis=0, keepdims=True)
        ep[s] = e.astype(BF16)
        g = e * gbf[0:1]
        one_sum = jnp.sum(g, axis=1, keepdims=True)
        two_sum = jnp.sum(g * xh, axis=1, keepdims=True)
        lane = lax.broadcasted_iota(jnp.int32, (rows, 128), 1)
        packed = jnp.where(lane == 0, one_sum, jnp.where(lane == 1, two_sum, 0.0)).T
        st[s, 0] = packed[:8, :length]
        st[s, 1] = packed[:8, length:]
        e_core(s).start()
        s_core(s).start()

    def send_on(s):
        e_core(s).wait_recv()
        s_core(s).wait_recv()
        both = ep[s, mine].astype(F32) + er[s].astype(F32)
        es[s, 0] = both[:, :half].astype(BF16)
        es[s, 1] = both[:, half:].astype(BF16)
        ss_[s] = st[s, core] + sr_[s]
        e_y(s).start()
        s_y(s).start()

    def loop_two(t):
        @pl.when(t < slots)
        def _():
            project_back(t)

        @pl.when(t >= 1)
        def _():
            send_on(t - 1)

        @pl.when(jnp.logical_and(t >= 1, t < m))
        def _():
            sum1.forward(t)

        @pl.when(jnp.logical_and(t >= 1, t <= m))
        def _():
            sum2.pass_on(t - 1)

        @pl.when(t == m + 1)
        def _():
            sum2.reduce()

    each(slots + 1, loop_two)
    grads = qkv[...].astype(BF16)
    src3[0] = grads[:feat].reshape(src3.shape[1:])
    src3[1] = grads[feat:].reshape(src3.shape[1:])
    sum3.begin()
    h_copies = [
        remote(gsum, gh.at[k], hs.at[k], hr.at[k], d) for k, d in enumerate((at.sib, at.yp, at.diag))
    ]
    for copy in h_copies:
        copy.start()

    def share(i):
        return remote(gf, gq.at[me], qs.at[i], qr.at[me], (i, at.head))

    def share_in(i):
        return remote(gf, gq.at[i], qs.at[i], qr.at[i], (i, at.head))

    def input_part(s):
        e_y(s).wait_recv()
        s_y(s).wait_recv()
        e = es[s, y].astype(F32) + ey[s].astype(F32)
        sums = ss_[s] + sy[s]
        cols = jnp.concatenate([sums, jnp.zeros((120, length), F32)], axis=0).T
        first, second = cols[:, 0:1] / D, cols[:, 1:2] / D
        x = jnp.concatenate([xg[s, 0, mine], xg[s, 1, mine]], axis=1).astype(F32)
        mean, inv = row_stats(x)
        xh = (xg[s, y, mine].astype(F32) - mean) * inv
        gain = jnp.where(y == 0, gbf[0:1, :half], gbf[0:1, half:])
        grad = rf[s] + inv * (e * gain - first - xh * second)
        lo, hi = grad[:, :feat], grad[:, feat:]

        @pl.when(core == 0)
        def _():
            ib[s, 0] = lo
            isd[s] = hi

        @pl.when(core == 1)
        def _():
            ib[s, 1] = hi
            isd[s] = lo

        i_back(s).start()

    def loop_three(t):
        input_part(t)

        @pl.when(t < m - 1)
        def _():
            sum2.forward(t + 1)

        @pl.when(t >= slots - m)
        def _():
            sum3.pass_on(t - (slots - m))

        @pl.when(t == 0)
        def _():
            for copy in h_copies:
                copy.wait()
            total = gsum[...] + gh[0] + gh[1] + gh[2]
            row = lax.broadcasted_iota(jnp.int32, total.shape, 0)
            total = jnp.where(row < 2, total, gs_two[...])
            for h in range(4):

                @pl.when(at.head == h)
                def _():
                    gf[...] = total[:, h * feat : (h + 1) * feat]

            gq[me] = gf[...]
            for d in range(1, n):
                share(lax.rem(me + d, n)).start()

    each(slots, loop_three)
    sum3.reduce()
    for d in range(1, n):
        share_in(lax.rem(me + d, n)).wait_recv()
    gains[...] = jnp.sum(gq[...], axis=0)
    for d in range(1, m):
        sum3.forward(d)

    def finish(s):
        e_core(s).wait_send()
        s_core(s).wait_send()
        e_y(s).wait_send()
        s_y(s).wait_send()
        i_back(s).wait()

        def sent(j, carry):
            kv_copy(s, j).wait_send()
            return carry

        lax.fori_loop(at.lowest(s, me), me, sent, 0)

    each(slots, finish)

    for part in (sum1, sum2, sum3):
        part.finish()
    for d in range(1, n):
        share(lax.rem(me + d, n)).wait_send()

    def place(s):
        ig[s] = ib[perm[s]]

    each(slots, place)


def call(kernel, ident, n, operands, outs, scratch, flops):
    specs = [
        pl.BlockSpec(memory_space=pltpu.SMEM if o.ndim == 1 else VMEM) for o in operands
    ]
    return pl.pallas_call(
        functools.partial(kernel, n),
        out_shape=[jax.ShapeDtypeStruct(s, t) for s, t in outs],
        in_specs=specs,
        out_specs=[pl.BlockSpec(memory_space=VMEM)] * len(outs),
        scratch_shapes=scratch,
        compiler_params=pltpu.CompilerParams(
            collective_id=ident, has_side_effects=True, vmem_limit_bytes=VMEM_LIMIT
        ),
        cost_estimate=pl.CostEstimate(flops=flops, bytes_accessed=20 << 20, transcendentals=0),
        name=kernel.__name__,
    )(*operands)


def body(
    inputs,
    doc_lengths,
    attn_gain,
    attn_bias,
    w_qkv,
    w_out,
    ffn_gain,
    ffn_bias,
    w_up,
    w_down,
    cotangent,
):
    n = lax.axis_size("seq")
    slots, _, length, feat = inputs.shape
    rows, half, hl = 2 * length, 2 * feat, feat // HEAD_DIM
    held = slots * n * half * length * 2
    if held > ROWS_LIMIT:
        return gathered_body(
            inputs, doc_lengths, attn_gain, attn_bias, w_qkv, w_out, ffn_gain, ffn_bias, w_up, w_down, cotangent
        )
    sem = pltpu.SemaphoreType.DMA
    me = lax.axis_index("seq")
    long = jnp.argmax(doc_lengths[:, 0]).astype(jnp.int32)
    ids = jnp.arange(slots, dtype=jnp.int32)
    perm = jnp.where(ids == 0, long, jnp.where(ids == long, 0, ids))
    ends = jnp.cumsum(doc_lengths, axis=1)[perm]
    positions = me * length + jnp.arange(length, dtype=jnp.int32)
    past = ends[:, :, None] <= positions[None, None, :]
    first_key = jnp.max(jnp.where(past, ends[:, :, None], 0), axis=1)
    last_key = jnp.min(jnp.where(past, 2**30, ends[:, :, None]), axis=1)
    bounds = jnp.zeros((slots, 8, rows), jnp.int32)
    bounds = bounds.at[:, 0].set(jnp.tile(first_key, (1, 2))).at[:, 1].set(jnp.tile(last_key, (1, 2)))
    half_dim = HEAD_DIM // 2
    freqs = rotary_base ** (-jnp.arange(half_dim, dtype=F32) / half_dim)
    angles = freqs[:, None] * positions.astype(F32)[None, :]
    cos = jnp.tile(jnp.cos(angles), (1, 2))
    sin = jnp.tile(jnp.sin(angles), (1, 2))
    w_t = w_qkv.reshape(D, 3 * feat).T
    gains = jnp.concatenate(
        [jnp.stack([attn_gain, attn_bias, ffn_gain, ffn_bias]), jnp.zeros((4, feat), F32)], axis=0
    )
    fulls = [((slots, 2, rows, half), BF16)] * 3
    kinds = (3, slots)
    xg, cg, ag, wog, gbf, n1, qt, kvn, kvo, kvb, att, lse = call(
        front,
        0,
        n,
        (perm, inputs, cotangent, gains, w_t, w_out, cos, sin, bounds),
        fulls
        + [
            ((D, D), BF16),
            ((8, D), F32),
            ((slots, rows, D), BF16),
            ((slots, feat, rows), BF16),
            ((slots, half, length), BF16),
            ((slots, half, length), BF16),
            ((slots, n, half, length), BF16),
            ((slots, feat, rows), F32),
            ((slots, 8, rows), F32),
        ],
        [
            VMEM((3, slots, rows, feat), BF16),
            VMEM((3, slots, rows, feat), BF16),
            VMEM((4, 8, feat), F32),
            VMEM((feat, rows), F32),
            VMEM((8, rows), F32),
            VMEM((8, rows), F32),
            *[sem(kinds)] * 6,
            *[sem((3,))] * 4,
            *[sem((slots, n))] * 2,
        ],
        3 * 10**9,
    )
    wide = VMEM((slots, rows, D), BF16)
    part = VMEM((slots, length, D), BF16)
    m = n // 2
    outputs, rl, rf, gl, gsum2 = call(
        middle,
        1,
        n,
        (perm, xg, ag, cg, wog, gbf, w_up, w_down),
        [
            ((slots, 2, length, feat), BF16),
            ((slots, rows, D), BF16),
            ((slots, length, half), F32),
            ((2, m, D // m, D), BF16),
            ((8, D), F32),
        ],
        [
            VMEM(w_up.shape, F32),
            VMEM(w_down.shape, F32),
            VMEM((slots, 2, rows, half), F32),
            *[wide] * 4,
            *[part] * 3,
            *[wide] * 2,
            part,
            VMEM((slots, 2, length, half), BF16),
            VMEM((slots, length, half), BF16),
            VMEM((slots, 2, length, feat), BF16),
            VMEM((slots, length, feat), BF16),
            *[sem((slots,))] * 12,
        ],
        15 * 10**9,
    )
    stat = VMEM((slots, 8, length), F32)
    quarter = [VMEM((m, D // m, D), BF16)] * 3
    small = (m, feat // m, D)
    input_grad, res1, res2, res3, gain_grads = call(
        back,
        2,
        n,
        (perm, xg, n1, gbf, w_t, w_out, rl, rf, att, lse, qt, kvn, kvo, kvb, cos, sin, bounds, gl, gsum2),
        [
            ((slots, 2, length, feat), F32),
            ((2, m, D // m, D), BF16),
            ((2, *small), BF16),
            ((2, *small), BF16),
            ((8, feat), F32),
        ],
        [
            VMEM((feat, D), F32),
            VMEM((feat, D), F32),
            VMEM((half, D), F32),
            VMEM((8, D), F32),
            VMEM((feat, rows), BF16),
            VMEM((feat, rows), F32),
            VMEM((8, rows), F32),
            VMEM((slots, half, length), F32),
            VMEM((slots, n, half, length), BF16),
            VMEM((slots, n, half, length), BF16),
            VMEM((slots, 3 * feat, rows), BF16),
            wide,
            part,
            VMEM((slots, 2, 8, length), F32),
            stat,
            VMEM((slots, 2, length, half), BF16),
            stat,
            VMEM((slots, length, half), BF16),
            stat,
            VMEM((slots, 2, length, feat), F32),
            VMEM((slots, length, feat), F32),
            *[VMEM((2, *small), BF16)] * 2,
            *quarter,
            *[VMEM(small, BF16)] * 6,
            VMEM((3, 8, D), F32),
            VMEM((n, 8, feat), F32),
            VMEM((8, feat), F32),
            *[sem((slots, n))] * 2,
            *[sem((slots,))] * 10,
            *[sem((3,))] * 2,
            *[sem((n,))] * 2,
            *[sem((m,))] * 24,
        ],
        10 * 10**9,
    )
    up_grad, down_grad = res1.reshape(2, D, D).astype(F32)
    out_grad, q_grad = res2.reshape(2, feat, D).astype(F32)
    qkv_grad = jnp.concatenate([q_grad[None], res3.reshape(2, feat, D).astype(F32)], axis=0)
    return (
        outputs,
        input_grad,
        jnp.transpose(qkv_grad, (2, 0, 1)),
        out_grad,
        up_grad,
        down_grad,
        gain_grads[0],
        gain_grads[1],
        gain_grads[2],
        gain_grads[3],
    )


def solution(mesh):
    in_specs = (
        P(None, None, "seq", "head"),
        P(),
        P("head"),
        P("head"),
        P(None, None, "head"),
        P("head", None),
        P("head"),
        P("head"),
        P(None, "head"),
        P("head", None),
        P(None, None, "seq", "head"),
    )
    out_specs = (
        P(None, None, "seq", "head"),
        P(None, None, "seq", "head"),
        P(None, None, "head"),
        P("head", None),
        P(None, "head"),
        P("head", None),
        P("head"),
        P("head"),
        P("head"),
        P("head"),
    )
    return jax.shard_map(body, mesh=mesh, in_specs=in_specs, out_specs=out_specs, check_vma=False)
```

```python
import functools
import types

import jax
import jax.numpy as jnp
from jax import lax
from jax.experimental import pallas as pl
from jax.experimental.pallas import tpu as pltpu
from jax.sharding import PartitionSpec as P

D = 768
HEAD_DIM = 64
BLOCK = 16


norm_eps = 1e-05
masked_score = -1e30
rotary_base = 10000.0

MESH = pl.DeviceIdType.MESH
VMEM = pltpu.VMEM
F32 = jnp.float32
BF16 = jnp.bfloat16
ROWS_LIMIT = 16 << 20
VMEM_LIMIT = 63 << 20


def passed_along(block, axis, distance):
    devices = range(lax.axis_size(axis))
    route = [(i - distance, i) for i in devices if i - distance in devices]
    return lax.ppermute(block, axis, route)


def from_behind(x, axis, by):
    devices = lax.axis_size(axis)
    return lax.ppermute(x, axis, [(i, (i + by) % devices) for i in range(devices)])


def segment_ids(doc_lengths, positions):
    doc_ends = jnp.cumsum(doc_lengths, axis=1)
    return jnp.sum((doc_ends[:, :, None] <= positions[None, None, :]).astype(jnp.int32), axis=1)


def rotate(values, positions, sign):
    half_dim = values.shape[-1] // 2
    freqs = rotary_base ** (-jnp.arange(half_dim, dtype=jnp.float32) / half_dim)
    angles = positions.astype(jnp.float32)[:, None, None] * freqs
    cosine = jnp.cos(angles)
    sine = sign * jnp.sin(angles)
    first_half = values[..., :half_dim]
    second_half = values[..., half_dim:]
    return jnp.concatenate(
        [first_half * cosine - second_half * sine, second_half * cosine + first_half * sine],
        axis=-1,
    )


def row_pair(first_sum, second_sum):
    return lax.psum((first_sum, second_sum), "head")


def normalize(share, gain, bias):
    row_total, row_square = row_pair(jnp.sum(share, axis=-1), jnp.sum(share * share, axis=-1))
    mean_value = row_total / D
    inv_std = lax.rsqrt(row_square / D - mean_value * mean_value + norm_eps)
    centered = (share - mean_value[..., None]) * inv_std[..., None]
    scaled = (centered * gain + bias).astype(jnp.bfloat16)
    gathered = lax.all_gather(scaled, "head", axis=3, tiled=True)
    return (gathered, centered, inv_std)


def norm_backward(partial_value, gain, centered, inv_std):
    share = lax.psum_scatter(partial_value, "head", scatter_dimension=3, tiled=True)
    scaled = share * gain
    first_mean, second_mean = row_pair(
        jnp.sum(scaled, axis=-1), jnp.sum(scaled * centered, axis=-1)
    )
    grad_in = inv_std[..., None] * (
        scaled - first_mean[..., None] / D - centered * (second_mean[..., None] / D)
    )
    gain_grad = jnp.sum(share * centered, axis=(0, 1, 2))
    bias_grad = jnp.sum(share, axis=(0, 1, 2))
    return (grad_in, gain_grad, bias_grad)


def branch_total(partial_value):
    return lax.psum_scatter(partial_value, "head", scatter_dimension=3, tiled=True)


def gradient_rows(share):
    return lax.all_gather(share, "head", axis=3, tiled=True)


def mask_rule(query_pos, query_seg, key_pos, key_seg):
    query_block = (query_pos // BLOCK)[:, None]
    key_block = (key_pos // BLOCK)[None, :]
    order = jnp.stack([key_block < query_block, key_block <= query_block])
    same_doc = query_seg[:, :, None] == key_seg[:, None, :]
    return jnp.logical_and(order[None, :, None], same_doc[:, None, None])


def absorb(state_now, scores, allowed, value_piece):
    run_max, run_sum, run_acc = state_now
    masked = jnp.where(allowed, scores, masked_score)
    new_max = jnp.maximum(run_max, jnp.max(masked, axis=-1))
    weights_now = jnp.where(allowed, jnp.exp(masked - new_max[..., None]), 0.0)
    factor = jnp.exp(run_max - new_max)
    new_sum = run_sum * factor + jnp.sum(weights_now, axis=-1)
    added = jnp.einsum(
        "schlk,skhd->schld",
        weights_now,
        value_piece.astype(jnp.float32),
        precision=lax.Precision.HIGHEST,
    )
    return (new_max, new_sum, run_acc * factor[..., None] + added)


def gathered_body(
    inputs,
    doc_lengths,
    attn_gain,
    attn_bias,
    w_qkv,
    w_out,
    ffn_gain,
    ffn_bias,
    w_up,
    w_down,
    cotangent,
):
    seqs_here, _, local_len, _ = inputs.shape
    head_local = w_qkv.shape[2] // HEAD_DIM
    first_pos = lax.axis_index("seq") * local_len
    positions = first_pos + jnp.arange(local_len, dtype=jnp.int32)
    segments = segment_ids(doc_lengths, positions)
    inputs_wide = inputs.astype(jnp.float32)
    normed_one, centered_one, inv_one = normalize(inputs_wide, attn_gain, attn_bias)
    projected = jnp.einsum("scld,dtk->scltk", normed_one, w_qkv, preferred_element_type=jnp.float32)
    split_rows = projected.reshape(seqs_here, 2, local_len, 3, head_local, HEAD_DIM)
    queries = (rotate(split_rows[:, :, :, 0], positions, 1.0) * HEAD_DIM ** (-0.5)).astype(
        jnp.bfloat16
    )
    key_rows = rotate(split_rows[:, :, :, 1], positions, 1.0).astype(jnp.bfloat16)
    value_rows = split_rows[:, :, :, 2].astype(jnp.bfloat16)
    clean_keys = key_rows[:, 1].reshape(seqs_here, local_len, head_local * HEAD_DIM)
    clean_values = value_rows[:, 1].reshape(seqs_here, local_len, head_local * HEAD_DIM)
    block_ids = positions // BLOCK
    own_allowed = jnp.logical_and(
        (block_ids[:, None] == block_ids[None, :])[None],
        segments[:, :, None] == segments[:, None, :],
    )[:, None, None]
    noisy_scores = jnp.einsum(
        "sclhd,skhd->schlk", queries[:, :1], key_rows[:, 0], preferred_element_type=jnp.float32
    )
    half_shape = (seqs_here, 1, head_local, local_len)
    empty_state = (
        jnp.full(half_shape, masked_score, jnp.float32),
        jnp.zeros(half_shape, jnp.float32),
        jnp.zeros(half_shape + (HEAD_DIM,), jnp.float32),
    )
    noisy_state = absorb(empty_state, noisy_scores, own_allowed, value_rows[:, 0])
    start_state = jax.tree.map(
        lambda first, second: jnp.concatenate([first, second], axis=1), noisy_state, empty_state
    )
    piece_keys = lax.all_gather(clean_keys, "seq", axis=1, tiled=True)
    piece_values = lax.all_gather(clean_values, "seq", axis=1, tiled=True)
    piece_len = piece_keys.shape[1]
    key_pos = jnp.arange(piece_len, dtype=jnp.int32)
    key_seg = segment_ids(doc_lengths, key_pos)
    key_heads = piece_keys.reshape(seqs_here, piece_len, head_local, HEAD_DIM)
    value_heads = piece_values.reshape(seqs_here, piece_len, head_local, HEAD_DIM)
    scores = jnp.einsum("sclhd,skhd->schlk", queries, key_heads, preferred_element_type=jnp.float32)
    final_max, final_sum, final_acc = absorb(
        start_state, scores, mask_rule(positions, segments, key_pos, key_seg), value_heads
    )
    attended = final_acc / final_sum[..., None]
    log_total = final_max + jnp.log(final_sum)
    attended_low = attended.astype(jnp.bfloat16)
    out_heads = w_out.reshape(head_local, HEAD_DIM, w_out.shape[1])
    attn_share = branch_total(
        jnp.einsum("schld,hdm->sclm", attended_low, out_heads, preferred_element_type=jnp.float32)
    )
    hidden_res = inputs_wide + attn_share
    normed_two, centered_two, inv_two = normalize(hidden_res, ffn_gain, ffn_bias)
    up_value = jnp.einsum("scld,df->sclf", normed_two, w_up, preferred_element_type=jnp.float32)
    activated, gelu_back = jax.vjp(lambda inner: jax.nn.gelu(inner, approximate=True), up_value)
    act_low = activated.astype(jnp.bfloat16)
    ffn_share = branch_total(
        jnp.einsum("sclf,fm->sclm", act_low, w_down, preferred_element_type=jnp.float32)
    )
    outputs = (hidden_res + ffn_share).astype(jnp.bfloat16)
    grad_out = cotangent.astype(jnp.float32)
    grad_full = gradient_rows(cotangent)
    down_grad = jnp.einsum("sclf,sclm->fm", act_low, grad_full, preferred_element_type=jnp.float32)
    act_grad = jnp.einsum("sclm,fm->sclf", grad_full, w_down, preferred_element_type=jnp.float32)
    up_pre_grad = gelu_back(act_grad)[0].astype(jnp.bfloat16)
    up_grad = jnp.einsum(
        "scld,sclf->df", normed_two, up_pre_grad, preferred_element_type=jnp.float32
    )
    normed_two_grad = jnp.einsum(
        "sclf,df->scld", up_pre_grad, w_up, preferred_element_type=jnp.float32
    )
    back_two, ffn_gain_grad, ffn_bias_grad = norm_backward(
        normed_two_grad, ffn_gain, centered_two, inv_two
    )
    resid_grad = grad_out + back_two
    resid_full = gradient_rows(resid_grad.astype(jnp.bfloat16))
    out_grad = jnp.einsum(
        "schld,sclm->hdm", attended_low, resid_full, preferred_element_type=jnp.float32
    ).reshape(w_out.shape)
    attended_grad = jnp.einsum(
        "sclm,hdm->schld", resid_full, out_heads, preferred_element_type=jnp.float32
    ).astype(jnp.bfloat16)
    grad_wide = attended_grad.astype(jnp.float32)
    row_delta = jnp.sum(grad_wide * attended, axis=-1)
    noisy_probs = jnp.where(own_allowed, jnp.exp(noisy_scores - log_total[:, :1, :, :, None]), 0.0)
    noisy_prob_grad = jnp.einsum(
        "schld,skhd->schlk",
        attended_grad[:, :1],
        value_rows[:, 0],
        preferred_element_type=jnp.float32,
    )
    noisy_score_grad = (noisy_probs * (noisy_prob_grad - row_delta[:, :1, :, :, None])).astype(
        jnp.bfloat16
    )
    noisy_query_grad = jnp.einsum(
        "schlk,skhd->schld", noisy_score_grad, key_rows[:, 0], preferred_element_type=jnp.float32
    )
    noisy_key_grad = jnp.einsum(
        "schlk,sclhd->skhd", noisy_score_grad, queries[:, :1], preferred_element_type=jnp.float32
    )
    noisy_value_grad = jnp.einsum(
        "schlk,schld->skhd", noisy_probs, grad_wide[:, :1], precision=lax.Precision.HIGHEST
    )
    query_start = jnp.concatenate([noisy_query_grad, jnp.zeros_like(noisy_query_grad)], axis=1)
    flat_zero = jnp.zeros((seqs_here, local_len, head_local * HEAD_DIM), jnp.float32)

    def piece_grads(piece_keys, piece_values, first_row, query_total):
        key_pos = first_row + jnp.arange(local_len, dtype=jnp.int32)
        key_seg = segment_ids(doc_lengths, key_pos)
        key_heads = piece_keys.reshape(seqs_here, local_len, head_local, HEAD_DIM)
        value_heads = piece_values.reshape(seqs_here, local_len, head_local, HEAD_DIM)
        scores = jnp.einsum(
            "sclhd,skhd->schlk", queries, key_heads, preferred_element_type=jnp.float32
        )
        allowed = mask_rule(positions, segments, key_pos, key_seg)
        weights_now = jnp.where(allowed, jnp.exp(scores - log_total[..., None]), 0.0)
        prob_grad = jnp.einsum(
            "schld,skhd->schlk", attended_grad, value_heads, preferred_element_type=jnp.float32
        )
        score_grad = (weights_now * (prob_grad - row_delta[..., None])).astype(jnp.bfloat16)
        query_out = query_total + jnp.einsum(
            "schlk,skhd->schld", score_grad, key_heads, preferred_element_type=jnp.float32
        )
        key_part = jnp.einsum(
            "schlk,sclhd->skhd", score_grad, queries, preferred_element_type=jnp.float32
        )
        value_part = jnp.einsum(
            "schlk,schld->skhd", weights_now, grad_wide, precision=lax.Precision.HIGHEST
        )
        return (key_part.reshape(flat_zero.shape), value_part.reshape(flat_zero.shape), query_out)

    def cycle_body(cycle_step, carried):
        piece_keys, piece_values, key_acc, value_acc, query_acc = carried
        source = (lax.axis_index("seq") - cycle_step) % lax.axis_size("seq")
        first_row = source * local_len
        key_part, value_part, query_acc = piece_grads(
            piece_keys, piece_values, first_row, query_acc
        )
        key_acc = key_acc + key_part
        value_acc = value_acc + value_part
        piece_keys, piece_values = passed_along((piece_keys, piece_values), "seq", 1)
        key_acc, value_acc = (
            from_behind(key_acc.astype(jnp.bfloat16), "seq", 1).astype(key_acc.dtype),
            from_behind(value_acc.astype(jnp.bfloat16), "seq", 1).astype(value_acc.dtype),
        )
        return (piece_keys, piece_values, key_acc, value_acc, query_acc)

    cycle_start = (clean_keys, clean_values, flat_zero, flat_zero, query_start)
    _, _, clean_key_grad, clean_value_grad, query_acc = lax.fori_loop(
        0, lax.axis_size("seq"), cycle_body, cycle_start
    )
    head_shape = (seqs_here, local_len, head_local, HEAD_DIM)
    query_total = rotate(jnp.transpose(query_acc, (0, 1, 3, 2, 4)), positions, -1.0) * HEAD_DIM ** (
        -0.5
    )
    key_total = rotate(
        jnp.stack([noisy_key_grad, clean_key_grad.reshape(head_shape)], axis=1), positions, -1.0
    )
    value_total = jnp.stack([noisy_value_grad, clean_value_grad.reshape(head_shape)], axis=1)
    qkv_pre_grad = (
        jnp.stack([query_total, key_total, value_total], axis=3)
        .reshape(seqs_here, 2, local_len, 3, head_local * HEAD_DIM)
        .astype(jnp.bfloat16)
    )
    qkv_grad = jnp.einsum(
        "scld,scltk->dtk", normed_one, qkv_pre_grad, preferred_element_type=jnp.float32
    )
    normed_one_grad = jnp.einsum(
        "scltk,dtk->scld", qkv_pre_grad, w_qkv, preferred_element_type=jnp.float32
    )
    back_one, attn_gain_grad, attn_bias_grad = norm_backward(
        normed_one_grad, attn_gain, centered_one, inv_one
    )
    input_grad = resid_grad + back_one
    (
        qkv_grad,
        out_grad,
        up_grad,
        down_grad,
        attn_gain_grad,
        attn_bias_grad,
        ffn_gain_grad,
        ffn_bias_grad,
    ) = lax.psum(
        (
            qkv_grad,
            out_grad,
            up_grad,
            down_grad,
            attn_gain_grad,
            attn_bias_grad,
            ffn_gain_grad,
            ffn_bias_grad,
        ),
        "seq",
    )
    return (
        outputs,
        input_grad,
        qkv_grad,
        out_grad,
        up_grad,
        down_grad,
        attn_gain_grad,
        attn_bias_grad,
        ffn_gain_grad,
        ffn_bias_grad,
    )


def dot(a, b, ca, cb):
    return lax.dot_general(a, b, (((ca,), (cb,)), ((), ())), preferred_element_type=F32)


def remote(src, dst, send, recv, device):
    return pltpu.make_async_remote_copy(
        src_ref=src, dst_ref=dst, send_sem=send, recv_sem=recv, device_id=device, device_id_type=MESH
    )


class Place:
    def __init__(self, n):
        self.n = n
        self.me = lax.axis_index("seq")
        self.head = lax.axis_index("head")
        self.core = lax.rem(self.head, 2)
        self.y = lax.div(self.head, 2)
        self.sib = (self.me, self.y * 2 + 1 - self.core)
        self.yp = (self.me, (1 - self.y) * 2 + self.core)
        self.diag = (self.me, (1 - self.y) * 2 + 1 - self.core)
        self.half = n // 2
        self.band = max(1, n // 8)

    def lowest(self, slot, i):
        near = i - self.band
        short = jnp.where(i >= self.half, jnp.minimum(near, self.half), near)
        return jnp.where(slot == 0, 0, jnp.maximum(short, 0))

    def spot(self, slot, block, other):
        window = self.half + self.band
        near = self.half + lax.rem(other, self.band)
        late = jnp.where(block >= self.half, other - self.half, near)
        return jnp.where(slot == 0, other, self.n + (slot - 1) * window + late)

    def spots(self, slots):
        return self.n + (slots - 1) * (self.half + self.band)

    def greet(self, near, everyone):
        bar = pltpu.get_barrier_semaphore()
        for d in near:
            pl.semaphore_signal(bar, inc=1, device_id=d, device_id_type=MESH)
        count = len(near)
        if everyone:
            for d in range(1, self.n):
                there = lax.rem(self.me + d, self.n)
                pl.semaphore_signal(bar, inc=1, device_id=(there, self.head), device_id_type=MESH)
            count += self.n - 1
        pl.semaphore_wait(bar, count)


def each(count, step):
    def run(i, carry):
        step(i)
        return carry

    lax.fori_loop(0, count, run, 0)


def row_stats(x):
    mean = jnp.sum(x, axis=1, keepdims=True) / D
    var = jnp.sum(x * x, axis=1, keepdims=True) / D - mean * mean
    return mean, lax.rsqrt(var + norm_eps)


def whole_rows(ref, s):
    return jnp.concatenate([ref[s, 0], ref[s, 1]], axis=1)


def turn(v, cosine, sine):
    parts = []
    for h in range(v.shape[0] // HEAD_DIM):
        a = v[h * 64 : h * 64 + 32]
        b = v[h * 64 + 32 : h * 64 + 64]
        parts += [a * cosine - b * sine, b * cosine + a * sine]
    return jnp.concatenate(parts, axis=0)


def masks(me, length, start, end):
    shape = (length, 2 * length)
    key = lax.broadcasted_iota(jnp.int32, shape, 0)
    row = lax.broadcasted_iota(jnp.int32, shape, 1)
    noisy = row < length
    at = jnp.where(noisy, row, row - length)
    key_block = key >> 4
    row_block = at >> 4
    pos = key + me * length
    same = jnp.logical_and(pos >= start, pos < end)
    clean = jnp.logical_and(same, key_block < row_block + jnp.where(noisy, 0, 1))
    own = jnp.logical_and(same, key_block == row_block)[:, :length]
    return clean, own


class Sum:
    def __init__(self, at, src, res, gx, part, gz, own, xs, xr, zs, zr, cs, cr, fs, fr, ls):
        self.m = at.n // 2
        self.lo = lax.rem(at.me, 2)
        self.hi = lax.div(at.me, 2)
        self.head = at.head
        self.pair = (at.me + 1 - 2 * self.lo, at.head)
        self.src, self.res, self.gx, self.part, self.gz = src, res, gx, part, gz
        self.xs, self.xr, self.zs, self.zr = xs, xr, zs, zr
        self.cs, self.cr, self.fs, self.fr, self.ls = cs, cr, fs, fr, ls
        self.own = own

    def piece(self, half, k):
        size = self.gx.shape[1]
        return half, pl.ds(pl.multiple_of(k * size, 16), size)

    def at_z(self, k):
        return (2 * k + self.lo, self.head)

    def x(self, k):
        return remote(self.src.at[self.piece(1 - self.lo, k)], self.gx.at[k], self.xs.at[k], self.xr.at[k], self.pair)

    def z(self, k):
        return remote(self.part.at[k], self.gz.at[self.hi], self.zs.at[k], self.zr.at[self.hi], self.at_z(k))

    def z_in(self, k):
        return remote(self.part.at[k], self.gz.at[k], self.zs.at[k], self.zr.at[k], self.at_z(k))

    def c(self, k):
        there = self.res.at[self.lo, self.hi]
        return remote(self.own, there, self.cs.at[k], self.cr.at[self.hi], self.at_z(k))

    def c_in(self, k):
        part = self.res.at[self.lo, k]
        return remote(part, part, self.cs.at[k], self.cr.at[k], self.at_z(k))

    def f(self, k):
        part = self.res.at[self.lo, k]
        return remote(part, part, self.fs.at[k], self.fr.at[k], self.pair)

    def f_own(self):
        there = self.res.at[self.lo, self.hi]
        return remote(self.own, there, self.fs.at[self.hi], self.fr.at[self.hi], self.pair)

    def keep(self):
        return pltpu.make_async_copy(self.own, self.res.at[self.lo, self.hi], self.ls)

    def others(self):
        return [lax.rem(self.hi + d, self.m) for d in range(1, self.m)]

    def begin(self):
        each(self.m, lambda k: self.x(k).start())

    def pass_on(self, k):
        self.x(k).wait_recv()
        self.part[k] = (self.src[self.piece(self.lo, k)].astype(F32) + self.gx[k].astype(F32)).astype(BF16)

        @pl.when(k != self.hi)
        def _():
            self.z(k).start()

    def reduce(self):
        total = self.part[self.hi].astype(F32)
        for k in self.others():
            self.z_in(k).wait_recv()
            total += self.gz[k].astype(F32)
        self.own[...] = total.astype(BF16)
        self.keep().start()
        for k in self.others():
            self.c(k).start()
        self.f_own().start()

    def forward(self, d):
        k = lax.rem(self.hi + d, self.m)
        self.c_in(k).wait_recv()
        self.f(k).start()

    def finish(self):
        each(self.m, lambda k: self.x(k).wait_send())
        for k in self.others():
            self.z(k).wait_send()
            self.c(k).wait_send()
            self.f(k).wait()
        self.f_own().wait()
        self.keep().wait()


def layer(n, names, *refs):
    r = types.SimpleNamespace(**dict(zip(names, refs)))
    at = Place(n)
    slots, rows, feat = r.x_in.shape
    length = rows // 2
    half = 2 * feat
    hl = feat // HEAD_DIM
    m = n // 2
    core, y, me = at.core, at.y, at.me
    mine = pl.ds(length * core, length)
    other = pl.ds(length * (1 - core), length)
    early, late = slice(0, length), slice(length, rows)
    heads = [slice(h * HEAD_DIM, (h + 1) * HEAD_DIM) for h in range(hl)]
    fulls = (r.xg, r.cg, r.ag)
    owns = (r.x_in, r.c_in, r.own_att)
    lands = (r.land.at[0], r.land.at[1], r.land.at[0])
    quarter = D // m
    sum1 = Sum(
        at, r.gl, r.res1, r.gx1, r.act.at[:m, :quarter], r.gz1, r.own1, *[getattr(r, "u%d" % i) for i in range(9)]
    )
    src2 = r.act.at[m : m + 2, :feat]
    sum2 = Sum(at, src2, r.res2, r.gx2, r.pt2, r.gz2, r.own2, *[getattr(r, "v%d" % i) for i in range(9)])
    sum3 = Sum(at, r.src3, r.res3, r.gx3, r.pt3, r.gz3, r.own3, *[getattr(r, "w%d" % i) for i in range(9)])

    def sib_copy(k, s):
        return remote(owns[k].at[s], lands[k].at[s], r.ss.at[k, s], r.sr.at[k, s], at.sib)

    def build(k, s):
        a, b = owns[k][s], lands[k][s]

        @pl.when(core == 0)
        def _():
            fulls[k][s, y] = jnp.concatenate([a, b], axis=1)

        @pl.when(core == 1)
        def _():
            fulls[k][s, y] = jnp.concatenate([b, a], axis=1)

    def y_copy(k, s):
        part = fulls[k].at[s, y, mine]
        return remote(part, part, r.ys.at[k, s], r.yr.at[k, s], at.yp)

    def f_copy(k, s):
        part = fulls[k].at[s, 1 - y, mine]
        return remote(part, part, r.fs.at[k, s], r.fr.at[k, s], at.sib)

    def kv_copy(s, i):
        return remote(r.kvo.at[s], r.kvb.at[at.spot(s, me, me)], r.ks.at[s, i], r.kr.at[s, me], (i, at.head))

    def kv_in(s, j):
        return remote(r.kvo.at[s], r.kvb.at[at.spot(s, j, j)], r.ks.at[s, j], r.kr.at[s, j], (j, at.head))

    def dkv_copy(s, j):
        return remote(
            r.kvb.at[at.spot(s, j, j)], r.dla.at[at.spot(s, j, me)], r.ds.at[s, j], r.dr.at[s, me], (j, at.head)
        )

    def dkv_in(s, i):
        here = r.dla.at[at.spot(s, me, i)]
        return remote(here, here, r.ds.at[s, i], r.dr.at[s, i], (i, at.head))

    def readers(s, step):
        for d in range(1, n):
            i = me + d

            @pl.when(jnp.logical_and(i < n, at.lowest(s, i) <= me))
            def _():
                step(i)

    def e_core(s):
        return remote(r.ep.at[s, other], r.er.at[s], r.e1s.at[s], r.e1r.at[s], at.sib)

    def e_y(s):
        return remote(r.er.at[s], r.ey.at[s], r.e2s.at[s], r.e2r.at[s], at.yp)

    def e_back(s):
        return remote(r.ey.at[s], r.eb.at[s], r.e3s.at[s], r.e3r.at[s], at.sib)

    def held(first, s, k):
        return (s, pl.ds(first, length), pl.ds(pl.multiple_of(k * half, 128), half))

    def f_core(s):
        return remote(r.ag.at[s, :, other], r.fc.at[s], r.f1s.at[s], r.f1r.at[s], at.sib)

    def f_y(s):
        return remote(r.upre.at[held(0, s, 1 - y)], r.fy.at[s], r.f2s.at[s], r.f2r.at[s], at.yp)

    def f_back(s):
        return remote(r.osd.at[s], r.out.at[s, core], r.f3s.at[s], r.f3r.at[s], at.sib)

    def b_core(s):
        return remote(r.n2.at[s, other], r.er.at[s], r.a1s.at[s], r.a1r.at[s], at.sib)

    def s_core(s):
        return remote(r.st.at[s, 1 - core], r.sl.at[s], r.b1s.at[s], r.b1r.at[s], at.sib)

    def b_y(s):
        return remote(r.upre.at[held(length, s, 1 - y)], r.bey.at[s], r.a2s.at[s], r.a2r.at[s], at.yp)

    def s_y(s):
        return remote(r.sh.at[s], r.sy.at[s], r.b2s.at[s], r.b2r.at[s], at.yp)

    def b_back(s):
        return remote(r.isd.at[s], r.ig.at[s, core], r.a3s.at[s], r.a3r.at[s], at.sib)

    at.greet([at.sib, at.yp, at.diag], True)
    each(slots, lambda s: sib_copy(0, s).start())
    r.gland[at.head] = r.gb_in[...]
    g_copies = [
        remote(r.gb_in, r.gland.at[at.head], r.gs.at[k], r.gr.at[k], d)
        for k, d in enumerate((at.sib, at.yp, at.diag))
    ]
    for copy in g_copies:
        copy.start()

    def first_y(s):
        sib_copy(0, s).wait_recv()
        build(0, s)
        y_copy(0, s).start()

    each(slots, first_y)

    def wo_block(who):
        return r.wog.at[pl.ds(pl.multiple_of(feat * who, 16), feat)]

    wo_sib = remote(r.wo_in, wo_block(at.head), r.ws.at[0], r.wr.at[0], at.sib)
    wo_y = remote(r.wo_in, wo_block(at.head), r.ws.at[1], r.wr.at[1], at.yp)
    wo_f = remote(wo_block(at.yp[1]), wo_block(at.yp[1]), r.ws.at[2], r.wr.at[2], at.sib)
    wo_y.start()
    wo_sib.start()
    each(slots, lambda s: sib_copy(1, s).start())
    r.wog[pl.ds(pl.multiple_of(feat * at.head, 16), feat)] = r.wo_in[...]
    for copy in g_copies:
        copy.wait()
    r.gbf[...] = jnp.concatenate([r.gland[i] for i in range(4)], axis=1)
    r.mrow[...] = jnp.zeros_like(r.mrow)
    r.lrow[...] = jnp.ones_like(r.lrow)
    r.og[...] = jnp.zeros_like(r.og)
    r.qq[...] = jnp.zeros_like(r.qq)
    r.qkv[...] = jnp.zeros_like(r.qkv)
    r.gsum[...] = jnp.zeros_like(r.gsum)
    r.gtwo[...] = jnp.zeros_like(r.gtwo)
    r.drow[...] = jnp.zeros_like(r.drow)

    def project(s):
        x = whole_rows(r.xg, s).astype(F32)
        mean, inv = row_stats(x)
        normed = ((x - mean) * inv * r.gbf[0:1] + r.gbf[1:2]).astype(BF16)
        r.n1[s] = normed
        pt = dot(r.w_t[...], normed, 1, 1)
        qk = turn(pt[:half], r.cos[...], r.sin[...])
        r.qt[s] = (qk[:feat] * HEAD_DIM**-0.5).astype(BF16)
        kv = jnp.concatenate([qk[feat:], pt[half:]], axis=0).astype(BF16)
        r.kvn[s] = kv[:, :length]
        r.kvo[s] = kv[:, length:]
        readers(s, lambda i: kv_copy(s, i).start())

    def arrive(t):
        @pl.when(t < slots)
        def _():
            y_copy(0, t).wait_recv()
            f_copy(0, t).start()

        @pl.when(t >= 1)
        def _():
            f_copy(0, t - 1).wait_recv()
            project(t - 1)

    each(slots + 1, arrive)

    def cot_on(s):
        sib_copy(1, s).wait_recv()
        build(1, s)
        y_copy(1, s).start()

    each(2, cot_on)

    def attend(s):
        start, end = r.bounds[s, 0:1], r.bounds[s, 1:2]
        clean, noisy = masks(me, length, start, end)
        kc, kn = r.kvo[s], r.kvn[s]
        q = [r.qt[s, hd] for hd in heads]
        sc = [dot(kc[hd], q[h], 0, 0) for h, hd in enumerate(heads)]
        sn = [dot(kn[hd], q[h][:, :length], 0, 0) for h, hd in enumerate(heads)]
        sc = [jnp.where(clean, v, masked_score) for v in sc]
        sn = [jnp.where(noisy, v, masked_score) for v in sn]
        top = []
        for h in range(hl):
            tc = jnp.max(sc[h], axis=0, keepdims=True)
            tn = jnp.max(sn[h], axis=0, keepdims=True)
            top.append(jnp.concatenate([jnp.maximum(tc[:, :length], tn), tc[:, length:]], axis=1))
        pc = [jnp.exp(sc[h] - top[h]) for h in range(hl)]
        pn = [jnp.exp(sn[h] - top[h][:, :length]) for h in range(hl)]
        oc = [dot(kc[feat:][hd], pc[h].astype(BF16), 1, 0) for h, hd in enumerate(heads)]
        on = [dot(kn[feat:][hd], pn[h].astype(BF16), 1, 0) for h, hd in enumerate(heads)]
        for h, hd in enumerate(heads):
            tc = jnp.sum(pc[h], axis=0, keepdims=True)
            tn = jnp.sum(pn[h], axis=0, keepdims=True)
            r.mrow[h : h + 1] = top[h]
            r.lrow[h : h + 1] = jnp.concatenate([tc[:, :length] + tn, tc[:, length:]], axis=1)
            r.acc[hd, early] = oc[h][:, :length] + on[h]
            r.acc[hd, late] = oc[h][:, length:]

        def one(j, carry):
            kv_in(s, j).wait_recv()
            kv = r.kvb[at.spot(s, j, j)]
            q = [r.qt[s, hd] for hd in heads]
            old = [r.mrow[h : h + 1] for h in range(hl)]
            total = [r.lrow[h : h + 1] for h in range(hl)]
            pos = lax.broadcasted_iota(jnp.int32, (length, rows), 0) + j * length
            allowed = pos >= start
            sc = [dot(kv[hd], q[h], 0, 0) for h, hd in enumerate(heads)]
            sc = [jnp.where(allowed, v, masked_score) for v in sc]
            new = [jnp.maximum(old[h], jnp.max(sc[h], axis=0, keepdims=True)) for h in range(hl)]
            p = [jnp.exp(sc[h] - new[h]) for h in range(hl)]
            add = [dot(kv[feat:][hd], p[h].astype(BF16), 1, 0) for h, hd in enumerate(heads)]
            scale = [jnp.exp(old[h] - new[h]) for h in range(hl)]
            for h, hd in enumerate(heads):
                r.mrow[h : h + 1] = new[h]
                r.lrow[h : h + 1] = total[h] * scale[h] + jnp.sum(p[h], axis=0, keepdims=True)
                r.acc[hd] = r.acc[hd] * scale[h] + add[h]
            return carry

        lax.fori_loop(at.lowest(s, me), me, one, 0)
        for h, hd in enumerate(heads):
            r.att[s, hd] = r.acc[hd] / r.lrow[h : h + 1]
        r.lse[s] = r.mrow[...] + jnp.log(r.lrow[...])
        r.own_att[s] = r.att[s].T.astype(BF16)
        sib_copy(2, s).start()

    def forward(s):
        x = whole_rows(r.xg, s).astype(F32)
        branch = dot(r.ag[s, 0], r.wog[:half], 1, 0) + dot(r.ag[s, 1], r.wog[half:], 1, 0)
        h = x + branch
        for yy in range(2):
            for cc in range(2):

                @pl.when(jnp.logical_and(y == yy, core == cc))
                def _():
                    r.hp[s] = h[cc * length : (cc + 1) * length, yy * half : (yy + 1) * half]

        mean, inv = row_stats(h)
        r.iv[s] = inv
        normed = ((h - mean) * inv * r.gbf[2:3] + r.gbf[3:4]).astype(BF16)
        r.n2[s] = normed
        up = dot(normed, r.wu[...], 1, 0)
        cube = 0.7978845608028654 * (up + 0.044715 * up * up * up)
        t = jnp.tanh(cube)
        r.act[s] = (0.5 * up * (1.0 + t)).astype(BF16)
        slope = 0.5 * (1.0 + t) + 0.5 * up * (1.0 - t * t) * (
            0.7978845608028654 * (1.0 + 3 * 0.044715 * up * up)
        )
        da = dot(whole_rows(r.cg, s), r.wd[...], 1, 1)
        pre = (da * slope).astype(BF16)
        r.upre[s] = pre
        r.ep[s] = dot(pre, r.wu[...], 1, 1).astype(BF16)
        e_core(s).start()

    def stage(t, offset, step):
        s = t - offset

        @pl.when(jnp.logical_and(s >= 0, s < slots))
        def _():
            step(s)

    def att_on(s):
        sib_copy(2, s).wait_recv()
        build(2, s)
        y_copy(2, s).start()

    def att_back(s):
        y_copy(2, s).wait_recv()
        f_copy(2, s).start()

    def cot_back(s):
        y_copy(1, s).wait_recv()
        f_copy(1, s).start()

    def feed(s):
        @pl.when(s == 0)
        def _():
            wo_y.wait_recv()
            wo_f.start()
            wo_sib.wait_recv()
            wo_f.wait_recv()

        f_copy(1, s).wait_recv()
        f_copy(2, s).wait_recv()
        forward(s)

    def e_on(s):
        e_core(s).wait_recv()
        r.er[s] = (r.ep[s, mine].astype(F32) + r.er[s].astype(F32)).astype(BF16)
        e_y(s).start()

    def e_total(s):
        e_y(s).wait_recv()
        r.ey[s] = (r.er[s].astype(F32) + r.ey[s].astype(F32)).astype(BF16)
        e_y(s).wait_send()
        e_back(s).start()

    def loop_one(t):
        stage(t, 1, att_on)

        @pl.when(jnp.logical_and(t >= 1, t < slots - 1))
        def _():
            cot_on(t + 1)

        stage(t, 2, cot_back)
        stage(t, 2, att_back)

        @pl.when(t == slots)
        def _():
            each(slots - 2, e_on)

        @pl.when(t == slots + 1)
        def _():
            e_on(slots - 2)

        stage(t, 0, attend)
        stage(t, 2, feed)

    each(slots + 2, loop_one)

    wide = slots * rows

    def up_tile(i):
        cols = pl.ds(pl.multiple_of(i * 256, 256), 256)
        left = r.n2[...].reshape(wide, D)
        part = dot(left, r.upre[:, :, cols].reshape(wide, 256), 0, 0).astype(BF16)
        r.gl[0, :, cols] = part

    def down_tile(i):
        cols = pl.ds(pl.multiple_of(lax.rem(i, 3) * 128, 128), 128)
        out_cols = pl.ds(pl.multiple_of(i * 128, 128), 128)
        left = r.act[...].reshape(wide, D)
        part = dot(left, r.cg[:, lax.div(i, 3), :, cols].reshape(wide, 128), 0, 0).astype(BF16)
        r.gl[1, :, out_cols] = part

    e_on(slots - 1)
    each(D // 256, up_tile)
    each(D // 128, down_tile)
    sum1.begin()
    e_total(0)
    e_total(1)

    def two_back(s):
        e_back(s).wait_recv()
        e_back(s).wait_send()
        e_core(s).wait_send()

        @pl.when(core == 0)
        def _():
            r.ep[s, early] = r.ey[s]
            r.ep[s, late] = r.eb[s]

        @pl.when(core == 1)
        def _():
            r.ep[s, early] = r.eb[s]
            r.ep[s, late] = r.ey[s]

        e = r.ep[s].astype(F32)
        xh = (r.n2[s].astype(F32) - r.gbf[3:4]) * r.ginv[0:1]
        r.gtwo[2:3] += jnp.sum(e * xh, axis=0, keepdims=True)
        r.gtwo[3:4] += jnp.sum(e, axis=0, keepdims=True)
        g = e * r.gbf[2:3]
        first = jnp.sum(g, axis=1, keepdims=True) / D
        second = jnp.sum(g * xh, axis=1, keepdims=True) / D
        resid = whole_rows(r.cg, s).astype(F32) + r.iv[s] * (g - first - xh * second)
        r.ep[s] = resid.astype(BF16)

    r.ginv[...] = 1.0 / r.gbf[2:3] + jnp.zeros_like(r.ginv)

    def head_grads(s, kv, lanes, allowed):
        q = [r.qt[s, hd, lanes] for hd in heads]
        d_out = [r.do[hd, lanes] for hd in heads]
        sc = [dot(kv[hd], q[h], 0, 0) for h, hd in enumerate(heads)]
        dp = [dot(kv[feat:][hd], d_out[h], 0, 0) for h, hd in enumerate(heads)]
        p = [
            jnp.exp(jnp.where(allowed, sc[h], masked_score) - r.lse[s, h : h + 1, lanes])
            for h in range(hl)
        ]
        ds = [(p[h] * (dp[h] - r.drow[h : h + 1, lanes])).astype(BF16) for h in range(hl)]
        dv = [dot(d_out[h], p[h].astype(BF16), 1, 1) for h in range(hl)]
        dk = [dot(q[h], ds[h], 1, 1) for h in range(hl)]
        dq_add = [dot(kv[hd], ds[h], 1, 0) for h, hd in enumerate(heads)]
        return [jnp.concatenate(v, axis=0) for v in (dq_add, dk, dv)]

    def attend_back(s):
        low_rows = r.ep[s]
        d_out = dot(r.wo_in[...], low_rows, 1, 1).astype(BF16)
        r.do[...] = d_out
        a = r.att[s]
        r.og[...] += dot(a.astype(BF16), low_rows, 1, 0)
        prod = d_out.astype(F32) * a
        for h, hd in enumerate(heads):
            r.drow[h : h + 1] = jnp.sum(prod[hd], axis=0, keepdims=True)
        start, end = r.bounds[s, 0:1], r.bounds[s, 1:2]
        clean, noisy = masks(me, length, start, end)
        dqa, dk, dv = head_grads(s, r.kvo[s], slice(0, rows), clean)
        dqn, dkn, dvn = head_grads(s, r.kvn[s], early, noisy)
        r.acc[...] = dqa
        r.acc[:, early] += dqn
        r.dkv[s, :feat] = dk
        r.dkv[s, feat:] = dv
        r.qp[s, half:, early] = dvn.astype(BF16)
        r.qp[s, feat:half, early] = turn(dkn, r.cos[:, :length], -r.sin[:, :length]).astype(BF16)

        def one(j, carry):
            spot = at.spot(s, j, j)
            kv = r.kvb[spot]
            pos = lax.broadcasted_iota(jnp.int32, (length, rows), 0) + j * length
            dqa, dk, dv = head_grads(s, kv, slice(0, rows), pos >= start)
            r.acc[...] += dqa
            r.kvb[spot, :feat] = dk.astype(BF16)
            r.kvb[spot, feat:] = dv.astype(BF16)
            dkv_copy(s, j).start()
            return carry

        lax.fori_loop(at.lowest(s, me), me, one, 0)
        r.qp[s, :feat] = (turn(r.acc[...], r.cos[...], -r.sin[...]) * HEAD_DIM**-0.5).astype(BF16)
        r.qq[...] += dot(r.qp[s, :feat], r.n1[s], 1, 0)

    def f_start(s):
        y_copy(2, s).wait_send()
        f_copy(2, s).wait_send()
        ff = dot(r.act[s], r.wd[...], 1, 0)
        r.ag[s, 0] = ff[:, :half].astype(BF16)
        r.ag[s, 1] = ff[:, half:].astype(BF16)
        f_core(s).start()

    def f_on(s):
        f_core(s).wait_recv()
        for k in range(2):
            r.upre[held(0, s, k)] = (r.ag[s, k, mine].astype(F32) + r.fc[s, k].astype(F32)).astype(BF16)
        f_y(s).start()

    def f_end(s):
        f_y(s).wait_recv()
        total = r.hp[s] + (r.upre[held(0, s, y)].astype(F32) + r.fy[s].astype(F32))
        lo = total[:, :feat].astype(BF16)
        hi = total[:, feat:].astype(BF16)

        @pl.when(core == 0)
        def _():
            r.out[s, 0] = lo
            r.osd[s] = hi

        @pl.when(core == 1)
        def _():
            r.out[s, 1] = hi
            r.osd[s] = lo

        f_back(s).start()

    def loop_two(t):
        def run(s):
            two_back(s)
            attend_back(s)

        stage(t, 1, f_on)
        stage(t, -2, e_total)
        stage(t, 0, run)

        @pl.when(jnp.logical_or(t == 3, t == 5))
        def _():
            sum1.pass_on(lax.div(t - 3, 2))

    each(slots, f_start)
    each(slots, loop_two)
    src2[0] = r.og[...].astype(BF16)
    src2[1] = r.qq[...].astype(BF16)
    sum2.begin()
    f_on(slots - 1)
    sum1.pass_on(2)
    sum1.pass_on(3)

    def project_back(s):
        def add(i):
            dkv_in(s, i).wait_recv()
            r.dkv[s] += r.dla[at.spot(s, me, i)].astype(F32)

        readers(s, add)
        total = r.dkv[s]
        r.qp[s, feat:half, late] = turn(total[:feat], r.cos[:, late], -r.sin[:, late]).astype(BF16)
        r.qp[s, half:, late] = total[feat:].astype(BF16)
        pre = r.qp[s]
        r.qkv[...] += dot(pre[feat:], r.n1[s], 1, 0)
        e = dot(pre, r.w_t[...], 0, 0)
        x = whole_rows(r.xg, s).astype(F32)
        mean, inv = row_stats(x)
        xh = (x - mean) * inv
        r.gsum[0:1] += jnp.sum(e * xh, axis=0, keepdims=True)
        r.gsum[1:2] += jnp.sum(e, axis=0, keepdims=True)
        r.n2[s] = e.astype(BF16)
        g = e * r.gbf[0:1]
        one_sum = jnp.sum(g, axis=1, keepdims=True)
        two_sum = jnp.sum(g * xh, axis=1, keepdims=True)
        lane = lax.broadcasted_iota(jnp.int32, (rows, 128), 1)
        packed = jnp.where(lane == 0, one_sum, jnp.where(lane == 1, two_sum, 0.0)).T
        r.st[s, 0] = packed[:8, :length]
        r.st[s, 1] = packed[:8, length:]
        b_core(s).start()
        s_core(s).start()

    def b_on(s):
        b_core(s).wait_recv()
        s_core(s).wait_recv()
        both = r.n2[s, mine].astype(F32) + r.er[s].astype(F32)
        r.upre[s, late] = both.astype(BF16)
        r.sh[s] = r.st[s, core] + r.sl[s]
        b_y(s).start()
        s_y(s).start()

    def b_end(s):
        b_y(s).wait_recv()
        s_y(s).wait_recv()
        e = r.upre[held(length, s, y)].astype(F32) + r.bey[s].astype(F32)
        sums = r.sh[s] + r.sy[s]
        cols = jnp.concatenate([sums, jnp.zeros((120, length), F32)], axis=0).T
        first, second = cols[:, 0:1] / D, cols[:, 1:2] / D
        x = jnp.concatenate([r.xg[s, 0, mine], r.xg[s, 1, mine]], axis=1).astype(F32)
        mean, inv = row_stats(x)
        xh = (r.xg[s, y, mine].astype(F32) - mean) * inv
        gain = jnp.where(y == 0, r.gbf[0:1, :half], r.gbf[0:1, half:])
        resid = r.ep[s, mine].astype(F32)
        resid = jnp.where(y == 0, resid[:, :half], resid[:, half:])
        grad = resid + inv * (e * gain - first - xh * second)
        lo, hi = grad[:, :feat], grad[:, feat:]

        @pl.when(core == 0)
        def _():
            r.ig[s, 0] = lo
            r.isd[s] = hi

        @pl.when(core == 1)
        def _():
            r.ig[s, 1] = hi
            r.isd[s] = lo

        b_back(s).start()

    def loop_three(t):
        stage(t, 0, f_end)
        stage(t, 1, b_on)
        stage(t, 0, project_back)

        pl.when(t == 2)(sum1.reduce)

        @pl.when(jnp.logical_or(t == 3, t == 4))
        def _():
            sum2.pass_on(2 * t - 6)
            sum2.pass_on(2 * t - 5)

    each(slots, loop_three)
    grads = r.qkv[...].astype(BF16)
    r.src3[0] = grads[:feat]
    r.src3[1] = grads[feat:]
    sum3.begin()
    b_on(slots - 1)
    h_copies = [
        remote(r.gsum, r.gh.at[k], r.hs.at[k], r.hr.at[k], d)
        for k, d in enumerate((at.sib, at.yp, at.diag))
    ]
    for copy in h_copies:
        copy.start()
    sum2.reduce()

    def share(i):
        return remote(r.gf, r.gq.at[me], r.qs.at[i], r.qr.at[me], (i, at.head))

    def share_in(i):
        return remote(r.gf, r.gq.at[i], r.qs.at[i], r.qr.at[i], (i, at.head))

    def gains_on():
        for copy in h_copies:
            copy.wait()
        total = r.gsum[...] + r.gh[0] + r.gh[1] + r.gh[2] + r.gtwo[...]
        for h in range(4):

            @pl.when(at.head == h)
            def _():
                r.gf[...] = total[:, h * feat : (h + 1) * feat]

        r.gq[me] = r.gf[...]
        for d in range(1, n):
            share(lax.rem(me + d, n)).start()

    def loop_four(t):
        stage(t, 0, b_end)
        pl.when(t == 0)(gains_on)

        @pl.when(jnp.logical_or(t == 1, t >= 4))
        def _():
            sum1.forward(jnp.where(t == 1, 1, t - 2))

        @pl.when(jnp.logical_or(t == 2, t == 3))
        def _():
            sum3.pass_on(2 * t - 4)
            sum3.pass_on(2 * t - 3)

    each(slots, loop_four)
    sum3.reduce()
    for d in range(1, n):
        share_in(lax.rem(me + d, n)).wait_recv()
    r.gains[...] = jnp.sum(r.gq[...], axis=0)
    for d in range(1, m):
        sum2.forward(d)
    for d in range(1, m):
        sum3.forward(d)

    def finish(s):
        for k in range(3):
            sib_copy(k, s).wait_send()
        for k in range(2):
            y_copy(k, s).wait_send()
            f_copy(k, s).wait_send()
        readers(s, lambda i: kv_copy(s, i).wait_send())
        f_core(s).wait_send()
        f_y(s).wait_send()
        f_back(s).wait()
        b_core(s).wait_send()
        s_core(s).wait_send()
        b_y(s).wait_send()
        s_y(s).wait_send()
        b_back(s).wait()

        def sent(j, carry):
            dkv_copy(s, j).wait_send()
            return carry

        lax.fori_loop(at.lowest(s, me), me, sent, 0)

    each(slots, finish)
    wo_sib.wait_send()
    wo_y.wait_send()
    wo_f.wait_send()
    for part in (sum1, sum2, sum3):
        part.finish()
    for d in range(1, n):
        share(lax.rem(me + d, n)).wait_send()


def body(
    inputs,
    doc_lengths,
    attn_gain,
    attn_bias,
    w_qkv,
    w_out,
    ffn_gain,
    ffn_bias,
    w_up,
    w_down,
    cotangent,
):
    n = lax.axis_size("seq")
    slots, _, length, feat = inputs.shape
    rows, half, m = 2 * length, 2 * feat, n // 2
    held = slots * n * half * length * 2
    if held > ROWS_LIMIT or m != 4:
        return gathered_body(
            inputs, doc_lengths, attn_gain, attn_bias, w_qkv, w_out, ffn_gain, ffn_bias, w_up, w_down, cotangent
        )
    me = lax.axis_index("seq")
    long = jnp.argmax(doc_lengths[:, 0]).astype(jnp.int32)
    ids = jnp.arange(slots, dtype=jnp.int32)

    def swap(v):
        pick = lax.dynamic_index_in_dim(v, long, 0, keepdims=True)
        where = ids.reshape((slots,) + (1,) * (v.ndim - 1))
        return jnp.where(where == 0, pick, jnp.where(where == long, v[:1], v))

    ends = jnp.cumsum(swap(doc_lengths), axis=1)
    positions = me * length + jnp.arange(length, dtype=jnp.int32)
    past = ends[:, :, None] <= positions[None, None, :]
    first_key = jnp.max(jnp.where(past, ends[:, :, None], 0), axis=1)
    last_key = jnp.min(jnp.where(past, 2**30, ends[:, :, None]), axis=1)
    pair = jnp.stack([jnp.tile(first_key, (1, 2)), jnp.tile(last_key, (1, 2))], axis=1)
    bounds = jnp.pad(pair, ((0, 0), (0, 6), (0, 0)))
    half_dim = HEAD_DIM // 2
    freqs = rotary_base ** (-jnp.arange(half_dim, dtype=F32) / half_dim)
    angles = freqs[:, None] * positions.astype(F32)[None, :]
    cos = jnp.tile(jnp.cos(angles), (1, 2))
    sin = jnp.tile(jnp.sin(angles), (1, 2))
    w_t = w_qkv.reshape(D, 3 * feat).T
    gains = jnp.concatenate(
        [jnp.stack([attn_gain, attn_bias, ffn_gain, ffn_bias]), jnp.zeros((4, feat), F32)], axis=0
    )
    operands = dict(
        x_in=swap(inputs).reshape(slots, rows, feat), c_in=swap(cotangent).reshape(slots, rows, feat),
        gb_in=gains, w_t=w_t, wo_in=w_out, wu=w_up, wd=w_down, cos=cos, sin=sin, bounds=bounds,
    )
    small = (m, feat // m, D)
    quarter = (m, D // m, D)
    outs = dict(
        out=((slots, 2, length, feat), BF16), ig=((slots, 2, length, feat), F32), res1=((2, *quarter), BF16),
        res2=((2, *small), BF16), res3=((2, *small), BF16), gains=((8, feat), F32),
    )
    blocks = n + (slots - 1) * (n // 2 + max(1, n // 8))
    full, wide = (slots, 2, rows, half), (slots, rows, D)
    part, stat = (slots, length, D), (slots, 8, length)
    halves, own_half = (slots, 2, length, half), (slots, length, half)
    buffers = dict(
        land=((2, slots, rows, feat), BF16), own_att=((slots, rows, feat), BF16), gland=((4, 8, feat), F32),
        gbf=((8, D), F32), ginv=((8, D), F32), xg=(full, BF16), cg=(full, BF16), ag=(full, BF16),
        wog=((D, D), BF16), n1=(wide, BF16), qt=((slots, feat, rows), BF16),
        kvn=((slots, half, length), BF16), kvo=((slots, half, length), BF16), kvb=((blocks, half, length), BF16),
        att=((slots, feat, rows), F32), lse=((slots, 8, rows), F32), acc=((feat, rows), F32),
        mrow=((8, rows), F32), lrow=((8, rows), F32), hp=(own_half, F32), iv=((slots, rows, 1), F32),
        n2=(wide, BF16), act=(wide, BF16), upre=(wide, BF16), ep=(wide, BF16), er=(part, BF16), ey=(part, BF16),
        eb=(part, BF16), fc=(halves, BF16), fy=(own_half, BF16),
        osd=((slots, length, feat), BF16), gl=((2, D, D), BF16), gx1=(quarter, BF16), gz1=(quarter, BF16),
        own1=(quarter[1:], BF16), do=((feat, rows), BF16), drow=((8, rows), F32),
        dkv=((slots, half, length), F32), dla=((blocks, half, length), BF16), qp=((slots, 3 * feat, rows), BF16),
        og=((feat, D), F32), qq=((feat, D), F32), qkv=((half, D), F32), gsum=((8, D), F32), gtwo=((8, D), F32),
        st=((slots, 2, 8, length), F32), sl=(stat, F32), sh=(stat, F32), sy=(stat, F32),
        bey=(own_half, BF16), isd=((slots, length, feat), F32), src3=((2, feat, D), BF16),
        gx2=(small, BF16), pt2=(small, BF16), gz2=(small, BF16), own2=(small[1:], BF16),
        gx3=(small, BF16), pt3=(small, BF16), gz3=(small, BF16), own3=(small[1:], BF16),
        gh=((3, 8, D), F32), gq=((n, 8, feat), F32), gf=((8, feat), F32),
    )
    sems = {k: (3, slots) for k in ("ss", "sr", "ys", "yr", "fs", "fr")}
    sems |= {k: (3,) for k in ("gs", "gr", "ws", "wr", "hs", "hr")}
    sems |= {k: (slots, n) for k in ("ks", "kr", "ds", "dr")}
    sems |= {k + i + e: (slots,) for k in "efab" for i in "123" for e in "sr" if k + i != "b3"}
    sems |= {"qs": (n,), "qr": (n,)}
    sems |= {"%s%d" % (k, i): (m,) for k in "uvw" for i in range(8)}
    sem = pltpu.SemaphoreType.DMA
    scratch = {k: VMEM(*v) for k, v in buffers.items()}
    scratch |= {k: sem(v) for k, v in sems.items()}
    scratch |= {k + "8": sem for k in "uvw"}
    vmem = pl.BlockSpec(memory_space=VMEM)
    names = [*operands, *outs, *scratch]
    got = pl.pallas_call(
        functools.partial(layer, n, names),
        out_shape=[jax.ShapeDtypeStruct(*v) for v in outs.values()],
        in_specs=[vmem] * len(operands),
        out_specs=[pl.BlockSpec(memory_space=pl.ANY) if k.startswith("res") else vmem for k in outs],
        scratch_shapes=list(scratch.values()),
        compiler_params=pltpu.CompilerParams(
            collective_id=0, has_side_effects=True, vmem_limit_bytes=VMEM_LIMIT
        ),
        name="layer",
    )(*operands.values())
    outputs, input_grad, res1, res2, res3, gain_grads = got
    up_grad, down_grad = res1.reshape(2, D, D).astype(F32)
    out_grad, q_grad = res2.reshape(2, feat, D).astype(F32)
    qkv_grad = jnp.concatenate([q_grad[None], res3.reshape(2, feat, D).astype(F32)], axis=0)
    return (
        swap(outputs),
        swap(input_grad),
        jnp.transpose(qkv_grad, (2, 0, 1)),
        out_grad,
        up_grad,
        down_grad,
        gain_grads[0],
        gain_grads[1],
        gain_grads[2],
        gain_grads[3],
    )


def solution(mesh):
    in_specs = (
        P(None, None, "seq", "head"),
        P(),
        P("head"),
        P("head"),
        P(None, None, "head"),
        P("head", None),
        P("head"),
        P("head"),
        P(None, "head"),
        P("head", None),
        P(None, None, "seq", "head"),
    )
    out_specs = (
        P(None, None, "seq", "head"),
        P(None, None, "seq", "head"),
        P(None, None, "head"),
        P("head", None),
        P(None, "head"),
        P("head", None),
        P("head"),
        P("head"),
        P("head"),
        P("head"),
    )
    return jax.shard_map(body, mesh=mesh, in_specs=in_specs, out_specs=out_specs, check_vma=False)
```

```python
import functools
import types

import jax
import jax.numpy as jnp
from jax import lax
from jax.experimental import pallas as pl
from jax.experimental.pallas import tpu as pltpu
from jax.sharding import PartitionSpec as P

D = 768
HEAD_DIM = 64
BLOCK = 16


norm_eps = 1e-05
masked_score = -1e30
rotary_base = 10000.0

MESH = pl.DeviceIdType.MESH
VMEM = pltpu.VMEM
F32 = jnp.float32
BF16 = jnp.bfloat16
ROWS_LIMIT = 16 << 20
VMEM_LIMIT = 63 << 20


def passed_along(block, axis, distance):
    devices = range(lax.axis_size(axis))
    route = [(i - distance, i) for i in devices if i - distance in devices]
    return lax.ppermute(block, axis, route)


def from_behind(x, axis, by):
    devices = lax.axis_size(axis)
    return lax.ppermute(x, axis, [(i, (i + by) % devices) for i in range(devices)])


def segment_ids(doc_lengths, positions):
    doc_ends = jnp.cumsum(doc_lengths, axis=1)
    return jnp.sum((doc_ends[:, :, None] <= positions[None, None, :]).astype(jnp.int32), axis=1)


def rotate(values, positions, sign):
    half_dim = values.shape[-1] // 2
    freqs = rotary_base ** (-jnp.arange(half_dim, dtype=jnp.float32) / half_dim)
    angles = positions.astype(jnp.float32)[:, None, None] * freqs
    cosine = jnp.cos(angles)
    sine = sign * jnp.sin(angles)
    first_half = values[..., :half_dim]
    second_half = values[..., half_dim:]
    return jnp.concatenate(
        [first_half * cosine - second_half * sine, second_half * cosine + first_half * sine],
        axis=-1,
    )


def row_pair(first_sum, second_sum):
    return lax.psum((first_sum, second_sum), "head")


def normalize(share, gain, bias):
    row_total, row_square = row_pair(jnp.sum(share, axis=-1), jnp.sum(share * share, axis=-1))
    mean_value = row_total / D
    inv_std = lax.rsqrt(row_square / D - mean_value * mean_value + norm_eps)
    centered = (share - mean_value[..., None]) * inv_std[..., None]
    scaled = (centered * gain + bias).astype(jnp.bfloat16)
    gathered = lax.all_gather(scaled, "head", axis=3, tiled=True)
    return (gathered, centered, inv_std)


def norm_backward(partial_value, gain, centered, inv_std):
    share = lax.psum_scatter(partial_value, "head", scatter_dimension=3, tiled=True)
    scaled = share * gain
    first_mean, second_mean = row_pair(
        jnp.sum(scaled, axis=-1), jnp.sum(scaled * centered, axis=-1)
    )
    grad_in = inv_std[..., None] * (
        scaled - first_mean[..., None] / D - centered * (second_mean[..., None] / D)
    )
    gain_grad = jnp.sum(share * centered, axis=(0, 1, 2))
    bias_grad = jnp.sum(share, axis=(0, 1, 2))
    return (grad_in, gain_grad, bias_grad)


def branch_total(partial_value):
    return lax.psum_scatter(partial_value, "head", scatter_dimension=3, tiled=True)


def gradient_rows(share):
    return lax.all_gather(share, "head", axis=3, tiled=True)


def mask_rule(query_pos, query_seg, key_pos, key_seg):
    query_block = (query_pos // BLOCK)[:, None]
    key_block = (key_pos // BLOCK)[None, :]
    order = jnp.stack([key_block < query_block, key_block <= query_block])
    same_doc = query_seg[:, :, None] == key_seg[:, None, :]
    return jnp.logical_and(order[None, :, None], same_doc[:, None, None])


def absorb(state_now, scores, allowed, value_piece):
    run_max, run_sum, run_acc = state_now
    masked = jnp.where(allowed, scores, masked_score)
    new_max = jnp.maximum(run_max, jnp.max(masked, axis=-1))
    weights_now = jnp.where(allowed, jnp.exp(masked - new_max[..., None]), 0.0)
    factor = jnp.exp(run_max - new_max)
    new_sum = run_sum * factor + jnp.sum(weights_now, axis=-1)
    added = jnp.einsum(
        "schlk,skhd->schld",
        weights_now,
        value_piece.astype(jnp.float32),
        precision=lax.Precision.HIGHEST,
    )
    return (new_max, new_sum, run_acc * factor[..., None] + added)


def gathered_body(
    inputs,
    doc_lengths,
    attn_gain,
    attn_bias,
    w_qkv,
    w_out,
    ffn_gain,
    ffn_bias,
    w_up,
    w_down,
    cotangent,
):
    seqs_here, _, local_len, _ = inputs.shape
    head_local = w_qkv.shape[2] // HEAD_DIM
    first_pos = lax.axis_index("seq") * local_len
    positions = first_pos + jnp.arange(local_len, dtype=jnp.int32)
    segments = segment_ids(doc_lengths, positions)
    inputs_wide = inputs.astype(jnp.float32)
    normed_one, centered_one, inv_one = normalize(inputs_wide, attn_gain, attn_bias)
    projected = jnp.einsum("scld,dtk->scltk", normed_one, w_qkv, preferred_element_type=jnp.float32)
    split_rows = projected.reshape(seqs_here, 2, local_len, 3, head_local, HEAD_DIM)
    queries = (rotate(split_rows[:, :, :, 0], positions, 1.0) * HEAD_DIM ** (-0.5)).astype(
        jnp.bfloat16
    )
    key_rows = rotate(split_rows[:, :, :, 1], positions, 1.0).astype(jnp.bfloat16)
    value_rows = split_rows[:, :, :, 2].astype(jnp.bfloat16)
    clean_keys = key_rows[:, 1].reshape(seqs_here, local_len, head_local * HEAD_DIM)
    clean_values = value_rows[:, 1].reshape(seqs_here, local_len, head_local * HEAD_DIM)
    block_ids = positions // BLOCK
    own_allowed = jnp.logical_and(
        (block_ids[:, None] == block_ids[None, :])[None],
        segments[:, :, None] == segments[:, None, :],
    )[:, None, None]
    noisy_scores = jnp.einsum(
        "sclhd,skhd->schlk", queries[:, :1], key_rows[:, 0], preferred_element_type=jnp.float32
    )
    half_shape = (seqs_here, 1, head_local, local_len)
    empty_state = (
        jnp.full(half_shape, masked_score, jnp.float32),
        jnp.zeros(half_shape, jnp.float32),
        jnp.zeros(half_shape + (HEAD_DIM,), jnp.float32),
    )
    noisy_state = absorb(empty_state, noisy_scores, own_allowed, value_rows[:, 0])
    start_state = jax.tree.map(
        lambda first, second: jnp.concatenate([first, second], axis=1), noisy_state, empty_state
    )
    piece_keys = lax.all_gather(clean_keys, "seq", axis=1, tiled=True)
    piece_values = lax.all_gather(clean_values, "seq", axis=1, tiled=True)
    piece_len = piece_keys.shape[1]
    key_pos = jnp.arange(piece_len, dtype=jnp.int32)
    key_seg = segment_ids(doc_lengths, key_pos)
    key_heads = piece_keys.reshape(seqs_here, piece_len, head_local, HEAD_DIM)
    value_heads = piece_values.reshape(seqs_here, piece_len, head_local, HEAD_DIM)
    scores = jnp.einsum("sclhd,skhd->schlk", queries, key_heads, preferred_element_type=jnp.float32)
    final_max, final_sum, final_acc = absorb(
        start_state, scores, mask_rule(positions, segments, key_pos, key_seg), value_heads
    )
    attended = final_acc / final_sum[..., None]
    log_total = final_max + jnp.log(final_sum)
    attended_low = attended.astype(jnp.bfloat16)
    out_heads = w_out.reshape(head_local, HEAD_DIM, w_out.shape[1])
    attn_share = branch_total(
        jnp.einsum("schld,hdm->sclm", attended_low, out_heads, preferred_element_type=jnp.float32)
    )
    hidden_res = inputs_wide + attn_share
    normed_two, centered_two, inv_two = normalize(hidden_res, ffn_gain, ffn_bias)
    up_value = jnp.einsum("scld,df->sclf", normed_two, w_up, preferred_element_type=jnp.float32)
    activated, gelu_back = jax.vjp(lambda inner: jax.nn.gelu(inner, approximate=True), up_value)
    act_low = activated.astype(jnp.bfloat16)
    ffn_share = branch_total(
        jnp.einsum("sclf,fm->sclm", act_low, w_down, preferred_element_type=jnp.float32)
    )
    outputs = (hidden_res + ffn_share).astype(jnp.bfloat16)
    grad_out = cotangent.astype(jnp.float32)
    grad_full = gradient_rows(cotangent)
    down_grad = jnp.einsum("sclf,sclm->fm", act_low, grad_full, preferred_element_type=jnp.float32)
    act_grad = jnp.einsum("sclm,fm->sclf", grad_full, w_down, preferred_element_type=jnp.float32)
    up_pre_grad = gelu_back(act_grad)[0].astype(jnp.bfloat16)
    up_grad = jnp.einsum(
        "scld,sclf->df", normed_two, up_pre_grad, preferred_element_type=jnp.float32
    )
    normed_two_grad = jnp.einsum(
        "sclf,df->scld", up_pre_grad, w_up, preferred_element_type=jnp.float32
    )
    back_two, ffn_gain_grad, ffn_bias_grad = norm_backward(
        normed_two_grad, ffn_gain, centered_two, inv_two
    )
    resid_grad = grad_out + back_two
    resid_full = gradient_rows(resid_grad.astype(jnp.bfloat16))
    out_grad = jnp.einsum(
        "schld,sclm->hdm", attended_low, resid_full, preferred_element_type=jnp.float32
    ).reshape(w_out.shape)
    attended_grad = jnp.einsum(
        "sclm,hdm->schld", resid_full, out_heads, preferred_element_type=jnp.float32
    ).astype(jnp.bfloat16)
    grad_wide = attended_grad.astype(jnp.float32)
    row_delta = jnp.sum(grad_wide * attended, axis=-1)
    noisy_probs = jnp.where(own_allowed, jnp.exp(noisy_scores - log_total[:, :1, :, :, None]), 0.0)
    noisy_prob_grad = jnp.einsum(
        "schld,skhd->schlk",
        attended_grad[:, :1],
        value_rows[:, 0],
        preferred_element_type=jnp.float32,
    )
    noisy_score_grad = (noisy_probs * (noisy_prob_grad - row_delta[:, :1, :, :, None])).astype(
        jnp.bfloat16
    )
    noisy_query_grad = jnp.einsum(
        "schlk,skhd->schld", noisy_score_grad, key_rows[:, 0], preferred_element_type=jnp.float32
    )
    noisy_key_grad = jnp.einsum(
        "schlk,sclhd->skhd", noisy_score_grad, queries[:, :1], preferred_element_type=jnp.float32
    )
    noisy_value_grad = jnp.einsum(
        "schlk,schld->skhd", noisy_probs, grad_wide[:, :1], precision=lax.Precision.HIGHEST
    )
    query_start = jnp.concatenate([noisy_query_grad, jnp.zeros_like(noisy_query_grad)], axis=1)
    flat_zero = jnp.zeros((seqs_here, local_len, head_local * HEAD_DIM), jnp.float32)

    def piece_grads(piece_keys, piece_values, first_row, query_total):
        key_pos = first_row + jnp.arange(local_len, dtype=jnp.int32)
        key_seg = segment_ids(doc_lengths, key_pos)
        key_heads = piece_keys.reshape(seqs_here, local_len, head_local, HEAD_DIM)
        value_heads = piece_values.reshape(seqs_here, local_len, head_local, HEAD_DIM)
        scores = jnp.einsum(
            "sclhd,skhd->schlk", queries, key_heads, preferred_element_type=jnp.float32
        )
        allowed = mask_rule(positions, segments, key_pos, key_seg)
        weights_now = jnp.where(allowed, jnp.exp(scores - log_total[..., None]), 0.0)
        prob_grad = jnp.einsum(
            "schld,skhd->schlk", attended_grad, value_heads, preferred_element_type=jnp.float32
        )
        score_grad = (weights_now * (prob_grad - row_delta[..., None])).astype(jnp.bfloat16)
        query_out = query_total + jnp.einsum(
            "schlk,skhd->schld", score_grad, key_heads, preferred_element_type=jnp.float32
        )
        key_part = jnp.einsum(
            "schlk,sclhd->skhd", score_grad, queries, preferred_element_type=jnp.float32
        )
        value_part = jnp.einsum(
            "schlk,schld->skhd", weights_now, grad_wide, precision=lax.Precision.HIGHEST
        )
        return (key_part.reshape(flat_zero.shape), value_part.reshape(flat_zero.shape), query_out)

    def cycle_body(cycle_step, carried):
        piece_keys, piece_values, key_acc, value_acc, query_acc = carried
        source = (lax.axis_index("seq") - cycle_step) % lax.axis_size("seq")
        first_row = source * local_len
        key_part, value_part, query_acc = piece_grads(
            piece_keys, piece_values, first_row, query_acc
        )
        key_acc = key_acc + key_part
        value_acc = value_acc + value_part
        piece_keys, piece_values = passed_along((piece_keys, piece_values), "seq", 1)
        key_acc, value_acc = (
            from_behind(key_acc.astype(jnp.bfloat16), "seq", 1).astype(key_acc.dtype),
            from_behind(value_acc.astype(jnp.bfloat16), "seq", 1).astype(value_acc.dtype),
        )
        return (piece_keys, piece_values, key_acc, value_acc, query_acc)

    cycle_start = (clean_keys, clean_values, flat_zero, flat_zero, query_start)
    _, _, clean_key_grad, clean_value_grad, query_acc = lax.fori_loop(
        0, lax.axis_size("seq"), cycle_body, cycle_start
    )
    head_shape = (seqs_here, local_len, head_local, HEAD_DIM)
    query_total = rotate(jnp.transpose(query_acc, (0, 1, 3, 2, 4)), positions, -1.0) * HEAD_DIM ** (
        -0.5
    )
    key_total = rotate(
        jnp.stack([noisy_key_grad, clean_key_grad.reshape(head_shape)], axis=1), positions, -1.0
    )
    value_total = jnp.stack([noisy_value_grad, clean_value_grad.reshape(head_shape)], axis=1)
    qkv_pre_grad = (
        jnp.stack([query_total, key_total, value_total], axis=3)
        .reshape(seqs_here, 2, local_len, 3, head_local * HEAD_DIM)
        .astype(jnp.bfloat16)
    )
    qkv_grad = jnp.einsum(
        "scld,scltk->dtk", normed_one, qkv_pre_grad, preferred_element_type=jnp.float32
    )
    normed_one_grad = jnp.einsum(
        "scltk,dtk->scld", qkv_pre_grad, w_qkv, preferred_element_type=jnp.float32
    )
    back_one, attn_gain_grad, attn_bias_grad = norm_backward(
        normed_one_grad, attn_gain, centered_one, inv_one
    )
    input_grad = resid_grad + back_one
    (
        qkv_grad,
        out_grad,
        up_grad,
        down_grad,
        attn_gain_grad,
        attn_bias_grad,
        ffn_gain_grad,
        ffn_bias_grad,
    ) = lax.psum(
        (
            qkv_grad,
            out_grad,
            up_grad,
            down_grad,
            attn_gain_grad,
            attn_bias_grad,
            ffn_gain_grad,
            ffn_bias_grad,
        ),
        "seq",
    )
    return (
        outputs,
        input_grad,
        qkv_grad,
        out_grad,
        up_grad,
        down_grad,
        attn_gain_grad,
        attn_bias_grad,
        ffn_gain_grad,
        ffn_bias_grad,
    )


def dot(a, b, ca, cb):
    return lax.dot_general(a, b, (((ca,), (cb,)), ((), ())), preferred_element_type=F32)


def remote(src, dst, send, recv, device):
    return pltpu.make_async_remote_copy(
        src_ref=src, dst_ref=dst, send_sem=send, recv_sem=recv, device_id=device, device_id_type=MESH
    )


class Place:
    def __init__(self, n):
        self.n = n
        self.me = lax.axis_index("seq")
        self.head = lax.axis_index("head")
        self.core = lax.rem(self.head, 2)
        self.y = lax.div(self.head, 2)
        self.sib = (self.me, self.y * 2 + 1 - self.core)
        self.yp = (self.me, (1 - self.y) * 2 + self.core)
        self.diag = (self.me, (1 - self.y) * 2 + 1 - self.core)
        self.half = n // 2
        self.band = max(1, n // 8)

    def lowest(self, slot, i):
        near = i - self.band
        short = jnp.where(i >= self.half, jnp.minimum(near, self.half), near)
        return jnp.where(slot == 0, 0, jnp.maximum(short, 0))

    def spot(self, slot, block, other):
        window = self.half + self.band
        near = self.half + lax.rem(other, self.band)
        late = jnp.where(block >= self.half, other - self.half, near)
        return jnp.where(slot == 0, other, self.n + (slot - 1) * window + late)

    def spots(self, slots):
        return self.n + (slots - 1) * (self.half + self.band)

    def greet(self, near, everyone):
        bar = pltpu.get_barrier_semaphore()
        for d in near:
            pl.semaphore_signal(bar, inc=1, device_id=d, device_id_type=MESH)
        count = len(near)
        if everyone:
            for d in range(1, self.n):
                there = lax.rem(self.me + d, self.n)
                pl.semaphore_signal(bar, inc=1, device_id=(there, self.head), device_id_type=MESH)
            count += self.n - 1
        pl.semaphore_wait(bar, count)


def each(count, step):
    def run(i, carry):
        step(i)
        return carry

    lax.fori_loop(0, count, run, 0)


def row_stats(x):
    mean = jnp.sum(x, axis=1, keepdims=True) / D
    var = jnp.sum(x * x, axis=1, keepdims=True) / D - mean * mean
    return mean, lax.rsqrt(var + norm_eps)


def whole_rows(ref, s):
    return jnp.concatenate([ref[s, 0], ref[s, 1]], axis=1)


def turn(v, cosine, sine):
    parts = []
    for h in range(v.shape[0] // HEAD_DIM):
        a = v[h * 64 : h * 64 + 32]
        b = v[h * 64 + 32 : h * 64 + 64]
        parts += [a * cosine - b * sine, b * cosine + a * sine]
    return jnp.concatenate(parts, axis=0)


def masks(me, length, start, end):
    shape = (length, 2 * length)
    key = lax.broadcasted_iota(jnp.int32, shape, 0)
    row = lax.broadcasted_iota(jnp.int32, shape, 1)
    noisy = row < length
    at = jnp.where(noisy, row, row - length)
    key_block = key >> 4
    row_block = at >> 4
    pos = key + me * length
    same = jnp.logical_and(pos >= start, pos < end)
    clean = jnp.logical_and(same, key_block < row_block + jnp.where(noisy, 0, 1))
    own = jnp.logical_and(same, key_block == row_block)[:, :length]
    return clean, own


class Sum:
    def __init__(self, at, src, res, gx, part, gz, own, xs, xr, zs, zr, cs, cr, fs, fr, ls, ds):
        self.m = at.n // 2
        self.lo = lax.rem(at.me, 2)
        self.hi = lax.div(at.me, 2)
        self.head = at.head
        self.pair = (at.me + 1 - 2 * self.lo, at.head)
        self.src, self.res, self.gx, self.part, self.gz = src, res, gx, part, gz
        self.xs, self.xr, self.zs, self.zr = xs, xr, zs, zr
        self.cs, self.cr, self.fs, self.fr, self.ls, self.ds = cs, cr, fs, fr, ls, ds
        self.pieces = ds.shape[0]
        self.own = own

    def piece(self, half, k):
        size = self.gx.shape[1]
        return half, pl.ds(pl.multiple_of(k * size, 16), size)

    def at_z(self, k):
        return (2 * k + self.lo, self.head)

    def x(self, k):
        return remote(self.src.at[self.piece(1 - self.lo, k)], self.gx.at[k], self.xs.at[k], self.xr.at[k], self.pair)

    def z(self, k):
        return remote(self.part.at[k], self.gz.at[self.hi], self.zs.at[k], self.zr.at[self.hi], self.at_z(k))

    def z_in(self, k):
        return remote(self.part.at[k], self.gz.at[k], self.zs.at[k], self.zr.at[k], self.at_z(k))

    def piece_of(self, k, p):
        size = self.gx.shape[1] // self.pieces
        return pl.ds(p * size, size)

    def c_own(self, p, step):
        rows = self.piece_of(self.hi, p)
        there = self.res.at[self.lo, self.hi, rows]
        sent = self.cs.at[self.hi, p] if step > 0 else self.ds.at[p]
        return remote(self.own.at[rows], there, sent, self.cr.at[self.hi, p], self.at_z(self.hi + step))

    def c_on(self, k, p, step):
        part = self.res.at[self.lo, k, self.piece_of(k, p)]
        return remote(part, part, self.cs.at[k, p], self.cr.at[k, p], self.at_z(self.hi + step))

    def f(self, k, p):
        part = self.res.at[self.lo, k, self.piece_of(k, p)]
        return remote(part, part, self.fs.at[k, p], self.fr.at[k, p], self.pair)

    def f_own(self, p):
        rows = self.piece_of(self.hi, p)
        there = self.res.at[self.lo, self.hi, rows]
        return remote(self.own.at[rows], there, self.fs.at[self.hi, p], self.fr.at[self.hi, p], self.pair)

    def keep(self):
        return pltpu.make_async_copy(self.own, self.res.at[self.lo, self.hi], self.ls)

    def others(self):
        return [lax.rem(self.hi + d, self.m) for d in range(1, self.m)]

    def turn_of(self, i):
        return lax.rem(self.hi + 1 + i, self.m)

    def begin(self):
        each(self.m, lambda i: self.x(self.turn_of(i)).start())

    def pass_on(self, i):
        k = self.turn_of(i)
        self.x(k).wait_recv()
        self.part[k] = (self.src[self.piece(self.lo, k)].astype(F32) + self.gx[k].astype(F32)).astype(BF16)

        @pl.when(k != self.hi)
        def _():
            self.z(k).start()

    def ends(self, step, run):
        there = self.hi + step
        pl.when(jnp.logical_and(there >= 0, there < self.m))(run)

    def reduce(self):
        total = self.part[self.hi].astype(F32)
        for k in self.others():
            self.z_in(k).wait_recv()
            total += self.gz[k].astype(F32)
        self.own[...] = total.astype(BF16)
        self.keep().start()
        for p in range(self.pieces):
            self.ends(1, lambda: self.c_own(p, 1).start())
            self.ends(-1, lambda: self.c_own(p, -1).start())
            self.f_own(p).start()

    def forward(self, d):
        for p in range(self.pieces):
            for step in (1, -1):

                def run():
                    k = self.hi - step * d
                    self.c_on(k, p, step).wait_recv()
                    self.ends(step, lambda: self.c_on(k, p, step).start())
                    self.f(k, p).start()

                self.ends(-step * d, run)

    def finish(self):
        each(self.m, lambda k: self.x(k).wait_send())
        for k in self.others():
            self.z(k).wait_send()
        for p in range(self.pieces):
            for step in (1, -1):
                self.ends(step, lambda: self.c_own(p, step).wait_send())
                for d in range(1, self.m):

                    def run():
                        k = self.hi - step * d
                        self.ends(step, lambda: self.c_on(k, p, step).wait_send())
                        self.f(k, p).wait_send()

                    self.ends(-step * d, run)
            self.f_own(p).wait_send()
            each(self.m, lambda k: self.f(k, p).wait_recv())
        self.keep().wait()


def layer(n, names, *refs):
    r = types.SimpleNamespace(**dict(zip(names, refs)))
    at = Place(n)
    slots, rows, feat = r.x_in.shape
    length = rows // 2
    half = 2 * feat
    hl = feat // HEAD_DIM
    m = n // 2
    core, y, me = at.core, at.y, at.me
    mine = pl.ds(length * core, length)
    other = pl.ds(length * (1 - core), length)
    early, late = slice(0, length), slice(length, rows)
    heads = [slice(h * HEAD_DIM, (h + 1) * HEAD_DIM) for h in range(hl)]
    fulls = (r.xg, r.cg, r.ag)
    owns = (r.x_in, r.c_in, r.own_att)
    lands = (r.land.at[0], r.land.at[1], r.land.at[0])
    quarter = D // m
    sum1 = Sum(
        at, r.gl, r.res1, r.gx1, r.act.at[:m, :quarter], r.gz1, r.own1, *[getattr(r, "u%d" % i) for i in range(10)]
    )
    src2 = r.act.at[m : m + 2, :feat]
    sum2 = Sum(at, src2, r.res2, r.gx2, r.pt2, r.gz2, r.own2, *[getattr(r, "v%d" % i) for i in range(10)])
    sum3 = Sum(at, r.src3, r.res3, r.gx3, r.pt3, r.gz3, r.own3, *[getattr(r, "w%d" % i) for i in range(10)])

    def sib_copy(k, s):
        return remote(owns[k].at[s], lands[k].at[s], r.ss.at[k, s], r.sr.at[k, s], at.sib)

    def build(k, s):
        a, b = owns[k][s], lands[k][s]

        @pl.when(core == 0)
        def _():
            fulls[k][s, y] = jnp.concatenate([a, b], axis=1)

        @pl.when(core == 1)
        def _():
            fulls[k][s, y] = jnp.concatenate([b, a], axis=1)

    def y_copy(k, s):
        part = fulls[k].at[s, y, mine]
        return remote(part, part, r.ys.at[k, s], r.yr.at[k, s], at.yp)

    def f_copy(k, s):
        part = fulls[k].at[s, 1 - y, mine]
        return remote(part, part, r.fs.at[k, s], r.fr.at[k, s], at.sib)

    def kv_copy(s, i):
        return remote(r.kvo.at[s], r.kvb.at[at.spot(s, me, me)], r.ks.at[s, i], r.kr.at[s, me], (i, at.head))

    def kv_in(s, j):
        return remote(r.kvo.at[s], r.kvb.at[at.spot(s, j, j)], r.ks.at[s, j], r.kr.at[s, j], (j, at.head))

    def dkv_copy(s, j):
        return remote(
            r.kvb.at[at.spot(s, j, j)], r.dla.at[at.spot(s, j, me)], r.ds.at[s, j], r.dr.at[s, me], (j, at.head)
        )

    def dkv_in(s, i):
        here = r.dla.at[at.spot(s, me, i)]
        return remote(here, here, r.ds.at[s, i], r.dr.at[s, i], (i, at.head))

    def readers(s, step):
        for d in range(1, n):
            i = me + d

            @pl.when(jnp.logical_and(i < n, at.lowest(s, i) <= me))
            def _():
                step(i)

    def e_core(s):
        return remote(r.ep.at[s, other], r.er.at[s], r.e1s.at[s], r.e1r.at[s], at.sib)

    def e_y(s):
        return remote(r.er.at[s], r.ey.at[s], r.e2s.at[s], r.e2r.at[s], at.yp)

    def e_back(s):
        return remote(r.ey.at[s], r.eb.at[s], r.e3s.at[s], r.e3r.at[s], at.sib)

    def held(first, s, k):
        return (s, pl.ds(first, length), pl.ds(pl.multiple_of(k * half, 128), half))

    def f_core(s):
        return remote(r.ag.at[s, :, other], r.fc.at[s], r.f1s.at[s], r.f1r.at[s], at.sib)

    def f_y(s):
        return remote(r.upre.at[held(0, s, 1 - y)], r.fy.at[s], r.f2s.at[s], r.f2r.at[s], at.yp)

    def f_back(s):
        return remote(r.osd.at[s], r.out.at[s, core], r.f3s.at[s], r.f3r.at[s], at.sib)

    def b_core(s):
        return remote(r.n2.at[s, other], r.er.at[s], r.a1s.at[s], r.a1r.at[s], at.sib)

    def s_core(s):
        return remote(r.st.at[s, 1 - core], r.sl.at[s], r.b1s.at[s], r.b1r.at[s], at.sib)

    def b_y(s):
        return remote(r.upre.at[held(length, s, 1 - y)], r.bey.at[s], r.a2s.at[s], r.a2r.at[s], at.yp)

    def s_y(s):
        return remote(r.sh.at[s], r.sy.at[s], r.b2s.at[s], r.b2r.at[s], at.yp)

    def b_back(s):
        return remote(r.isd.at[s], r.ig.at[s, core], r.a3s.at[s], r.a3r.at[s], at.sib)

    at.greet([at.sib, at.yp, at.diag], True)
    each(slots, lambda s: sib_copy(0, s).start())
    r.gland[at.head] = r.gb_in[...]
    g_copies = [
        remote(r.gb_in, r.gland.at[at.head], r.gs.at[k], r.gr.at[k], d)
        for k, d in enumerate((at.sib, at.yp, at.diag))
    ]
    for copy in g_copies:
        copy.start()

    def first_y(s):
        sib_copy(0, s).wait_recv()
        build(0, s)
        y_copy(0, s).start()

    each(slots, first_y)

    def wo_block(who):
        return r.wog.at[pl.ds(pl.multiple_of(feat * who, 16), feat)]

    wo_sib = remote(r.wo_in, wo_block(at.head), r.ws.at[0], r.wr.at[0], at.sib)
    wo_y = remote(r.wo_in, wo_block(at.head), r.ws.at[1], r.wr.at[1], at.yp)
    wo_f = remote(wo_block(at.yp[1]), wo_block(at.yp[1]), r.ws.at[2], r.wr.at[2], at.sib)
    wo_y.start()
    wo_sib.start()
    each(slots, lambda s: sib_copy(1, s).start())
    r.wog[pl.ds(pl.multiple_of(feat * at.head, 16), feat)] = r.wo_in[...]
    for copy in g_copies:
        copy.wait()
    r.gbf[...] = jnp.concatenate([r.gland[i] for i in range(4)], axis=1)
    r.mrow[...] = jnp.zeros_like(r.mrow)
    r.lrow[...] = jnp.ones_like(r.lrow)
    r.og[...] = jnp.zeros_like(r.og)
    r.qq[...] = jnp.zeros_like(r.qq)
    r.qkv[...] = jnp.zeros_like(r.qkv)
    r.gsum[...] = jnp.zeros_like(r.gsum)
    r.gtwo[...] = jnp.zeros_like(r.gtwo)
    r.drow[...] = jnp.zeros_like(r.drow)

    def project(s):
        x = whole_rows(r.xg, s).astype(F32)
        mean, inv = row_stats(x)
        normed = ((x - mean) * inv * r.gbf[0:1] + r.gbf[1:2]).astype(BF16)
        r.n1[s] = normed
        pt = dot(r.w_t[...], normed, 1, 1)
        qk = turn(pt[:half], r.cos[...], r.sin[...])
        r.qt[s] = (qk[:feat] * HEAD_DIM**-0.5).astype(BF16)
        kv = jnp.concatenate([qk[feat:], pt[half:]], axis=0).astype(BF16)
        r.kvn[s] = kv[:, :length]
        r.kvo[s] = kv[:, length:]
        readers(s, lambda i: kv_copy(s, i).start())

    def arrive(t):
        @pl.when(t < slots)
        def _():
            y_copy(0, t).wait_recv()
            f_copy(0, t).start()

        @pl.when(t >= 1)
        def _():
            f_copy(0, t - 1).wait_recv()
            project(t - 1)

    each(slots + 1, arrive)

    def cot_on(s):
        sib_copy(1, s).wait_recv()
        build(1, s)
        y_copy(1, s).start()

    each(2, cot_on)

    def attend(s):
        start, end = r.bounds[s, 0:1], r.bounds[s, 1:2]
        clean, noisy = masks(me, length, start, end)
        kc, kn = r.kvo[s], r.kvn[s]
        q = [r.qt[s, hd] for hd in heads]
        sc = [dot(kc[hd], q[h], 0, 0) for h, hd in enumerate(heads)]
        sn = [dot(kn[hd], q[h][:, :length], 0, 0) for h, hd in enumerate(heads)]
        sc = [jnp.where(clean, v, masked_score) for v in sc]
        sn = [jnp.where(noisy, v, masked_score) for v in sn]
        top = []
        for h in range(hl):
            tc = jnp.max(sc[h], axis=0, keepdims=True)
            tn = jnp.max(sn[h], axis=0, keepdims=True)
            top.append(jnp.concatenate([jnp.maximum(tc[:, :length], tn), tc[:, length:]], axis=1))
        pc = [jnp.exp(sc[h] - top[h]) for h in range(hl)]
        pn = [jnp.exp(sn[h] - top[h][:, :length]) for h in range(hl)]
        oc = [dot(kc[feat:][hd], pc[h].astype(BF16), 1, 0) for h, hd in enumerate(heads)]
        on = [dot(kn[feat:][hd], pn[h].astype(BF16), 1, 0) for h, hd in enumerate(heads)]
        for h, hd in enumerate(heads):
            tc = jnp.sum(pc[h], axis=0, keepdims=True)
            tn = jnp.sum(pn[h], axis=0, keepdims=True)
            r.mrow[h : h + 1] = top[h]
            r.lrow[h : h + 1] = jnp.concatenate([tc[:, :length] + tn, tc[:, length:]], axis=1)
            r.acc[hd, early] = oc[h][:, :length] + on[h]
            r.acc[hd, late] = oc[h][:, length:]

        def one(j, carry):
            kv_in(s, j).wait_recv()
            kv = r.kvb[at.spot(s, j, j)]
            q = [r.qt[s, hd] for hd in heads]
            old = [r.mrow[h : h + 1] for h in range(hl)]
            total = [r.lrow[h : h + 1] for h in range(hl)]
            pos = lax.broadcasted_iota(jnp.int32, (length, rows), 0) + j * length
            allowed = pos >= start
            sc = [dot(kv[hd], q[h], 0, 0) for h, hd in enumerate(heads)]
            sc = [jnp.where(allowed, v, masked_score) for v in sc]
            new = [jnp.maximum(old[h], jnp.max(sc[h], axis=0, keepdims=True)) for h in range(hl)]
            p = [jnp.exp(sc[h] - new[h]) for h in range(hl)]
            add = [dot(kv[feat:][hd], p[h].astype(BF16), 1, 0) for h, hd in enumerate(heads)]
            scale = [jnp.exp(old[h] - new[h]) for h in range(hl)]
            for h, hd in enumerate(heads):
                r.mrow[h : h + 1] = new[h]
                r.lrow[h : h + 1] = total[h] * scale[h] + jnp.sum(p[h], axis=0, keepdims=True)
                r.acc[hd] = r.acc[hd] * scale[h] + add[h]
            return carry

        lax.fori_loop(at.lowest(s, me), me, one, 0)
        for h, hd in enumerate(heads):
            r.att[s, hd] = r.acc[hd] / r.lrow[h : h + 1]
        r.lse[s] = r.mrow[...] + jnp.log(r.lrow[...])
        r.own_att[s] = r.att[s].T.astype(BF16)
        sib_copy(2, s).start()

    def forward(s):
        x = whole_rows(r.xg, s).astype(F32)
        branch = dot(r.ag[s, 0], r.wog[:half], 1, 0) + dot(r.ag[s, 1], r.wog[half:], 1, 0)
        h = x + branch
        for yy in range(2):
            for cc in range(2):

                @pl.when(jnp.logical_and(y == yy, core == cc))
                def _():
                    r.hp[s] = h[cc * length : (cc + 1) * length, yy * half : (yy + 1) * half]

        mean, inv = row_stats(h)
        r.iv[s] = inv
        normed = ((h - mean) * inv * r.gbf[2:3] + r.gbf[3:4]).astype(BF16)
        r.n2[s] = normed
        up = dot(normed, r.wu[...], 1, 0)
        cube = 0.7978845608028654 * (up + 0.044715 * up * up * up)
        t = jnp.tanh(cube)
        r.act[s] = (0.5 * up * (1.0 + t)).astype(BF16)
        slope = 0.5 * (1.0 + t) + 0.5 * up * (1.0 - t * t) * (
            0.7978845608028654 * (1.0 + 3 * 0.044715 * up * up)
        )
        da = dot(whole_rows(r.cg, s), r.wd[...], 1, 1)
        pre = (da * slope).astype(BF16)
        r.upre[s] = pre
        r.ep[s] = dot(pre, r.wu[...], 1, 1).astype(BF16)
        e_core(s).start()

    def stage(t, offset, step):
        s = t - offset

        @pl.when(jnp.logical_and(s >= 0, s < slots))
        def _():
            step(s)

    def att_on(s):
        sib_copy(2, s).wait_recv()
        build(2, s)
        y_copy(2, s).start()

    def att_back(s):
        y_copy(2, s).wait_recv()
        f_copy(2, s).start()

    def cot_back(s):
        y_copy(1, s).wait_recv()
        f_copy(1, s).start()

    def feed(s):
        @pl.when(s == 0)
        def _():
            wo_y.wait_recv()
            wo_f.start()
            wo_sib.wait_recv()
            wo_f.wait_recv()

        f_copy(1, s).wait_recv()
        f_copy(2, s).wait_recv()
        forward(s)

    def e_on(s):
        e_core(s).wait_recv()
        r.er[s] = (r.ep[s, mine].astype(F32) + r.er[s].astype(F32)).astype(BF16)
        e_y(s).start()

    def e_total(s):
        e_y(s).wait_recv()
        r.ey[s] = (r.er[s].astype(F32) + r.ey[s].astype(F32)).astype(BF16)
        e_y(s).wait_send()
        e_back(s).start()

    def loop_one(t):
        stage(t, 1, att_on)

        @pl.when(jnp.logical_and(t >= 1, t < slots - 1))
        def _():
            cot_on(t + 1)

        stage(t, 2, cot_back)
        stage(t, 2, att_back)

        @pl.when(t == slots)
        def _():
            each(slots - 2, e_on)

        @pl.when(t == slots + 1)
        def _():
            e_on(slots - 2)

        stage(t, 0, attend)
        stage(t, 2, feed)

    each(slots + 2, loop_one)

    wide = slots * rows

    def up_tile(i):
        cols = pl.ds(pl.multiple_of(i * 256, 256), 256)
        left = r.n2[...].reshape(wide, D)
        part = dot(left, r.upre[:, :, cols].reshape(wide, 256), 0, 0).astype(BF16)
        r.gl[0, :, cols] = part

    def down_tile(i):
        cols = pl.ds(pl.multiple_of(lax.rem(i, 3) * 128, 128), 128)
        out_cols = pl.ds(pl.multiple_of(i * 128, 128), 128)
        left = r.act[...].reshape(wide, D)
        part = dot(left, r.cg[:, lax.div(i, 3), :, cols].reshape(wide, 128), 0, 0).astype(BF16)
        r.gl[1, :, out_cols] = part

    e_on(slots - 1)
    each(D // 256, up_tile)
    each(D // 128, down_tile)
    sum1.begin()
    e_total(0)
    e_total(1)

    def two_back(s):
        e_back(s).wait_recv()
        e_back(s).wait_send()
        e_core(s).wait_send()

        @pl.when(core == 0)
        def _():
            r.ep[s, early] = r.ey[s]
            r.ep[s, late] = r.eb[s]

        @pl.when(core == 1)
        def _():
            r.ep[s, early] = r.eb[s]
            r.ep[s, late] = r.ey[s]

        e = r.ep[s].astype(F32)
        xh = (r.n2[s].astype(F32) - r.gbf[3:4]) * r.ginv[0:1]
        r.gtwo[2:3] += jnp.sum(e * xh, axis=0, keepdims=True)
        r.gtwo[3:4] += jnp.sum(e, axis=0, keepdims=True)
        g = e * r.gbf[2:3]
        first = jnp.sum(g, axis=1, keepdims=True) / D
        second = jnp.sum(g * xh, axis=1, keepdims=True) / D
        resid = whole_rows(r.cg, s).astype(F32) + r.iv[s] * (g - first - xh * second)
        r.ep[s] = resid.astype(BF16)

    r.ginv[...] = 1.0 / r.gbf[2:3] + jnp.zeros_like(r.ginv)

    def head_grads(s, kv, lanes, allowed):
        q = [r.qt[s, hd, lanes] for hd in heads]
        d_out = [r.do[hd, lanes] for hd in heads]
        sc = [dot(kv[hd], q[h], 0, 0) for h, hd in enumerate(heads)]
        dp = [dot(kv[feat:][hd], d_out[h], 0, 0) for h, hd in enumerate(heads)]
        p = [
            jnp.exp(jnp.where(allowed, sc[h], masked_score) - r.lse[s, h : h + 1, lanes])
            for h in range(hl)
        ]
        ds = [(p[h] * (dp[h] - r.drow[h : h + 1, lanes])).astype(BF16) for h in range(hl)]
        dv = [dot(d_out[h], p[h].astype(BF16), 1, 1) for h in range(hl)]
        dk = [dot(q[h], ds[h], 1, 1) for h in range(hl)]
        dq_add = [dot(kv[hd], ds[h], 1, 0) for h, hd in enumerate(heads)]
        return [jnp.concatenate(v, axis=0) for v in (dq_add, dk, dv)]

    def attend_back(s):
        low_rows = r.ep[s]
        d_out = dot(r.wo_in[...], low_rows, 1, 1).astype(BF16)
        r.do[...] = d_out
        a = r.att[s]
        r.og[...] += dot(a.astype(BF16), low_rows, 1, 0)
        prod = d_out.astype(F32) * a
        for h, hd in enumerate(heads):
            r.drow[h : h + 1] = jnp.sum(prod[hd], axis=0, keepdims=True)
        start, end = r.bounds[s, 0:1], r.bounds[s, 1:2]
        clean, noisy = masks(me, length, start, end)
        dqa, dk, dv = head_grads(s, r.kvo[s], slice(0, rows), clean)
        dqn, dkn, dvn = head_grads(s, r.kvn[s], early, noisy)
        r.acc[...] = dqa
        r.acc[:, early] += dqn
        r.dkv[s, :feat] = dk
        r.dkv[s, feat:] = dv
        r.qp[s, half:, early] = dvn.astype(BF16)
        r.qp[s, feat:half, early] = turn(dkn, r.cos[:, :length], -r.sin[:, :length]).astype(BF16)

        def one(j, carry):
            spot = at.spot(s, j, j)
            kv = r.kvb[spot]
            pos = lax.broadcasted_iota(jnp.int32, (length, rows), 0) + j * length
            dqa, dk, dv = head_grads(s, kv, slice(0, rows), pos >= start)
            r.acc[...] += dqa
            r.kvb[spot, :feat] = dk.astype(BF16)
            r.kvb[spot, feat:] = dv.astype(BF16)
            dkv_copy(s, j).start()
            return carry

        lax.fori_loop(at.lowest(s, me), me, one, 0)
        r.qp[s, :feat] = (turn(r.acc[...], r.cos[...], -r.sin[...]) * HEAD_DIM**-0.5).astype(BF16)
        r.qq[...] += dot(r.qp[s, :feat], r.n1[s], 1, 0)

    def f_start(s):
        y_copy(2, s).wait_send()
        f_copy(2, s).wait_send()
        ff = dot(r.act[s], r.wd[...], 1, 0)
        r.ag[s, 0] = ff[:, :half].astype(BF16)
        r.ag[s, 1] = ff[:, half:].astype(BF16)
        f_core(s).start()

    def f_on(s):
        f_core(s).wait_recv()
        for k in range(2):
            r.upre[held(0, s, k)] = (r.ag[s, k, mine].astype(F32) + r.fc[s, k].astype(F32)).astype(BF16)
        f_y(s).start()

    def f_end(s):
        f_y(s).wait_recv()
        total = r.hp[s] + (r.upre[held(0, s, y)].astype(F32) + r.fy[s].astype(F32))
        lo = total[:, :feat].astype(BF16)
        hi = total[:, feat:].astype(BF16)

        @pl.when(core == 0)
        def _():
            r.out[s, 0] = lo
            r.osd[s] = hi

        @pl.when(core == 1)
        def _():
            r.out[s, 1] = hi
            r.osd[s] = lo

        f_back(s).start()

    def loop_two(t):
        def run(s):
            two_back(s)
            attend_back(s)

        stage(t, 1, f_on)
        stage(t, -2, e_total)
        stage(t, 0, run)

        @pl.when(jnp.logical_or(t == 3, t == 5))
        def _():
            sum1.pass_on(lax.div(t - 3, 2))

    each(slots, f_start)
    each(slots, loop_two)
    src2[0] = r.og[...].astype(BF16)
    src2[1] = r.qq[...].astype(BF16)
    sum2.begin()
    f_on(slots - 1)
    sum1.pass_on(2)
    sum1.pass_on(3)

    def project_back(s):
        def add(i):
            dkv_in(s, i).wait_recv()
            r.dkv[s] += r.dla[at.spot(s, me, i)].astype(F32)

        readers(s, add)
        total = r.dkv[s]
        r.qp[s, feat:half, late] = turn(total[:feat], r.cos[:, late], -r.sin[:, late]).astype(BF16)
        r.qp[s, half:, late] = total[feat:].astype(BF16)
        pre = r.qp[s]
        r.qkv[...] += dot(pre[feat:], r.n1[s], 1, 0)
        e = dot(pre, r.w_t[...], 0, 0)
        x = whole_rows(r.xg, s).astype(F32)
        mean, inv = row_stats(x)
        xh = (x - mean) * inv
        r.gsum[0:1] += jnp.sum(e * xh, axis=0, keepdims=True)
        r.gsum[1:2] += jnp.sum(e, axis=0, keepdims=True)
        r.n2[s] = e.astype(BF16)
        g = e * r.gbf[0:1]
        one_sum = jnp.sum(g, axis=1, keepdims=True)
        two_sum = jnp.sum(g * xh, axis=1, keepdims=True)
        lane = lax.broadcasted_iota(jnp.int32, (rows, 128), 1)
        packed = jnp.where(lane == 0, one_sum, jnp.where(lane == 1, two_sum, 0.0)).T
        r.st[s, 0] = packed[:8, :length]
        r.st[s, 1] = packed[:8, length:]
        b_core(s).start()
        s_core(s).start()

    def b_on(s):
        b_core(s).wait_recv()
        s_core(s).wait_recv()
        both = r.n2[s, mine].astype(F32) + r.er[s].astype(F32)
        r.upre[s, late] = both.astype(BF16)
        r.sh[s] = r.st[s, core] + r.sl[s]
        b_y(s).start()
        s_y(s).start()

    def b_end(s):
        b_y(s).wait_recv()
        s_y(s).wait_recv()
        e = r.upre[held(length, s, y)].astype(F32) + r.bey[s].astype(F32)
        sums = r.sh[s] + r.sy[s]
        cols = jnp.concatenate([sums, jnp.zeros((120, length), F32)], axis=0).T
        first, second = cols[:, 0:1] / D, cols[:, 1:2] / D
        x = jnp.concatenate([r.xg[s, 0, mine], r.xg[s, 1, mine]], axis=1).astype(F32)
        mean, inv = row_stats(x)
        xh = (r.xg[s, y, mine].astype(F32) - mean) * inv
        gain = jnp.where(y == 0, r.gbf[0:1, :half], r.gbf[0:1, half:])
        resid = r.ep[s, mine].astype(F32)
        resid = jnp.where(y == 0, resid[:, :half], resid[:, half:])
        grad = resid + inv * (e * gain - first - xh * second)
        lo, hi = grad[:, :feat], grad[:, feat:]

        @pl.when(core == 0)
        def _():
            r.ig[s, 0] = lo
            r.isd[s] = hi

        @pl.when(core == 1)
        def _():
            r.ig[s, 1] = hi
            r.isd[s] = lo

        b_back(s).start()

    def loop_three(t):
        stage(t, 0, f_end)
        stage(t, 1, b_on)
        stage(t, 0, project_back)

        pl.when(t == 2)(sum1.reduce)

        @pl.when(jnp.logical_or(t == 3, t == 4))
        def _():
            sum2.pass_on(2 * t - 6)
            sum2.pass_on(2 * t - 5)

    each(slots, loop_three)
    grads = r.qkv[...].astype(BF16)
    r.src3[0] = grads[:feat]
    r.src3[1] = grads[feat:]
    sum3.begin()
    b_on(slots - 1)
    h_copies = [
        remote(r.gsum, r.gh.at[k], r.hs.at[k], r.hr.at[k], d)
        for k, d in enumerate((at.sib, at.yp, at.diag))
    ]
    for copy in h_copies:
        copy.start()
    sum2.reduce()

    def share(i):
        return remote(r.gf, r.gq.at[me], r.qs.at[i], r.qr.at[me], (i, at.head))

    def share_in(i):
        return remote(r.gf, r.gq.at[i], r.qs.at[i], r.qr.at[i], (i, at.head))

    def gains_on():
        for copy in h_copies:
            copy.wait()
        total = r.gsum[...] + r.gh[0] + r.gh[1] + r.gh[2] + r.gtwo[...]
        for h in range(4):

            @pl.when(at.head == h)
            def _():
                r.gf[...] = total[:, h * feat : (h + 1) * feat]

        r.gq[me] = r.gf[...]
        for d in range(1, n):
            share(lax.rem(me + d, n)).start()

    def loop_four(t):
        stage(t, 0, b_end)
        pl.when(t == 0)(gains_on)

        @pl.when(jnp.logical_or(t == 1, t >= 4))
        def _():
            sum1.forward(jnp.where(t == 1, 1, t - 2))

        @pl.when(jnp.logical_or(t == 2, t == 3))
        def _():
            sum3.pass_on(2 * t - 4)
            sum3.pass_on(2 * t - 3)

    each(slots, loop_four)
    sum3.reduce()
    for d in range(1, n):
        share_in(lax.rem(me + d, n)).wait_recv()
    r.gains[...] = jnp.sum(r.gq[...], axis=0)
    for d in range(1, m):
        sum2.forward(d)
    for d in range(1, m):
        sum3.forward(d)

    def finish(s):
        for k in range(3):
            sib_copy(k, s).wait_send()
        for k in range(2):
            y_copy(k, s).wait_send()
            f_copy(k, s).wait_send()
        readers(s, lambda i: kv_copy(s, i).wait_send())
        f_core(s).wait_send()
        f_y(s).wait_send()
        f_back(s).wait()
        b_core(s).wait_send()
        s_core(s).wait_send()
        b_y(s).wait_send()
        s_y(s).wait_send()
        b_back(s).wait()

        def sent(j, carry):
            dkv_copy(s, j).wait_send()
            return carry

        lax.fori_loop(at.lowest(s, me), me, sent, 0)

    each(slots, finish)
    wo_sib.wait_send()
    wo_y.wait_send()
    wo_f.wait_send()
    for part in (sum1, sum2, sum3):
        part.finish()
    for d in range(1, n):
        share(lax.rem(me + d, n)).wait_send()


def body(
    inputs,
    doc_lengths,
    attn_gain,
    attn_bias,
    w_qkv,
    w_out,
    ffn_gain,
    ffn_bias,
    w_up,
    w_down,
    cotangent,
):
    n = lax.axis_size("seq")
    slots, _, length, feat = inputs.shape
    rows, half, m = 2 * length, 2 * feat, n // 2
    held = slots * n * half * length * 2
    if held > ROWS_LIMIT or m != 4:
        return gathered_body(
            inputs, doc_lengths, attn_gain, attn_bias, w_qkv, w_out, ffn_gain, ffn_bias, w_up, w_down, cotangent
        )
    me = lax.axis_index("seq")
    long = jnp.argmax(doc_lengths[:, 0]).astype(jnp.int32)
    ids = jnp.arange(slots, dtype=jnp.int32)

    def swap(v):
        pick = lax.dynamic_index_in_dim(v, long, 0, keepdims=True)
        where = ids.reshape((slots,) + (1,) * (v.ndim - 1))
        return jnp.where(where == 0, pick, jnp.where(where == long, v[:1], v))

    ends = jnp.cumsum(swap(doc_lengths), axis=1)
    positions = me * length + jnp.arange(length, dtype=jnp.int32)
    past = ends[:, :, None] <= positions[None, None, :]
    first_key = jnp.max(jnp.where(past, ends[:, :, None], 0), axis=1)
    last_key = jnp.min(jnp.where(past, 2**30, ends[:, :, None]), axis=1)
    pair = jnp.stack([jnp.tile(first_key, (1, 2)), jnp.tile(last_key, (1, 2))], axis=1)
    bounds = jnp.pad(pair, ((0, 0), (0, 6), (0, 0)))
    half_dim = HEAD_DIM // 2
    freqs = rotary_base ** (-jnp.arange(half_dim, dtype=F32) / half_dim)
    angles = freqs[:, None] * positions.astype(F32)[None, :]
    cos = jnp.tile(jnp.cos(angles), (1, 2))
    sin = jnp.tile(jnp.sin(angles), (1, 2))
    w_t = w_qkv.reshape(D, 3 * feat).T
    gains = jnp.concatenate(
        [jnp.stack([attn_gain, attn_bias, ffn_gain, ffn_bias]), jnp.zeros((4, feat), F32)], axis=0
    )
    operands = dict(
        x_in=swap(inputs).reshape(slots, rows, feat), c_in=swap(cotangent).reshape(slots, rows, feat),
        gb_in=gains, w_t=w_t, wo_in=w_out, wu=w_up, wd=w_down, cos=cos, sin=sin, bounds=bounds,
    )
    small = (m, feat // m, D)
    quarter = (m, D // m, D)
    outs = dict(
        out=((slots, 2, length, feat), BF16), ig=((slots, 2, length, feat), F32), res1=((2, *quarter), BF16),
        res2=((2, *small), BF16), res3=((2, *small), BF16), gains=((8, feat), F32),
    )
    blocks = n + (slots - 1) * (n // 2 + max(1, n // 8))
    full, wide = (slots, 2, rows, half), (slots, rows, D)
    part, stat = (slots, length, D), (slots, 8, length)
    halves, own_half = (slots, 2, length, half), (slots, length, half)
    buffers = dict(
        land=((2, slots, rows, feat), BF16), own_att=((slots, rows, feat), BF16), gland=((4, 8, feat), F32),
        gbf=((8, D), F32), ginv=((8, D), F32), xg=(full, BF16), cg=(full, BF16), ag=(full, BF16),
        wog=((D, D), BF16), n1=(wide, BF16), qt=((slots, feat, rows), BF16),
        kvn=((slots, half, length), BF16), kvo=((slots, half, length), BF16), kvb=((blocks, half, length), BF16),
        att=((slots, feat, rows), F32), lse=((slots, 8, rows), F32), acc=((feat, rows), F32),
        mrow=((8, rows), F32), lrow=((8, rows), F32), hp=(own_half, F32), iv=((slots, rows, 1), F32),
        n2=(wide, BF16), act=(wide, BF16), upre=(wide, BF16), ep=(wide, BF16), er=(part, BF16), ey=(part, BF16),
        eb=(part, BF16), fc=(halves, BF16), fy=(own_half, BF16),
        osd=((slots, length, feat), BF16), gl=((2, D, D), BF16), gx1=(quarter, BF16), gz1=(quarter, BF16),
        own1=(quarter[1:], BF16), do=((feat, rows), BF16), drow=((8, rows), F32),
        dkv=((slots, half, length), F32), dla=((blocks, half, length), BF16), qp=((slots, 3 * feat, rows), BF16),
        og=((feat, D), F32), qq=((feat, D), F32), qkv=((half, D), F32), gsum=((8, D), F32), gtwo=((8, D), F32),
        st=((slots, 2, 8, length), F32), sl=(stat, F32), sh=(stat, F32), sy=(stat, F32),
        bey=(own_half, BF16), isd=((slots, length, feat), F32), src3=((2, feat, D), BF16),
        gx2=(small, BF16), pt2=(small, BF16), gz2=(small, BF16), own2=(small[1:], BF16),
        gx3=(small, BF16), pt3=(small, BF16), gz3=(small, BF16), own3=(small[1:], BF16),
        gh=((3, 8, D), F32), gq=((n, 8, feat), F32), gf=((8, feat), F32),
    )
    sems = {k: (3, slots) for k in ("ss", "sr", "ys", "yr", "fs", "fr")}
    sems |= {k: (3,) for k in ("gs", "gr", "ws", "wr", "hs", "hr")}
    sems |= {k: (slots, n) for k in ("ks", "kr", "ds", "dr")}
    sems |= {k + i + e: (slots,) for k in "efab" for i in "123" for e in "sr" if k + i != "b3"}
    sems |= {"qs": (n,), "qr": (n,)}
    pieces = {"u": 2, "v": 1, "w": 1}
    sems |= {"%s%d" % (k, i): (m,) for k in "uvw" for i in range(4)}
    sems |= {"%s%d" % (k, i): (m, pieces[k]) for k in "uvw" for i in range(4, 8)}
    sems |= {k + "9": (pieces[k],) for k in "uvw"}
    sem = pltpu.SemaphoreType.DMA
    scratch = {k: VMEM(*v) for k, v in buffers.items()}
    scratch |= {k: sem(v) for k, v in sems.items()}
    scratch |= {k + "8": sem for k in "uvw"}
    vmem = pl.BlockSpec(memory_space=VMEM)
    names = [*operands, *outs, *scratch]
    got = pl.pallas_call(
        functools.partial(layer, n, names),
        out_shape=[jax.ShapeDtypeStruct(*v) for v in outs.values()],
        in_specs=[vmem] * len(operands),
        out_specs=[pl.BlockSpec(memory_space=pl.ANY) if k.startswith("res") else vmem for k in outs],
        scratch_shapes=list(scratch.values()),
        compiler_params=pltpu.CompilerParams(
            collective_id=0, has_side_effects=True, vmem_limit_bytes=VMEM_LIMIT
        ),
        name="layer",
    )(*operands.values())
    outputs, input_grad, res1, res2, res3, gain_grads = got
    up_grad, down_grad = res1.reshape(2, D, D).astype(F32)
    out_grad, q_grad = res2.reshape(2, feat, D).astype(F32)
    qkv_grad = jnp.concatenate([q_grad[None], res3.reshape(2, feat, D).astype(F32)], axis=0)
    return (
        swap(outputs),
        swap(input_grad),
        jnp.transpose(qkv_grad, (2, 0, 1)),
        out_grad,
        up_grad,
        down_grad,
        gain_grads[0],
        gain_grads[1],
        gain_grads[2],
        gain_grads[3],
    )


def solution(mesh):
    in_specs = (
        P(None, None, "seq", "head"),
        P(),
        P("head"),
        P("head"),
        P(None, None, "head"),
        P("head", None),
        P("head"),
        P("head"),
        P(None, "head"),
        P("head", None),
        P(None, None, "seq", "head"),
    )
    out_specs = (
        P(None, None, "seq", "head"),
        P(None, None, "seq", "head"),
        P(None, None, "head"),
        P("head", None),
        P(None, "head"),
        P("head", None),
        P("head"),
        P("head"),
        P("head"),
        P("head"),
    )
    return jax.shard_map(body, mesh=mesh, in_specs=in_specs, out_specs=out_specs, check_vma=False)
```

```python
import functools
import types

import jax
import jax.numpy as jnp
from jax import lax
from jax.experimental import pallas as pl
from jax.experimental.pallas import tpu as pltpu
from jax.sharding import PartitionSpec as P

D = 768
HEAD_DIM = 64
BLOCK = 16


norm_eps = 1e-05
masked_score = -1e30
rotary_base = 10000.0

MESH = pl.DeviceIdType.MESH
VMEM = pltpu.VMEM
F32 = jnp.float32
BF16 = jnp.bfloat16
ROWS_LIMIT = 16 << 20
VMEM_LIMIT = 63 << 20
LONG_SLOT = 3


def passed_along(block, axis, distance):
    devices = range(lax.axis_size(axis))
    route = [(i - distance, i) for i in devices if i - distance in devices]
    return lax.ppermute(block, axis, route)


def from_behind(x, axis, by):
    devices = lax.axis_size(axis)
    return lax.ppermute(x, axis, [(i, (i + by) % devices) for i in range(devices)])


def segment_ids(doc_lengths, positions):
    doc_ends = jnp.cumsum(doc_lengths, axis=1)
    return jnp.sum((doc_ends[:, :, None] <= positions[None, None, :]).astype(jnp.int32), axis=1)


def rotate(values, positions, sign):
    half_dim = values.shape[-1] // 2
    freqs = rotary_base ** (-jnp.arange(half_dim, dtype=jnp.float32) / half_dim)
    angles = positions.astype(jnp.float32)[:, None, None] * freqs
    cosine = jnp.cos(angles)
    sine = sign * jnp.sin(angles)
    first_half = values[..., :half_dim]
    second_half = values[..., half_dim:]
    return jnp.concatenate(
        [first_half * cosine - second_half * sine, second_half * cosine + first_half * sine],
        axis=-1,
    )


def row_pair(first_sum, second_sum):
    return lax.psum((first_sum, second_sum), "head")


def normalize(share, gain, bias):
    row_total, row_square = row_pair(jnp.sum(share, axis=-1), jnp.sum(share * share, axis=-1))
    mean_value = row_total / D
    inv_std = lax.rsqrt(row_square / D - mean_value * mean_value + norm_eps)
    centered = (share - mean_value[..., None]) * inv_std[..., None]
    scaled = (centered * gain + bias).astype(jnp.bfloat16)
    gathered = lax.all_gather(scaled, "head", axis=3, tiled=True)
    return (gathered, centered, inv_std)


def norm_backward(partial_value, gain, centered, inv_std):
    share = lax.psum_scatter(partial_value, "head", scatter_dimension=3, tiled=True)
    scaled = share * gain
    first_mean, second_mean = row_pair(
        jnp.sum(scaled, axis=-1), jnp.sum(scaled * centered, axis=-1)
    )
    grad_in = inv_std[..., None] * (
        scaled - first_mean[..., None] / D - centered * (second_mean[..., None] / D)
    )
    gain_grad = jnp.sum(share * centered, axis=(0, 1, 2))
    bias_grad = jnp.sum(share, axis=(0, 1, 2))
    return (grad_in, gain_grad, bias_grad)


def branch_total(partial_value):
    return lax.psum_scatter(partial_value, "head", scatter_dimension=3, tiled=True)


def gradient_rows(share):
    return lax.all_gather(share, "head", axis=3, tiled=True)


def mask_rule(query_pos, query_seg, key_pos, key_seg):
    query_block = (query_pos // BLOCK)[:, None]
    key_block = (key_pos // BLOCK)[None, :]
    order = jnp.stack([key_block < query_block, key_block <= query_block])
    same_doc = query_seg[:, :, None] == key_seg[:, None, :]
    return jnp.logical_and(order[None, :, None], same_doc[:, None, None])


def absorb(state_now, scores, allowed, value_piece):
    run_max, run_sum, run_acc = state_now
    masked = jnp.where(allowed, scores, masked_score)
    new_max = jnp.maximum(run_max, jnp.max(masked, axis=-1))
    weights_now = jnp.where(allowed, jnp.exp(masked - new_max[..., None]), 0.0)
    factor = jnp.exp(run_max - new_max)
    new_sum = run_sum * factor + jnp.sum(weights_now, axis=-1)
    added = jnp.einsum(
        "schlk,skhd->schld",
        weights_now,
        value_piece.astype(jnp.float32),
        precision=lax.Precision.HIGHEST,
    )
    return (new_max, new_sum, run_acc * factor[..., None] + added)


def gathered_body(
    inputs,
    doc_lengths,
    attn_gain,
    attn_bias,
    w_qkv,
    w_out,
    ffn_gain,
    ffn_bias,
    w_up,
    w_down,
    cotangent,
):
    seqs_here, _, local_len, _ = inputs.shape
    head_local = w_qkv.shape[2] // HEAD_DIM
    first_pos = lax.axis_index("seq") * local_len
    positions = first_pos + jnp.arange(local_len, dtype=jnp.int32)
    segments = segment_ids(doc_lengths, positions)
    inputs_wide = inputs.astype(jnp.float32)
    normed_one, centered_one, inv_one = normalize(inputs_wide, attn_gain, attn_bias)
    projected = jnp.einsum("scld,dtk->scltk", normed_one, w_qkv, preferred_element_type=jnp.float32)
    split_rows = projected.reshape(seqs_here, 2, local_len, 3, head_local, HEAD_DIM)
    queries = (rotate(split_rows[:, :, :, 0], positions, 1.0) * HEAD_DIM ** (-0.5)).astype(
        jnp.bfloat16
    )
    key_rows = rotate(split_rows[:, :, :, 1], positions, 1.0).astype(jnp.bfloat16)
    value_rows = split_rows[:, :, :, 2].astype(jnp.bfloat16)
    clean_keys = key_rows[:, 1].reshape(seqs_here, local_len, head_local * HEAD_DIM)
    clean_values = value_rows[:, 1].reshape(seqs_here, local_len, head_local * HEAD_DIM)
    block_ids = positions // BLOCK
    own_allowed = jnp.logical_and(
        (block_ids[:, None] == block_ids[None, :])[None],
        segments[:, :, None] == segments[:, None, :],
    )[:, None, None]
    noisy_scores = jnp.einsum(
        "sclhd,skhd->schlk", queries[:, :1], key_rows[:, 0], preferred_element_type=jnp.float32
    )
    half_shape = (seqs_here, 1, head_local, local_len)
    empty_state = (
        jnp.full(half_shape, masked_score, jnp.float32),
        jnp.zeros(half_shape, jnp.float32),
        jnp.zeros(half_shape + (HEAD_DIM,), jnp.float32),
    )
    noisy_state = absorb(empty_state, noisy_scores, own_allowed, value_rows[:, 0])
    start_state = jax.tree.map(
        lambda first, second: jnp.concatenate([first, second], axis=1), noisy_state, empty_state
    )
    piece_keys = lax.all_gather(clean_keys, "seq", axis=1, tiled=True)
    piece_values = lax.all_gather(clean_values, "seq", axis=1, tiled=True)
    piece_len = piece_keys.shape[1]
    key_pos = jnp.arange(piece_len, dtype=jnp.int32)
    key_seg = segment_ids(doc_lengths, key_pos)
    key_heads = piece_keys.reshape(seqs_here, piece_len, head_local, HEAD_DIM)
    value_heads = piece_values.reshape(seqs_here, piece_len, head_local, HEAD_DIM)
    scores = jnp.einsum("sclhd,skhd->schlk", queries, key_heads, preferred_element_type=jnp.float32)
    final_max, final_sum, final_acc = absorb(
        start_state, scores, mask_rule(positions, segments, key_pos, key_seg), value_heads
    )
    attended = final_acc / final_sum[..., None]
    log_total = final_max + jnp.log(final_sum)
    attended_low = attended.astype(jnp.bfloat16)
    out_heads = w_out.reshape(head_local, HEAD_DIM, w_out.shape[1])
    attn_share = branch_total(
        jnp.einsum("schld,hdm->sclm", attended_low, out_heads, preferred_element_type=jnp.float32)
    )
    hidden_res = inputs_wide + attn_share
    normed_two, centered_two, inv_two = normalize(hidden_res, ffn_gain, ffn_bias)
    up_value = jnp.einsum("scld,df->sclf", normed_two, w_up, preferred_element_type=jnp.float32)
    activated, gelu_back = jax.vjp(lambda inner: jax.nn.gelu(inner, approximate=True), up_value)
    act_low = activated.astype(jnp.bfloat16)
    ffn_share = branch_total(
        jnp.einsum("sclf,fm->sclm", act_low, w_down, preferred_element_type=jnp.float32)
    )
    outputs = (hidden_res + ffn_share).astype(jnp.bfloat16)
    grad_out = cotangent.astype(jnp.float32)
    grad_full = gradient_rows(cotangent)
    down_grad = jnp.einsum("sclf,sclm->fm", act_low, grad_full, preferred_element_type=jnp.float32)
    act_grad = jnp.einsum("sclm,fm->sclf", grad_full, w_down, preferred_element_type=jnp.float32)
    up_pre_grad = gelu_back(act_grad)[0].astype(jnp.bfloat16)
    up_grad = jnp.einsum(
        "scld,sclf->df", normed_two, up_pre_grad, preferred_element_type=jnp.float32
    )
    normed_two_grad = jnp.einsum(
        "sclf,df->scld", up_pre_grad, w_up, preferred_element_type=jnp.float32
    )
    back_two, ffn_gain_grad, ffn_bias_grad = norm_backward(
        normed_two_grad, ffn_gain, centered_two, inv_two
    )
    resid_grad = grad_out + back_two
    resid_full = gradient_rows(resid_grad.astype(jnp.bfloat16))
    out_grad = jnp.einsum(
        "schld,sclm->hdm", attended_low, resid_full, preferred_element_type=jnp.float32
    ).reshape(w_out.shape)
    attended_grad = jnp.einsum(
        "sclm,hdm->schld", resid_full, out_heads, preferred_element_type=jnp.float32
    ).astype(jnp.bfloat16)
    grad_wide = attended_grad.astype(jnp.float32)
    row_delta = jnp.sum(grad_wide * attended, axis=-1)
    noisy_probs = jnp.where(own_allowed, jnp.exp(noisy_scores - log_total[:, :1, :, :, None]), 0.0)
    noisy_prob_grad = jnp.einsum(
        "schld,skhd->schlk",
        attended_grad[:, :1],
        value_rows[:, 0],
        preferred_element_type=jnp.float32,
    )
    noisy_score_grad = (noisy_probs * (noisy_prob_grad - row_delta[:, :1, :, :, None])).astype(
        jnp.bfloat16
    )
    noisy_query_grad = jnp.einsum(
        "schlk,skhd->schld", noisy_score_grad, key_rows[:, 0], preferred_element_type=jnp.float32
    )
    noisy_key_grad = jnp.einsum(
        "schlk,sclhd->skhd", noisy_score_grad, queries[:, :1], preferred_element_type=jnp.float32
    )
    noisy_value_grad = jnp.einsum(
        "schlk,schld->skhd", noisy_probs, grad_wide[:, :1], precision=lax.Precision.HIGHEST
    )
    query_start = jnp.concatenate([noisy_query_grad, jnp.zeros_like(noisy_query_grad)], axis=1)
    flat_zero = jnp.zeros((seqs_here, local_len, head_local * HEAD_DIM), jnp.float32)

    def piece_grads(piece_keys, piece_values, first_row, query_total):
        key_pos = first_row + jnp.arange(local_len, dtype=jnp.int32)
        key_seg = segment_ids(doc_lengths, key_pos)
        key_heads = piece_keys.reshape(seqs_here, local_len, head_local, HEAD_DIM)
        value_heads = piece_values.reshape(seqs_here, local_len, head_local, HEAD_DIM)
        scores = jnp.einsum(
            "sclhd,skhd->schlk", queries, key_heads, preferred_element_type=jnp.float32
        )
        allowed = mask_rule(positions, segments, key_pos, key_seg)
        weights_now = jnp.where(allowed, jnp.exp(scores - log_total[..., None]), 0.0)
        prob_grad = jnp.einsum(
            "schld,skhd->schlk", attended_grad, value_heads, preferred_element_type=jnp.float32
        )
        score_grad = (weights_now * (prob_grad - row_delta[..., None])).astype(jnp.bfloat16)
        query_out = query_total + jnp.einsum(
            "schlk,skhd->schld", score_grad, key_heads, preferred_element_type=jnp.float32
        )
        key_part = jnp.einsum(
            "schlk,sclhd->skhd", score_grad, queries, preferred_element_type=jnp.float32
        )
        value_part = jnp.einsum(
            "schlk,schld->skhd", weights_now, grad_wide, precision=lax.Precision.HIGHEST
        )
        return (key_part.reshape(flat_zero.shape), value_part.reshape(flat_zero.shape), query_out)

    def cycle_body(cycle_step, carried):
        piece_keys, piece_values, key_acc, value_acc, query_acc = carried
        source = (lax.axis_index("seq") - cycle_step) % lax.axis_size("seq")
        first_row = source * local_len
        key_part, value_part, query_acc = piece_grads(
            piece_keys, piece_values, first_row, query_acc
        )
        key_acc = key_acc + key_part
        value_acc = value_acc + value_part
        piece_keys, piece_values = passed_along((piece_keys, piece_values), "seq", 1)
        key_acc, value_acc = (
            from_behind(key_acc.astype(jnp.bfloat16), "seq", 1).astype(key_acc.dtype),
            from_behind(value_acc.astype(jnp.bfloat16), "seq", 1).astype(value_acc.dtype),
        )
        return (piece_keys, piece_values, key_acc, value_acc, query_acc)

    cycle_start = (clean_keys, clean_values, flat_zero, flat_zero, query_start)
    _, _, clean_key_grad, clean_value_grad, query_acc = lax.fori_loop(
        0, lax.axis_size("seq"), cycle_body, cycle_start
    )
    head_shape = (seqs_here, local_len, head_local, HEAD_DIM)
    query_total = rotate(jnp.transpose(query_acc, (0, 1, 3, 2, 4)), positions, -1.0) * HEAD_DIM ** (
        -0.5
    )
    key_total = rotate(
        jnp.stack([noisy_key_grad, clean_key_grad.reshape(head_shape)], axis=1), positions, -1.0
    )
    value_total = jnp.stack([noisy_value_grad, clean_value_grad.reshape(head_shape)], axis=1)
    qkv_pre_grad = (
        jnp.stack([query_total, key_total, value_total], axis=3)
        .reshape(seqs_here, 2, local_len, 3, head_local * HEAD_DIM)
        .astype(jnp.bfloat16)
    )
    qkv_grad = jnp.einsum(
        "scld,scltk->dtk", normed_one, qkv_pre_grad, preferred_element_type=jnp.float32
    )
    normed_one_grad = jnp.einsum(
        "scltk,dtk->scld", qkv_pre_grad, w_qkv, preferred_element_type=jnp.float32
    )
    back_one, attn_gain_grad, attn_bias_grad = norm_backward(
        normed_one_grad, attn_gain, centered_one, inv_one
    )
    input_grad = resid_grad + back_one
    (
        qkv_grad,
        out_grad,
        up_grad,
        down_grad,
        attn_gain_grad,
        attn_bias_grad,
        ffn_gain_grad,
        ffn_bias_grad,
    ) = lax.psum(
        (
            qkv_grad,
            out_grad,
            up_grad,
            down_grad,
            attn_gain_grad,
            attn_bias_grad,
            ffn_gain_grad,
            ffn_bias_grad,
        ),
        "seq",
    )
    return (
        outputs,
        input_grad,
        qkv_grad,
        out_grad,
        up_grad,
        down_grad,
        attn_gain_grad,
        attn_bias_grad,
        ffn_gain_grad,
        ffn_bias_grad,
    )


def dot(a, b, ca, cb):
    return lax.dot_general(a, b, (((ca,), (cb,)), ((), ())), preferred_element_type=F32)


def remote(src, dst, send, recv, device):
    return pltpu.make_async_remote_copy(
        src_ref=src, dst_ref=dst, send_sem=send, recv_sem=recv, device_id=device, device_id_type=MESH
    )


class Place:
    def __init__(self, n):
        self.n = n
        self.me = lax.axis_index("seq")
        self.head = lax.axis_index("head")
        self.core = lax.rem(self.head, 2)
        self.y = lax.div(self.head, 2)
        self.sib = (self.me, self.y * 2 + 1 - self.core)
        self.yp = (self.me, (1 - self.y) * 2 + self.core)
        self.diag = (self.me, (1 - self.y) * 2 + 1 - self.core)
        self.half = n // 2
        self.band = max(1, n // 8)

    def lowest(self, slot, i):
        near = i - self.band
        short = jnp.where(i >= self.half, jnp.minimum(near, self.half), near)
        return jnp.where(slot == LONG_SLOT, 0, jnp.maximum(short, 0))

    def spot(self, slot, block, other):
        window = self.half + self.band
        near = self.half + lax.rem(other, self.band)
        late = jnp.where(block >= self.half, other - self.half, near)
        order = slot - jnp.where(slot > LONG_SLOT, 1, 0)
        return jnp.where(slot == LONG_SLOT, other, self.n + order * window + late)

    def spots(self, slots):
        return self.n + (slots - 1) * (self.half + self.band)

    def greet(self, near, everyone):
        bar = pltpu.get_barrier_semaphore()
        for d in near:
            pl.semaphore_signal(bar, inc=1, device_id=d, device_id_type=MESH)
        count = len(near)
        if everyone:
            for d in range(1, self.n):
                there = lax.rem(self.me + d, self.n)
                pl.semaphore_signal(bar, inc=1, device_id=(there, self.head), device_id_type=MESH)
            count += self.n - 1
        pl.semaphore_wait(bar, count)


def each(count, step):
    def run(i, carry):
        step(i)
        return carry

    lax.fori_loop(0, count, run, 0)


def row_stats(x):
    mean = jnp.sum(x, axis=1, keepdims=True) / D
    var = jnp.sum(x * x, axis=1, keepdims=True) / D - mean * mean
    return mean, lax.rsqrt(var + norm_eps)


def whole_rows(ref, s):
    return jnp.concatenate([ref[s, 0], ref[s, 1]], axis=1)


def turn(v, cosine, sine):
    parts = []
    for h in range(v.shape[0] // HEAD_DIM):
        a = v[h * 64 : h * 64 + 32]
        b = v[h * 64 + 32 : h * 64 + 64]
        parts += [a * cosine - b * sine, b * cosine + a * sine]
    return jnp.concatenate(parts, axis=0)


def masks(me, length, start, end):
    shape = (length, 2 * length)
    key = lax.broadcasted_iota(jnp.int32, shape, 0)
    row = lax.broadcasted_iota(jnp.int32, shape, 1)
    noisy = row < length
    at = jnp.where(noisy, row, row - length)
    key_block = key >> 4
    row_block = at >> 4
    pos = key + me * length
    same = jnp.logical_and(pos >= start, pos < end)
    clean = jnp.logical_and(same, key_block < row_block + jnp.where(noisy, 0, 1))
    own = jnp.logical_and(same, key_block == row_block)[:, :length]
    return clean, own


class Sum:
    def __init__(self, at, src, res, gx, part, gz, own, xs, xr, zs, zr, cs, cr, fs, fr, ls, ds):
        self.m = at.n // 2
        self.lo = lax.rem(at.me, 2)
        self.hi = lax.div(at.me, 2)
        self.head = at.head
        self.pair = (at.me + 1 - 2 * self.lo, at.head)
        self.src, self.res, self.gx, self.part, self.gz = src, res, gx, part, gz
        self.xs, self.xr, self.zs, self.zr = xs, xr, zs, zr
        self.cs, self.cr, self.fs, self.fr, self.ls, self.ds = cs, cr, fs, fr, ls, ds
        self.pieces = ds.shape[0]
        self.own = own

    def piece(self, half, k):
        size = self.gx.shape[1]
        return half, pl.ds(pl.multiple_of(k * size, 16), size)

    def at_z(self, k):
        return (2 * k + self.lo, self.head)

    def x(self, k):
        return remote(self.src.at[self.piece(1 - self.lo, k)], self.gx.at[k], self.xs.at[k], self.xr.at[k], self.pair)

    def z(self, k):
        return remote(self.part.at[k], self.gz.at[self.hi], self.zs.at[k], self.zr.at[self.hi], self.at_z(k))

    def z_in(self, k):
        return remote(self.part.at[k], self.gz.at[k], self.zs.at[k], self.zr.at[k], self.at_z(k))

    def piece_of(self, k, p):
        size = self.gx.shape[1] // self.pieces
        return pl.ds(p * size, size)

    def c_own(self, p, step):
        rows = self.piece_of(self.hi, p)
        there = self.res.at[self.lo, self.hi, rows]
        sent = self.cs.at[self.hi, p] if step > 0 else self.ds.at[p]
        return remote(self.own.at[rows], there, sent, self.cr.at[self.hi, p], self.at_z(self.hi + step))

    def c_on(self, k, p, step):
        part = self.res.at[self.lo, k, self.piece_of(k, p)]
        return remote(part, part, self.cs.at[k, p], self.cr.at[k, p], self.at_z(self.hi + step))

    def f(self, k, p):
        part = self.res.at[self.lo, k, self.piece_of(k, p)]
        return remote(part, part, self.fs.at[k, p], self.fr.at[k, p], self.pair)

    def f_own(self, p):
        rows = self.piece_of(self.hi, p)
        there = self.res.at[self.lo, self.hi, rows]
        return remote(self.own.at[rows], there, self.fs.at[self.hi, p], self.fr.at[self.hi, p], self.pair)

    def keep(self):
        return pltpu.make_async_copy(self.own, self.res.at[self.lo, self.hi], self.ls)

    def others(self):
        return [lax.rem(self.hi + d, self.m) for d in range(1, self.m)]

    def turn_of(self, i):
        return lax.rem(self.hi + 1 + i, self.m)

    def begin(self):
        each(self.m, lambda i: self.x(self.turn_of(i)).start())

    def pass_on(self, i):
        k = self.turn_of(i)
        self.x(k).wait_recv()
        self.part[k] = (self.src[self.piece(self.lo, k)].astype(F32) + self.gx[k].astype(F32)).astype(BF16)

        @pl.when(k != self.hi)
        def _():
            self.z(k).start()

    def ends(self, step, run):
        there = self.hi + step
        pl.when(jnp.logical_and(there >= 0, there < self.m))(run)

    def reduce(self):
        total = self.part[self.hi].astype(F32)
        for k in self.others():
            self.z_in(k).wait_recv()
            total += self.gz[k].astype(F32)
        self.own[...] = total.astype(BF16)
        self.keep().start()
        for p in range(self.pieces):
            self.ends(1, lambda: self.c_own(p, 1).start())
            self.ends(-1, lambda: self.c_own(p, -1).start())
            self.f_own(p).start()

    def forward(self, d):
        for p in range(self.pieces):
            for step in (1, -1):

                def run():
                    k = self.hi - step * d
                    self.c_on(k, p, step).wait_recv()
                    self.ends(step, lambda: self.c_on(k, p, step).start())
                    self.f(k, p).start()

                self.ends(-step * d, run)

    def finish(self):
        each(self.m, lambda k: self.x(k).wait_send())
        for k in self.others():
            self.z(k).wait_send()
        for p in range(self.pieces):
            for step in (1, -1):
                self.ends(step, lambda: self.c_own(p, step).wait_send())
                for d in range(1, self.m):

                    def run():
                        k = self.hi - step * d
                        self.ends(step, lambda: self.c_on(k, p, step).wait_send())
                        self.f(k, p).wait_send()

                    self.ends(-step * d, run)
            self.f_own(p).wait_send()
            each(self.m, lambda k: self.f(k, p).wait_recv())
        self.keep().wait()


def layer(n, names, *refs):
    r = types.SimpleNamespace(**dict(zip(names, refs)))
    at = Place(n)
    slots, rows, feat = r.x_in.shape
    length = rows // 2
    half = 2 * feat
    hl = feat // HEAD_DIM
    m = n // 2
    core, y, me = at.core, at.y, at.me
    mine = pl.ds(length * core, length)
    other = pl.ds(length * (1 - core), length)
    early, late = slice(0, length), slice(length, rows)
    heads = [slice(h * HEAD_DIM, (h + 1) * HEAD_DIM) for h in range(hl)]
    fulls = (r.xg, r.cg, r.ag)
    owns = (r.x_in, r.c_in, r.own_att)
    lands = (r.land.at[0], r.land.at[1], r.land.at[0])
    quarter = D // m
    sum1 = Sum(
        at, r.gl, r.res1, r.gx1, r.act.at[:m, :quarter], r.gz1, r.own1, *[getattr(r, "u%d" % i) for i in range(10)]
    )
    src2 = r.act.at[m : m + 2, :feat]
    sum2 = Sum(at, src2, r.res2.at[:2], r.gx2, r.pt2, r.gz2, r.own2, *[getattr(r, "v%d" % i) for i in range(10)])
    sum3 = Sum(at, r.src3, r.res2.at[2:], r.gx3, r.pt3, r.gz3, r.own3, *[getattr(r, "w%d" % i) for i in range(10)])

    def sib_copy(k, s):
        return remote(owns[k].at[s], lands[k].at[s], r.ss.at[k, s], r.sr.at[k, s], at.sib)

    def build(k, s):
        a, b = owns[k][s], lands[k][s]

        @pl.when(core == 0)
        def _():
            fulls[k][s, y] = jnp.concatenate([a, b], axis=1)

        @pl.when(core == 1)
        def _():
            fulls[k][s, y] = jnp.concatenate([b, a], axis=1)

    def y_copy(k, s):
        part = fulls[k].at[s, y, mine]
        return remote(part, part, r.ys.at[k, s], r.yr.at[k, s], at.yp)

    def f_copy(k, s):
        part = fulls[k].at[s, 1 - y, mine]
        return remote(part, part, r.fs.at[k, s], r.fr.at[k, s], at.sib)

    def kv_copy(s, i):
        return remote(r.kvo.at[s], r.kvb.at[at.spot(s, me, me)], r.ks.at[s, i], r.kr.at[s, me], (i, at.head))

    def kv_in(s, j):
        return remote(r.kvo.at[s], r.kvb.at[at.spot(s, j, j)], r.ks.at[s, j], r.kr.at[s, j], (j, at.head))

    def dkv_copy(s, j):
        return remote(
            r.kvb.at[at.spot(s, j, j)], r.dla.at[at.spot(s, j, me)], r.ds.at[s, j], r.dr.at[s, me], (j, at.head)
        )

    def dkv_in(s, i):
        here = r.dla.at[at.spot(s, me, i)]
        return remote(here, here, r.ds.at[s, i], r.dr.at[s, i], (i, at.head))

    def readers(s, step):
        for d in range(1, n):
            i = me + d

            @pl.when(jnp.logical_and(i < n, at.lowest(s, i) <= me))
            def _():
                step(i)

    def e_core(s):
        return remote(r.ep.at[s, other], r.er.at[s], r.e1s.at[s], r.e1r.at[s], at.sib)

    def e_y(s):
        return remote(r.er.at[s], r.ey.at[s], r.e2s.at[s], r.e2r.at[s], at.yp)

    def e_back(s):
        return remote(r.ey.at[s], r.eb.at[s], r.e3s.at[s], r.e3r.at[s], at.sib)

    def held(first, s, k):
        return (s, pl.ds(first, length), pl.ds(pl.multiple_of(k * half, 128), half))

    def f_core(s):
        return remote(r.ag.at[s, :, other], r.fc.at[s], r.f1s.at[s], r.f1r.at[s], at.sib)

    def f_y(s):
        return remote(r.upre.at[held(0, s, 1 - y)], r.fy.at[s], r.f2s.at[s], r.f2r.at[s], at.yp)

    def f_back(s):
        return remote(r.osd.at[s], r.out.at[s, core], r.f3s.at[s], r.f3r.at[s], at.sib)

    def b_core(s):
        return remote(r.n2.at[s, other], r.er.at[s], r.a1s.at[s], r.a1r.at[s], at.sib)

    def s_core(s):
        return remote(r.st.at[s, 1 - core], r.sl.at[s], r.b1s.at[s], r.b1r.at[s], at.sib)

    def b_y(s):
        return remote(r.upre.at[held(length, s, 1 - y)], r.bey.at[s], r.a2s.at[s], r.a2r.at[s], at.yp)

    def s_y(s):
        return remote(r.sh.at[s], r.sy.at[s], r.b2s.at[s], r.b2r.at[s], at.yp)

    def b_back(s):
        return remote(r.isd.at[s], r.ig.at[s, core], r.a3s.at[s], r.a3r.at[s], at.sib)

    at.greet([at.sib, at.yp, at.diag], True)
    each(slots, lambda s: sib_copy(0, s).start())
    r.gb_in[...] = jnp.zeros_like(r.gb_in)
    for i, vector in enumerate((r.ga, r.ba, r.gf_in, r.bf_in)):
        r.gb_in[i : i + 1] = vector[...]
    r.gland[at.head] = r.gb_in[...]
    g_copies = [
        remote(r.gb_in, r.gland.at[at.head], r.gs.at[k], r.gr.at[k], d)
        for k, d in enumerate((at.sib, at.yp, at.diag))
    ]
    for copy in g_copies:
        copy.start()

    def first_y(s):
        sib_copy(0, s).wait_recv()
        build(0, s)
        y_copy(0, s).start()

    each(slots, first_y)

    def wo_block(who):
        return r.wog.at[pl.ds(pl.multiple_of(feat * who, 16), feat)]

    wo_sib = remote(r.wo_in, wo_block(at.head), r.ws.at[0], r.wr.at[0], at.sib)
    wo_y = remote(r.wo_in, wo_block(at.head), r.ws.at[1], r.wr.at[1], at.yp)
    wo_f = remote(wo_block(at.yp[1]), wo_block(at.yp[1]), r.ws.at[2], r.wr.at[2], at.sib)
    wo_y.start()
    wo_sib.start()
    each(slots, lambda s: sib_copy(1, s).start())
    r.wog[pl.ds(pl.multiple_of(feat * at.head, 16), feat)] = r.wo_in[...]
    for copy in g_copies:
        copy.wait()
    r.gbf[...] = jnp.concatenate([r.gland[i] for i in range(4)], axis=1)
    r.cos[...] = jnp.concatenate([r.cos_in[...]] * 2, axis=1)
    r.sin[...] = jnp.concatenate([r.sin_in[...]] * 2, axis=1)
    long, most = 0, r.docs[0, 0]
    for i in range(1, slots):
        long = jnp.where(r.docs[i, 0] > most, i, long)
        most = jnp.maximum(r.docs[i, 0], most)
    lane = lax.broadcasted_iota(jnp.int32, (8, rows), 1)
    pos = jnp.where(lane < length, lane, lane - length) + me * length
    for s in range(slots):
        row = long if s == LONG_SLOT else jnp.where(long == s, LONG_SLOT, s)
        end = 0
        first_key, last_key = jnp.zeros_like(pos), jnp.full_like(pos, 2**30)
        for j in range(r.docs.shape[1]):
            end = end + r.docs[row, j]
            first_key = jnp.where(pos >= end, end, first_key)
            last_key = jnp.where(pos < end, jnp.minimum(last_key, end), last_key)
        r.bounds[s] = jnp.where(lax.broadcasted_iota(jnp.int32, (8, rows), 0) == 0, first_key, last_key)
    r.mrow[...] = jnp.zeros_like(r.mrow)
    r.lrow[...] = jnp.ones_like(r.lrow)
    r.og[...] = jnp.zeros_like(r.og)
    r.qq[...] = jnp.zeros_like(r.qq)
    r.qkv[...] = jnp.zeros_like(r.qkv)
    r.gsum[...] = jnp.zeros_like(r.gsum)
    r.gtwo[...] = jnp.zeros_like(r.gtwo)
    r.drow[...] = jnp.zeros_like(r.drow)

    def project(s):
        x = whole_rows(r.xg, s).astype(F32)
        mean, inv = row_stats(x)
        normed = ((x - mean) * inv * r.gbf[0:1] + r.gbf[1:2]).astype(BF16)
        r.n1[s] = normed
        pt = dot(r.w_t[...], normed, 1, 1)
        qk = turn(pt[:half], r.cos[...], r.sin[...])
        r.qt[s] = (qk[:feat] * HEAD_DIM**-0.5).astype(BF16)
        kv = jnp.concatenate([qk[feat:], pt[half:]], axis=0).astype(BF16)
        r.kvn[s] = kv[:, :length]
        r.kvo[s] = kv[:, length:]
        readers(s, lambda i: kv_copy(s, i).start())

    def arrive(t):
        @pl.when(t < slots)
        def _():
            y_copy(0, t).wait_recv()
            f_copy(0, t).start()

        @pl.when(t >= 1)
        def _():
            f_copy(0, t - 1).wait_recv()
            project(t - 1)

    each(slots + 1, arrive)

    def cot_on(s):
        sib_copy(1, s).wait_recv()
        build(1, s)
        y_copy(1, s).start()

    each(2, cot_on)

    def attend(s):
        start, end = r.bounds[s, 0:1], r.bounds[s, 1:2]
        clean, noisy = masks(me, length, start, end)
        kc, kn = r.kvo[s], r.kvn[s]
        q = [r.qt[s, hd] for hd in heads]
        sc = [dot(kc[hd], q[h], 0, 0) for h, hd in enumerate(heads)]
        sn = [dot(kn[hd], q[h][:, :length], 0, 0) for h, hd in enumerate(heads)]
        sc = [jnp.where(clean, v, masked_score) for v in sc]
        sn = [jnp.where(noisy, v, masked_score) for v in sn]
        top = []
        for h in range(hl):
            tc = jnp.max(sc[h], axis=0, keepdims=True)
            tn = jnp.max(sn[h], axis=0, keepdims=True)
            top.append(jnp.concatenate([jnp.maximum(tc[:, :length], tn), tc[:, length:]], axis=1))
        pc = [jnp.exp(sc[h] - top[h]) for h in range(hl)]
        pn = [jnp.exp(sn[h] - top[h][:, :length]) for h in range(hl)]
        oc = [dot(kc[feat:][hd], pc[h].astype(BF16), 1, 0) for h, hd in enumerate(heads)]
        on = [dot(kn[feat:][hd], pn[h].astype(BF16), 1, 0) for h, hd in enumerate(heads)]
        for h, hd in enumerate(heads):
            tc = jnp.sum(pc[h], axis=0, keepdims=True)
            tn = jnp.sum(pn[h], axis=0, keepdims=True)
            r.mrow[h : h + 1] = top[h]
            r.lrow[h : h + 1] = jnp.concatenate([tc[:, :length] + tn, tc[:, length:]], axis=1)
            r.acc[hd, early] = oc[h][:, :length] + on[h]
            r.acc[hd, late] = oc[h][:, length:]

        def one(j, carry):
            kv_in(s, j).wait_recv()
            kv = r.kvb[at.spot(s, j, j)]
            q = [r.qt[s, hd] for hd in heads]
            old = [r.mrow[h : h + 1] for h in range(hl)]
            total = [r.lrow[h : h + 1] for h in range(hl)]
            pos = lax.broadcasted_iota(jnp.int32, (length, rows), 0) + j * length
            allowed = pos >= start
            sc = [dot(kv[hd], q[h], 0, 0) for h, hd in enumerate(heads)]
            sc = [jnp.where(allowed, v, masked_score) for v in sc]
            new = [jnp.maximum(old[h], jnp.max(sc[h], axis=0, keepdims=True)) for h in range(hl)]
            p = [jnp.exp(sc[h] - new[h]) for h in range(hl)]
            add = [dot(kv[feat:][hd], p[h].astype(BF16), 1, 0) for h, hd in enumerate(heads)]
            scale = [jnp.exp(old[h] - new[h]) for h in range(hl)]
            for h, hd in enumerate(heads):
                r.mrow[h : h + 1] = new[h]
                r.lrow[h : h + 1] = total[h] * scale[h] + jnp.sum(p[h], axis=0, keepdims=True)
                r.acc[hd] = r.acc[hd] * scale[h] + add[h]
            return carry

        lax.fori_loop(at.lowest(s, me), me, one, 0)
        for h, hd in enumerate(heads):
            r.att[s, hd] = r.acc[hd] / r.lrow[h : h + 1]
        r.lse[s] = r.mrow[...] + jnp.log(r.lrow[...])
        r.own_att[s] = r.att[s].T.astype(BF16)
        sib_copy(2, s).start()

    def forward(s):
        x = whole_rows(r.xg, s).astype(F32)
        branch = dot(r.ag[s, 0], r.wog[:half], 1, 0) + dot(r.ag[s, 1], r.wog[half:], 1, 0)
        h = x + branch
        for yy in range(2):
            for cc in range(2):

                @pl.when(jnp.logical_and(y == yy, core == cc))
                def _():
                    r.hp[s] = h[cc * length : (cc + 1) * length, yy * half : (yy + 1) * half]

        mean, inv = row_stats(h)
        r.iv[s] = inv
        normed = ((h - mean) * inv * r.gbf[2:3] + r.gbf[3:4]).astype(BF16)
        r.n2[s] = normed
        up = dot(normed, r.wu[...], 1, 0)
        cube = 0.7978845608028654 * (up + 0.044715 * up * up * up)
        t = jnp.tanh(cube)
        r.act[s] = (0.5 * up * (1.0 + t)).astype(BF16)
        slope = 0.5 * (1.0 + t) + 0.5 * up * (1.0 - t * t) * (
            0.7978845608028654 * (1.0 + 3 * 0.044715 * up * up)
        )
        da = dot(whole_rows(r.cg, s), r.wd[...], 1, 1)
        pre = (da * slope).astype(BF16)
        r.upre[s] = pre
        r.ep[s] = dot(pre, r.wu[...], 1, 1).astype(BF16)
        e_core(s).start()

    def stage(t, offset, step):
        s = t - offset

        @pl.when(jnp.logical_and(s >= 0, s < slots))
        def _():
            step(s)

    def att_on(s):
        sib_copy(2, s).wait_recv()
        build(2, s)
        y_copy(2, s).start()

    def att_back(s):
        y_copy(2, s).wait_recv()
        f_copy(2, s).start()

    def cot_back(s):
        y_copy(1, s).wait_recv()
        f_copy(1, s).start()

    def feed(s):
        @pl.when(s == 0)
        def _():
            wo_y.wait_recv()
            wo_f.start()
            wo_sib.wait_recv()
            wo_f.wait_recv()

        f_copy(1, s).wait_recv()
        f_copy(2, s).wait_recv()
        forward(s)

    def e_on(s):
        e_core(s).wait_recv()
        r.er[s] = (r.ep[s, mine].astype(F32) + r.er[s].astype(F32)).astype(BF16)
        e_y(s).start()

    def e_total(s):
        e_y(s).wait_recv()
        r.ey[s] = (r.er[s].astype(F32) + r.ey[s].astype(F32)).astype(BF16)
        e_y(s).wait_send()
        e_back(s).start()

    def loop_one(t):
        stage(t, 1, att_on)

        @pl.when(jnp.logical_and(t >= 1, t < slots - 1))
        def _():
            cot_on(t + 1)

        stage(t, 2, cot_back)
        stage(t, 2, att_back)

        @pl.when(t == slots)
        def _():
            each(slots - 2, e_on)

        @pl.when(t == slots + 1)
        def _():
            e_on(slots - 2)

        stage(t, 0, attend)
        stage(t, 2, feed)

    each(slots + 2, loop_one)

    wide = slots * rows

    def up_tile(i):
        cols = pl.ds(pl.multiple_of(i * 256, 256), 256)
        left = r.n2[...].reshape(wide, D)
        part = dot(left, r.upre[:, :, cols].reshape(wide, 256), 0, 0).astype(BF16)
        r.gl[0, :, cols] = part

    def down_tile(i):
        cols = pl.ds(pl.multiple_of(lax.rem(i, 3) * 128, 128), 128)
        out_cols = pl.ds(pl.multiple_of(i * 128, 128), 128)
        left = r.act[...].reshape(wide, D)
        part = dot(left, r.cg[:, lax.div(i, 3), :, cols].reshape(wide, 128), 0, 0).astype(BF16)
        r.gl[1, :, out_cols] = part

    e_on(slots - 1)
    each(D // 256, up_tile)
    each(D // 128, down_tile)
    sum1.begin()
    e_total(0)
    e_total(1)

    def two_back(s):
        e_back(s).wait_recv()
        e_back(s).wait_send()
        e_core(s).wait_send()

        @pl.when(core == 0)
        def _():
            r.ep[s, early] = r.ey[s]
            r.ep[s, late] = r.eb[s]

        @pl.when(core == 1)
        def _():
            r.ep[s, early] = r.eb[s]
            r.ep[s, late] = r.ey[s]

        e = r.ep[s].astype(F32)
        xh = (r.n2[s].astype(F32) - r.gbf[3:4]) * r.ginv[0:1]
        r.gtwo[2:3] += jnp.sum(e * xh, axis=0, keepdims=True)
        r.gtwo[3:4] += jnp.sum(e, axis=0, keepdims=True)
        g = e * r.gbf[2:3]
        first = jnp.sum(g, axis=1, keepdims=True) / D
        second = jnp.sum(g * xh, axis=1, keepdims=True) / D
        resid = whole_rows(r.cg, s).astype(F32) + r.iv[s] * (g - first - xh * second)
        r.ep[s] = resid.astype(BF16)

    r.ginv[...] = 1.0 / r.gbf[2:3] + jnp.zeros_like(r.ginv)

    def head_grads(s, kv, lanes, allowed):
        q = [r.qt[s, hd, lanes] for hd in heads]
        d_out = [r.do[hd, lanes] for hd in heads]
        sc = [dot(kv[hd], q[h], 0, 0) for h, hd in enumerate(heads)]
        dp = [dot(kv[feat:][hd], d_out[h], 0, 0) for h, hd in enumerate(heads)]
        p = [
            jnp.exp(jnp.where(allowed, sc[h], masked_score) - r.lse[s, h : h + 1, lanes])
            for h in range(hl)
        ]
        ds = [(p[h] * (dp[h] - r.drow[h : h + 1, lanes])).astype(BF16) for h in range(hl)]
        dv = [dot(d_out[h], p[h].astype(BF16), 1, 1) for h in range(hl)]
        dk = [dot(q[h], ds[h], 1, 1) for h in range(hl)]
        dq_add = [dot(kv[hd], ds[h], 1, 0) for h, hd in enumerate(heads)]
        return [jnp.concatenate(v, axis=0) for v in (dq_add, dk, dv)]

    def attend_back(s):
        low_rows = r.ep[s]
        d_out = dot(r.wo_in[...], low_rows, 1, 1).astype(BF16)
        r.do[...] = d_out
        a = r.att[s]
        r.og[...] += dot(a.astype(BF16), low_rows, 1, 0)
        prod = d_out.astype(F32) * a
        for h, hd in enumerate(heads):
            r.drow[h : h + 1] = jnp.sum(prod[hd], axis=0, keepdims=True)
        start, end = r.bounds[s, 0:1], r.bounds[s, 1:2]
        clean, noisy = masks(me, length, start, end)
        dqa, dk, dv = head_grads(s, r.kvo[s], slice(0, rows), clean)
        dqn, dkn, dvn = head_grads(s, r.kvn[s], early, noisy)
        r.acc[...] = dqa
        r.acc[:, early] += dqn
        r.dkv[s, :feat] = dk
        r.dkv[s, feat:] = dv
        r.qp[s, half:, early] = dvn.astype(BF16)
        r.qp[s, feat:half, early] = turn(dkn, r.cos[:, :length], -r.sin[:, :length]).astype(BF16)

        def one(j, carry):
            spot = at.spot(s, j, j)
            kv = r.kvb[spot]
            pos = lax.broadcasted_iota(jnp.int32, (length, rows), 0) + j * length
            dqa, dk, dv = head_grads(s, kv, slice(0, rows), pos >= start)
            r.acc[...] += dqa
            r.kvb[spot, :feat] = dk.astype(BF16)
            r.kvb[spot, feat:] = dv.astype(BF16)
            dkv_copy(s, j).start()
            return carry

        lax.fori_loop(at.lowest(s, me), me, one, 0)
        r.qp[s, :feat] = (turn(r.acc[...], r.cos[...], -r.sin[...]) * HEAD_DIM**-0.5).astype(BF16)
        r.qq[...] += dot(r.qp[s, :feat], r.n1[s], 1, 0)

    def f_start(s):
        y_copy(2, s).wait_send()
        f_copy(2, s).wait_send()
        ff = dot(r.act[s], r.wd[...], 1, 0)
        r.ag[s, 0] = ff[:, :half].astype(BF16)
        r.ag[s, 1] = ff[:, half:].astype(BF16)
        f_core(s).start()

    def f_on(s):
        f_core(s).wait_recv()
        for k in range(2):
            r.upre[held(0, s, k)] = (r.ag[s, k, mine].astype(F32) + r.fc[s, k].astype(F32)).astype(BF16)
        f_y(s).start()

    def f_end(s):
        f_y(s).wait_recv()
        total = r.hp[s] + (r.upre[held(0, s, y)].astype(F32) + r.fy[s].astype(F32))
        turned = total.T.astype(BF16)
        lo, hi = turned[:feat], turned[feat:]

        @pl.when(core == 0)
        def _():
            r.out[s, 0] = lo
            r.osd[s] = hi

        @pl.when(core == 1)
        def _():
            r.out[s, 1] = hi
            r.osd[s] = lo

        f_back(s).start()

    def loop_two(t):
        def run(s):
            two_back(s)
            attend_back(s)

        stage(t, 1, f_on)
        stage(t, -2, e_total)
        stage(t, 0, run)

        @pl.when(jnp.logical_or(t == 3, t == 5))
        def _():
            sum1.pass_on(lax.div(t - 3, 2))

    each(slots, f_start)
    each(slots, loop_two)
    src2[0] = r.og[...].astype(BF16)
    src2[1] = r.qq[...].astype(BF16)
    sum2.begin()
    f_on(slots - 1)
    sum1.pass_on(2)
    sum1.pass_on(3)

    def project_back(s):
        def add(i):
            dkv_in(s, i).wait_recv()
            r.dkv[s] += r.dla[at.spot(s, me, i)].astype(F32)

        readers(s, add)
        total = r.dkv[s]
        r.qp[s, feat:half, late] = turn(total[:feat], r.cos[:, late], -r.sin[:, late]).astype(BF16)
        r.qp[s, half:, late] = total[feat:].astype(BF16)
        pre = r.qp[s]
        r.qkv[...] += dot(pre[feat:], r.n1[s], 1, 0)
        e = dot(pre, r.w_t[...], 0, 0)
        x = whole_rows(r.xg, s).astype(F32)
        mean, inv = row_stats(x)
        xh = (x - mean) * inv
        r.gsum[0:1] += jnp.sum(e * xh, axis=0, keepdims=True)
        r.gsum[1:2] += jnp.sum(e, axis=0, keepdims=True)
        r.n2[s] = e.astype(BF16)
        g = e * r.gbf[0:1]
        one_sum = jnp.sum(g, axis=1, keepdims=True)
        two_sum = jnp.sum(g * xh, axis=1, keepdims=True)
        lane = lax.broadcasted_iota(jnp.int32, (rows, 128), 1)
        packed = jnp.where(lane == 0, one_sum, jnp.where(lane == 1, two_sum, 0.0)).T
        r.st[s, 0] = packed[:8, :length]
        r.st[s, 1] = packed[:8, length:]
        b_core(s).start()
        s_core(s).start()

    def b_on(s):
        b_core(s).wait_recv()
        s_core(s).wait_recv()
        both = r.n2[s, mine].astype(F32) + r.er[s].astype(F32)
        r.upre[s, late] = both.astype(BF16)
        r.sh[s] = r.st[s, core] + r.sl[s]
        b_y(s).start()
        s_y(s).start()

    def b_end(s):
        b_y(s).wait_recv()
        s_y(s).wait_recv()
        e = r.upre[held(length, s, y)].astype(F32) + r.bey[s].astype(F32)
        sums = r.sh[s] + r.sy[s]
        cols = jnp.concatenate([sums, jnp.zeros((120, length), F32)], axis=0).T
        first, second = cols[:, 0:1] / D, cols[:, 1:2] / D
        x = jnp.concatenate([r.xg[s, 0, mine], r.xg[s, 1, mine]], axis=1).astype(F32)
        mean, inv = row_stats(x)
        xh = (r.xg[s, y, mine].astype(F32) - mean) * inv
        gain = jnp.where(y == 0, r.gbf[0:1, :half], r.gbf[0:1, half:])
        resid = r.ep[s, mine].astype(F32)
        resid = jnp.where(y == 0, resid[:, :half], resid[:, half:])
        grad = resid + inv * (e * gain - first - xh * second)
        turned = grad.T
        lo, hi = turned[:feat], turned[feat:]

        @pl.when(core == 0)
        def _():
            r.ig[s, 0] = lo
            r.isd[s] = hi

        @pl.when(core == 1)
        def _():
            r.ig[s, 1] = hi
            r.isd[s] = lo

        b_back(s).start()

    def loop_three(t):
        stage(t, 0, f_end)
        stage(t, 1, b_on)
        stage(t, 0, project_back)

        pl.when(t == 2)(sum1.reduce)

        @pl.when(jnp.logical_or(t == 3, t == 4))
        def _():
            sum2.pass_on(2 * t - 6)
            sum2.pass_on(2 * t - 5)

    each(slots, loop_three)
    grads = r.qkv[...].astype(BF16)
    r.src3[0] = grads[:feat]
    r.src3[1] = grads[feat:]
    sum3.begin()
    b_on(slots - 1)
    h_copies = [
        remote(r.gsum, r.gh.at[k], r.hs.at[k], r.hr.at[k], d)
        for k, d in enumerate((at.sib, at.yp, at.diag))
    ]
    for copy in h_copies:
        copy.start()
    sum2.reduce()

    def share(i):
        return remote(r.gf, r.gq.at[me], r.qs.at[i], r.qr.at[me], (i, at.head))

    def share_in(i):
        return remote(r.gf, r.gq.at[i], r.qs.at[i], r.qr.at[i], (i, at.head))

    def gains_on():
        for copy in h_copies:
            copy.wait()
        total = r.gsum[...] + r.gh[0] + r.gh[1] + r.gh[2] + r.gtwo[...]
        for h in range(4):

            @pl.when(at.head == h)
            def _():
                r.gf[...] = total[:, h * feat : (h + 1) * feat]

        r.gq[me] = r.gf[...]
        for d in range(1, n):
            share(lax.rem(me + d, n)).start()

    def loop_four(t):
        stage(t, 0, b_end)
        pl.when(t == 0)(gains_on)

        @pl.when(jnp.logical_or(t == 1, t >= 4))
        def _():
            sum1.forward(jnp.where(t == 1, 1, t - 2))

        @pl.when(jnp.logical_or(t == 2, t == 3))
        def _():
            sum3.pass_on(2 * t - 4)
            sum3.pass_on(2 * t - 3)

    each(slots, loop_four)
    sum3.reduce()
    for d in range(1, n):
        share_in(lax.rem(me + d, n)).wait_recv()
    r.gains[...] = jnp.sum(r.gq[...], axis=0)
    for d in range(1, m):
        sum2.forward(d)
    for d in range(1, m):
        sum3.forward(d)

    def finish(s):
        for k in range(3):
            sib_copy(k, s).wait_send()
        for k in range(2):
            y_copy(k, s).wait_send()
            f_copy(k, s).wait_send()
        readers(s, lambda i: kv_copy(s, i).wait_send())
        f_core(s).wait_send()
        f_y(s).wait_send()
        f_back(s).wait()
        b_core(s).wait_send()
        s_core(s).wait_send()
        b_y(s).wait_send()
        s_y(s).wait_send()
        b_back(s).wait()

        def sent(j, carry):
            dkv_copy(s, j).wait_send()
            return carry

        lax.fori_loop(at.lowest(s, me), me, sent, 0)

    each(slots, finish)
    wo_sib.wait_send()
    wo_y.wait_send()
    wo_f.wait_send()
    for part in (sum1, sum2, sum3):
        part.finish()
    for d in range(1, n):
        share(lax.rem(me + d, n)).wait_send()


def body(
    inputs,
    doc_lengths,
    attn_gain,
    attn_bias,
    w_qkv,
    w_out,
    ffn_gain,
    ffn_bias,
    w_up,
    w_down,
    cotangent,
):
    n = lax.axis_size("seq")
    slots, _, length, feat = inputs.shape
    rows, half, m = 2 * length, 2 * feat, n // 2
    held = slots * n * half * length * 2
    if held > ROWS_LIMIT or m != 4:
        return gathered_body(
            inputs, doc_lengths, attn_gain, attn_bias, w_qkv, w_out, ffn_gain, ffn_bias, w_up, w_down, cotangent
        )
    me = lax.axis_index("seq")
    long = jnp.argmax(doc_lengths[:, 0]).astype(jnp.int32)
    ids = jnp.arange(slots, dtype=jnp.int32)

    def swap(v):
        pick = lax.dynamic_index_in_dim(v, long, 0, keepdims=True)
        where = ids.reshape((slots,) + (1,) * (v.ndim - 1))
        kept = v[LONG_SLOT : LONG_SLOT + 1]
        return jnp.where(where == LONG_SLOT, pick, jnp.where(where == long, kept, v))

    positions = me * length + jnp.arange(length, dtype=jnp.int32)
    half_dim = HEAD_DIM // 2
    freqs = rotary_base ** (-jnp.arange(half_dim, dtype=F32) / half_dim)
    angles = freqs[:, None] * positions.astype(F32)[None, :]
    w_t = w_qkv.reshape(D, 3 * feat).T
    operands = dict(
        x_in=swap(inputs).reshape(slots, rows, feat), c_in=swap(cotangent).reshape(slots, rows, feat),
        ga=attn_gain[None], ba=attn_bias[None], gf_in=ffn_gain[None], bf_in=ffn_bias[None],
        w_t=w_t, wo_in=w_out, wu=w_up, wd=w_down, cos_in=jnp.cos(angles), sin_in=jnp.sin(angles), docs=doc_lengths,
    )
    small = (m, feat // m, D)
    quarter = (m, D // m, D)
    outs = dict(
        out=((slots, 2, feat, length), BF16), ig=((slots, 2, feat, length), F32), res1=((2, *quarter), BF16),
        res2=((4, *small), BF16), gains=((8, feat), F32),
    )
    blocks = n + (slots - 1) * (n // 2 + max(1, n // 8))
    full, wide = (slots, 2, rows, half), (slots, rows, D)
    part, stat = (slots, length, D), (slots, 8, length)
    halves, own_half = (slots, 2, length, half), (slots, length, half)
    buffers = dict(
        land=((2, slots, rows, feat), BF16), own_att=((slots, rows, feat), BF16), gland=((4, 8, feat), F32),
        gbf=((8, D), F32), ginv=((8, D), F32), xg=(full, BF16), cg=(full, BF16), ag=(full, BF16),
        wog=((D, D), BF16), n1=(wide, BF16), qt=((slots, feat, rows), BF16),
        kvn=((slots, half, length), BF16), kvo=((slots, half, length), BF16), kvb=((blocks, half, length), BF16),
        att=((slots, feat, rows), F32), lse=((slots, 8, rows), F32), acc=((feat, rows), F32),
        mrow=((8, rows), F32), lrow=((8, rows), F32), hp=(own_half, F32), iv=((slots, rows, 1), F32),
        n2=(wide, BF16), act=(wide, BF16), upre=(wide, BF16), ep=(wide, BF16), er=(part, BF16), ey=(part, BF16),
        eb=(part, BF16), fc=(halves, BF16), fy=(own_half, BF16),
        osd=((slots, feat, length), BF16), gl=((2, D, D), BF16), gx1=(quarter, BF16), gz1=(quarter, BF16),
        own1=(quarter[1:], BF16), do=((feat, rows), BF16), drow=((8, rows), F32),
        dkv=((slots, half, length), F32), dla=((blocks, half, length), BF16), qp=((slots, 3 * feat, rows), BF16),
        og=((feat, D), F32), qq=((feat, D), F32), qkv=((half, D), F32), gsum=((8, D), F32), gtwo=((8, D), F32),
        st=((slots, 2, 8, length), F32), sl=(stat, F32), sh=(stat, F32), sy=(stat, F32),
        bey=(own_half, BF16), isd=((slots, feat, length), F32), src3=((2, feat, D), BF16),
        gx2=(small, BF16), pt2=(small, BF16), gz2=(small, BF16), own2=(small[1:], BF16),
        gx3=(small, BF16), pt3=(small, BF16), gz3=(small, BF16), own3=(small[1:], BF16),
        gb_in=((8, feat), F32), cos=((half_dim, rows), F32), sin=((half_dim, rows), F32),
        bounds=((slots, 8, rows), jnp.int32), gh=((3, 8, D), F32), gq=((n, 8, feat), F32), gf=((8, feat), F32),
    )
    sems = {k: (3, slots) for k in ("ss", "sr", "ys", "yr", "fs", "fr")}
    sems |= {k: (3,) for k in ("gs", "gr", "ws", "wr", "hs", "hr")}
    sems |= {k: (slots, n) for k in ("ks", "kr", "ds", "dr")}
    sems |= {k + i + e: (slots,) for k in "efab" for i in "123" for e in "sr" if k + i != "b3"}
    sems |= {"qs": (n,), "qr": (n,)}
    pieces = {"u": 2, "v": 1, "w": 1}
    sems |= {"%s%d" % (k, i): (m,) for k in "uvw" for i in range(4)}
    sems |= {"%s%d" % (k, i): (m, pieces[k]) for k in "uvw" for i in range(4, 8)}
    sems |= {k + "9": (pieces[k],) for k in "uvw"}
    sem = pltpu.SemaphoreType.DMA
    scratch = {k: VMEM(*v) for k, v in buffers.items()}
    scratch |= {k: sem(v) for k, v in sems.items()}
    scratch |= {k + "8": sem for k in "uvw"}
    vmem = pl.BlockSpec(memory_space=VMEM)
    names = [*operands, *outs, *scratch]
    got = pl.pallas_call(
        functools.partial(layer, n, names),
        out_shape=[jax.ShapeDtypeStruct(*v) for v in outs.values()],
        in_specs=[pl.BlockSpec(memory_space=pltpu.SMEM) if k == "docs" else vmem for k in operands],
        out_specs=[pl.BlockSpec(memory_space=pl.ANY) if k.startswith("res") else vmem for k in outs],
        scratch_shapes=list(scratch.values()),
        compiler_params=pltpu.CompilerParams(
            collective_id=0, has_side_effects=True, vmem_limit_bytes=VMEM_LIMIT
        ),
        name="layer",
    )(*operands.values())
    outputs, input_grad, res1, res2, gain_grads = got
    up_grad, down_grad = res1.reshape(2, D, D).astype(F32)
    small_grads = res2.reshape(4, feat, D)
    out_grad = small_grads[0].astype(F32)
    qkv_grad = small_grads[1:].astype(F32)
    return (
        jnp.swapaxes(swap(outputs), 2, 3),
        jnp.swapaxes(swap(input_grad), 2, 3),
        jnp.transpose(qkv_grad, (2, 0, 1)),
        out_grad,
        up_grad,
        down_grad,
        gain_grads[0],
        gain_grads[1],
        gain_grads[2],
        gain_grads[3],
    )


def solution(mesh):
    in_specs = (
        P(None, None, "seq", "head"),
        P(),
        P("head"),
        P("head"),
        P(None, None, "head"),
        P("head", None),
        P("head"),
        P("head"),
        P(None, "head"),
        P("head", None),
        P(None, None, "seq", "head"),
    )
    out_specs = (
        P(None, None, "seq", "head"),
        P(None, None, "seq", "head"),
        P(None, None, "head"),
        P("head", None),
        P(None, "head"),
        P("head", None),
        P("head"),
        P("head"),
        P("head"),
        P("head"),
    )
    return jax.shard_map(body, mesh=mesh, in_specs=in_specs, out_specs=out_specs, check_vma=False)
```

```python
import functools
import types

import jax
import jax.numpy as jnp
from jax import lax
from jax.experimental import pallas as pl
from jax.experimental.pallas import tpu as pltpu
from jax.sharding import PartitionSpec as P

D = 768
HEAD_DIM = 64
BLOCK = 16


norm_eps = 1e-05
masked_score = -1e30
rotary_base = 10000.0

MESH = pl.DeviceIdType.MESH
VMEM = pltpu.VMEM
F32 = jnp.float32
BF16 = jnp.bfloat16
ROWS_LIMIT = 16 << 20
VMEM_LIMIT = 63 << 20
LONG_SLOT = 3


def passed_along(block, axis, distance):
    devices = range(lax.axis_size(axis))
    route = [(i - distance, i) for i in devices if i - distance in devices]
    return lax.ppermute(block, axis, route)


def from_behind(x, axis, by):
    devices = lax.axis_size(axis)
    return lax.ppermute(x, axis, [(i, (i + by) % devices) for i in range(devices)])


def segment_ids(doc_lengths, positions):
    doc_ends = jnp.cumsum(doc_lengths, axis=1)
    return jnp.sum((doc_ends[:, :, None] <= positions[None, None, :]).astype(jnp.int32), axis=1)


def rotate(values, positions, sign):
    half_dim = values.shape[-1] // 2
    freqs = rotary_base ** (-jnp.arange(half_dim, dtype=jnp.float32) / half_dim)
    angles = positions.astype(jnp.float32)[:, None, None] * freqs
    cosine = jnp.cos(angles)
    sine = sign * jnp.sin(angles)
    first_half = values[..., :half_dim]
    second_half = values[..., half_dim:]
    return jnp.concatenate(
        [first_half * cosine - second_half * sine, second_half * cosine + first_half * sine],
        axis=-1,
    )


def row_pair(first_sum, second_sum):
    return lax.psum((first_sum, second_sum), "head")


def normalize(share, gain, bias):
    row_total, row_square = row_pair(jnp.sum(share, axis=-1), jnp.sum(share * share, axis=-1))
    mean_value = row_total / D
    inv_std = lax.rsqrt(row_square / D - mean_value * mean_value + norm_eps)
    centered = (share - mean_value[..., None]) * inv_std[..., None]
    scaled = (centered * gain + bias).astype(jnp.bfloat16)
    gathered = lax.all_gather(scaled, "head", axis=3, tiled=True)
    return (gathered, centered, inv_std)


def norm_backward(partial_value, gain, centered, inv_std):
    share = lax.psum_scatter(partial_value, "head", scatter_dimension=3, tiled=True)
    scaled = share * gain
    first_mean, second_mean = row_pair(
        jnp.sum(scaled, axis=-1), jnp.sum(scaled * centered, axis=-1)
    )
    grad_in = inv_std[..., None] * (
        scaled - first_mean[..., None] / D - centered * (second_mean[..., None] / D)
    )
    gain_grad = jnp.sum(share * centered, axis=(0, 1, 2))
    bias_grad = jnp.sum(share, axis=(0, 1, 2))
    return (grad_in, gain_grad, bias_grad)


def branch_total(partial_value):
    return lax.psum_scatter(partial_value, "head", scatter_dimension=3, tiled=True)


def gradient_rows(share):
    return lax.all_gather(share, "head", axis=3, tiled=True)


def mask_rule(query_pos, query_seg, key_pos, key_seg):
    query_block = (query_pos // BLOCK)[:, None]
    key_block = (key_pos // BLOCK)[None, :]
    order = jnp.stack([key_block < query_block, key_block <= query_block])
    same_doc = query_seg[:, :, None] == key_seg[:, None, :]
    return jnp.logical_and(order[None, :, None], same_doc[:, None, None])


def absorb(state_now, scores, allowed, value_piece):
    run_max, run_sum, run_acc = state_now
    masked = jnp.where(allowed, scores, masked_score)
    new_max = jnp.maximum(run_max, jnp.max(masked, axis=-1))
    weights_now = jnp.where(allowed, jnp.exp(masked - new_max[..., None]), 0.0)
    factor = jnp.exp(run_max - new_max)
    new_sum = run_sum * factor + jnp.sum(weights_now, axis=-1)
    added = jnp.einsum(
        "schlk,skhd->schld",
        weights_now,
        value_piece.astype(jnp.float32),
        precision=lax.Precision.HIGHEST,
    )
    return (new_max, new_sum, run_acc * factor[..., None] + added)


def gathered_body(
    inputs,
    doc_lengths,
    attn_gain,
    attn_bias,
    w_qkv,
    w_out,
    ffn_gain,
    ffn_bias,
    w_up,
    w_down,
    cotangent,
):
    seqs_here, _, local_len, _ = inputs.shape
    head_local = w_qkv.shape[2] // HEAD_DIM
    first_pos = lax.axis_index("seq") * local_len
    positions = first_pos + jnp.arange(local_len, dtype=jnp.int32)
    segments = segment_ids(doc_lengths, positions)
    inputs_wide = inputs.astype(jnp.float32)
    normed_one, centered_one, inv_one = normalize(inputs_wide, attn_gain, attn_bias)
    projected = jnp.einsum("scld,dtk->scltk", normed_one, w_qkv, preferred_element_type=jnp.float32)
    split_rows = projected.reshape(seqs_here, 2, local_len, 3, head_local, HEAD_DIM)
    queries = (rotate(split_rows[:, :, :, 0], positions, 1.0) * HEAD_DIM ** (-0.5)).astype(
        jnp.bfloat16
    )
    key_rows = rotate(split_rows[:, :, :, 1], positions, 1.0).astype(jnp.bfloat16)
    value_rows = split_rows[:, :, :, 2].astype(jnp.bfloat16)
    clean_keys = key_rows[:, 1].reshape(seqs_here, local_len, head_local * HEAD_DIM)
    clean_values = value_rows[:, 1].reshape(seqs_here, local_len, head_local * HEAD_DIM)
    block_ids = positions // BLOCK
    own_allowed = jnp.logical_and(
        (block_ids[:, None] == block_ids[None, :])[None],
        segments[:, :, None] == segments[:, None, :],
    )[:, None, None]
    noisy_scores = jnp.einsum(
        "sclhd,skhd->schlk", queries[:, :1], key_rows[:, 0], preferred_element_type=jnp.float32
    )
    half_shape = (seqs_here, 1, head_local, local_len)
    empty_state = (
        jnp.full(half_shape, masked_score, jnp.float32),
        jnp.zeros(half_shape, jnp.float32),
        jnp.zeros(half_shape + (HEAD_DIM,), jnp.float32),
    )
    noisy_state = absorb(empty_state, noisy_scores, own_allowed, value_rows[:, 0])
    start_state = jax.tree.map(
        lambda first, second: jnp.concatenate([first, second], axis=1), noisy_state, empty_state
    )
    piece_keys = lax.all_gather(clean_keys, "seq", axis=1, tiled=True)
    piece_values = lax.all_gather(clean_values, "seq", axis=1, tiled=True)
    piece_len = piece_keys.shape[1]
    key_pos = jnp.arange(piece_len, dtype=jnp.int32)
    key_seg = segment_ids(doc_lengths, key_pos)
    key_heads = piece_keys.reshape(seqs_here, piece_len, head_local, HEAD_DIM)
    value_heads = piece_values.reshape(seqs_here, piece_len, head_local, HEAD_DIM)
    scores = jnp.einsum("sclhd,skhd->schlk", queries, key_heads, preferred_element_type=jnp.float32)
    final_max, final_sum, final_acc = absorb(
        start_state, scores, mask_rule(positions, segments, key_pos, key_seg), value_heads
    )
    attended = final_acc / final_sum[..., None]
    log_total = final_max + jnp.log(final_sum)
    attended_low = attended.astype(jnp.bfloat16)
    out_heads = w_out.reshape(head_local, HEAD_DIM, w_out.shape[1])
    attn_share = branch_total(
        jnp.einsum("schld,hdm->sclm", attended_low, out_heads, preferred_element_type=jnp.float32)
    )
    hidden_res = inputs_wide + attn_share
    normed_two, centered_two, inv_two = normalize(hidden_res, ffn_gain, ffn_bias)
    up_value = jnp.einsum("scld,df->sclf", normed_two, w_up, preferred_element_type=jnp.float32)
    activated, gelu_back = jax.vjp(lambda inner: jax.nn.gelu(inner, approximate=True), up_value)
    act_low = activated.astype(jnp.bfloat16)
    ffn_share = branch_total(
        jnp.einsum("sclf,fm->sclm", act_low, w_down, preferred_element_type=jnp.float32)
    )
    outputs = (hidden_res + ffn_share).astype(jnp.bfloat16)
    grad_out = cotangent.astype(jnp.float32)
    grad_full = gradient_rows(cotangent)
    down_grad = jnp.einsum("sclf,sclm->fm", act_low, grad_full, preferred_element_type=jnp.float32)
    act_grad = jnp.einsum("sclm,fm->sclf", grad_full, w_down, preferred_element_type=jnp.float32)
    up_pre_grad = gelu_back(act_grad)[0].astype(jnp.bfloat16)
    up_grad = jnp.einsum(
        "scld,sclf->df", normed_two, up_pre_grad, preferred_element_type=jnp.float32
    )
    normed_two_grad = jnp.einsum(
        "sclf,df->scld", up_pre_grad, w_up, preferred_element_type=jnp.float32
    )
    back_two, ffn_gain_grad, ffn_bias_grad = norm_backward(
        normed_two_grad, ffn_gain, centered_two, inv_two
    )
    resid_grad = grad_out + back_two
    resid_full = gradient_rows(resid_grad.astype(jnp.bfloat16))
    out_grad = jnp.einsum(
        "schld,sclm->hdm", attended_low, resid_full, preferred_element_type=jnp.float32
    ).reshape(w_out.shape)
    attended_grad = jnp.einsum(
        "sclm,hdm->schld", resid_full, out_heads, preferred_element_type=jnp.float32
    ).astype(jnp.bfloat16)
    grad_wide = attended_grad.astype(jnp.float32)
    row_delta = jnp.sum(grad_wide * attended, axis=-1)
    noisy_probs = jnp.where(own_allowed, jnp.exp(noisy_scores - log_total[:, :1, :, :, None]), 0.0)
    noisy_prob_grad = jnp.einsum(
        "schld,skhd->schlk",
        attended_grad[:, :1],
        value_rows[:, 0],
        preferred_element_type=jnp.float32,
    )
    noisy_score_grad = (noisy_probs * (noisy_prob_grad - row_delta[:, :1, :, :, None])).astype(
        jnp.bfloat16
    )
    noisy_query_grad = jnp.einsum(
        "schlk,skhd->schld", noisy_score_grad, key_rows[:, 0], preferred_element_type=jnp.float32
    )
    noisy_key_grad = jnp.einsum(
        "schlk,sclhd->skhd", noisy_score_grad, queries[:, :1], preferred_element_type=jnp.float32
    )
    noisy_value_grad = jnp.einsum(
        "schlk,schld->skhd", noisy_probs, grad_wide[:, :1], precision=lax.Precision.HIGHEST
    )
    query_start = jnp.concatenate([noisy_query_grad, jnp.zeros_like(noisy_query_grad)], axis=1)
    flat_zero = jnp.zeros((seqs_here, local_len, head_local * HEAD_DIM), jnp.float32)

    def piece_grads(piece_keys, piece_values, first_row, query_total):
        key_pos = first_row + jnp.arange(local_len, dtype=jnp.int32)
        key_seg = segment_ids(doc_lengths, key_pos)
        key_heads = piece_keys.reshape(seqs_here, local_len, head_local, HEAD_DIM)
        value_heads = piece_values.reshape(seqs_here, local_len, head_local, HEAD_DIM)
        scores = jnp.einsum(
            "sclhd,skhd->schlk", queries, key_heads, preferred_element_type=jnp.float32
        )
        allowed = mask_rule(positions, segments, key_pos, key_seg)
        weights_now = jnp.where(allowed, jnp.exp(scores - log_total[..., None]), 0.0)
        prob_grad = jnp.einsum(
            "schld,skhd->schlk", attended_grad, value_heads, preferred_element_type=jnp.float32
        )
        score_grad = (weights_now * (prob_grad - row_delta[..., None])).astype(jnp.bfloat16)
        query_out = query_total + jnp.einsum(
            "schlk,skhd->schld", score_grad, key_heads, preferred_element_type=jnp.float32
        )
        key_part = jnp.einsum(
            "schlk,sclhd->skhd", score_grad, queries, preferred_element_type=jnp.float32
        )
        value_part = jnp.einsum(
            "schlk,schld->skhd", weights_now, grad_wide, precision=lax.Precision.HIGHEST
        )
        return (key_part.reshape(flat_zero.shape), value_part.reshape(flat_zero.shape), query_out)

    def cycle_body(cycle_step, carried):
        piece_keys, piece_values, key_acc, value_acc, query_acc = carried
        source = (lax.axis_index("seq") - cycle_step) % lax.axis_size("seq")
        first_row = source * local_len
        key_part, value_part, query_acc = piece_grads(
            piece_keys, piece_values, first_row, query_acc
        )
        key_acc = key_acc + key_part
        value_acc = value_acc + value_part
        piece_keys, piece_values = passed_along((piece_keys, piece_values), "seq", 1)
        key_acc, value_acc = (
            from_behind(key_acc.astype(jnp.bfloat16), "seq", 1).astype(key_acc.dtype),
            from_behind(value_acc.astype(jnp.bfloat16), "seq", 1).astype(value_acc.dtype),
        )
        return (piece_keys, piece_values, key_acc, value_acc, query_acc)

    cycle_start = (clean_keys, clean_values, flat_zero, flat_zero, query_start)
    _, _, clean_key_grad, clean_value_grad, query_acc = lax.fori_loop(
        0, lax.axis_size("seq"), cycle_body, cycle_start
    )
    head_shape = (seqs_here, local_len, head_local, HEAD_DIM)
    query_total = rotate(jnp.transpose(query_acc, (0, 1, 3, 2, 4)), positions, -1.0) * HEAD_DIM ** (
        -0.5
    )
    key_total = rotate(
        jnp.stack([noisy_key_grad, clean_key_grad.reshape(head_shape)], axis=1), positions, -1.0
    )
    value_total = jnp.stack([noisy_value_grad, clean_value_grad.reshape(head_shape)], axis=1)
    qkv_pre_grad = (
        jnp.stack([query_total, key_total, value_total], axis=3)
        .reshape(seqs_here, 2, local_len, 3, head_local * HEAD_DIM)
        .astype(jnp.bfloat16)
    )
    qkv_grad = jnp.einsum(
        "scld,scltk->dtk", normed_one, qkv_pre_grad, preferred_element_type=jnp.float32
    )
    normed_one_grad = jnp.einsum(
        "scltk,dtk->scld", qkv_pre_grad, w_qkv, preferred_element_type=jnp.float32
    )
    back_one, attn_gain_grad, attn_bias_grad = norm_backward(
        normed_one_grad, attn_gain, centered_one, inv_one
    )
    input_grad = resid_grad + back_one
    (
        qkv_grad,
        out_grad,
        up_grad,
        down_grad,
        attn_gain_grad,
        attn_bias_grad,
        ffn_gain_grad,
        ffn_bias_grad,
    ) = lax.psum(
        (
            qkv_grad,
            out_grad,
            up_grad,
            down_grad,
            attn_gain_grad,
            attn_bias_grad,
            ffn_gain_grad,
            ffn_bias_grad,
        ),
        "seq",
    )
    return (
        outputs,
        input_grad,
        qkv_grad,
        out_grad,
        up_grad,
        down_grad,
        attn_gain_grad,
        attn_bias_grad,
        ffn_gain_grad,
        ffn_bias_grad,
    )


def dot(a, b, ca, cb):
    return lax.dot_general(a, b, (((ca,), (cb,)), ((), ())), preferred_element_type=F32)


def remote(src, dst, send, recv, device):
    return pltpu.make_async_remote_copy(
        src_ref=src, dst_ref=dst, send_sem=send, recv_sem=recv, device_id=device, device_id_type=MESH
    )


class Place:
    def __init__(self, n):
        self.n = n
        self.me = lax.axis_index("seq")
        self.head = lax.axis_index("head")
        self.core = lax.rem(self.head, 2)
        self.y = lax.div(self.head, 2)
        self.sib = (self.me, self.y * 2 + 1 - self.core)
        self.yp = (self.me, (1 - self.y) * 2 + self.core)
        self.diag = (self.me, (1 - self.y) * 2 + 1 - self.core)
        self.half = n // 2
        self.band = max(1, n // 8)

    def lowest(self, slot, i):
        near = i - self.band
        short = jnp.where(i >= self.half, jnp.minimum(near, self.half), near)
        return jnp.where(slot == LONG_SLOT, 0, jnp.maximum(short, 0))

    def spot(self, slot, block, other):
        window = self.half + self.band
        near = self.half + lax.rem(other, self.band)
        late = jnp.where(block >= self.half, other - self.half, near)
        order = slot - jnp.where(slot > LONG_SLOT, 1, 0)
        return jnp.where(slot == LONG_SLOT, other, self.n + order * window + late)

    def spots(self, slots):
        return self.n + (slots - 1) * (self.half + self.band)

    def greet(self, near, everyone):
        bar = pltpu.get_barrier_semaphore()
        for d in near:
            pl.semaphore_signal(bar, inc=1, device_id=d, device_id_type=MESH)
        count = len(near)
        if everyone:
            for d in range(1, self.n):
                there = lax.rem(self.me + d, self.n)
                pl.semaphore_signal(bar, inc=1, device_id=(there, self.head), device_id_type=MESH)
            count += self.n - 1
        pl.semaphore_wait(bar, count)


def each(count, step):
    def run(i, carry):
        step(i)
        return carry

    lax.fori_loop(0, count, run, 0)


def row_stats(x):
    mean = jnp.sum(x, axis=1, keepdims=True) / D
    var = jnp.sum(x * x, axis=1, keepdims=True) / D - mean * mean
    return mean, lax.rsqrt(var + norm_eps)


def whole_rows(ref, s):
    return jnp.concatenate([ref[s, 0], ref[s, 1]], axis=1)


def turn(v, cosine, sine):
    parts = []
    for h in range(v.shape[0] // HEAD_DIM):
        a = v[h * 64 : h * 64 + 32]
        b = v[h * 64 + 32 : h * 64 + 64]
        parts += [a * cosine - b * sine, b * cosine + a * sine]
    return jnp.concatenate(parts, axis=0)


def masks(me, length, start, end):
    shape = (length, 2 * length)
    key = lax.broadcasted_iota(jnp.int32, shape, 0)
    row = lax.broadcasted_iota(jnp.int32, shape, 1)
    noisy = row < length
    at = jnp.where(noisy, row, row - length)
    key_block = key >> 4
    row_block = at >> 4
    pos = key + me * length
    same = jnp.logical_and(pos >= start, pos < end)
    clean = jnp.logical_and(same, key_block < row_block + jnp.where(noisy, 0, 1))
    own = jnp.logical_and(same, key_block == row_block)[:, :length]
    return clean, own


class Sum:
    def __init__(self, at, src, res, gx, part, gz, own, xs, xr, zs, zr, cs, cr, fs, fr, ls, ds):
        self.m = at.n // 2
        self.lo = lax.rem(at.me, 2)
        self.hi = lax.div(at.me, 2)
        self.head = at.head
        self.pair = (at.me + 1 - 2 * self.lo, at.head)
        self.src, self.res, self.gx, self.part, self.gz = src, res, gx, part, gz
        self.xs, self.xr, self.zs, self.zr = xs, xr, zs, zr
        self.cs, self.cr, self.fs, self.fr, self.ls, self.ds = cs, cr, fs, fr, ls, ds
        self.pieces = ds.shape[0]
        self.own = own

    def piece(self, half, k):
        size = self.gx.shape[1]
        return half, pl.ds(pl.multiple_of(k * size, 16), size)

    def at_z(self, k):
        return (2 * k + self.lo, self.head)

    def x(self, k):
        return remote(self.src.at[self.piece(1 - self.lo, k)], self.gx.at[k], self.xs.at[k], self.xr.at[k], self.pair)

    def z(self, k):
        return remote(self.part.at[k], self.gz.at[self.hi], self.zs.at[k], self.zr.at[self.hi], self.at_z(k))

    def z_in(self, k):
        return remote(self.part.at[k], self.gz.at[k], self.zs.at[k], self.zr.at[k], self.at_z(k))

    def piece_of(self, k, p):
        size = self.gx.shape[1] // self.pieces
        return pl.ds(p * size, size)

    def c_own(self, p, step):
        rows = self.piece_of(self.hi, p)
        there = self.res.at[self.lo, self.hi, rows]
        sent = self.cs.at[self.hi, p] if step > 0 else self.ds.at[p]
        return remote(self.own.at[rows], there, sent, self.cr.at[self.hi, p], self.at_z(self.hi + step))

    def c_on(self, k, p, step):
        part = self.res.at[self.lo, k, self.piece_of(k, p)]
        return remote(part, part, self.cs.at[k, p], self.cr.at[k, p], self.at_z(self.hi + step))

    def f(self, k, p):
        part = self.res.at[self.lo, k, self.piece_of(k, p)]
        return remote(part, part, self.fs.at[k, p], self.fr.at[k, p], self.pair)

    def f_own(self, p):
        rows = self.piece_of(self.hi, p)
        there = self.res.at[self.lo, self.hi, rows]
        return remote(self.own.at[rows], there, self.fs.at[self.hi, p], self.fr.at[self.hi, p], self.pair)

    def keep(self):
        return pltpu.make_async_copy(self.own, self.res.at[self.lo, self.hi], self.ls)

    def others(self):
        return [lax.rem(self.hi + d, self.m) for d in range(1, self.m)]

    def turn_of(self, i):
        return lax.rem(self.hi + 1 + i, self.m)

    def begin(self):
        each(self.m, lambda i: self.x(self.turn_of(i)).start())

    def pass_on(self, i):
        k = self.turn_of(i)
        self.x(k).wait_recv()
        self.part[k] = (self.src[self.piece(self.lo, k)].astype(F32) + self.gx[k].astype(F32)).astype(BF16)

        @pl.when(k != self.hi)
        def _():
            self.z(k).start()

    def ends(self, step, run):
        there = self.hi + step
        pl.when(jnp.logical_and(there >= 0, there < self.m))(run)

    def reduce(self):
        total = self.part[self.hi].astype(F32)
        for k in self.others():
            self.z_in(k).wait_recv()
            total += self.gz[k].astype(F32)
        self.own[...] = total.astype(BF16)
        self.keep().start()
        for p in range(self.pieces):
            self.ends(1, lambda: self.c_own(p, 1).start())
            self.ends(-1, lambda: self.c_own(p, -1).start())
            self.f_own(p).start()

    def forward(self, d):
        for p in range(self.pieces):
            for step in (1, -1):

                def run():
                    k = self.hi - step * d
                    self.c_on(k, p, step).wait_recv()
                    self.ends(step, lambda: self.c_on(k, p, step).start())
                    self.f(k, p).start()

                self.ends(-step * d, run)

    def finish(self):
        each(self.m, lambda k: self.x(k).wait_send())
        for k in self.others():
            self.z(k).wait_send()
        for p in range(self.pieces):
            for step in (1, -1):
                self.ends(step, lambda: self.c_own(p, step).wait_send())
                for d in range(1, self.m):

                    def run():
                        k = self.hi - step * d
                        self.ends(step, lambda: self.c_on(k, p, step).wait_send())
                        self.f(k, p).wait_send()

                    self.ends(-step * d, run)
            self.f_own(p).wait_send()
            each(self.m, lambda k: self.f(k, p).wait_recv())
        self.keep().wait()


def layer(n, names, *refs):
    r = types.SimpleNamespace(**dict(zip(names, refs)))
    at = Place(n)
    slots, rows, feat = r.x_in.shape
    length = rows // 2
    half = 2 * feat
    hl = feat // HEAD_DIM
    m = n // 2
    core, y, me = at.core, at.y, at.me
    mine = pl.ds(length * core, length)
    other = pl.ds(length * (1 - core), length)
    early, late = slice(0, length), slice(length, rows)
    heads = [slice(h * HEAD_DIM, (h + 1) * HEAD_DIM) for h in range(hl)]
    fulls = (r.xg, r.cg, r.ag)
    owns = (r.x_in, r.c_in, r.own_att)
    lands = (r.land.at[0], r.land.at[1], r.land.at[0])
    quarter = D // m
    sum1 = Sum(
        at, r.gl, r.res1, r.gx1, r.act.at[:m, :quarter], r.gz1, r.own1, *[getattr(r, "u%d" % i) for i in range(10)]
    )
    src2 = r.act.at[m : m + 2, :feat]
    sum2 = Sum(at, src2, r.res2.at[:2], r.gx2, r.pt2, r.gz2, r.own2, *[getattr(r, "v%d" % i) for i in range(10)])
    sum3 = Sum(at, r.src3, r.res2.at[2:], r.gx3, r.pt3, r.gz3, r.own3, *[getattr(r, "w%d" % i) for i in range(10)])

    def sib_copy(k, s):
        return remote(owns[k].at[s], lands[k].at[s], r.ss.at[k, s], r.sr.at[k, s], at.sib)

    def build(k, s):
        a, b = owns[k][s], lands[k][s]

        @pl.when(core == 0)
        def _():
            fulls[k][s, y] = jnp.concatenate([a, b], axis=1)

        @pl.when(core == 1)
        def _():
            fulls[k][s, y] = jnp.concatenate([b, a], axis=1)

    def y_copy(k, s):
        part = fulls[k].at[s, y, mine]
        return remote(part, part, r.ys.at[k, s], r.yr.at[k, s], at.yp)

    def f_copy(k, s):
        part = fulls[k].at[s, 1 - y, mine]
        return remote(part, part, r.fs.at[k, s], r.fr.at[k, s], at.sib)

    def kv_copy(s, i):
        return remote(r.kvo.at[s], r.kvb.at[at.spot(s, me, me)], r.ks.at[s, i], r.kr.at[s, me], (i, at.head))

    def kv_in(s, j):
        return remote(r.kvo.at[s], r.kvb.at[at.spot(s, j, j)], r.ks.at[s, j], r.kr.at[s, j], (j, at.head))

    def dkv_copy(s, j):
        return remote(
            r.kvb.at[at.spot(s, j, j)], r.dla.at[at.spot(s, j, me)], r.ds.at[s, j], r.dr.at[s, me], (j, at.head)
        )

    def dkv_in(s, i):
        here = r.dla.at[at.spot(s, me, i)]
        return remote(here, here, r.ds.at[s, i], r.dr.at[s, i], (i, at.head))

    def readers(s, step):
        for d in range(1, n):
            i = me + d

            @pl.when(jnp.logical_and(i < n, at.lowest(s, i) <= me))
            def _():
                step(i)

    def e_core(s):
        return remote(r.ep.at[s, other], r.er.at[s], r.e1s.at[s], r.e1r.at[s], at.sib)

    def e_y(s):
        return remote(r.er.at[s], r.ey.at[s], r.e2s.at[s], r.e2r.at[s], at.yp)

    def e_back(s):
        return remote(r.ey.at[s], r.eb.at[s], r.e3s.at[s], r.e3r.at[s], at.sib)

    def held(first, s, k):
        return (s, pl.ds(first, length), pl.ds(pl.multiple_of(k * half, 128), half))

    def f_core(s):
        return remote(r.ag.at[s, :, other], r.fc.at[s], r.f1s.at[s], r.f1r.at[s], at.sib)

    def f_y(s):
        return remote(r.upre.at[held(0, s, 1 - y)], r.fy.at[s], r.f2s.at[s], r.f2r.at[s], at.yp)

    def f_back(s):
        return remote(r.osd.at[s], r.out.at[s, core], r.f3s.at[s], r.f3r.at[s], at.sib)

    def b_core(s):
        return remote(r.n2.at[s, other], r.er.at[s], r.a1s.at[s], r.a1r.at[s], at.sib)

    def s_core(s):
        return remote(r.st.at[s, 1 - core], r.sl.at[s], r.b1s.at[s], r.b1r.at[s], at.sib)

    def b_y(s):
        return remote(r.upre.at[held(length, s, 1 - y)], r.bey.at[s], r.a2s.at[s], r.a2r.at[s], at.yp)

    def s_y(s):
        return remote(r.sh.at[s], r.sy.at[s], r.b2s.at[s], r.b2r.at[s], at.yp)

    def b_back(s):
        return remote(r.isd.at[s], r.ig.at[s, core], r.a3s.at[s], r.a3r.at[s], at.sib)

    at.greet([at.sib, at.yp, at.diag], True)
    each(slots, lambda s: sib_copy(0, s).start())
    r.gb_in[...] = jnp.zeros_like(r.gb_in)
    for i, vector in enumerate((r.ga, r.ba, r.gf_in, r.bf_in)):
        r.gb_in[i : i + 1] = vector[...]
    r.gland[at.head] = r.gb_in[...]
    g_copies = [
        remote(r.gb_in, r.gland.at[at.head], r.gs.at[k], r.gr.at[k], d)
        for k, d in enumerate((at.sib, at.yp, at.diag))
    ]
    for copy in g_copies:
        copy.start()

    def first_y(s):
        sib_copy(0, s).wait_recv()
        build(0, s)
        y_copy(0, s).start()

    each(slots, first_y)

    def wo_block(who):
        return r.wog.at[pl.ds(pl.multiple_of(feat * who, 16), feat)]

    wo_sib = remote(r.wo_in, wo_block(at.head), r.ws.at[0], r.wr.at[0], at.sib)
    wo_y = remote(r.wo_in, wo_block(at.head), r.ws.at[1], r.wr.at[1], at.yp)
    wo_f = remote(wo_block(at.yp[1]), wo_block(at.yp[1]), r.ws.at[2], r.wr.at[2], at.sib)
    wo_y.start()
    wo_sib.start()
    each(slots, lambda s: sib_copy(1, s).start())
    r.wog[pl.ds(pl.multiple_of(feat * at.head, 16), feat)] = r.wo_in[...]
    for copy in g_copies:
        copy.wait()
    r.gbf[...] = jnp.concatenate([r.gland[i] for i in range(4)], axis=1)
    r.cos[...] = jnp.concatenate([r.cos_in[...]] * 2, axis=1)
    r.sin[...] = jnp.concatenate([r.sin_in[...]] * 2, axis=1)
    long, most = 0, r.docs[0, 0]
    for i in range(1, slots):
        long = jnp.where(r.docs[i, 0] > most, i, long)
        most = jnp.maximum(r.docs[i, 0], most)
    lane = lax.broadcasted_iota(jnp.int32, (8, rows), 1)
    pos = jnp.where(lane < length, lane, lane - length) + me * length
    for s in range(slots):
        row = long if s == LONG_SLOT else jnp.where(long == s, LONG_SLOT, s)
        end = 0
        first_key, last_key = jnp.zeros_like(pos), jnp.full_like(pos, 2**30)
        for j in range(r.docs.shape[1]):
            end = end + r.docs[row, j]
            first_key = jnp.where(pos >= end, end, first_key)
            last_key = jnp.where(pos < end, jnp.minimum(last_key, end), last_key)
        r.bounds[s] = jnp.where(lax.broadcasted_iota(jnp.int32, (8, rows), 0) == 0, first_key, last_key)
    r.mrow[...] = jnp.zeros_like(r.mrow)
    r.lrow[...] = jnp.ones_like(r.lrow)
    r.og[...] = jnp.zeros_like(r.og)
    r.qq[...] = jnp.zeros_like(r.qq)
    r.qkv[...] = jnp.zeros_like(r.qkv)
    r.gsum[...] = jnp.zeros_like(r.gsum)
    r.gtwo[...] = jnp.zeros_like(r.gtwo)
    r.drow[...] = jnp.zeros_like(r.drow)

    def project(s):
        x = whole_rows(r.xg, s).astype(F32)
        mean, inv = row_stats(x)
        normed = ((x - mean) * inv * r.gbf[0:1] + r.gbf[1:2]).astype(BF16)
        r.n1[s] = normed
        pt = dot(r.w_t[...], normed, 1, 1)
        qk = turn(pt[:half], r.cos[...], r.sin[...])
        r.qt[s] = (qk[:feat] * HEAD_DIM**-0.5).astype(BF16)
        kv = jnp.concatenate([qk[feat:], pt[half:]], axis=0).astype(BF16)
        r.kvn[s] = kv[:, :length]
        r.kvo[s] = kv[:, length:]
        readers(s, lambda i: kv_copy(s, i).start())

    def arrive(t):
        @pl.when(t < slots)
        def _():
            y_copy(0, t).wait_recv()
            f_copy(0, t).start()

        @pl.when(t >= 1)
        def _():
            f_copy(0, t - 1).wait_recv()
            project(t - 1)

    each(slots + 1, arrive)

    def cot_on(s):
        sib_copy(1, s).wait_recv()
        build(1, s)
        y_copy(1, s).start()

    each(2, cot_on)

    def attend(s):
        start, end = r.bounds[s, 0:1], r.bounds[s, 1:2]
        clean, noisy = masks(me, length, start, end)
        kc, kn = r.kvo[s], r.kvn[s]
        q = [r.qt[s, hd] for hd in heads]
        sc = [dot(kc[hd], q[h], 0, 0) for h, hd in enumerate(heads)]
        sn = [dot(kn[hd], q[h][:, :length], 0, 0) for h, hd in enumerate(heads)]
        sc = [jnp.where(clean, v, masked_score) for v in sc]
        sn = [jnp.where(noisy, v, masked_score) for v in sn]
        top = []
        for h in range(hl):
            tc = jnp.max(sc[h], axis=0, keepdims=True)
            tn = jnp.max(sn[h], axis=0, keepdims=True)
            top.append(jnp.concatenate([jnp.maximum(tc[:, :length], tn), tc[:, length:]], axis=1))
        pc = [jnp.exp(sc[h] - top[h]) for h in range(hl)]
        pn = [jnp.exp(sn[h] - top[h][:, :length]) for h in range(hl)]
        oc = [dot(kc[feat:][hd], pc[h].astype(BF16), 1, 0) for h, hd in enumerate(heads)]
        on = [dot(kn[feat:][hd], pn[h].astype(BF16), 1, 0) for h, hd in enumerate(heads)]
        for h, hd in enumerate(heads):
            tc = jnp.sum(pc[h], axis=0, keepdims=True)
            tn = jnp.sum(pn[h], axis=0, keepdims=True)
            r.mrow[h : h + 1] = top[h]
            r.lrow[h : h + 1] = jnp.concatenate([tc[:, :length] + tn, tc[:, length:]], axis=1)
            r.acc[hd, early] = oc[h][:, :length] + on[h]
            r.acc[hd, late] = oc[h][:, length:]

        def one(j, carry):
            kv_in(s, j).wait_recv()
            kv = r.kvb[at.spot(s, j, j)]
            q = [r.qt[s, hd] for hd in heads]
            old = [r.mrow[h : h + 1] for h in range(hl)]
            total = [r.lrow[h : h + 1] for h in range(hl)]
            pos = lax.broadcasted_iota(jnp.int32, (length, rows), 0) + j * length
            allowed = pos >= start
            sc = [dot(kv[hd], q[h], 0, 0) for h, hd in enumerate(heads)]
            sc = [jnp.where(allowed, v, masked_score) for v in sc]
            new = [jnp.maximum(old[h], jnp.max(sc[h], axis=0, keepdims=True)) for h in range(hl)]
            p = [jnp.exp(sc[h] - new[h]) for h in range(hl)]
            add = [dot(kv[feat:][hd], p[h].astype(BF16), 1, 0) for h, hd in enumerate(heads)]
            scale = [jnp.exp(old[h] - new[h]) for h in range(hl)]
            for h, hd in enumerate(heads):
                r.mrow[h : h + 1] = new[h]
                r.lrow[h : h + 1] = total[h] * scale[h] + jnp.sum(p[h], axis=0, keepdims=True)
                r.acc[hd] = r.acc[hd] * scale[h] + add[h]
            return carry

        lax.fori_loop(at.lowest(s, me), me, one, 0)
        for h, hd in enumerate(heads):
            r.att[s, hd] = r.acc[hd] / r.lrow[h : h + 1]
        r.lse[s] = r.mrow[...] + jnp.log(r.lrow[...])
        r.own_att[s] = r.att[s].T.astype(BF16)
        sib_copy(2, s).start()

    def forward(s):
        x = whole_rows(r.xg, s).astype(F32)
        branch = dot(r.ag[s, 0], r.wog[:half], 1, 0) + dot(r.ag[s, 1], r.wog[half:], 1, 0)
        h = x + branch
        for yy in range(2):
            for cc in range(2):

                @pl.when(jnp.logical_and(y == yy, core == cc))
                def _():
                    r.hp[s] = h[cc * length : (cc + 1) * length, yy * half : (yy + 1) * half]

        mean, inv = row_stats(h)
        r.iv[s] = inv
        normed = ((h - mean) * inv * r.gbf[2:3] + r.gbf[3:4]).astype(BF16)
        r.n2[s] = normed
        up = dot(normed, r.wu[...], 1, 0)
        cube = 0.7978845608028654 * (up + 0.044715 * up * up * up)
        t = jnp.tanh(cube)
        r.act[s] = (0.5 * up * (1.0 + t)).astype(BF16)
        slope = 0.5 * (1.0 + t) + 0.5 * up * (1.0 - t * t) * (
            0.7978845608028654 * (1.0 + 3 * 0.044715 * up * up)
        )
        da = dot(whole_rows(r.cg, s), r.wd[...], 1, 1)
        pre = (da * slope).astype(BF16)
        r.upre[s] = pre
        r.ep[s] = dot(pre, r.wu[...], 1, 1).astype(BF16)
        e_core(s).start()

    def stage(t, offset, step):
        s = t - offset

        @pl.when(jnp.logical_and(s >= 0, s < slots))
        def _():
            step(s)

    def att_on(s):
        sib_copy(2, s).wait_recv()
        build(2, s)
        y_copy(2, s).start()

    def att_back(s):
        y_copy(2, s).wait_recv()
        f_copy(2, s).start()

    def cot_back(s):
        y_copy(1, s).wait_recv()
        f_copy(1, s).start()

    def feed(s):
        @pl.when(s == 0)
        def _():
            wo_y.wait_recv()
            wo_f.start()
            wo_sib.wait_recv()
            wo_f.wait_recv()

        f_copy(1, s).wait_recv()
        f_copy(2, s).wait_recv()
        forward(s)

    def e_on(s):
        e_core(s).wait_recv()
        r.er[s] = (r.ep[s, mine].astype(F32) + r.er[s].astype(F32)).astype(BF16)
        e_y(s).start()

    def e_total(s):
        e_y(s).wait_recv()
        r.ey[s] = (r.er[s].astype(F32) + r.ey[s].astype(F32)).astype(BF16)
        e_y(s).wait_send()
        e_back(s).start()

    def loop_one(t):
        stage(t, 1, att_on)

        @pl.when(jnp.logical_and(t >= 1, t < slots - 1))
        def _():
            cot_on(t + 1)

        stage(t, 2, cot_back)
        stage(t, 2, att_back)

        @pl.when(t == slots)
        def _():
            each(slots - 2, e_on)

        @pl.when(t == slots + 1)
        def _():
            e_on(slots - 2)

        stage(t, 0, attend)
        stage(t, 2, feed)

    each(slots + 2, loop_one)

    wide = slots * rows

    def up_tile(i):
        cols = pl.ds(pl.multiple_of(i * 256, 256), 256)
        left = r.n2[...].reshape(wide, D)
        part = dot(left, r.upre[:, :, cols].reshape(wide, 256), 0, 0).astype(BF16)
        r.gl[0, :, cols] = part

    def down_tile(i):
        cols = pl.ds(pl.multiple_of(lax.rem(i, 3) * 128, 128), 128)
        out_cols = pl.ds(pl.multiple_of(i * 128, 128), 128)
        left = r.act[...].reshape(wide, D)
        part = dot(left, r.cg[:, lax.div(i, 3), :, cols].reshape(wide, 128), 0, 0).astype(BF16)
        r.gl[1, :, out_cols] = part

    e_on(slots - 1)
    @pl.when(sum1.lo == 0)
    def _():
        each(D // 128, down_tile)
        sum1.begin()
        each(D // 256, up_tile)

    @pl.when(sum1.lo == 1)
    def _():
        each(D // 256, up_tile)
        sum1.begin()
        each(D // 128, down_tile)

    e_total(0)
    e_total(1)

    def two_back(s):
        e_back(s).wait_recv()
        e_back(s).wait_send()
        e_core(s).wait_send()

        @pl.when(core == 0)
        def _():
            r.ep[s, early] = r.ey[s]
            r.ep[s, late] = r.eb[s]

        @pl.when(core == 1)
        def _():
            r.ep[s, early] = r.eb[s]
            r.ep[s, late] = r.ey[s]

        e = r.ep[s].astype(F32)
        xh = (r.n2[s].astype(F32) - r.gbf[3:4]) * r.ginv[0:1]
        r.gtwo[2:3] += jnp.sum(e * xh, axis=0, keepdims=True)
        r.gtwo[3:4] += jnp.sum(e, axis=0, keepdims=True)
        g = e * r.gbf[2:3]
        first = jnp.sum(g, axis=1, keepdims=True) / D
        second = jnp.sum(g * xh, axis=1, keepdims=True) / D
        resid = whole_rows(r.cg, s).astype(F32) + r.iv[s] * (g - first - xh * second)
        r.ep[s] = resid.astype(BF16)

    r.ginv[...] = 1.0 / r.gbf[2:3] + jnp.zeros_like(r.ginv)

    def head_grads(s, kv, lanes, allowed):
        q = [r.qt[s, hd, lanes] for hd in heads]
        d_out = [r.do[hd, lanes] for hd in heads]
        sc = [dot(kv[hd], q[h], 0, 0) for h, hd in enumerate(heads)]
        dp = [dot(kv[feat:][hd], d_out[h], 0, 0) for h, hd in enumerate(heads)]
        p = [
            jnp.exp(jnp.where(allowed, sc[h], masked_score) - r.lse[s, h : h + 1, lanes])
            for h in range(hl)
        ]
        ds = [(p[h] * (dp[h] - r.drow[h : h + 1, lanes])).astype(BF16) for h in range(hl)]
        dv = [dot(d_out[h], p[h].astype(BF16), 1, 1) for h in range(hl)]
        dk = [dot(q[h], ds[h], 1, 1) for h in range(hl)]
        dq_add = [dot(kv[hd], ds[h], 1, 0) for h, hd in enumerate(heads)]
        return [jnp.concatenate(v, axis=0) for v in (dq_add, dk, dv)]

    def attend_back(s):
        low_rows = r.ep[s]
        d_out = dot(r.wo_in[...], low_rows, 1, 1).astype(BF16)
        r.do[...] = d_out
        a = r.att[s]
        r.og[...] += dot(a.astype(BF16), low_rows, 1, 0)
        prod = d_out.astype(F32) * a
        for h, hd in enumerate(heads):
            r.drow[h : h + 1] = jnp.sum(prod[hd], axis=0, keepdims=True)
        start, end = r.bounds[s, 0:1], r.bounds[s, 1:2]
        clean, noisy = masks(me, length, start, end)
        dqa, dk, dv = head_grads(s, r.kvo[s], slice(0, rows), clean)
        dqn, dkn, dvn = head_grads(s, r.kvn[s], early, noisy)
        r.acc[...] = dqa
        r.acc[:, early] += dqn
        r.dkv[s, :feat] = dk
        r.dkv[s, feat:] = dv
        r.qp[s, half:, early] = dvn.astype(BF16)
        r.qp[s, feat:half, early] = turn(dkn, r.cos[:, :length], -r.sin[:, :length]).astype(BF16)

        def one(j, carry):
            spot = at.spot(s, j, j)
            kv = r.kvb[spot]
            pos = lax.broadcasted_iota(jnp.int32, (length, rows), 0) + j * length
            dqa, dk, dv = head_grads(s, kv, slice(0, rows), pos >= start)
            r.acc[...] += dqa
            r.kvb[spot, :feat] = dk.astype(BF16)
            r.kvb[spot, feat:] = dv.astype(BF16)
            dkv_copy(s, j).start()
            return carry

        lax.fori_loop(at.lowest(s, me), me, one, 0)
        r.qp[s, :feat] = (turn(r.acc[...], r.cos[...], -r.sin[...]) * HEAD_DIM**-0.5).astype(BF16)
        r.qq[...] += dot(r.qp[s, :feat], r.n1[s], 1, 0)

    def f_start(s):
        y_copy(2, s).wait_send()
        f_copy(2, s).wait_send()
        ff = dot(r.act[s], r.wd[...], 1, 0)
        r.ag[s, 0] = ff[:, :half].astype(BF16)
        r.ag[s, 1] = ff[:, half:].astype(BF16)
        f_core(s).start()

    def f_on(s):
        f_core(s).wait_recv()
        for k in range(2):
            r.upre[held(0, s, k)] = (r.ag[s, k, mine].astype(F32) + r.fc[s, k].astype(F32)).astype(BF16)
        f_y(s).start()

    def f_end(s):
        f_y(s).wait_recv()
        total = r.hp[s] + (r.upre[held(0, s, y)].astype(F32) + r.fy[s].astype(F32))
        turned = total.T.astype(BF16)
        lo, hi = turned[:feat], turned[feat:]

        @pl.when(core == 0)
        def _():
            r.out[s, 0] = lo
            r.osd[s] = hi

        @pl.when(core == 1)
        def _():
            r.out[s, 1] = hi
            r.osd[s] = lo

        f_back(s).start()

    def loop_two(t):
        def run(s):
            two_back(s)
            attend_back(s)

        stage(t, 1, f_on)
        stage(t, -2, e_total)
        stage(t, 0, run)

        @pl.when(jnp.logical_or(t == 3, t == 5))
        def _():
            sum1.pass_on(lax.div(t - 3, 2))

    each(slots, f_start)
    each(slots, loop_two)
    src2[0] = r.og[...].astype(BF16)
    src2[1] = r.qq[...].astype(BF16)
    sum2.begin()
    f_on(slots - 1)
    sum1.pass_on(2)
    sum1.pass_on(3)

    def project_back(s):
        def add(i):
            dkv_in(s, i).wait_recv()
            r.dkv[s] += r.dla[at.spot(s, me, i)].astype(F32)

        readers(s, add)
        total = r.dkv[s]
        r.qp[s, feat:half, late] = turn(total[:feat], r.cos[:, late], -r.sin[:, late]).astype(BF16)
        r.qp[s, half:, late] = total[feat:].astype(BF16)
        pre = r.qp[s]
        r.qkv[...] += dot(pre[feat:], r.n1[s], 1, 0)
        e = dot(pre, r.w_t[...], 0, 0)
        x = whole_rows(r.xg, s).astype(F32)
        mean, inv = row_stats(x)
        xh = (x - mean) * inv
        r.gsum[0:1] += jnp.sum(e * xh, axis=0, keepdims=True)
        r.gsum[1:2] += jnp.sum(e, axis=0, keepdims=True)
        r.n2[s] = e.astype(BF16)
        g = e * r.gbf[0:1]
        one_sum = jnp.sum(g, axis=1, keepdims=True)
        two_sum = jnp.sum(g * xh, axis=1, keepdims=True)
        lane = lax.broadcasted_iota(jnp.int32, (rows, 128), 1)
        packed = jnp.where(lane == 0, one_sum, jnp.where(lane == 1, two_sum, 0.0)).T
        r.st[s, 0] = packed[:8, :length]
        r.st[s, 1] = packed[:8, length:]
        b_core(s).start()
        s_core(s).start()

    def b_on(s):
        b_core(s).wait_recv()
        s_core(s).wait_recv()
        both = r.n2[s, mine].astype(F32) + r.er[s].astype(F32)
        r.upre[s, late] = both.astype(BF16)
        r.sh[s] = r.st[s, core] + r.sl[s]
        b_y(s).start()
        s_y(s).start()

    def b_end(s):
        b_y(s).wait_recv()
        s_y(s).wait_recv()
        e = r.upre[held(length, s, y)].astype(F32) + r.bey[s].astype(F32)
        sums = r.sh[s] + r.sy[s]
        cols = jnp.concatenate([sums, jnp.zeros((120, length), F32)], axis=0).T
        first, second = cols[:, 0:1] / D, cols[:, 1:2] / D
        x = jnp.concatenate([r.xg[s, 0, mine], r.xg[s, 1, mine]], axis=1).astype(F32)
        mean, inv = row_stats(x)
        xh = (r.xg[s, y, mine].astype(F32) - mean) * inv
        gain = jnp.where(y == 0, r.gbf[0:1, :half], r.gbf[0:1, half:])
        resid = r.ep[s, mine].astype(F32)
        resid = jnp.where(y == 0, resid[:, :half], resid[:, half:])
        grad = resid + inv * (e * gain - first - xh * second)
        turned = grad.T
        lo, hi = turned[:feat], turned[feat:]

        @pl.when(core == 0)
        def _():
            r.ig[s, 0] = lo
            r.isd[s] = hi

        @pl.when(core == 1)
        def _():
            r.ig[s, 1] = hi
            r.isd[s] = lo

        b_back(s).start()

    def loop_three(t):
        stage(t, 0, f_end)
        stage(t, 1, b_on)
        stage(t, 0, project_back)

        pl.when(t == 2)(sum1.reduce)

        @pl.when(jnp.logical_or(t == 3, t == 4))
        def _():
            sum2.pass_on(2 * t - 6)
            sum2.pass_on(2 * t - 5)

    each(slots, loop_three)
    grads = r.qkv[...].astype(BF16)
    r.src3[0] = grads[:feat]
    r.src3[1] = grads[feat:]
    sum3.begin()
    b_on(slots - 1)
    h_copies = [
        remote(r.gsum, r.gh.at[k], r.hs.at[k], r.hr.at[k], d)
        for k, d in enumerate((at.sib, at.yp, at.diag))
    ]
    for copy in h_copies:
        copy.start()
    sum2.reduce()

    def share(i):
        return remote(r.gf, r.gq.at[me], r.qs.at[i], r.qr.at[me], (i, at.head))

    def share_in(i):
        return remote(r.gf, r.gq.at[i], r.qs.at[i], r.qr.at[i], (i, at.head))

    def gains_on():
        for copy in h_copies:
            copy.wait()
        total = r.gsum[...] + r.gh[0] + r.gh[1] + r.gh[2] + r.gtwo[...]
        for h in range(4):

            @pl.when(at.head == h)
            def _():
                r.gf[...] = total[:, h * feat : (h + 1) * feat]

        r.gq[me] = r.gf[...]
        for d in range(1, n):
            share(lax.rem(me + d, n)).start()

    def loop_four(t):
        stage(t, 0, b_end)
        pl.when(t == 0)(gains_on)

        @pl.when(jnp.logical_or(t == 1, t >= 4))
        def _():
            sum1.forward(jnp.where(t == 1, 1, t - 2))

        @pl.when(jnp.logical_or(t == 2, t == 3))
        def _():
            sum3.pass_on(2 * t - 4)
            sum3.pass_on(2 * t - 3)

    each(slots, loop_four)
    sum3.reduce()
    for d in range(1, n):
        share_in(lax.rem(me + d, n)).wait_recv()
    r.gains[...] = jnp.sum(r.gq[...], axis=0)
    for d in range(1, m):
        sum2.forward(d)
    for d in range(1, m):
        sum3.forward(d)

    def finish(s):
        for k in range(3):
            sib_copy(k, s).wait_send()
        for k in range(2):
            y_copy(k, s).wait_send()
            f_copy(k, s).wait_send()
        readers(s, lambda i: kv_copy(s, i).wait_send())
        f_core(s).wait_send()
        f_y(s).wait_send()
        f_back(s).wait()
        b_core(s).wait_send()
        s_core(s).wait_send()
        b_y(s).wait_send()
        s_y(s).wait_send()
        b_back(s).wait()

        def sent(j, carry):
            dkv_copy(s, j).wait_send()
            return carry

        lax.fori_loop(at.lowest(s, me), me, sent, 0)

    each(slots, finish)
    wo_sib.wait_send()
    wo_y.wait_send()
    wo_f.wait_send()
    for part in (sum1, sum2, sum3):
        part.finish()
    for d in range(1, n):
        share(lax.rem(me + d, n)).wait_send()


def body(
    inputs,
    doc_lengths,
    attn_gain,
    attn_bias,
    w_qkv,
    w_out,
    ffn_gain,
    ffn_bias,
    w_up,
    w_down,
    cotangent,
):
    n = lax.axis_size("seq")
    slots, _, length, feat = inputs.shape
    rows, half, m = 2 * length, 2 * feat, n // 2
    held = slots * n * half * length * 2
    if held > ROWS_LIMIT or m != 4:
        return gathered_body(
            inputs, doc_lengths, attn_gain, attn_bias, w_qkv, w_out, ffn_gain, ffn_bias, w_up, w_down, cotangent
        )
    me = lax.axis_index("seq")
    long = jnp.argmax(doc_lengths[:, 0]).astype(jnp.int32)
    ids = jnp.arange(slots, dtype=jnp.int32)

    def swap(v):
        pick = lax.dynamic_index_in_dim(v, long, 0, keepdims=True)
        where = ids.reshape((slots,) + (1,) * (v.ndim - 1))
        kept = v[LONG_SLOT : LONG_SLOT + 1]
        return jnp.where(where == LONG_SLOT, pick, jnp.where(where == long, kept, v))

    positions = me * length + jnp.arange(length, dtype=jnp.int32)
    half_dim = HEAD_DIM // 2
    freqs = rotary_base ** (-jnp.arange(half_dim, dtype=F32) / half_dim)
    angles = freqs[:, None] * positions.astype(F32)[None, :]
    w_t = w_qkv.reshape(D, 3 * feat).T
    operands = dict(
        x_in=swap(inputs.reshape(slots, rows, feat)), c_in=swap(cotangent.reshape(slots, rows, feat)),
        ga=attn_gain[None], ba=attn_bias[None], gf_in=ffn_gain[None], bf_in=ffn_bias[None],
        w_t=w_t, wo_in=w_out, wu=w_up, wd=w_down, cos_in=jnp.cos(angles), sin_in=jnp.sin(angles), docs=doc_lengths,
    )
    small = (m, feat // m, D)
    quarter = (m, D // m, D)
    outs = dict(
        out=((slots, 2, feat, length), BF16), ig=((slots, 2, feat, length), F32), res1=((2, *quarter), BF16),
        res2=((4, *small), BF16), gains=((8, feat), F32),
    )
    blocks = n + (slots - 1) * (n // 2 + max(1, n // 8))
    full, wide = (slots, 2, rows, half), (slots, rows, D)
    part, stat = (slots, length, D), (slots, 8, length)
    halves, own_half = (slots, 2, length, half), (slots, length, half)
    buffers = dict(
        land=((2, slots, rows, feat), BF16), own_att=((slots, rows, feat), BF16), gland=((4, 8, feat), F32),
        gbf=((8, D), F32), ginv=((8, D), F32), xg=(full, BF16), cg=(full, BF16), ag=(full, BF16),
        wog=((D, D), BF16), n1=(wide, BF16), qt=((slots, feat, rows), BF16),
        kvn=((slots, half, length), BF16), kvo=((slots, half, length), BF16), kvb=((blocks, half, length), BF16),
        att=((slots, feat, rows), F32), lse=((slots, 8, rows), F32), acc=((feat, rows), F32),
        mrow=((8, rows), F32), lrow=((8, rows), F32), hp=(own_half, F32), iv=((slots, rows, 1), F32),
        n2=(wide, BF16), act=(wide, BF16), upre=(wide, BF16), ep=(wide, BF16), er=(part, BF16), ey=(part, BF16),
        eb=(part, BF16), fc=(halves, BF16), fy=(own_half, BF16),
        osd=((slots, feat, length), BF16), gl=((2, D, D), BF16), gx1=(quarter, BF16), gz1=(quarter, BF16),
        own1=(quarter[1:], BF16), do=((feat, rows), BF16), drow=((8, rows), F32),
        dkv=((slots, half, length), F32), dla=((blocks, half, length), BF16), qp=((slots, 3 * feat, rows), BF16),
        og=((feat, D), F32), qq=((feat, D), F32), qkv=((half, D), F32), gsum=((8, D), F32), gtwo=((8, D), F32),
        st=((slots, 2, 8, length), F32), sl=(stat, F32), sh=(stat, F32), sy=(stat, F32),
        bey=(own_half, BF16), isd=((slots, feat, length), F32), src3=((2, feat, D), BF16),
        gx2=(small, BF16), pt2=(small, BF16), gz2=(small, BF16), own2=(small[1:], BF16),
        gx3=(small, BF16), pt3=(small, BF16), gz3=(small, BF16), own3=(small[1:], BF16),
        gb_in=((8, feat), F32), cos=((half_dim, rows), F32), sin=((half_dim, rows), F32),
        bounds=((slots, 8, rows), jnp.int32), gh=((3, 8, D), F32), gq=((n, 8, feat), F32), gf=((8, feat), F32),
    )
    sems = {k: (3, slots) for k in ("ss", "sr", "ys", "yr", "fs", "fr")}
    sems |= {k: (3,) for k in ("gs", "gr", "ws", "wr", "hs", "hr")}
    sems |= {k: (slots, n) for k in ("ks", "kr", "ds", "dr")}
    sems |= {k + i + e: (slots,) for k in "efab" for i in "123" for e in "sr" if k + i != "b3"}
    sems |= {"qs": (n,), "qr": (n,)}
    pieces = {"u": 2, "v": 1, "w": 1}
    sems |= {"%s%d" % (k, i): (m,) for k in "uvw" for i in range(4)}
    sems |= {"%s%d" % (k, i): (m, pieces[k]) for k in "uvw" for i in range(4, 8)}
    sems |= {k + "9": (pieces[k],) for k in "uvw"}
    sem = pltpu.SemaphoreType.DMA
    scratch = {k: VMEM(*v) for k, v in buffers.items()}
    scratch |= {k: sem(v) for k, v in sems.items()}
    scratch |= {k + "8": sem for k in "uvw"}
    vmem = pl.BlockSpec(memory_space=VMEM)
    names = [*operands, *outs, *scratch]
    got = pl.pallas_call(
        functools.partial(layer, n, names),
        out_shape=[jax.ShapeDtypeStruct(*v) for v in outs.values()],
        in_specs=[pl.BlockSpec(memory_space=pltpu.SMEM) if k == "docs" else vmem for k in operands],
        out_specs=[pl.BlockSpec(memory_space=pl.ANY) if k.startswith("res") else vmem for k in outs],
        scratch_shapes=list(scratch.values()),
        compiler_params=pltpu.CompilerParams(
            collective_id=0, has_side_effects=True, vmem_limit_bytes=VMEM_LIMIT
        ),
        name="layer",
    )(*operands.values())
    outputs, input_grad, res1, res2, gain_grads = got
    up_grad, down_grad = res1.reshape(2, D, D).astype(F32)
    small_grads = res2.reshape(4, feat, D)
    out_grad = small_grads[0].astype(F32)
    qkv_grad = small_grads[1:].astype(F32)
    return (
        jnp.swapaxes(swap(outputs), 2, 3),
        jnp.swapaxes(swap(input_grad), 2, 3),
        jnp.transpose(qkv_grad, (2, 0, 1)),
        out_grad,
        up_grad,
        down_grad,
        gain_grads[0],
        gain_grads[1],
        gain_grads[2],
        gain_grads[3],
    )


def solution(mesh):
    in_specs = (
        P(None, None, "seq", "head"),
        P(),
        P("head"),
        P("head"),
        P(None, None, "head"),
        P("head", None),
        P("head"),
        P("head"),
        P(None, "head"),
        P("head", None),
        P(None, None, "seq", "head"),
    )
    out_specs = (
        P(None, None, "seq", "head"),
        P(None, None, "seq", "head"),
        P(None, None, "head"),
        P("head", None),
        P(None, "head"),
        P("head", None),
        P("head"),
        P("head"),
        P("head"),
        P("head"),
    )
    return jax.shard_map(body, mesh=mesh, in_specs=in_specs, out_specs=out_specs, check_vma=False)
```

```python
import functools
import types

import jax
import jax.numpy as jnp
from jax import lax
from jax.experimental import pallas as pl
from jax.experimental.pallas import tpu as pltpu
from jax.sharding import PartitionSpec as P

D = 768
HEAD_DIM = 64
BLOCK = 16


norm_eps = 1e-05
masked_score = -1e30
rotary_base = 10000.0

MESH = pl.DeviceIdType.MESH
VMEM = pltpu.VMEM
F32 = jnp.float32
BF16 = jnp.bfloat16
ROWS_LIMIT = 16 << 20
VMEM_LIMIT = 63 << 20
LONG_SLOT = 3


def passed_along(block, axis, distance):
    devices = range(lax.axis_size(axis))
    route = [(i - distance, i) for i in devices if i - distance in devices]
    return lax.ppermute(block, axis, route)


def from_behind(x, axis, by):
    devices = lax.axis_size(axis)
    return lax.ppermute(x, axis, [(i, (i + by) % devices) for i in range(devices)])


def segment_ids(doc_lengths, positions):
    doc_ends = jnp.cumsum(doc_lengths, axis=1)
    return jnp.sum((doc_ends[:, :, None] <= positions[None, None, :]).astype(jnp.int32), axis=1)


def rotate(values, positions, sign):
    half_dim = values.shape[-1] // 2
    freqs = rotary_base ** (-jnp.arange(half_dim, dtype=jnp.float32) / half_dim)
    angles = positions.astype(jnp.float32)[:, None, None] * freqs
    cosine = jnp.cos(angles)
    sine = sign * jnp.sin(angles)
    first_half = values[..., :half_dim]
    second_half = values[..., half_dim:]
    return jnp.concatenate(
        [first_half * cosine - second_half * sine, second_half * cosine + first_half * sine],
        axis=-1,
    )


def row_pair(first_sum, second_sum):
    return lax.psum((first_sum, second_sum), "head")


def normalize(share, gain, bias):
    row_total, row_square = row_pair(jnp.sum(share, axis=-1), jnp.sum(share * share, axis=-1))
    mean_value = row_total / D
    inv_std = lax.rsqrt(row_square / D - mean_value * mean_value + norm_eps)
    centered = (share - mean_value[..., None]) * inv_std[..., None]
    scaled = (centered * gain + bias).astype(jnp.bfloat16)
    gathered = lax.all_gather(scaled, "head", axis=3, tiled=True)
    return (gathered, centered, inv_std)


def norm_backward(partial_value, gain, centered, inv_std):
    share = lax.psum_scatter(partial_value, "head", scatter_dimension=3, tiled=True)
    scaled = share * gain
    first_mean, second_mean = row_pair(
        jnp.sum(scaled, axis=-1), jnp.sum(scaled * centered, axis=-1)
    )
    grad_in = inv_std[..., None] * (
        scaled - first_mean[..., None] / D - centered * (second_mean[..., None] / D)
    )
    gain_grad = jnp.sum(share * centered, axis=(0, 1, 2))
    bias_grad = jnp.sum(share, axis=(0, 1, 2))
    return (grad_in, gain_grad, bias_grad)


def branch_total(partial_value):
    return lax.psum_scatter(partial_value, "head", scatter_dimension=3, tiled=True)


def gradient_rows(share):
    return lax.all_gather(share, "head", axis=3, tiled=True)


def mask_rule(query_pos, query_seg, key_pos, key_seg):
    query_block = (query_pos // BLOCK)[:, None]
    key_block = (key_pos // BLOCK)[None, :]
    order = jnp.stack([key_block < query_block, key_block <= query_block])
    same_doc = query_seg[:, :, None] == key_seg[:, None, :]
    return jnp.logical_and(order[None, :, None], same_doc[:, None, None])


def absorb(state_now, scores, allowed, value_piece):
    run_max, run_sum, run_acc = state_now
    masked = jnp.where(allowed, scores, masked_score)
    new_max = jnp.maximum(run_max, jnp.max(masked, axis=-1))
    weights_now = jnp.where(allowed, jnp.exp(masked - new_max[..., None]), 0.0)
    factor = jnp.exp(run_max - new_max)
    new_sum = run_sum * factor + jnp.sum(weights_now, axis=-1)
    added = jnp.einsum(
        "schlk,skhd->schld",
        weights_now,
        value_piece.astype(jnp.float32),
        precision=lax.Precision.HIGHEST,
    )
    return (new_max, new_sum, run_acc * factor[..., None] + added)


def gathered_body(
    inputs,
    doc_lengths,
    attn_gain,
    attn_bias,
    w_qkv,
    w_out,
    ffn_gain,
    ffn_bias,
    w_up,
    w_down,
    cotangent,
):
    seqs_here, _, local_len, _ = inputs.shape
    head_local = w_qkv.shape[2] // HEAD_DIM
    first_pos = lax.axis_index("seq") * local_len
    positions = first_pos + jnp.arange(local_len, dtype=jnp.int32)
    segments = segment_ids(doc_lengths, positions)
    inputs_wide = inputs.astype(jnp.float32)
    normed_one, centered_one, inv_one = normalize(inputs_wide, attn_gain, attn_bias)
    projected = jnp.einsum("scld,dtk->scltk", normed_one, w_qkv, preferred_element_type=jnp.float32)
    split_rows = projected.reshape(seqs_here, 2, local_len, 3, head_local, HEAD_DIM)
    queries = (rotate(split_rows[:, :, :, 0], positions, 1.0) * HEAD_DIM ** (-0.5)).astype(
        jnp.bfloat16
    )
    key_rows = rotate(split_rows[:, :, :, 1], positions, 1.0).astype(jnp.bfloat16)
    value_rows = split_rows[:, :, :, 2].astype(jnp.bfloat16)
    clean_keys = key_rows[:, 1].reshape(seqs_here, local_len, head_local * HEAD_DIM)
    clean_values = value_rows[:, 1].reshape(seqs_here, local_len, head_local * HEAD_DIM)
    block_ids = positions // BLOCK
    own_allowed = jnp.logical_and(
        (block_ids[:, None] == block_ids[None, :])[None],
        segments[:, :, None] == segments[:, None, :],
    )[:, None, None]
    noisy_scores = jnp.einsum(
        "sclhd,skhd->schlk", queries[:, :1], key_rows[:, 0], preferred_element_type=jnp.float32
    )
    half_shape = (seqs_here, 1, head_local, local_len)
    empty_state = (
        jnp.full(half_shape, masked_score, jnp.float32),
        jnp.zeros(half_shape, jnp.float32),
        jnp.zeros(half_shape + (HEAD_DIM,), jnp.float32),
    )
    noisy_state = absorb(empty_state, noisy_scores, own_allowed, value_rows[:, 0])
    start_state = jax.tree.map(
        lambda first, second: jnp.concatenate([first, second], axis=1), noisy_state, empty_state
    )
    piece_keys = lax.all_gather(clean_keys, "seq", axis=1, tiled=True)
    piece_values = lax.all_gather(clean_values, "seq", axis=1, tiled=True)
    piece_len = piece_keys.shape[1]
    key_pos = jnp.arange(piece_len, dtype=jnp.int32)
    key_seg = segment_ids(doc_lengths, key_pos)
    key_heads = piece_keys.reshape(seqs_here, piece_len, head_local, HEAD_DIM)
    value_heads = piece_values.reshape(seqs_here, piece_len, head_local, HEAD_DIM)
    scores = jnp.einsum("sclhd,skhd->schlk", queries, key_heads, preferred_element_type=jnp.float32)
    final_max, final_sum, final_acc = absorb(
        start_state, scores, mask_rule(positions, segments, key_pos, key_seg), value_heads
    )
    attended = final_acc / final_sum[..., None]
    log_total = final_max + jnp.log(final_sum)
    attended_low = attended.astype(jnp.bfloat16)
    out_heads = w_out.reshape(head_local, HEAD_DIM, w_out.shape[1])
    attn_share = branch_total(
        jnp.einsum("schld,hdm->sclm", attended_low, out_heads, preferred_element_type=jnp.float32)
    )
    hidden_res = inputs_wide + attn_share
    normed_two, centered_two, inv_two = normalize(hidden_res, ffn_gain, ffn_bias)
    up_value = jnp.einsum("scld,df->sclf", normed_two, w_up, preferred_element_type=jnp.float32)
    activated, gelu_back = jax.vjp(lambda inner: jax.nn.gelu(inner, approximate=True), up_value)
    act_low = activated.astype(jnp.bfloat16)
    ffn_share = branch_total(
        jnp.einsum("sclf,fm->sclm", act_low, w_down, preferred_element_type=jnp.float32)
    )
    outputs = (hidden_res + ffn_share).astype(jnp.bfloat16)
    grad_out = cotangent.astype(jnp.float32)
    grad_full = gradient_rows(cotangent)
    down_grad = jnp.einsum("sclf,sclm->fm", act_low, grad_full, preferred_element_type=jnp.float32)
    act_grad = jnp.einsum("sclm,fm->sclf", grad_full, w_down, preferred_element_type=jnp.float32)
    up_pre_grad = gelu_back(act_grad)[0].astype(jnp.bfloat16)
    up_grad = jnp.einsum(
        "scld,sclf->df", normed_two, up_pre_grad, preferred_element_type=jnp.float32
    )
    normed_two_grad = jnp.einsum(
        "sclf,df->scld", up_pre_grad, w_up, preferred_element_type=jnp.float32
    )
    back_two, ffn_gain_grad, ffn_bias_grad = norm_backward(
        normed_two_grad, ffn_gain, centered_two, inv_two
    )
    resid_grad = grad_out + back_two
    resid_full = gradient_rows(resid_grad.astype(jnp.bfloat16))
    out_grad = jnp.einsum(
        "schld,sclm->hdm", attended_low, resid_full, preferred_element_type=jnp.float32
    ).reshape(w_out.shape)
    attended_grad = jnp.einsum(
        "sclm,hdm->schld", resid_full, out_heads, preferred_element_type=jnp.float32
    ).astype(jnp.bfloat16)
    grad_wide = attended_grad.astype(jnp.float32)
    row_delta = jnp.sum(grad_wide * attended, axis=-1)
    noisy_probs = jnp.where(own_allowed, jnp.exp(noisy_scores - log_total[:, :1, :, :, None]), 0.0)
    noisy_prob_grad = jnp.einsum(
        "schld,skhd->schlk",
        attended_grad[:, :1],
        value_rows[:, 0],
        preferred_element_type=jnp.float32,
    )
    noisy_score_grad = (noisy_probs * (noisy_prob_grad - row_delta[:, :1, :, :, None])).astype(
        jnp.bfloat16
    )
    noisy_query_grad = jnp.einsum(
        "schlk,skhd->schld", noisy_score_grad, key_rows[:, 0], preferred_element_type=jnp.float32
    )
    noisy_key_grad = jnp.einsum(
        "schlk,sclhd->skhd", noisy_score_grad, queries[:, :1], preferred_element_type=jnp.float32
    )
    noisy_value_grad = jnp.einsum(
        "schlk,schld->skhd", noisy_probs, grad_wide[:, :1], precision=lax.Precision.HIGHEST
    )
    query_start = jnp.concatenate([noisy_query_grad, jnp.zeros_like(noisy_query_grad)], axis=1)
    flat_zero = jnp.zeros((seqs_here, local_len, head_local * HEAD_DIM), jnp.float32)

    def piece_grads(piece_keys, piece_values, first_row, query_total):
        key_pos = first_row + jnp.arange(local_len, dtype=jnp.int32)
        key_seg = segment_ids(doc_lengths, key_pos)
        key_heads = piece_keys.reshape(seqs_here, local_len, head_local, HEAD_DIM)
        value_heads = piece_values.reshape(seqs_here, local_len, head_local, HEAD_DIM)
        scores = jnp.einsum(
            "sclhd,skhd->schlk", queries, key_heads, preferred_element_type=jnp.float32
        )
        allowed = mask_rule(positions, segments, key_pos, key_seg)
        weights_now = jnp.where(allowed, jnp.exp(scores - log_total[..., None]), 0.0)
        prob_grad = jnp.einsum(
            "schld,skhd->schlk", attended_grad, value_heads, preferred_element_type=jnp.float32
        )
        score_grad = (weights_now * (prob_grad - row_delta[..., None])).astype(jnp.bfloat16)
        query_out = query_total + jnp.einsum(
            "schlk,skhd->schld", score_grad, key_heads, preferred_element_type=jnp.float32
        )
        key_part = jnp.einsum(
            "schlk,sclhd->skhd", score_grad, queries, preferred_element_type=jnp.float32
        )
        value_part = jnp.einsum(
            "schlk,schld->skhd", weights_now, grad_wide, precision=lax.Precision.HIGHEST
        )
        return (key_part.reshape(flat_zero.shape), value_part.reshape(flat_zero.shape), query_out)

    def cycle_body(cycle_step, carried):
        piece_keys, piece_values, key_acc, value_acc, query_acc = carried
        source = (lax.axis_index("seq") - cycle_step) % lax.axis_size("seq")
        first_row = source * local_len
        key_part, value_part, query_acc = piece_grads(
            piece_keys, piece_values, first_row, query_acc
        )
        key_acc = key_acc + key_part
        value_acc = value_acc + value_part
        piece_keys, piece_values = passed_along((piece_keys, piece_values), "seq", 1)
        key_acc, value_acc = (
            from_behind(key_acc.astype(jnp.bfloat16), "seq", 1).astype(key_acc.dtype),
            from_behind(value_acc.astype(jnp.bfloat16), "seq", 1).astype(value_acc.dtype),
        )
        return (piece_keys, piece_values, key_acc, value_acc, query_acc)

    cycle_start = (clean_keys, clean_values, flat_zero, flat_zero, query_start)
    _, _, clean_key_grad, clean_value_grad, query_acc = lax.fori_loop(
        0, lax.axis_size("seq"), cycle_body, cycle_start
    )
    head_shape = (seqs_here, local_len, head_local, HEAD_DIM)
    query_total = rotate(jnp.transpose(query_acc, (0, 1, 3, 2, 4)), positions, -1.0) * HEAD_DIM ** (
        -0.5
    )
    key_total = rotate(
        jnp.stack([noisy_key_grad, clean_key_grad.reshape(head_shape)], axis=1), positions, -1.0
    )
    value_total = jnp.stack([noisy_value_grad, clean_value_grad.reshape(head_shape)], axis=1)
    qkv_pre_grad = (
        jnp.stack([query_total, key_total, value_total], axis=3)
        .reshape(seqs_here, 2, local_len, 3, head_local * HEAD_DIM)
        .astype(jnp.bfloat16)
    )
    qkv_grad = jnp.einsum(
        "scld,scltk->dtk", normed_one, qkv_pre_grad, preferred_element_type=jnp.float32
    )
    normed_one_grad = jnp.einsum(
        "scltk,dtk->scld", qkv_pre_grad, w_qkv, preferred_element_type=jnp.float32
    )
    back_one, attn_gain_grad, attn_bias_grad = norm_backward(
        normed_one_grad, attn_gain, centered_one, inv_one
    )
    input_grad = resid_grad + back_one
    (
        qkv_grad,
        out_grad,
        up_grad,
        down_grad,
        attn_gain_grad,
        attn_bias_grad,
        ffn_gain_grad,
        ffn_bias_grad,
    ) = lax.psum(
        (
            qkv_grad,
            out_grad,
            up_grad,
            down_grad,
            attn_gain_grad,
            attn_bias_grad,
            ffn_gain_grad,
            ffn_bias_grad,
        ),
        "seq",
    )
    return (
        outputs,
        input_grad,
        qkv_grad,
        out_grad,
        up_grad,
        down_grad,
        attn_gain_grad,
        attn_bias_grad,
        ffn_gain_grad,
        ffn_bias_grad,
    )


def dot(a, b, ca, cb):
    return lax.dot_general(a, b, (((ca,), (cb,)), ((), ())), preferred_element_type=F32)


def remote(src, dst, send, recv, device):
    return pltpu.make_async_remote_copy(
        src_ref=src, dst_ref=dst, send_sem=send, recv_sem=recv, device_id=device, device_id_type=MESH
    )


class Place:
    def __init__(self, n):
        self.n = n
        self.me = lax.axis_index("seq")
        self.head = lax.axis_index("head")
        self.core = lax.rem(self.head, 2)
        self.y = lax.div(self.head, 2)
        self.sib = (self.me, self.y * 2 + 1 - self.core)
        self.yp = (self.me, (1 - self.y) * 2 + self.core)
        self.diag = (self.me, (1 - self.y) * 2 + 1 - self.core)
        self.half = n // 2
        self.band = max(1, n // 8)

    def lowest(self, slot, i):
        near = i - self.band
        short = jnp.where(i >= self.half, jnp.minimum(near, self.half), near)
        return jnp.where(slot == LONG_SLOT, 0, jnp.maximum(short, 0))

    def spot(self, slot, block, other):
        window = self.half + self.band
        near = self.half + lax.rem(other, self.band)
        late = jnp.where(block >= self.half, other - self.half, near)
        order = slot - jnp.where(slot > LONG_SLOT, 1, 0)
        return jnp.where(slot == LONG_SLOT, other, self.n + order * window + late)

    def spots(self, slots):
        return self.n + (slots - 1) * (self.half + self.band)

    def greet(self, near, everyone):
        bar = pltpu.get_barrier_semaphore()
        for d in near:
            pl.semaphore_signal(bar, inc=1, device_id=d, device_id_type=MESH)
        count = len(near)
        if everyone:
            for d in range(1, self.n):
                there = lax.rem(self.me + d, self.n)
                pl.semaphore_signal(bar, inc=1, device_id=(there, self.head), device_id_type=MESH)
            count += self.n - 1
        pl.semaphore_wait(bar, count)


def each(count, step):
    def run(i, carry):
        step(i)
        return carry

    lax.fori_loop(0, count, run, 0)


def row_stats(x):
    mean = jnp.sum(x, axis=1, keepdims=True) / D
    var = jnp.sum(x * x, axis=1, keepdims=True) / D - mean * mean
    return mean, lax.rsqrt(var + norm_eps)


def whole_rows(ref, s):
    return jnp.concatenate([ref[s, 0], ref[s, 1]], axis=1)


def turn(v, cosine, sine):
    parts = []
    for h in range(v.shape[0] // HEAD_DIM):
        a = v[h * 64 : h * 64 + 32]
        b = v[h * 64 + 32 : h * 64 + 64]
        parts += [a * cosine - b * sine, b * cosine + a * sine]
    return jnp.concatenate(parts, axis=0)


def masks(me, length, start, end):
    shape = (length, 2 * length)
    key = lax.broadcasted_iota(jnp.int32, shape, 0)
    row = lax.broadcasted_iota(jnp.int32, shape, 1)
    noisy = row < length
    at = jnp.where(noisy, row, row - length)
    key_block = key >> 4
    row_block = at >> 4
    pos = key + me * length
    same = jnp.logical_and(pos >= start, pos < end)
    clean = jnp.logical_and(same, key_block < row_block + jnp.where(noisy, 0, 1))
    own = jnp.logical_and(same, key_block == row_block)[:, :length]
    return clean, own


class Sum:
    def __init__(self, at, src, res, gx, part, gz, own, xs, xr, zs, zr, cs, cr, fs, fr, ls, ds):
        self.m = at.n // 2
        self.lo = lax.rem(at.me, 2)
        self.hi = lax.div(at.me, 2)
        self.head = at.head
        self.pair = (at.me + 1 - 2 * self.lo, at.head)
        self.src, self.res, self.gx, self.part, self.gz = src, res, gx, part, gz
        self.xs, self.xr, self.zs, self.zr = xs, xr, zs, zr
        self.cs, self.cr, self.fs, self.fr, self.ls, self.ds = cs, cr, fs, fr, ls, ds
        self.pieces = ds.shape[0]
        self.own = own

    def piece(self, half, k):
        size = self.gx.shape[1]
        return half, pl.ds(pl.multiple_of(k * size, 16), size)

    def at_z(self, k):
        return (2 * k + self.lo, self.head)

    def x(self, k):
        return remote(self.src.at[self.piece(1 - self.lo, k)], self.gx.at[k], self.xs.at[k], self.xr.at[k], self.pair)

    def z(self, k):
        return remote(self.part.at[k], self.gz.at[self.hi], self.zs.at[k], self.zr.at[self.hi], self.at_z(k))

    def z_in(self, k):
        return remote(self.part.at[k], self.gz.at[k], self.zs.at[k], self.zr.at[k], self.at_z(k))

    def piece_of(self, k, p):
        size = self.gx.shape[1] // self.pieces
        return pl.ds(p * size, size)

    def c_own(self, p, step):
        rows = self.piece_of(self.hi, p)
        there = self.res.at[self.lo, self.hi, rows]
        sent = self.cs.at[self.hi, p] if step > 0 else self.ds.at[p]
        return remote(self.own.at[rows], there, sent, self.cr.at[self.hi, p], self.at_z(self.hi + step))

    def c_on(self, k, p, step):
        part = self.res.at[self.lo, k, self.piece_of(k, p)]
        return remote(part, part, self.cs.at[k, p], self.cr.at[k, p], self.at_z(self.hi + step))

    def f(self, k, p):
        part = self.res.at[self.lo, k, self.piece_of(k, p)]
        return remote(part, part, self.fs.at[k, p], self.fr.at[k, p], self.pair)

    def f_own(self, p):
        rows = self.piece_of(self.hi, p)
        there = self.res.at[self.lo, self.hi, rows]
        return remote(self.own.at[rows], there, self.fs.at[self.hi, p], self.fr.at[self.hi, p], self.pair)

    def keep(self):
        return pltpu.make_async_copy(self.own, self.res.at[self.lo, self.hi], self.ls)

    def others(self):
        return [lax.rem(self.hi + d, self.m) for d in range(1, self.m)]

    def turn_of(self, i):
        return lax.rem(self.hi + 1 + i, self.m)

    def begin(self):
        each(self.m, lambda i: self.x(self.turn_of(i)).start())

    def pass_on(self, i):
        k = self.turn_of(i)
        self.x(k).wait_recv()
        self.part[k] = (self.src[self.piece(self.lo, k)].astype(F32) + self.gx[k].astype(F32)).astype(BF16)

        @pl.when(k != self.hi)
        def _():
            self.z(k).start()

    def ends(self, step, run):
        there = self.hi + step
        pl.when(jnp.logical_and(there >= 0, there < self.m))(run)

    def reduce(self):
        total = self.part[self.hi].astype(F32)
        for k in self.others():
            self.z_in(k).wait_recv()
            total += self.gz[k].astype(F32)
        self.own[...] = total.astype(BF16)
        self.keep().start()
        for p in range(self.pieces):
            self.ends(1, lambda: self.c_own(p, 1).start())
            self.ends(-1, lambda: self.c_own(p, -1).start())
            self.f_own(p).start()

    def forward(self, d):
        for p in range(self.pieces):
            for step in (1, -1):

                def run():
                    k = self.hi - step * d
                    self.c_on(k, p, step).wait_recv()
                    self.ends(step, lambda: self.c_on(k, p, step).start())
                    self.f(k, p).start()

                self.ends(-step * d, run)

    def finish(self):
        each(self.m, lambda k: self.x(k).wait_send())
        for k in self.others():
            self.z(k).wait_send()
        for p in range(self.pieces):
            for step in (1, -1):
                self.ends(step, lambda: self.c_own(p, step).wait_send())
                for d in range(1, self.m):

                    def run():
                        k = self.hi - step * d
                        self.ends(step, lambda: self.c_on(k, p, step).wait_send())
                        self.f(k, p).wait_send()

                    self.ends(-step * d, run)
            self.f_own(p).wait_send()
            each(self.m, lambda k: self.f(k, p).wait_recv())
        self.keep().wait()


def layer(n, names, *refs):
    r = types.SimpleNamespace(**dict(zip(names, refs)))
    at = Place(n)
    slots, rows, feat = r.x_in.shape
    length = rows // 2
    half = 2 * feat
    hl = feat // HEAD_DIM
    m = n // 2
    core, y, me = at.core, at.y, at.me
    mine = pl.ds(length * core, length)
    other = pl.ds(length * (1 - core), length)
    early, late = slice(0, length), slice(length, rows)
    heads = [slice(h * HEAD_DIM, (h + 1) * HEAD_DIM) for h in range(hl)]
    fulls = (r.xg, r.cg, r.ag)
    owns = (r.x_in, r.c_in, r.own_att)
    lands = (r.land.at[0], r.land.at[1], r.land.at[0])
    quarter = D // m
    sum1 = Sum(
        at, r.gl, r.res1, r.gx1, r.act.at[:m, :quarter], r.gz1, r.own1, *[getattr(r, "u%d" % i) for i in range(10)]
    )
    src2 = r.act.at[m : m + 2, :feat]
    sum2 = Sum(at, src2, r.res2.at[:2], r.gx2, r.pt2, r.gz2, r.own2, *[getattr(r, "v%d" % i) for i in range(10)])
    sum3 = Sum(at, r.src3, r.res2.at[2:], r.gx3, r.pt3, r.gz3, r.own3, *[getattr(r, "w%d" % i) for i in range(10)])

    def sib_copy(k, s):
        return remote(owns[k].at[s], lands[k].at[s], r.ss.at[k, s], r.sr.at[k, s], at.sib)

    def build(k, s):
        a, b = owns[k][s], lands[k][s]

        @pl.when(core == 0)
        def _():
            fulls[k][s, y] = jnp.concatenate([a, b], axis=1)

        @pl.when(core == 1)
        def _():
            fulls[k][s, y] = jnp.concatenate([b, a], axis=1)

    def y_copy(k, s):
        part = fulls[k].at[s, y, mine]
        return remote(part, part, r.ys.at[k, s], r.yr.at[k, s], at.yp)

    def f_copy(k, s):
        part = fulls[k].at[s, 1 - y, mine]
        return remote(part, part, r.fs.at[k, s], r.fr.at[k, s], at.sib)

    def kv_copy(s, i):
        return remote(r.kvo.at[s], r.kvb.at[at.spot(s, me, me)], r.ks.at[s, i], r.kr.at[s, me], (i, at.head))

    def kv_in(s, j):
        return remote(r.kvo.at[s], r.kvb.at[at.spot(s, j, j)], r.ks.at[s, j], r.kr.at[s, j], (j, at.head))

    def dkv_copy(s, j):
        return remote(
            r.kvb.at[at.spot(s, j, j)], r.dla.at[at.spot(s, j, me)], r.ds.at[s, j], r.dr.at[s, me], (j, at.head)
        )

    def dkv_in(s, i):
        here = r.dla.at[at.spot(s, me, i)]
        return remote(here, here, r.ds.at[s, i], r.dr.at[s, i], (i, at.head))

    def readers(s, step):
        for d in range(1, n):
            i = me + d

            @pl.when(jnp.logical_and(i < n, at.lowest(s, i) <= me))
            def _():
                step(i)

    def e_core(s):
        return remote(r.ep.at[s, other], r.er.at[s], r.e1s.at[s], r.e1r.at[s], at.sib)

    def e_y(s):
        return remote(r.er.at[s], r.ey.at[s], r.e2s.at[s], r.e2r.at[s], at.yp)

    def e_back(s):
        return remote(r.ey.at[s], r.eb.at[s], r.e3s.at[s], r.e3r.at[s], at.sib)

    def held(first, s, k):
        return (s, pl.ds(first, length), pl.ds(pl.multiple_of(k * half, 128), half))

    def f_core(s):
        return remote(r.ag.at[s, :, other], r.fc.at[s], r.f1s.at[s], r.f1r.at[s], at.sib)

    def f_y(s):
        return remote(r.upre.at[held(0, s, 1 - y)], r.fy.at[s], r.f2s.at[s], r.f2r.at[s], at.yp)

    def f_back(s):
        return remote(r.osd.at[s], r.out.at[s, core], r.f3s.at[s], r.f3r.at[s], at.sib)

    def b_core(s):
        return remote(r.n2.at[s, other], r.er.at[s], r.a1s.at[s], r.a1r.at[s], at.sib)

    def s_core(s):
        return remote(r.st.at[s, 1 - core], r.sl.at[s], r.b1s.at[s], r.b1r.at[s], at.sib)

    def b_y(s):
        return remote(r.upre.at[held(length, s, 1 - y)], r.bey.at[s], r.a2s.at[s], r.a2r.at[s], at.yp)

    def s_y(s):
        return remote(r.sh.at[s], r.sy.at[s], r.b2s.at[s], r.b2r.at[s], at.yp)

    def b_back(s):
        return remote(r.isd.at[s], r.ig.at[s, core], r.a3s.at[s], r.a3r.at[s], at.sib)

    at.greet([at.sib, at.yp, at.diag], True)
    each(slots, lambda s: sib_copy(0, s).start())
    r.gb_in[...] = jnp.zeros_like(r.gb_in)
    for i, vector in enumerate((r.ga, r.ba, r.gf_in, r.bf_in)):
        r.gb_in[i : i + 1] = vector[...]
    r.gland[at.head] = r.gb_in[...]
    g_copies = [
        remote(r.gb_in, r.gland.at[at.head], r.gs.at[k], r.gr.at[k], d)
        for k, d in enumerate((at.sib, at.yp, at.diag))
    ]
    for copy in g_copies:
        copy.start()

    def first_y(s):
        sib_copy(0, s).wait_recv()
        build(0, s)
        y_copy(0, s).start()

    each(slots, first_y)

    def wo_block(who):
        return r.wog.at[pl.ds(pl.multiple_of(feat * who, 16), feat)]

    wo_sib = remote(r.wo_in, wo_block(at.head), r.ws.at[0], r.wr.at[0], at.sib)
    wo_y = remote(r.wo_in, wo_block(at.head), r.ws.at[1], r.wr.at[1], at.yp)
    wo_f = remote(wo_block(at.yp[1]), wo_block(at.yp[1]), r.ws.at[2], r.wr.at[2], at.sib)
    wo_y.start()
    wo_sib.start()
    each(slots, lambda s: sib_copy(1, s).start())
    r.wog[pl.ds(pl.multiple_of(feat * at.head, 16), feat)] = r.wo_in[...]
    for copy in g_copies:
        copy.wait()
    r.gbf[...] = jnp.concatenate([r.gland[i] for i in range(4)], axis=1)
    r.cos[...] = jnp.concatenate([r.cos_in[...]] * 2, axis=1)
    r.sin[...] = jnp.concatenate([r.sin_in[...]] * 2, axis=1)
    long, most = 0, r.docs[0, 0]
    for i in range(1, slots):
        long = jnp.where(r.docs[i, 0] > most, i, long)
        most = jnp.maximum(r.docs[i, 0], most)
    lane = lax.broadcasted_iota(jnp.int32, (8, rows), 1)
    pos = jnp.where(lane < length, lane, lane - length) + me * length
    for s in range(slots):
        row = long if s == LONG_SLOT else jnp.where(long == s, LONG_SLOT, s)
        end = 0
        first_key, last_key = jnp.zeros_like(pos), jnp.full_like(pos, 2**30)
        for j in range(r.docs.shape[1]):
            end = end + r.docs[row, j]
            first_key = jnp.where(pos >= end, end, first_key)
            last_key = jnp.where(pos < end, jnp.minimum(last_key, end), last_key)
        r.bounds[s] = jnp.where(lax.broadcasted_iota(jnp.int32, (8, rows), 0) == 0, first_key, last_key)
    r.mrow[...] = jnp.zeros_like(r.mrow)
    r.lrow[...] = jnp.ones_like(r.lrow)
    r.og[...] = jnp.zeros_like(r.og)
    r.qq[...] = jnp.zeros_like(r.qq)
    r.qkv[...] = jnp.zeros_like(r.qkv)
    r.gsum[...] = jnp.zeros_like(r.gsum)
    r.gtwo[...] = jnp.zeros_like(r.gtwo)
    r.drow[...] = jnp.zeros_like(r.drow)

    def project(s):
        x = whole_rows(r.xg, s).astype(F32)
        mean, inv = row_stats(x)
        normed = ((x - mean) * inv * r.gbf[0:1] + r.gbf[1:2]).astype(BF16)
        r.n1[s] = normed
        pt = dot(r.w_t[...], normed, 1, 1)
        qk = turn(pt[:half], r.cos[...], r.sin[...])
        r.qt[s] = (qk[:feat] * HEAD_DIM**-0.5).astype(BF16)
        kv = jnp.concatenate([qk[feat:], pt[half:]], axis=0).astype(BF16)
        r.kvn[s] = kv[:, :length]
        r.kvo[s] = kv[:, length:]
        readers(s, lambda i: kv_copy(s, i).start())

    def arrive(t):
        @pl.when(t < slots)
        def _():
            y_copy(0, t).wait_recv()
            f_copy(0, t).start()

        @pl.when(t >= 1)
        def _():
            f_copy(0, t - 1).wait_recv()
            project(t - 1)

    each(slots + 1, arrive)

    def cot_on(s):
        sib_copy(1, s).wait_recv()
        build(1, s)
        y_copy(1, s).start()

    each(2, cot_on)

    def attend(s):
        start, end = r.bounds[s, 0:1], r.bounds[s, 1:2]
        clean, noisy = masks(me, length, start, end)
        kc, kn = r.kvo[s], r.kvn[s]
        q = [r.qt[s, hd] for hd in heads]
        sc = [dot(kc[hd], q[h], 0, 0) for h, hd in enumerate(heads)]
        sn = [dot(kn[hd], q[h][:, :length], 0, 0) for h, hd in enumerate(heads)]
        sc = [jnp.where(clean, v, masked_score) for v in sc]
        sn = [jnp.where(noisy, v, masked_score) for v in sn]
        top = []
        for h in range(hl):
            tc = jnp.max(sc[h], axis=0, keepdims=True)
            tn = jnp.max(sn[h], axis=0, keepdims=True)
            top.append(jnp.concatenate([jnp.maximum(tc[:, :length], tn), tc[:, length:]], axis=1))
        pc = [jnp.exp(sc[h] - top[h]) for h in range(hl)]
        pn = [jnp.exp(sn[h] - top[h][:, :length]) for h in range(hl)]
        oc = [dot(kc[feat:][hd], pc[h].astype(BF16), 1, 0) for h, hd in enumerate(heads)]
        on = [dot(kn[feat:][hd], pn[h].astype(BF16), 1, 0) for h, hd in enumerate(heads)]
        for h, hd in enumerate(heads):
            tc = jnp.sum(pc[h], axis=0, keepdims=True)
            tn = jnp.sum(pn[h], axis=0, keepdims=True)
            r.mrow[h : h + 1] = top[h]
            r.lrow[h : h + 1] = jnp.concatenate([tc[:, :length] + tn, tc[:, length:]], axis=1)
            r.acc[hd, early] = oc[h][:, :length] + on[h]
            r.acc[hd, late] = oc[h][:, length:]

        def one(j, carry):
            kv_in(s, j).wait_recv()
            kv = r.kvb[at.spot(s, j, j)]
            q = [r.qt[s, hd] for hd in heads]
            old = [r.mrow[h : h + 1] for h in range(hl)]
            total = [r.lrow[h : h + 1] for h in range(hl)]
            pos = lax.broadcasted_iota(jnp.int32, (length, rows), 0) + j * length
            allowed = pos >= start
            sc = [dot(kv[hd], q[h], 0, 0) for h, hd in enumerate(heads)]
            sc = [jnp.where(allowed, v, masked_score) for v in sc]
            new = [jnp.maximum(old[h], jnp.max(sc[h], axis=0, keepdims=True)) for h in range(hl)]
            p = [jnp.exp(sc[h] - new[h]) for h in range(hl)]
            add = [dot(kv[feat:][hd], p[h].astype(BF16), 1, 0) for h, hd in enumerate(heads)]
            scale = [jnp.exp(old[h] - new[h]) for h in range(hl)]
            for h, hd in enumerate(heads):
                r.mrow[h : h + 1] = new[h]
                r.lrow[h : h + 1] = total[h] * scale[h] + jnp.sum(p[h], axis=0, keepdims=True)
                r.acc[hd] = r.acc[hd] * scale[h] + add[h]
            return carry

        lax.fori_loop(at.lowest(s, me), me, one, 0)
        for h, hd in enumerate(heads):
            r.att[s, hd] = r.acc[hd] / r.lrow[h : h + 1]
        r.lse[s] = r.mrow[...] + jnp.log(r.lrow[...])
        r.own_att[s] = r.att[s].T.astype(BF16)
        sib_copy(2, s).start()

    def forward(s):
        x = whole_rows(r.xg, s).astype(F32)
        branch = dot(r.ag[s, 0], r.wog[:half], 1, 0) + dot(r.ag[s, 1], r.wog[half:], 1, 0)
        h = x + branch
        for yy in range(2):
            for cc in range(2):

                @pl.when(jnp.logical_and(y == yy, core == cc))
                def _():
                    r.hp[s] = h[cc * length : (cc + 1) * length, yy * half : (yy + 1) * half]

        mean, inv = row_stats(h)
        r.iv[s] = inv
        normed = ((h - mean) * inv * r.gbf[2:3] + r.gbf[3:4]).astype(BF16)
        r.n2[s] = normed
        up = dot(normed, r.wu[...], 1, 0)
        cube = 0.7978845608028654 * (up + 0.044715 * up * up * up)
        t = jnp.tanh(cube)
        r.act[s] = (0.5 * up * (1.0 + t)).astype(BF16)
        slope = 0.5 * (1.0 + t) + 0.5 * up * (1.0 - t * t) * (
            0.7978845608028654 * (1.0 + 3 * 0.044715 * up * up)
        )
        da = dot(whole_rows(r.cg, s), r.wd[...], 1, 1)
        pre = (da * slope).astype(BF16)
        r.upre[s] = pre
        r.ep[s] = dot(pre, r.wu[...], 1, 1).astype(BF16)
        e_core(s).start()

    def stage(t, offset, step):
        s = t - offset

        @pl.when(jnp.logical_and(s >= 0, s < slots))
        def _():
            step(s)

    def att_on(s):
        sib_copy(2, s).wait_recv()
        build(2, s)
        y_copy(2, s).start()

    def att_back(s):
        y_copy(2, s).wait_recv()
        f_copy(2, s).start()

    def cot_back(s):
        y_copy(1, s).wait_recv()
        f_copy(1, s).start()

    def feed(s):
        @pl.when(s == 0)
        def _():
            wo_y.wait_recv()
            wo_f.start()
            wo_sib.wait_recv()
            wo_f.wait_recv()

        f_copy(1, s).wait_recv()
        f_copy(2, s).wait_recv()
        forward(s)

    def e_on(s):
        e_core(s).wait_recv()
        r.er[s] = (r.ep[s, mine].astype(F32) + r.er[s].astype(F32)).astype(BF16)
        e_y(s).start()

    def e_total(s):
        e_y(s).wait_recv()
        r.ey[s] = (r.er[s].astype(F32) + r.ey[s].astype(F32)).astype(BF16)
        e_y(s).wait_send()
        e_back(s).start()

    def loop_one(t):
        stage(t, 1, att_on)

        @pl.when(jnp.logical_and(t >= 1, t < slots - 1))
        def _():
            cot_on(t + 1)

        stage(t, 2, cot_back)
        stage(t, 2, att_back)

        @pl.when(t == slots)
        def _():
            e_on(LONG_SLOT)
            each(LONG_SLOT, e_on)

        @pl.when(t == slots + 1)
        def _():
            e_on(slots - 2)

        stage(t, 0, attend)
        stage(t, 2, feed)

    each(slots + 2, loop_one)

    wide = slots * rows

    def up_tile(i):
        cols = pl.ds(pl.multiple_of(i * 256, 256), 256)
        left = r.n2[...].reshape(wide, D)
        part = dot(left, r.upre[:, :, cols].reshape(wide, 256), 0, 0).astype(BF16)
        r.gl[0, :, cols] = part

    def down_tile(i):
        cols = pl.ds(pl.multiple_of(lax.rem(i, 3) * 128, 128), 128)
        out_cols = pl.ds(pl.multiple_of(i * 128, 128), 128)
        left = r.act[...].reshape(wide, D)
        part = dot(left, r.cg[:, lax.div(i, 3), :, cols].reshape(wide, 128), 0, 0).astype(BF16)
        r.gl[1, :, out_cols] = part

    def long_first(t):
        return jnp.where(t == 0, LONG_SLOT, jnp.where(t <= LONG_SLOT, t - 1, t))

    e_on(slots - 1)
    @pl.when(sum1.lo == 0)
    def _():
        each(D // 128, down_tile)
        sum1.begin()
        each(D // 256, up_tile)

    @pl.when(sum1.lo == 1)
    def _():
        each(D // 256, up_tile)
        sum1.begin()
        each(D // 128, down_tile)

    e_total(long_first(0))
    e_total(long_first(1))

    def two_back(s):
        e_back(s).wait_recv()
        e_back(s).wait_send()
        e_core(s).wait_send()

        @pl.when(core == 0)
        def _():
            r.ep[s, early] = r.ey[s]
            r.ep[s, late] = r.eb[s]

        @pl.when(core == 1)
        def _():
            r.ep[s, early] = r.eb[s]
            r.ep[s, late] = r.ey[s]

        e = r.ep[s].astype(F32)
        xh = (r.n2[s].astype(F32) - r.gbf[3:4]) * r.ginv[0:1]
        r.gtwo[2:3] += jnp.sum(e * xh, axis=0, keepdims=True)
        r.gtwo[3:4] += jnp.sum(e, axis=0, keepdims=True)
        g = e * r.gbf[2:3]
        first = jnp.sum(g, axis=1, keepdims=True) / D
        second = jnp.sum(g * xh, axis=1, keepdims=True) / D
        resid = whole_rows(r.cg, s).astype(F32) + r.iv[s] * (g - first - xh * second)
        r.ep[s] = resid.astype(BF16)

    r.ginv[...] = 1.0 / r.gbf[2:3] + jnp.zeros_like(r.ginv)

    def head_grads(s, kv, lanes, allowed):
        q = [r.qt[s, hd, lanes] for hd in heads]
        d_out = [r.do[hd, lanes] for hd in heads]
        sc = [dot(kv[hd], q[h], 0, 0) for h, hd in enumerate(heads)]
        dp = [dot(kv[feat:][hd], d_out[h], 0, 0) for h, hd in enumerate(heads)]
        p = [
            jnp.exp(jnp.where(allowed, sc[h], masked_score) - r.lse[s, h : h + 1, lanes])
            for h in range(hl)
        ]
        ds = [(p[h] * (dp[h] - r.drow[h : h + 1, lanes])).astype(BF16) for h in range(hl)]
        dv = [dot(d_out[h], p[h].astype(BF16), 1, 1) for h in range(hl)]
        dk = [dot(q[h], ds[h], 1, 1) for h in range(hl)]
        dq_add = [dot(kv[hd], ds[h], 1, 0) for h, hd in enumerate(heads)]
        return [jnp.concatenate(v, axis=0) for v in (dq_add, dk, dv)]

    def attend_back(s):
        low_rows = r.ep[s]
        d_out = dot(r.wo_in[...], low_rows, 1, 1).astype(BF16)
        r.do[...] = d_out
        a = r.att[s]
        r.og[...] += dot(a.astype(BF16), low_rows, 1, 0)
        prod = d_out.astype(F32) * a
        for h, hd in enumerate(heads):
            r.drow[h : h + 1] = jnp.sum(prod[hd], axis=0, keepdims=True)
        start, end = r.bounds[s, 0:1], r.bounds[s, 1:2]
        clean, noisy = masks(me, length, start, end)
        dqa, dk, dv = head_grads(s, r.kvo[s], slice(0, rows), clean)
        dqn, dkn, dvn = head_grads(s, r.kvn[s], early, noisy)
        r.acc[...] = dqa
        r.acc[:, early] += dqn
        r.dkv[s, :feat] = dk
        r.dkv[s, feat:] = dv
        r.qp[s, half:, early] = dvn.astype(BF16)
        r.qp[s, feat:half, early] = turn(dkn, r.cos[:, :length], -r.sin[:, :length]).astype(BF16)

        def one(j, carry):
            spot = at.spot(s, j, j)
            kv = r.kvb[spot]
            pos = lax.broadcasted_iota(jnp.int32, (length, rows), 0) + j * length
            dqa, dk, dv = head_grads(s, kv, slice(0, rows), pos >= start)
            r.acc[...] += dqa
            r.kvb[spot, :feat] = dk.astype(BF16)
            r.kvb[spot, feat:] = dv.astype(BF16)
            dkv_copy(s, j).start()
            return carry

        lax.fori_loop(at.lowest(s, me), me, one, 0)
        r.qp[s, :feat] = (turn(r.acc[...], r.cos[...], -r.sin[...]) * HEAD_DIM**-0.5).astype(BF16)
        r.qq[...] += dot(r.qp[s, :feat], r.n1[s], 1, 0)

    def f_start(s):
        y_copy(2, s).wait_send()
        f_copy(2, s).wait_send()
        ff = dot(r.act[s], r.wd[...], 1, 0)
        r.ag[s, 0] = ff[:, :half].astype(BF16)
        r.ag[s, 1] = ff[:, half:].astype(BF16)
        f_core(s).start()

    def f_on(s):
        f_core(s).wait_recv()
        for k in range(2):
            r.upre[held(0, s, k)] = (r.ag[s, k, mine].astype(F32) + r.fc[s, k].astype(F32)).astype(BF16)
        f_y(s).start()

    def f_end(s):
        f_y(s).wait_recv()
        total = r.hp[s] + (r.upre[held(0, s, y)].astype(F32) + r.fy[s].astype(F32))
        turned = total.T.astype(BF16)
        lo, hi = turned[:feat], turned[feat:]

        @pl.when(core == 0)
        def _():
            r.out[s, 0] = lo
            r.osd[s] = hi

        @pl.when(core == 1)
        def _():
            r.out[s, 1] = hi
            r.osd[s] = lo

        f_back(s).start()

    def loop_two(t):
        def run(s):
            two_back(s)
            attend_back(s)

        stage(t, 1, lambda s: f_on(long_first(s)))
        stage(t, -2, lambda s: e_total(long_first(s)))
        stage(t, 0, lambda s: run(long_first(s)))

        @pl.when(jnp.logical_or(t == 3, t == 5))
        def _():
            sum1.pass_on(lax.div(t - 3, 2))

    each(slots, f_start)
    each(slots, loop_two)
    src2[0] = r.og[...].astype(BF16)
    src2[1] = r.qq[...].astype(BF16)
    sum2.begin()
    f_on(slots - 1)
    sum1.pass_on(2)
    sum1.pass_on(3)

    def project_back(s):
        def add(i):
            dkv_in(s, i).wait_recv()
            r.dkv[s] += r.dla[at.spot(s, me, i)].astype(F32)

        readers(s, add)
        total = r.dkv[s]
        r.qp[s, feat:half, late] = turn(total[:feat], r.cos[:, late], -r.sin[:, late]).astype(BF16)
        r.qp[s, half:, late] = total[feat:].astype(BF16)
        pre = r.qp[s]
        r.qkv[...] += dot(pre[feat:], r.n1[s], 1, 0)
        e = dot(pre, r.w_t[...], 0, 0)
        x = whole_rows(r.xg, s).astype(F32)
        mean, inv = row_stats(x)
        xh = (x - mean) * inv
        r.gsum[0:1] += jnp.sum(e * xh, axis=0, keepdims=True)
        r.gsum[1:2] += jnp.sum(e, axis=0, keepdims=True)
        r.n2[s] = e.astype(BF16)
        g = e * r.gbf[0:1]
        one_sum = jnp.sum(g, axis=1, keepdims=True)
        two_sum = jnp.sum(g * xh, axis=1, keepdims=True)
        lane = lax.broadcasted_iota(jnp.int32, (rows, 128), 1)
        packed = jnp.where(lane == 0, one_sum, jnp.where(lane == 1, two_sum, 0.0)).T
        r.st[s, 0] = packed[:8, :length]
        r.st[s, 1] = packed[:8, length:]
        b_core(s).start()
        s_core(s).start()

    def b_on(s):
        b_core(s).wait_recv()
        s_core(s).wait_recv()
        both = r.n2[s, mine].astype(F32) + r.er[s].astype(F32)
        r.upre[s, late] = both.astype(BF16)
        r.sh[s] = r.st[s, core] + r.sl[s]
        b_y(s).start()
        s_y(s).start()

    def b_end(s):
        b_y(s).wait_recv()
        s_y(s).wait_recv()
        e = r.upre[held(length, s, y)].astype(F32) + r.bey[s].astype(F32)
        sums = r.sh[s] + r.sy[s]
        cols = jnp.concatenate([sums, jnp.zeros((120, length), F32)], axis=0).T
        first, second = cols[:, 0:1] / D, cols[:, 1:2] / D
        x = jnp.concatenate([r.xg[s, 0, mine], r.xg[s, 1, mine]], axis=1).astype(F32)
        mean, inv = row_stats(x)
        xh = (r.xg[s, y, mine].astype(F32) - mean) * inv
        gain = jnp.where(y == 0, r.gbf[0:1, :half], r.gbf[0:1, half:])
        resid = r.ep[s, mine].astype(F32)
        resid = jnp.where(y == 0, resid[:, :half], resid[:, half:])
        grad = resid + inv * (e * gain - first - xh * second)
        turned = grad.T
        lo, hi = turned[:feat], turned[feat:]

        @pl.when(core == 0)
        def _():
            r.ig[s, 0] = lo
            r.isd[s] = hi

        @pl.when(core == 1)
        def _():
            r.ig[s, 1] = hi
            r.isd[s] = lo

        b_back(s).start()

    def loop_three(t):
        stage(t, 0, f_end)
        stage(t, 1, b_on)
        stage(t, 0, project_back)

        pl.when(t == 2)(sum1.reduce)

        @pl.when(jnp.logical_or(t == 3, t == 4))
        def _():
            sum2.pass_on(2 * t - 6)
            sum2.pass_on(2 * t - 5)

    each(slots, loop_three)
    grads = r.qkv[...].astype(BF16)
    r.src3[0] = grads[:feat]
    r.src3[1] = grads[feat:]
    sum3.begin()
    b_on(slots - 1)
    h_copies = [
        remote(r.gsum, r.gh.at[k], r.hs.at[k], r.hr.at[k], d)
        for k, d in enumerate((at.sib, at.yp, at.diag))
    ]
    for copy in h_copies:
        copy.start()
    sum2.reduce()

    def share(i):
        return remote(r.gf, r.gq.at[me], r.qs.at[i], r.qr.at[me], (i, at.head))

    def share_in(i):
        return remote(r.gf, r.gq.at[i], r.qs.at[i], r.qr.at[i], (i, at.head))

    def gains_on():
        for copy in h_copies:
            copy.wait()
        total = r.gsum[...] + r.gh[0] + r.gh[1] + r.gh[2] + r.gtwo[...]
        for h in range(4):

            @pl.when(at.head == h)
            def _():
                r.gf[...] = total[:, h * feat : (h + 1) * feat]

        r.gq[me] = r.gf[...]
        for d in range(1, n):
            share(lax.rem(me + d, n)).start()

    def loop_four(t):
        stage(t, 0, b_end)
        pl.when(t == 0)(gains_on)

        @pl.when(jnp.logical_or(t == 1, t >= 4))
        def _():
            sum1.forward(jnp.where(t == 1, 1, t - 2))

        @pl.when(jnp.logical_or(t == 2, t == 3))
        def _():
            sum3.pass_on(2 * t - 4)
            sum3.pass_on(2 * t - 3)

    each(slots, loop_four)
    sum3.reduce()
    for d in range(1, n):
        share_in(lax.rem(me + d, n)).wait_recv()
    r.gains[...] = jnp.sum(r.gq[...], axis=0)
    for d in range(1, m):
        sum2.forward(d)
    for d in range(1, m):
        sum3.forward(d)

    def finish(s):
        for k in range(3):
            sib_copy(k, s).wait_send()
        for k in range(2):
            y_copy(k, s).wait_send()
            f_copy(k, s).wait_send()
        readers(s, lambda i: kv_copy(s, i).wait_send())
        f_core(s).wait_send()
        f_y(s).wait_send()
        f_back(s).wait()
        b_core(s).wait_send()
        s_core(s).wait_send()
        b_y(s).wait_send()
        s_y(s).wait_send()
        b_back(s).wait()

        def sent(j, carry):
            dkv_copy(s, j).wait_send()
            return carry

        lax.fori_loop(at.lowest(s, me), me, sent, 0)

    each(slots, finish)
    wo_sib.wait_send()
    wo_y.wait_send()
    wo_f.wait_send()
    for part in (sum1, sum2, sum3):
        part.finish()
    for d in range(1, n):
        share(lax.rem(me + d, n)).wait_send()


def body(
    inputs,
    doc_lengths,
    attn_gain,
    attn_bias,
    w_qkv,
    w_out,
    ffn_gain,
    ffn_bias,
    w_up,
    w_down,
    cotangent,
):
    n = lax.axis_size("seq")
    slots, _, length, feat = inputs.shape
    rows, half, m = 2 * length, 2 * feat, n // 2
    held = slots * n * half * length * 2
    if held > ROWS_LIMIT or n != 8:
        return gathered_body(
            inputs, doc_lengths, attn_gain, attn_bias, w_qkv, w_out, ffn_gain, ffn_bias, w_up, w_down, cotangent
        )
    me = lax.axis_index("seq")
    long = jnp.argmax(doc_lengths[:, 0]).astype(jnp.int32)
    ids = jnp.arange(slots, dtype=jnp.int32)

    def swap(v):
        pick = lax.dynamic_index_in_dim(v, long, 0, keepdims=True)
        where = ids.reshape((slots,) + (1,) * (v.ndim - 1))
        kept = v[LONG_SLOT : LONG_SLOT + 1]
        return jnp.where(where == LONG_SLOT, pick, jnp.where(where == long, kept, v))

    positions = me * length + jnp.arange(length, dtype=jnp.int32)
    half_dim = HEAD_DIM // 2
    freqs = rotary_base ** (-jnp.arange(half_dim, dtype=F32) / half_dim)
    angles = freqs[:, None] * positions.astype(F32)[None, :]
    w_t = w_qkv.reshape(D, 3 * feat).T
    operands = dict(
        x_in=swap(inputs.reshape(slots, rows, feat)), c_in=swap(cotangent.reshape(slots, rows, feat)),
        ga=attn_gain[None], ba=attn_bias[None], gf_in=ffn_gain[None], bf_in=ffn_bias[None],
        w_t=w_t, wo_in=w_out, wu=w_up, wd=w_down, cos_in=jnp.cos(angles), sin_in=jnp.sin(angles), docs=doc_lengths,
    )
    small = (m, feat // m, D)
    quarter = (m, D // m, D)
    outs = dict(
        out=((slots, 2, feat, length), BF16), ig=((slots, 2, feat, length), F32), res1=((2, *quarter), BF16),
        res2=((4, *small), BF16), gains=((8, feat), F32),
    )
    blocks = n + (slots - 1) * (n // 2 + max(1, n // 8))
    full, wide = (slots, 2, rows, half), (slots, rows, D)
    part, stat = (slots, length, D), (slots, 8, length)
    halves, own_half = (slots, 2, length, half), (slots, length, half)
    buffers = dict(
        land=((2, slots, rows, feat), BF16), own_att=((slots, rows, feat), BF16), gland=((4, 8, feat), F32),
        gbf=((8, D), F32), ginv=((8, D), F32), xg=(full, BF16), cg=(full, BF16), ag=(full, BF16),
        wog=((D, D), BF16), n1=(wide, BF16), qt=((slots, feat, rows), BF16),
        kvn=((slots, half, length), BF16), kvo=((slots, half, length), BF16), kvb=((blocks, half, length), BF16),
        att=((slots, feat, rows), F32), lse=((slots, 8, rows), F32), acc=((feat, rows), F32),
        mrow=((8, rows), F32), lrow=((8, rows), F32), hp=(own_half, F32), iv=((slots, rows, 1), F32),
        n2=(wide, BF16), act=(wide, BF16), upre=(wide, BF16), ep=(wide, BF16), er=(part, BF16), ey=(part, BF16),
        eb=(part, BF16), fc=(halves, BF16), fy=(own_half, BF16),
        osd=((slots, feat, length), BF16), gl=((2, D, D), BF16), gx1=(quarter, BF16), gz1=(quarter, BF16),
        own1=(quarter[1:], BF16), do=((feat, rows), BF16), drow=((8, rows), F32),
        dkv=((slots, half, length), F32), dla=((blocks, half, length), BF16), qp=((slots, 3 * feat, rows), BF16),
        og=((feat, D), F32), qq=((feat, D), F32), qkv=((half, D), F32), gsum=((8, D), F32), gtwo=((8, D), F32),
        st=((slots, 2, 8, length), F32), sl=(stat, F32), sh=(stat, F32), sy=(stat, F32),
        bey=(own_half, BF16), isd=((slots, feat, length), F32), src3=((2, feat, D), BF16),
        gx2=(small, BF16), pt2=(small, BF16), gz2=(small, BF16), own2=(small[1:], BF16),
        gx3=(small, BF16), pt3=(small, BF16), gz3=(small, BF16), own3=(small[1:], BF16),
        gb_in=((8, feat), F32), cos=((half_dim, rows), F32), sin=((half_dim, rows), F32),
        bounds=((slots, 8, rows), jnp.int32), gh=((3, 8, D), F32), gq=((n, 8, feat), F32), gf=((8, feat), F32),
    )
    sems = {k: (3, slots) for k in ("ss", "sr", "ys", "yr", "fs", "fr")}
    sems |= {k: (3,) for k in ("gs", "gr", "ws", "wr", "hs", "hr")}
    sems |= {k: (slots, n) for k in ("ks", "kr", "ds", "dr")}
    sems |= {k + i + e: (slots,) for k in "efab" for i in "123" for e in "sr" if k + i != "b3"}
    sems |= {"qs": (n,), "qr": (n,)}
    pieces = {"u": 4, "v": 1, "w": 1}
    sems |= {"%s%d" % (k, i): (m,) for k in "uvw" for i in range(4)}
    sems |= {"%s%d" % (k, i): (m, pieces[k]) for k in "uvw" for i in range(4, 8)}
    sems |= {k + "9": (pieces[k],) for k in "uvw"}
    sem = pltpu.SemaphoreType.DMA
    scratch = {k: VMEM(*v) for k, v in buffers.items()}
    scratch |= {k: sem(v) for k, v in sems.items()}
    scratch |= {k + "8": sem for k in "uvw"}
    vmem = pl.BlockSpec(memory_space=VMEM)
    names = [*operands, *outs, *scratch]
    got = pl.pallas_call(
        functools.partial(layer, n, names),
        out_shape=[jax.ShapeDtypeStruct(*v) for v in outs.values()],
        in_specs=[pl.BlockSpec(memory_space=pltpu.SMEM) if k == "docs" else vmem for k in operands],
        out_specs=[pl.BlockSpec(memory_space=pl.ANY) if k.startswith("res") else vmem for k in outs],
        scratch_shapes=list(scratch.values()),
        compiler_params=pltpu.CompilerParams(
            collective_id=0, has_side_effects=True, vmem_limit_bytes=VMEM_LIMIT
        ),
        name="layer",
    )(*operands.values())
    outputs, input_grad, res1, res2, gain_grads = got
    up_grad, down_grad = res1.reshape(2, D, D).astype(F32)
    small_grads = res2.reshape(4, feat, D)
    out_grad = small_grads[0].astype(F32)
    qkv_grad = small_grads[1:].astype(F32)
    return (
        jnp.swapaxes(swap(outputs), 2, 3),
        jnp.swapaxes(swap(input_grad), 2, 3),
        jnp.transpose(qkv_grad, (2, 0, 1)),
        out_grad,
        up_grad,
        down_grad,
        gain_grads[0],
        gain_grads[1],
        gain_grads[2],
        gain_grads[3],
    )


def solution(mesh):
    in_specs = (
        P(None, None, "seq", "head"),
        P(),
        P("head"),
        P("head"),
        P(None, None, "head"),
        P("head", None),
        P("head"),
        P("head"),
        P(None, "head"),
        P("head", None),
        P(None, None, "seq", "head"),
    )
    out_specs = (
        P(None, None, "seq", "head"),
        P(None, None, "seq", "head"),
        P(None, None, "head"),
        P("head", None),
        P(None, "head"),
        P("head", None),
        P("head"),
        P("head"),
        P("head"),
        P("head"),
    )
    return jax.shard_map(body, mesh=mesh, in_specs=in_specs, out_specs=out_specs, check_vma=False)
```
